32 devices in a mesh: wide: 16 (over z, y, core), narrow: 2 (over x).
Axes of the slice: x: 2, y: 2, z: 4, core: 2. Of those that a mesh axis runs over, the one named last changes fastest.
Arguments:
- lifted_field: bfloat16 [16, 32, 16, 128], P('wide', None, 'narrow'), may hold values from -6 to 6
- spectral_weight: float32 [256, 16, 2, 32, 32], P('wide', 'narrow'), may hold values from -0.75 to 0.75
- mix_weight: bfloat16 [32, 32], replicated, may hold values from -1 to 1
- mix_bias: float32 [32], replicated, may hold values from -3 to 3
- head_weight: bfloat16 [32, 128], replicated, may hold values from -1 to 1
- head_bias: float32 [128], replicated, may hold values from -3 to 3
- out_weight: bfloat16 [128], replicated, may hold values from -0.5 to 0.5
- cotangent: float32 [16, 16, 128], P('wide', 'narrow'), may hold values from -6 to 6
Outputs:
- prediction: float32 [16, 16, 128], P('wide', 'narrow')
- grad_field: bfloat16 [16, 32, 16, 128], P('wide', None, 'narrow')
- grad_spectral: float32 [256, 16, 2, 32, 32], P('wide', 'narrow')
- grad_mix: float32 [32, 32], replicated
- grad_head: float32 [32, 128], replicated
The draws below stay inside these ranges and needn't reach their ends.
All inputs are finite; a program needn't handle non-finite values.
Results may differ from the reference program's by a relative error of at most 0.018.
Values may be sent and summed in bfloat16 or wider, within the bound.
No kernel may reach another device: no remote copies, remote signals or barrier semaphores. Data moves between devices by JAX's collectives and lax.ppermute only.
A program may use at most 64 MiB of HBM per device.

```python
import math
import jax
import jax.numpy as jnp
from jax import lax

C = 32
HID = 128
MX = 16
MY = 16
MZ = 16
NZ = 128
NX = 16
NY = 16


def plane_wave(number_key, offset_key, wave_count, length, lowest, highest):
    number = jax.random.randint(number_key, (wave_count, C, 1), lowest, highest, dtype=jnp.int32)
    positions = jnp.arange(length, dtype=jnp.int32)[None, None, :]
    turned = jnp.mod(number * positions, length).astype(jnp.float32) * (2.0 * math.pi / length)
    offsets = jax.random.uniform(offset_key, (wave_count, C, 1), jnp.float32, -math.pi, math.pi)
    return jnp.cos(turned + offsets)


def draw_lifted_field(base_key, part):
    subkeys = jax.random.split(base_key, 8)
    wave_count = 6
    rough_part = 0.8 * jnp.clip(jax.random.normal(subkeys[0], (NX, C, NY, NZ), jnp.float32), -4.0, 4.0)
    amplitude = jax.random.uniform(subkeys[1], (wave_count, C), jnp.float32, -0.4, 0.4)
    along_x = plane_wave(subkeys[2], subkeys[5], wave_count, NX, -7, 8)
    along_y = plane_wave(subkeys[3], subkeys[6], wave_count, NY, -7, 8)
    along_z = plane_wave(subkeys[4], subkeys[7], wave_count, NZ, 0, 16)
    summed = rough_part
    for wave_index in range(wave_count):
        x_part = jnp.transpose(along_x[wave_index])[:, :, None, None]
        y_part = (amplitude[wave_index][:, None] * along_y[wave_index])[None, :, :, None]
        z_part = along_z[wave_index][None, :, None, :]
        summed = summed + x_part * y_part * z_part
    return summed.astype(jnp.bfloat16)


def level_of(own_key, dims, shards, smallest, largest):
    factor_of, own = 1.0, jax.random.fold_in(own_key, 6)
    for position, parts in shards:
        steps = jnp.exp(jax.random.uniform(jax.random.fold_in(own, position), (parts,), jnp.float32, smallest / len(shards), largest / len(shards)))
        factor_of = factor_of * jnp.repeat(steps, dims[position] // parts).reshape([-1 if axis == position else 1 for axis in range(len(dims))])
    return factor_of


def noise(own_key, extent, spread, limit, cuts=(), held_as=jnp.bfloat16):
    values = jax.random.normal(own_key, extent, jnp.float32) * spread
    if len(cuts) > 0:
        values = level_of(own_key, extent, cuts, -0.22, 0.18) * values
    return jnp.clip(values, min=-limit, max=limit).astype(held_as)


def setup_inputs(seed: int = 0) -> dict:
    key_list = jax.random.split(jax.random.key(seed), 9)
    lifted_field = draw_lifted_field(jax.random.fold_in(key_list[8], 71), 0)
    spectral_weight = noise(key_list[1], (MX * MY, MZ, 2, C, C), (2 * C) ** -0.5, 0.75, ((0, 16), (1, 2)), jnp.float32)
    mix_weight = noise(key_list[2], (C, C), C ** -0.5, 1.0)
    mix_bias = noise(key_list[3], (C,), 0.5, 3.0, (), jnp.float32)
    head_weight = noise(key_list[4], (C, HID), C ** -0.5, 1.0)
    head_bias = noise(key_list[5], (HID,), 0.5, 3.0, (), jnp.float32)
    out_weight = noise(key_list[6], (HID,), HID ** -0.5, 0.5)
    cotangent = noise(key_list[7], (NX, NY, NZ), 1.0, 6.0, ((0, 16), (1, 2)), jnp.float32)
    return {"lifted_field": lifted_field, "spectral_weight": spectral_weight, "mix_weight": mix_weight, "mix_bias": mix_bias, "head_weight": head_weight, "head_bias": head_bias, "out_weight": out_weight, "cotangent": cotangent}


HIGHEST_PRECISION = lax.Precision.HIGHEST

def round_half(values):
    return lax.optimization_barrier(values.astype(jnp.bfloat16)).astype(jnp.float32)

def signed_freq(indices, kept_count):
    return jnp.where(indices < kept_count // 2, indices, indices - kept_count)

def phases(positions, frequency, length):
    turned = jnp.mod(positions[:, None] * frequency[None, :], length)
    return turned.astype(jnp.float32) * (2.0 * math.pi / length)

def real_forward(positions, length, kept_count, doubled):
    indices = jnp.arange(kept_count, dtype=jnp.int32)
    angles = phases(positions, indices, length)
    if doubled:
        scaling = 1.0 + (indices > 0).astype(jnp.float32)
    else:
        scaling = jnp.ones((kept_count,), jnp.float32)
    scaling = scaling * (1.0 / math.sqrt(length))
    return jnp.stack([jnp.cos(angles) * scaling, -jnp.sin(angles) * scaling], axis=1)

def real_inverse(positions, length, kept_count, doubled):
    return jnp.transpose(real_forward(positions, length, kept_count, doubled), (2, 1, 0))

def complex_forward(positions, frequency, length):
    angles = phases(positions, frequency, length)
    cosine = jnp.cos(angles) * (1.0 / math.sqrt(length))
    sine = jnp.sin(angles) * (1.0 / math.sqrt(length))
    return jnp.stack([jnp.stack([cosine, sine]), jnp.stack([-sine, cosine])])

def complex_inverse(positions, frequency, length):
    angles = phases(positions, frequency, length)
    cosine = jnp.transpose(jnp.cos(angles)) * (1.0 / math.sqrt(length))
    sine = jnp.transpose(jnp.sin(angles)) * (1.0 / math.sqrt(length))
    return jnp.stack([jnp.stack([cosine, -sine]), jnp.stack([sine, cosine])])

def activation(values):
    return jax.nn.gelu(values, approximate=False)

def activation_slope(values):
    cumulative = 0.5 * (1.0 + lax.erf(values * (1.0 / math.sqrt(2.0))))
    return cumulative + values * jnp.exp(-0.5 * values * values) * (1.0 / math.sqrt(2.0 * math.pi))

def mode_forward(spectrum, weights):
    real_part = spectrum[:, :, 0]
    imag_part = spectrum[:, :, 1]
    real_weight = weights[:, :, 0]
    imag_weight = weights[:, :, 1]

    def combine(spectrum_part, weight_part):
        return jnp.einsum('mki,mkio->mko', spectrum_part, weight_part, precision=HIGHEST_PRECISION)
    out_real = combine(real_part, real_weight) - combine(imag_part, imag_weight)
    out_imag = combine(imag_part, real_weight) + combine(real_part, imag_weight)
    return jnp.stack([out_real, out_imag], axis=2)

def mode_backward(spectrum, weights, gradient):
    real_part = spectrum[:, :, 0]
    imag_part = spectrum[:, :, 1]
    real_weight = weights[:, :, 0]
    imag_weight = weights[:, :, 1]
    real_grad = gradient[:, :, 0]
    imag_grad = gradient[:, :, 1]

    def pulled(weight_part, grad_part):
        return jnp.einsum('mkio,mko->mki', weight_part, grad_part, precision=HIGHEST_PRECISION)

    def product(spectrum_part, grad_part):
        return jnp.einsum('mki,mko->mkio', spectrum_part, grad_part, precision=HIGHEST_PRECISION)
    back_real = pulled(real_weight, real_grad) + pulled(imag_weight, imag_grad)
    back_imag = pulled(real_weight, imag_grad) - pulled(imag_weight, real_grad)
    weight_real = product(real_part, real_grad) + product(imag_part, imag_grad)
    weight_imag = product(real_part, imag_grad) - product(imag_part, real_grad)
    return (jnp.stack([back_real, back_imag], axis=2), jnp.stack([weight_real, weight_imag], axis=2))

def analysis(values, doubled):
    z_table = round_half(real_forward(jnp.arange(NZ, dtype=jnp.int32), NZ, MZ, doubled))
    y_table = round_half(complex_forward(jnp.arange(NY, dtype=jnp.int32), signed_freq(jnp.arange(MY, dtype=jnp.int32), MY), NY))
    x_table = complex_forward(jnp.arange(NX, dtype=jnp.int32), signed_freq(jnp.arange(MX, dtype=jnp.int32), MX), NX)

    def one_row(field_row):
        return jnp.einsum('cyz,zrk->krcy', field_row.astype(jnp.float32), z_table, precision=HIGHEST_PRECISION).astype(jnp.bfloat16)
    row_spectra = lax.map(one_row, values)
    planes = jnp.einsum('xkrcn,srnj->kscxj', row_spectra.astype(jnp.float32), y_table, precision=HIGHEST_PRECISION)
    spectrum = jnp.einsum('kscxj,tsxi->ijktc', planes, x_table, precision=HIGHEST_PRECISION)
    return spectrum.reshape(MX * MY, MZ, 2, C)

def synthesis(spectrum, doubled):
    z_table = round_half(real_inverse(jnp.arange(NZ, dtype=jnp.int32), NZ, MZ, doubled))
    y_table = round_half(complex_inverse(jnp.arange(NY, dtype=jnp.int32), signed_freq(jnp.arange(MY, dtype=jnp.int32), MY), NY))
    x_table = round_half(complex_inverse(jnp.arange(NX, dtype=jnp.int32), signed_freq(jnp.arange(MX, dtype=jnp.int32), MX), NX))
    grid_modes = spectrum.astype(jnp.float32).reshape(MX, MY, MZ, 2, C)
    planes = round_half(jnp.einsum('ijkrc,srix->kscxj', grid_modes, x_table, precision=HIGHEST_PRECISION))
    line_data = round_half(jnp.einsum('krcxj,srjn->xkscn', planes, y_table, precision=HIGHEST_PRECISION))
    return (line_data, z_table)

def reference(lifted_field, spectral_weight, mix_weight, mix_bias, head_weight, head_bias, out_weight, cotangent):
    mix_float = mix_weight.astype(jnp.float32)
    head_float = head_weight.astype(jnp.float32)
    out_float = out_weight.astype(jnp.float32)

    def branch_of(line_row, z_table):
        return jnp.einsum('krcn,krz->cnz', line_row, z_table, precision=HIGHEST_PRECISION)
    spectrum = analysis(lifted_field, False)
    lines_fwd, forward_z = synthesis(mode_forward(spectrum, spectral_weight).astype(jnp.bfloat16), True)

    def head_rows(row_items):
        field_row, line_row, target_row = row_items
        field_float = field_row.astype(jnp.float32)
        mixed = jnp.einsum('cyz,cd->dyz', field_float, mix_float, precision=HIGHEST_PRECISION)
        pre_act = branch_of(line_row, forward_z) + mixed + mix_bias[:, None, None]
        hidden = activation(pre_act).astype(jnp.bfloat16).astype(jnp.float32)
        head_pre = jnp.einsum('cyz,cj->jyz', hidden, head_float, precision=HIGHEST_PRECISION) + head_bias[:, None, None]
        active = round_half(activation(head_pre))
        predicted = jnp.einsum('jyz,j->yz', active, out_float, precision=HIGHEST_PRECISION)
        head_slope = round_half(target_row[None] * out_float[:, None, None] * activation_slope(head_pre))
        returned = jnp.einsum('jyz,cj->cyz', head_slope, head_float, precision=HIGHEST_PRECISION)
        grad_row = (returned * activation_slope(pre_act)).astype(jnp.bfloat16)
        head_grad = jnp.einsum('cyz,jyz->cj', hidden, head_slope, precision=HIGHEST_PRECISION)
        mix_grad = jnp.einsum('cyz,dyz->cd', field_float, grad_row.astype(jnp.float32), precision=HIGHEST_PRECISION)
        return (predicted, grad_row, head_grad, mix_grad)
    prediction, grad_pre, head_parts, mix_parts = lax.map(head_rows, (lifted_field, lines_fwd, cotangent))
    adjoint = analysis(grad_pre, True)
    back_modes, grad_spectral = mode_backward(spectrum, spectral_weight, adjoint)
    lines_back, adjoint_z = synthesis(back_modes.astype(jnp.bfloat16), False)

    def back_rows(row_items):
        back_row, grad_row = row_items
        through = branch_of(back_row, adjoint_z) + jnp.einsum('dyz,cd->cyz', grad_row.astype(jnp.float32), mix_float, precision=HIGHEST_PRECISION)
        return through.astype(jnp.bfloat16)
    grad_field = lax.map(back_rows, (lines_back, grad_pre))
    grad_mix = lax.optimization_barrier(jnp.sum(mix_parts, axis=0))
    grad_head = lax.optimization_barrier(jnp.sum(head_parts, axis=0))
    return (prediction, grad_field, grad_spectral, grad_mix, grad_head)
```

```python
import functools
import math

import jax
import jax.numpy as jnp
import numpy as np
from jax import lax
from jax.experimental import pallas as pl
from jax.experimental.pallas import tpu as pltpu
from jax.sharding import PartitionSpec as P

MX = 16
MY = 16
MZ = 16
F32 = jnp.float32
BF16 = jnp.bfloat16
VMEM_LIMIT = 32 * 1024 * 1024


def signed(indices, count):
    return np.where(indices < count // 2, indices, indices - count)


def wave(positions, frequency, length):
    turned = np.mod(np.multiply.outer(positions, frequency), length)
    angles = turned.astype(np.float32) * np.float32(2.0 * math.pi / length)
    scale = np.float32(1.0 / math.sqrt(length))
    return np.cos(angles) * scale, np.sin(angles) * scale


def z_table(length, doubled):
    cosine, sine = wave(np.arange(length), np.arange(MZ), length)
    table = np.stack([cosine.T, -sine.T], axis=1)
    if doubled:
        table[1:] *= 2.0
    return table.reshape(2 * MZ, length).astype(BF16)


def pair(cosine, sine, sign):
    return np.stack(
        [np.stack([cosine, -sign * sine], -1), np.stack([sign * sine, cosine], -1)], -2
    )


def y_tables(total_y, rows_y, kz, modes):
    cosine, sine = wave(np.arange(total_y), signed(np.arange(MY), MY), total_y)
    narrow = total_y // rows_y
    same = np.eye(kz, dtype=np.float32)
    forward = pair(cosine, sine, -1.0).reshape(narrow, rows_y, MY // modes, modes, 2, 2)
    inverse = pair(cosine, sine, 1.0).reshape(narrow, rows_y, MY // modes, modes, 2, 2)
    forward = np.einsum("nybjtr,kl->bjtkynlr", forward, same)
    inverse = np.einsum("nybjst,kl->bnyksjtl", inverse, same)
    blocks = MY // modes
    forward = forward.reshape(blocks, modes * 2 * kz, rows_y * narrow * kz * 2)
    inverse = inverse.reshape(blocks, narrow * rows_y * kz * 2, modes * 2 * kz)
    return forward.astype(BF16), inverse.astype(BF16)


def x_rows(total_x, wide, modes):
    cosine, sine = wave(np.arange(total_x), signed(np.arange(MX), MX), total_x)
    owner_freq = np.arange(wide) * modes // MY
    forward = pair(cosine, sine, -1.0)[:, owner_freq]
    inverse = pair(cosine, sine, 1.0)[:, owner_freq]
    forward = np.transpose(forward, (1, 2, 0, 3))
    inverse = np.transpose(inverse, (0, 2, 1, 3))

    def spread(table):
        shape = (wide, 2, wide, MZ, 2)
        return np.broadcast_to(table[:, :, :, None, :], shape).reshape(wide, 2, wide * MZ * 2)

    return spread(forward).astype(np.float32), spread(inverse).astype(np.float32)


def dot(a, b):
    return jnp.dot(a, b, preferred_element_type=F32)


def dot_nt(a, b):
    return lax.dot_general(a, b, (((1,), (1,)), ((), ())), preferred_element_type=F32)


def dot_tn(a, b):
    return lax.dot_general(a, b, (((0,), (0,)), ((), ())), preferred_element_type=F32)


def iota(shape, axis):
    return lax.broadcasted_iota(jnp.int32, shape, axis)


def halves(values):
    high = values.astype(BF16)
    return high, (values - high.astype(F32)).astype(BF16)


def x_matrix(rows):
    shape = (2 * MZ, rows.shape[1])
    row, column = iota(shape, 0), iota(shape, 1)
    same = (row >> 1) == ((column >> 1) & (MZ - 1))
    value = jnp.where((row & 1) == 0, rows[0:1], rows[1:2])
    return jnp.where(same, value, 0.0)


def analysed(pieces, rows, y_forward, copies, channels):
    high, low = halves(x_matrix(rows))
    turned = dot(high, pieces) + dot(low, pieces)
    rows_y = turned.shape[1] // channels
    lines = jnp.concatenate(
        [turned[:, y * channels : (y + 1) * channels] for y in range(rows_y)], axis=0
    )
    high, low = halves(jnp.concatenate([lines] * copies, axis=1))
    return dot(y_forward, high) + dot(y_forward, low)


def spread_lines(modes, y_inverse, narrow, rows_y):
    lines = dot(y_inverse, modes)
    step = lines.shape[0] // (narrow * rows_y)
    blocks = []
    for n in range(narrow):
        parts = [
            lines[(n * rows_y + y) * step : (n * rows_y + y + 1) * step] for y in range(rows_y)
        ]
        blocks.append(jnp.concatenate(parts, axis=1))
    return jnp.concatenate(blocks, axis=0).astype(BF16)


def repeat_rows(out_ref, block, lanes):
    height = block.shape[0]
    for w in range(out_ref.shape[0] // height):
        out_ref[w * height : (w + 1) * height, :lanes] = block


def selector(shape, condition):
    return jnp.where(condition(iota(shape, 0), iota(shape, 1)), 1.0, 0.0).astype(BF16)


def start_kernel(field_ref, turn_ref, table_ref, send_ref, field_out_ref):
    turned = dot(turn_ref[...], field_ref[...]).astype(BF16)
    field_out_ref[...] = turned
    spectra = dot_nt(table_ref[...], turned).astype(BF16)
    repeat_rows(send_ref, spectra, spectra.shape[1])


def weight_kernel(weight_ref, out_ref):
    _, kz, _, channels, _ = weight_ref.shape
    both = jnp.concatenate([weight_ref[0, :, 0], weight_ref[0, :, 1]], axis=-1)
    out_ref[0] = both.reshape(kz * channels, 2 * channels).astype(BF16)


def mode_kernel(
    narrow, pieces_ref, rows_ref, y_forward_ref, y_inverse_ref, weight_ref, spectrum_ref, send_ref
):
    modes, depth, width = weight_ref.shape
    channels = width // 2
    kz = depth // channels
    rows_y = pieces_ref.shape[1] // channels
    spectrum = analysed(pieces_ref[...], rows_ref[...], y_forward_ref[...], kz, channels)
    spectrum_ref[...] = spectrum[:, :channels]
    row, lane = iota(spectrum.shape, 0), iota(spectrum.shape, 1)
    blocked = jnp.where(row % kz == lane // channels, spectrum, 0.0)
    mixed = []
    for j in range(modes):
        left = blocked[j * 2 * kz : (j + 1) * 2 * kz].astype(BF16)
        product = dot(left, weight_ref[j])
        real, imag = product[:, :channels], product[:, channels:]
        mixed.append(real[:kz] - imag[kz:])
        mixed.append(imag[:kz] + real[kz:])
    mode = jnp.concatenate(mixed, axis=0).astype(BF16)
    block = spread_lines(mode, y_inverse_ref[...], narrow, rows_y)
    repeat_rows(send_ref, block, block.shape[1])


def cell_kernel(
    kz,
    pieces_ref,
    rows_ref,
    z_doubled_ref,
    field_ref,
    mix_ref,
    mix_bias_ref,
    head_ref,
    head_bias_ref,
    out_weight_ref,
    cotangent_ref,
    prediction_ref,
    grad_pre_ref,
    send_ref,
):
    channels = mix_ref.shape[0]
    hidden_units = head_ref.shape[1]
    rows_y = cotangent_ref.shape[0]
    lines = dot(x_matrix(rows_ref[...]).astype(BF16), pieces_ref[...]).astype(BF16)
    branch = dot_tn(lines, z_doubled_ref[...])
    mix, head = mix_ref[...], head_ref[...]
    mix_bias, head_bias = mix_bias_ref[...], head_bias_ref[...]
    out_weight = out_weight_ref[...]
    grad_mix = jnp.zeros((channels, channels), F32)
    grad_head = jnp.zeros((channels, hidden_units), F32)
    gradients = []

    def normal(values):
        cumulative = 0.5 * (1.0 + lax.erf(values * (1.0 / math.sqrt(2.0))))
        density = jnp.exp(-0.5 * values * values) * (1.0 / math.sqrt(2.0 * math.pi))
        return values * cumulative, cumulative + values * density

    for y in range(rows_y):
        cells = slice(y * channels, (y + 1) * channels)
        field = field_ref[cells]
        pre_act = branch[cells] + dot_tn(mix, field) + mix_bias
        hidden, pre_slope = normal(pre_act)
        hidden = hidden.astype(BF16)
        head_pre = dot_tn(head, hidden) + head_bias
        active, slope = normal(head_pre)
        active = active.astype(BF16).astype(F32)
        prediction_ref[y : y + 1] = jnp.sum(active * out_weight, axis=0, keepdims=True)
        head_slope = (cotangent_ref[y : y + 1] * out_weight * slope).astype(BF16)
        grad_pre = (dot(head, head_slope) * pre_slope).astype(BF16)
        grad_head += dot_nt(hidden, head_slope)
        grad_mix += dot_nt(field, grad_pre)
        gradients.append(grad_pre)

    gradient = jnp.concatenate(gradients, axis=0)
    grad_pre_ref[...] = gradient
    spectra = dot_nt(z_doubled_ref[...], gradient).astype(BF16)
    width = spectra.shape[1]
    repeat_rows(send_ref, spectra, width)
    wide_mix = jnp.concatenate(
        [grad_mix, jnp.zeros((channels, hidden_units - channels), F32)], axis=1
    )
    shares = jnp.concatenate([*halves(grad_head), *halves(wide_mix)], axis=0)
    piece = 2 * kz
    place = selector(
        (send_ref.shape[0], 4 * channels),
        lambda row, column: (row // piece == column % channels)
        & (row % piece == column // channels),
    )
    send_ref[:, width:] = dot(place, shares).astype(BF16)


def back_kernel(
    narrow,
    pieces_ref,
    rows_ref,
    y_forward_ref,
    y_inverse_ref,
    weight_ref,
    adjoint_ref,
    send_ref,
):
    modes, depth, width = weight_ref.shape
    channels = width // 2
    kz = depth // channels
    lanes = pieces_ref.shape[1] - 4 * channels
    rows_y = lanes // channels
    pieces = pieces_ref[:, :lanes]
    adjoint = analysed(pieces, rows_ref[...], y_forward_ref[...], 1, channels)
    adjoint_ref[...] = adjoint
    pulled = []
    for j in range(modes):
        real = adjoint[j * 2 * kz : j * 2 * kz + kz]
        imag = adjoint[j * 2 * kz + kz : (j + 1) * 2 * kz]
        left = jnp.concatenate(
            [jnp.concatenate([real, imag], axis=1), jnp.concatenate([imag, -real], axis=1)], axis=0
        )
        pulled.append(dot_nt(left.astype(BF16), weight_ref[j]))
    pulled = jnp.concatenate(pulled, axis=0)
    row, lane = iota(pulled.shape, 0), iota(pulled.shape, 1)
    pulled = jnp.where(row % kz == lane // channels, pulled, 0.0).astype(BF16)
    fold = selector((depth, channels), lambda row, column: row % channels == column)
    modes_back = dot(pulled, fold).astype(BF16)
    block = spread_lines(modes_back, y_inverse_ref[...], narrow, rows_y)
    repeat_rows(send_ref, block, lanes)
    piece = 2 * kz
    add = selector(
        (8, pieces_ref.shape[0]),
        lambda row, column: (row < 2) & ((column % piece) // 2 == row),
    )
    total = dot(add, pieces_ref[:, lanes:])
    total_high, total_low = halves(total[0:2])
    share = jnp.concatenate([total_high.astype(F32), total_low.astype(F32)], axis=0)
    if piece > 4:
        share = jnp.concatenate([share, jnp.zeros((piece - 4, share.shape[1]), F32)], axis=0)
    share = share.astype(BF16)
    for p in range(send_ref.shape[0] // piece):
        send_ref[p * piece : (p + 1) * piece, lanes:] = share


def outer_kernel(spectrum_ref, adjoint_ref, out_ref):
    kz = out_ref.shape[1]
    columns = jnp.transpose(spectrum_ref[0])
    adjoint = adjoint_ref[0]
    for k in range(kz):
        s_real, s_imag = columns[:, k : k + 1], columns[:, kz + k : kz + k + 1]
        a_real, a_imag = adjoint[k : k + 1], adjoint[kz + k : kz + k + 1]
        out_ref[0, k, 0] = s_real * a_real + s_imag * a_imag
        out_ref[0, k, 1] = s_real * a_imag - s_imag * a_real


def finish_kernel(
    kz,
    pieces_ref,
    rows_ref,
    z_table_ref,
    grad_pre_ref,
    mix_ref,
    turn_ref,
    grad_field_ref,
    grad_mix_ref,
    grad_head_ref,
):
    channels = mix_ref.shape[0]
    lanes = pieces_ref.shape[1] - 4 * channels
    rows_y = lanes // channels
    lines = dot(x_matrix(rows_ref[...]).astype(BF16), pieces_ref[:, :lanes]).astype(BF16)
    branch = dot_tn(lines, z_table_ref[...])
    parts = []
    for y in range(rows_y):
        cells = slice(y * channels, (y + 1) * channels)
        parts.append((branch[cells] + dot(mix_ref[...], grad_pre_ref[cells])).astype(BF16))
    grad_field_ref[...] = dot_tn(turn_ref[...], jnp.concatenate(parts, axis=0)).astype(BF16)
    piece = 2 * kz
    shares = pieces_ref[:, lanes:]

    def picked(first):
        shape = (channels, shares.shape[0])
        return dot(
            selector(
                shape,
                lambda row, column: (column // piece == row)
                & ((column % piece == first) | (column % piece == first + 2)),
            ),
            shares,
        )

    grad_head_ref[...] = picked(0)
    grad_mix_ref[...] = picked(1)[:, :channels]


def call(kernel, outs, name, flops=1 << 22):
    return pl.pallas_call(
        kernel,
        out_shape=[jax.ShapeDtypeStruct(shape, dtype) for shape, dtype in outs],
        compiler_params=pltpu.CompilerParams(vmem_limit_bytes=VMEM_LIMIT),
        cost_estimate=pl.CostEstimate(flops=flops, bytes_accessed=1 << 19, transcendentals=0),
        name=name,
    )


def body(
    lifted_field,
    spectral_weight,
    mix_weight,
    mix_bias,
    head_weight,
    head_bias,
    out_weight,
    cotangent,
):
    wide = lax.axis_size("wide")
    narrow = lax.axis_size("narrow")
    _, channels, rows_y, z_count = lifted_field.shape
    modes, kz = spectral_weight.shape[:2]
    hidden_units = head_weight.shape[1]
    total_x, total_y = wide, rows_y * narrow
    index = lax.axis_index("wide")
    cells = channels * rows_y
    extra = 4 * channels
    height = wide * 2 * MZ
    mode_lines = modes * 2 * kz

    z_plain = jnp.asarray(z_table(z_count, False))
    z_doubled = jnp.asarray(z_table(z_count, True))
    y_forward, y_inverse = y_tables(total_y, rows_y, kz, modes)
    block = index % (MY // modes)
    y_forward = lax.dynamic_index_in_dim(jnp.asarray(y_forward), block, 0, False)
    y_inverse = lax.dynamic_index_in_dim(jnp.asarray(y_inverse), block, 0, False)
    rows_forward, rows_inverse = x_rows(total_x, wide, modes)
    rows_forward = lax.dynamic_index_in_dim(jnp.asarray(rows_forward), index, 0, False)
    rows_inverse = lax.dynamic_index_in_dim(jnp.asarray(rows_inverse), index, 0, False)
    order = np.arange(cells).reshape(channels, rows_y).T.reshape(-1)
    turn = jnp.asarray(np.eye(cells, dtype=np.float32)[order].astype(BF16))

    def exchange(send):
        lanes = send.shape[1]
        pieces = send.reshape(wide * narrow, 2 * kz, lanes)
        got = lax.all_to_all(pieces, ("wide", "narrow"), split_axis=0, concat_axis=0, tiled=True)
        return got.reshape(height, lanes)

    send, field = call(
        start_kernel, [((height, cells), BF16), ((cells, z_count), BF16)], "start"
    )(lifted_field.reshape(cells, z_count), turn, z_plain)
    weight = pl.pallas_call(
        weight_kernel,
        grid=(modes,),
        in_specs=[pl.BlockSpec((1, kz, 2, channels, channels), lambda j: (j, 0, 0, 0, 0))],
        out_specs=pl.BlockSpec((1, kz * channels, 2 * channels), lambda j: (j, 0, 0)),
        out_shape=jax.ShapeDtypeStruct((modes, kz * channels, 2 * channels), BF16),
        cost_estimate=pl.CostEstimate(flops=1 << 20, bytes_accessed=5 << 20, transcendentals=0),
        name="weights",
    )(spectral_weight)
    pieces = exchange(send)
    spectrum, send = call(
        functools.partial(mode_kernel, narrow),
        [((mode_lines, channels), F32), ((height, cells), BF16)],
        "mode",
    )(pieces, rows_forward, y_forward, y_inverse, weight)
    pieces = exchange(send)
    prediction, grad_pre, send = call(
        functools.partial(cell_kernel, kz),
        [
            ((rows_y, z_count), F32),
            ((cells, z_count), BF16),
            ((height, cells + extra), BF16),
        ],
        "cell",
    )(
        pieces,
        rows_inverse,
        z_doubled,
        field,
        mix_weight,
        mix_bias[:, None],
        head_weight,
        head_bias[:, None],
        out_weight.astype(F32)[:, None],
        cotangent[0],
    )
    pieces = exchange(send)
    adjoint, send = call(
        functools.partial(back_kernel, narrow),
        [((mode_lines, channels), F32), ((height, cells + extra), BF16)],
        "back",
    )(pieces, rows_forward, y_forward, y_inverse, weight)
    pieces = exchange(send)
    grad_spectral = pl.pallas_call(
        outer_kernel,
        grid=(modes,),
        in_specs=[pl.BlockSpec((1, 2 * kz, channels), lambda j: (j, 0, 0))] * 2,
        out_specs=pl.BlockSpec((1, kz, 2, channels, channels), lambda j: (j, 0, 0, 0, 0)),
        out_shape=jax.ShapeDtypeStruct(spectral_weight.shape, F32),
        cost_estimate=pl.CostEstimate(flops=1 << 22, bytes_accessed=5 << 20, transcendentals=0),
        name="outer",
    )(spectrum.reshape(modes, 2 * kz, channels), adjoint.reshape(modes, 2 * kz, channels))
    grad_field, grad_mix, grad_head = call(
        functools.partial(finish_kernel, kz),
        [
            ((cells, z_count), BF16),
            ((channels, channels), F32),
            ((channels, hidden_units), F32),
        ],
        "finish",
    )(pieces, rows_inverse, z_plain, grad_pre, mix_weight, turn)
    return (
        prediction[None],
        grad_field.reshape(lifted_field.shape),
        grad_spectral,
        grad_mix,
        grad_head,
    )


def solution(mesh):
    return jax.shard_map(
        body,
        mesh=mesh,
        in_specs=(
            P("wide", None, "narrow", None),
            P("wide", "narrow", None, None, None),
            P(),
            P(),
            P(),
            P(),
            P(),
            P("wide", "narrow", None),
        ),
        out_specs=(
            P("wide", "narrow", None),
            P("wide", None, "narrow", None),
            P("wide", "narrow", None, None, None),
            P(),
            P(),
        ),
        check_vma=False,
    )
```

```python
import functools
import math

import jax
import jax.numpy as jnp
import numpy as np
from jax import lax
from jax.experimental import pallas as pl
from jax.experimental.pallas import tpu as pltpu
from jax.sharding import PartitionSpec as P

MX = 16
MY = 16
MZ = 16
F32 = jnp.float32
BF16 = jnp.bfloat16
VMEM_LIMIT = 32 * 1024 * 1024


def signed(indices, count):
    return np.where(indices < count // 2, indices, indices - count)


def wave(positions, frequency, length):
    turned = np.mod(np.multiply.outer(positions, frequency), length)
    angles = turned.astype(np.float32) * np.float32(2.0 * math.pi / length)
    scale = np.float32(1.0 / math.sqrt(length))
    return np.cos(angles) * scale, np.sin(angles) * scale


def pair(cosine, sine, sign):
    return np.stack(
        [np.stack([cosine, -sign * sine], -1), np.stack([sign * sine, cosine], -1)], -2
    )


def y_tables(total_y, rows_y, kz, modes):
    cosine, sine = wave(np.arange(total_y), signed(np.arange(MY), MY), total_y)
    narrow = total_y // rows_y
    same = np.eye(kz, dtype=np.float32)
    forward = pair(cosine, sine, -1.0).reshape(narrow, rows_y, MY // modes, modes, 2, 2)
    inverse = pair(cosine, sine, 1.0).reshape(narrow, rows_y, MY // modes, modes, 2, 2)
    forward = np.einsum("nybjtr,kl->bjtkynlr", forward, same)
    inverse = np.einsum("nybjst,kl->bnyksjtl", inverse, same)
    blocks = MY // modes
    forward = forward.reshape(blocks, modes * 2 * kz, rows_y * narrow * kz * 2)
    inverse = inverse.reshape(blocks, narrow * rows_y * kz * 2, modes * 2 * kz)
    return forward.astype(BF16), inverse.astype(BF16)


def dot(a, b):
    return jnp.dot(a, b, preferred_element_type=F32)


def dot_nt(a, b):
    return lax.dot_general(a, b, (((1,), (1,)), ((), ())), preferred_element_type=F32)


def dot_tn(a, b):
    return lax.dot_general(a, b, (((0,), (0,)), ((), ())), preferred_element_type=F32)


def grid_of(rows, columns):
    shape = (rows, columns)
    return lax.broadcasted_iota(jnp.int32, shape, 0), lax.broadcasted_iota(jnp.int32, shape, 1)


def selector(rows, columns, condition):
    return jnp.where(condition(*grid_of(rows, columns)), 1.0, 0.0).astype(BF16)


def halves(values):
    high = values.astype(BF16)
    return high, (values - high.astype(F32)).astype(BF16)


def stacked(refs, lanes=slice(None)):
    return jnp.concatenate([ref[:, lanes] for ref in refs], axis=0)


def cosine_of(phase, length):
    angles = (phase & (length - 1)).astype(F32) * (2.0 * math.pi / length)
    return jnp.cos(angles) * (1.0 / math.sqrt(length))


class Place:
    def __init__(self, wide, narrow, kz, modes, rows_y, channels, z_count, fold):
        self.wide, self.narrow, self.kz, self.modes = wide, narrow, kz, modes
        self.rows_y, self.channels, self.z_count, self.fold = rows_y, channels, z_count, fold
        self.inner = 1 << ((wide.bit_length() - 1) // 2)
        self.outer = wide // self.inner
        self.plane = self.inner * narrow
        self.lanes = rows_y * channels

    def here(self):
        wide, narrow = lax.axis_index("wide"), lax.axis_index("narrow")
        return wide // self.inner, wide % self.inner, narrow

    def frequency(self, wide):
        index = (wide * self.modes) // MY
        return jnp.where(index < MX // 2, index, index - MX)

    def z_table(self, doubled):
        row, z = grid_of(2 * MZ, self.z_count)
        _, _, narrow = self.here()
        part = row & 1
        line = row >> 1
        frequency = ((line // self.kz) ^ narrow) * self.kz + line % self.kz
        value = cosine_of(z * frequency + part * (self.z_count // 4), self.z_count)
        if doubled:
            value = jnp.where(frequency > 0, 2.0 * value, value)
        return value.astype(BF16)

    def expanded(self, small, same):
        rows, columns = grid_of(2 * MZ, small.shape[1])
        blocks = []
        for g in range(small.shape[0] // 2):
            value = jnp.where((rows & 1) == 0, small[2 * g : 2 * g + 1], small[2 * g + 1 : 2 * g + 2])
            blocks.append(jnp.where(same(rows >> 1, columns, g), value, 0.0))
        return jnp.concatenate(blocks, axis=0)

    def forward_x(self):
        outer, inner, narrow = self.here()
        plane = inner * self.narrow + narrow
        row, column = grid_of(2 * self.outer, self.plane * 2 * self.kz)
        source = plane ^ (column // (2 * self.kz))
        x = outer * self.inner + source // self.narrow
        frequency = self.frequency((outer ^ (row >> 1)) * self.inner + inner)
        quarter = self.wide // 4
        small = cosine_of(x * frequency + quarter * ((row & 1) - (column & 1)), self.wide)

        def same(line, column, _):
            source = plane ^ (column // (2 * self.kz))
            half, k = source % self.narrow, (column >> 1) % self.kz
            return line == half * self.kz + k

        return self.expanded(small, same)

    def inverse_x(self):
        outer, inner, narrow = self.here()
        row, column = grid_of(2 * self.inner, self.outer * 2 * MZ)
        source = outer ^ (column // (2 * MZ))
        x = outer * self.inner + (inner ^ (row >> 1))
        frequency = self.frequency(source * self.inner + inner)
        quarter = self.wide // 4
        small = cosine_of(x * frequency + quarter * ((column & 1) - (row & 1)), self.wide)

        def same(line, column, _):
            line = ((line // self.kz) ^ narrow) * self.kz + line % self.kz
            return line == (column >> 1) % MZ

        return self.expanded(small, same).astype(BF16)


def analysed(place, pieces, y_forward, copies):
    turned = sum(ref[:, : place.lanes].astype(F32) for ref in pieces)
    channels = place.channels
    lines = jnp.concatenate(
        [turned[:, y * channels : (y + 1) * channels] for y in range(place.rows_y)], axis=0
    )
    high, low = halves(jnp.concatenate([lines] * copies, axis=1))
    return dot(y_forward, high) + dot(y_forward, low)


def spread_lines(place, modes, y_inverse):
    lines = dot(y_inverse, modes)
    step = 2 * place.kz
    blocks = []
    for n in range(place.narrow):
        first = n * place.rows_y
        parts = [lines[(first + y) * step : (first + y + 1) * step] for y in range(place.rows_y)]
        blocks.append(jnp.concatenate(parts, axis=1))
    return jnp.concatenate(blocks, axis=0).astype(BF16)


def received_lines(place, pieces, z_table):
    blocks = []
    for half in range(place.narrow):
        own = [pieces[s][:, : place.lanes].astype(F32) for s in range(half, place.plane, place.narrow)]
        blocks.append(sum(own[1:], own[0]))
    return dot_tn(jnp.concatenate(blocks, axis=0).astype(BF16), z_table)


def start_kernel(place, field_ref, field_out_ref, *send_refs):
    channels, rows_y = place.channels, place.rows_y
    turn = selector(
        place.lanes,
        place.lanes,
        lambda row, column: (row % channels == column // rows_y)
        & (row // channels == column % rows_y),
    )
    turned = dot(turn, field_ref[...]).astype(BF16)
    field_out_ref[...] = turned
    spectra = dot_nt(place.z_table(False), turned)
    step = 2 * place.kz
    for t, ref in enumerate(send_refs):
        ref[...] = spectra[t * step : (t + 1) * step].astype(BF16)


def weight_kernel(weight_ref, out_ref):
    modes, kz, _, channels, _ = weight_ref.shape
    for j in range(modes):
        both = jnp.concatenate([weight_ref[j, :, 0], weight_ref[j, :, 1]], axis=-1)
        out_ref[j] = both.reshape(kz * channels, 2 * channels).astype(BF16)


def fold_kernel(place, *refs):
    pieces, sends = refs[: place.plane], refs[place.plane :]
    high, low = halves(place.forward_x())
    values = stacked(pieces, slice(0, place.lanes))
    partial = (dot(high, values) + dot(low, values)).astype(BF16)
    for s, ref in enumerate(sends):
        ref[:, : place.lanes] = partial[s * 2 * MZ : (s + 1) * 2 * MZ]
    if pieces[0].shape[1] > place.lanes:
        outer, _, _ = place.here()
        shares = sum(ref[:, place.lanes :].astype(F32) for ref in pieces)
        count = 2 * place.outer
        high, low = halves(shares[:count] + shares[count : 2 * count])
        split = jnp.concatenate([high, low], axis=0)
        place_of = selector(
            place.outer * 2 * MZ,
            2 * count,
            lambda row, column: (row % (2 * MZ) == column // place.outer)
            & ((row // (2 * MZ)) ^ outer == column % place.outer),
        )
        chosen = dot(place_of, split).astype(BF16)
        for s, ref in enumerate(sends):
            ref[:, place.lanes :] = chosen[s * 2 * MZ : (s + 1) * 2 * MZ]


def mode_kernel(place, *refs):
    pieces = refs[: place.outer]
    y_forward_ref, y_inverse_ref, weight_ref, spectrum_ref, send_ref = refs[place.outer :]
    kz, channels = place.kz, place.channels
    spectrum = analysed(place, pieces, y_forward_ref[...], kz)
    spectrum_ref[...] = spectrum[:, :channels]
    row, lane = grid_of(*spectrum.shape)
    blocked = jnp.where(row % kz == lane // channels, spectrum, 0.0)
    mixed = []
    for j in range(place.modes):
        left = blocked[j * 2 * kz : (j + 1) * 2 * kz].astype(BF16)
        product = dot(left, weight_ref[j])
        real, imag = product[:, :channels], product[:, channels:]
        mixed.append(real[:kz] - imag[kz:])
        mixed.append(imag[:kz] + real[kz:])
    mode = jnp.concatenate(mixed, axis=0).astype(BF16)
    send_ref[...] = spread_lines(place, mode, y_inverse_ref[...])


def part_kernel(place, *refs):
    pieces, sends = refs[: place.outer], refs[place.outer :]
    lines = dot(place.inverse_x(), stacked(pieces, slice(0, place.lanes))).astype(BF16)
    step = 2 * place.kz
    for s, ref in enumerate(sends):
        ref[:, : place.lanes] = lines[s * step : (s + 1) * step]
    if pieces[0].shape[1] > place.lanes:
        outer, _, _ = place.here()
        shares = stacked(pieces, slice(place.lanes, None))
        gather = selector(
            step,
            shares.shape[0],
            lambda row, column: (column % (2 * MZ) == row // place.outer)
            & ((column // (2 * MZ)) ^ outer == row % place.outer),
        )
        chosen = dot(gather, shares).astype(BF16)
        for ref in sends:
            ref[:, place.lanes :] = chosen


def normal(values):
    cumulative = 0.5 * (1.0 + lax.erf(values * (1.0 / math.sqrt(2.0))))
    density = jnp.exp(-0.5 * values * values) * (1.0 / math.sqrt(2.0 * math.pi))
    return values * cumulative, cumulative + values * density


def cell_kernel(place, *refs):
    pieces, refs = refs[: place.plane], refs[place.plane :]
    field_ref, mix_ref, mix_bias_ref, head_ref, head_bias_ref, out_weight_ref, cotangent_ref = refs[:7]
    prediction_ref, grad_pre_ref = refs[7:9]
    sends = refs[9 : 9 + (place.plane if place.fold else place.narrow)]
    channels, hidden_units = head_ref.shape
    z_table = place.z_table(True)
    branch = received_lines(place, pieces, z_table)
    mix, head = mix_ref[...], head_ref[...]
    mix_bias, head_bias = mix_bias_ref[...], head_bias_ref[...]
    out_weight = out_weight_ref[...]
    grad_mix = jnp.zeros((channels, channels), F32)
    grad_head = jnp.zeros((channels, hidden_units), F32)
    gradients = []
    for y in range(place.rows_y):
        cells = slice(y * channels, (y + 1) * channels)
        field = field_ref[cells]
        pre_act = branch[cells] + dot_tn(mix, field) + mix_bias
        hidden, pre_slope = normal(pre_act)
        hidden = hidden.astype(BF16)
        head_pre = dot_tn(head, hidden) + head_bias
        active, slope = normal(head_pre)
        active = active.astype(BF16).astype(F32)
        prediction_ref[y : y + 1] = jnp.sum(active * out_weight, axis=0, keepdims=True)
        head_slope = (cotangent_ref[y : y + 1] * out_weight * slope).astype(BF16)
        grad_pre = (dot(head, head_slope) * pre_slope).astype(BF16)
        grad_head += dot_nt(hidden, head_slope)
        grad_mix += dot_nt(field, grad_pre)
        gradients.append(grad_pre)

    gradient = jnp.concatenate(gradients, axis=0)
    grad_pre_ref[...] = gradient
    spectra = dot_nt(z_table, gradient)
    step = 2 * place.kz
    for s, ref in enumerate(sends):
        t = s % place.narrow
        ref[:, : place.lanes] = spectra[t * step : (t + 1) * step].astype(BF16)
    if not place.fold:
        refs[-2][...] = grad_mix
        refs[-1][...] = grad_head
        return
    wide_mix = jnp.concatenate(
        [grad_mix, jnp.zeros((channels, hidden_units - channels), F32)], axis=1
    )
    head_high, head_low = halves(grad_head)
    mix_high, mix_low = halves(wide_mix)
    shares = jnp.concatenate([head_high, mix_high, head_low, mix_low], axis=0)
    _, inner, narrow = place.here()
    plane = inner * place.narrow + narrow

    def chosen(row, column):
        kind, owner = (row % step) // place.outer, row % place.outer
        target = owner * place.plane + ((row // step) ^ plane)
        return column == kind * channels + target

    split = dot(selector(place.plane * step, 4 * channels, chosen), shares).astype(BF16)
    for s, ref in enumerate(sends):
        ref[:, place.lanes :] = split[s * step : (s + 1) * step]


def back_kernel(place, *refs):
    pieces = refs[: place.outer]
    y_forward_ref, y_inverse_ref, weight_ref, adjoint_ref, send_ref = refs[place.outer :]
    kz, channels = place.kz, place.channels
    adjoint = analysed(place, pieces, y_forward_ref[...], 1)
    adjoint_ref[...] = adjoint
    pulled = []
    for j in range(place.modes):
        real = adjoint[j * 2 * kz : j * 2 * kz + kz]
        imag = adjoint[j * 2 * kz + kz : (j + 1) * 2 * kz]
        left = jnp.concatenate(
            [jnp.concatenate([real, imag], axis=1), jnp.concatenate([imag, -real], axis=1)], axis=0
        )
        pulled.append(dot_nt(left.astype(BF16), weight_ref[j]))
    pulled = jnp.concatenate(pulled, axis=0)
    row, lane = grid_of(*pulled.shape)
    pulled = jnp.where(row % kz == lane // channels, pulled, 0.0).astype(BF16)
    gather = selector(
        kz * channels, channels, lambda row, column: row % channels == column
    )
    modes_back = dot(pulled, gather).astype(BF16)
    send_ref[:, : place.lanes] = spread_lines(place, modes_back, y_inverse_ref[...])
    if place.fold:
        shares = sum(ref[:, place.lanes :].astype(F32) for ref in pieces)
        high, low = halves(shares[0:2] + shares[2:4])
        rest = jnp.zeros((2 * MZ - 4, shares.shape[1]), F32)
        split = jnp.concatenate([high.astype(F32), low.astype(F32), rest], axis=0)
        send_ref[:, place.lanes :] = split.astype(BF16)


def outer_kernel(spectrum_ref, adjoint_ref, out_ref):
    modes, kz = out_ref.shape[:2]
    for j in range(modes):
        columns = jnp.transpose(spectrum_ref[j])
        adjoint = adjoint_ref[j]
        for k in range(kz):
            s_real, s_imag = columns[:, k : k + 1], columns[:, kz + k : kz + k + 1]
            a_real, a_imag = adjoint[k : k + 1], adjoint[kz + k : kz + k + 1]
            out_ref[j, k, 0] = s_real * a_real + s_imag * a_imag
            out_ref[j, k, 1] = s_real * a_imag - s_imag * a_real


def finish_kernel(place, *refs):
    pieces, refs = refs[: place.plane], refs[place.plane :]
    grad_pre_ref, mix_ref, grad_field_ref = refs[:3]
    channels, rows_y = place.channels, place.rows_y
    branch = received_lines(place, pieces, place.z_table(False))
    parts = []
    for y in range(rows_y):
        cells = slice(y * channels, (y + 1) * channels)
        parts.append((branch[cells] + dot(mix_ref[...], grad_pre_ref[cells])).astype(BF16))
    turn = selector(
        place.lanes,
        place.lanes,
        lambda row, column: (row // rows_y == column % channels)
        & (row % rows_y == column // channels),
    )
    grad_field_ref[...] = dot(turn, jnp.concatenate(parts, axis=0)).astype(BF16)
    if not place.fold:
        return
    grad_mix_ref, grad_head_ref = refs[3:]
    _, inner, narrow = place.here()
    plane = inner * place.narrow + narrow
    step = 2 * place.kz
    shares = stacked(pieces, slice(place.lanes, None))

    def picked(first):
        def condition(row, column):
            kind, owner = (column % step) // place.outer, column % place.outer
            target = owner * place.plane + ((column // step) ^ plane)
            return (target == row) & (kind % 2 == first)

        return dot(selector(channels, shares.shape[0], condition), shares)

    grad_head_ref[...] = picked(0)
    grad_mix_ref[...] = picked(1)[:, :channels]


def call(kernel, outs, name):
    return pl.pallas_call(
        kernel,
        out_shape=[jax.ShapeDtypeStruct(shape, dtype) for shape, dtype in outs],
        compiler_params=pltpu.CompilerParams(vmem_limit_bytes=VMEM_LIMIT),
        cost_estimate=pl.CostEstimate(flops=1 << 22, bytes_accessed=1 << 19, transcendentals=0),
        name=name,
    )


def body(
    lifted_field,
    spectral_weight,
    mix_weight,
    mix_bias,
    head_weight,
    head_bias,
    out_weight,
    cotangent,
):
    wide = lax.axis_size("wide")
    narrow = lax.axis_size("narrow")
    devices = wide * narrow
    _, channels, rows_y, z_count = lifted_field.shape
    modes, kz = spectral_weight.shape[:2]
    hidden_units = head_weight.shape[1]
    cells = channels * rows_y
    place = Place(wide, narrow, kz, modes, rows_y, channels, z_count, False)
    place.fold = devices == channels and 4 * place.outer == 2 * kz and hidden_units % 128 == 0
    extra = hidden_units if place.fold else 0
    step = 2 * kz
    mode_lines = modes * 2 * kz

    y_forward, y_inverse = y_tables(rows_y * narrow, rows_y, kz, modes)
    if len(y_forward) > 1:
        block = lax.axis_index("wide") % len(y_forward)
        y_forward = lax.dynamic_index_in_dim(jnp.asarray(y_forward), block, 0, False)
        y_inverse = lax.dynamic_index_in_dim(jnp.asarray(y_inverse), block, 0, False)
    else:
        y_forward, y_inverse = jnp.asarray(y_forward[0]), jnp.asarray(y_inverse[0])

    def moved(sends, stride):
        got = [sends[0]]
        for s in range(1, len(sends)):
            pairs = [(p, p ^ (s * stride)) for p in range(devices)]
            got.append(lax.ppermute(sends[s], ("wide", "narrow"), pairs))
        return got

    def along_plane(sends):
        return moved([sends[s % len(sends)] for s in range(place.plane)], 1)

    def along_outer(sends):
        return moved([sends[s % len(sends)] for s in range(place.outer)], place.plane)

    def fold(pieces, lanes):
        kernel = functools.partial(fold_kernel, place)
        return call(kernel, [((2 * MZ, lanes), BF16)] * place.outer, "fold")(*pieces)

    def part(pieces, lanes):
        kernel = functools.partial(part_kernel, place)
        return call(kernel, [((step, lanes), BF16)] * place.plane, "part")(*pieces)

    field, *sends = call(
        functools.partial(start_kernel, place),
        [((cells, z_count), BF16)] + [((step, cells), BF16)] * narrow,
        "start",
    )(lifted_field.reshape(cells, z_count))
    some = max(1, modes // 4)
    weight = pl.pallas_call(
        weight_kernel,
        grid=(modes // some,),
        in_specs=[pl.BlockSpec((some, kz, 2, channels, channels), lambda j: (j, 0, 0, 0, 0))],
        out_specs=pl.BlockSpec((some, kz * channels, 2 * channels), lambda j: (j, 0, 0)),
        out_shape=jax.ShapeDtypeStruct((modes, kz * channels, 2 * channels), BF16),
        compiler_params=pltpu.CompilerParams(vmem_limit_bytes=VMEM_LIMIT),
        cost_estimate=pl.CostEstimate(flops=1 << 20, bytes_accessed=5 << 20, transcendentals=0),
        name="weights",
    )(spectral_weight)
    pieces = along_outer(fold(along_plane(sends), cells))
    spectrum, send = call(
        functools.partial(mode_kernel, place),
        [((mode_lines, channels), F32), ((2 * MZ, cells), BF16)],
        "mode",
    )(*pieces, y_forward, y_inverse, weight)
    pieces = along_plane(part(along_outer([send]), cells))
    outs = [((rows_y, z_count), F32), ((cells, z_count), BF16)]
    if place.fold:
        outs += [((step, cells + extra), BF16)] * place.plane
    else:
        outs += [((step, cells), BF16)] * narrow
        outs += [((channels, channels), F32), ((channels, hidden_units), F32)]
    prediction, grad_pre, *sends = call(functools.partial(cell_kernel, place), outs, "cell")(
        *pieces,
        field,
        mix_weight,
        mix_bias[:, None],
        head_weight,
        head_bias[:, None],
        out_weight.astype(F32)[:, None],
        cotangent[0],
    )
    sums = ()
    if not place.fold:
        sums = lax.psum(tuple(sends[-2:]), ("wide", "narrow"))
        sends = sends[:-2]
    pieces = along_outer(fold(along_plane(sends), cells + extra))
    adjoint, send = call(
        functools.partial(back_kernel, place),
        [((mode_lines, channels), F32), ((2 * MZ, cells + extra), BF16)],
        "back",
    )(*pieces, y_forward, y_inverse, weight)
    pieces = along_plane(part(along_outer([send]), cells + extra))
    grad_spectral = pl.pallas_call(
        outer_kernel,
        grid=(modes // some,),
        in_specs=[pl.BlockSpec((some, 2 * kz, channels), lambda j: (j, 0, 0))] * 2,
        out_specs=pl.BlockSpec((some, kz, 2, channels, channels), lambda j: (j, 0, 0, 0, 0)),
        out_shape=jax.ShapeDtypeStruct(spectral_weight.shape, F32),
        compiler_params=pltpu.CompilerParams(vmem_limit_bytes=VMEM_LIMIT),
        cost_estimate=pl.CostEstimate(flops=1 << 22, bytes_accessed=5 << 20, transcendentals=0),
        name="outer",
    )(spectrum.reshape(modes, 2 * kz, channels), adjoint.reshape(modes, 2 * kz, channels))
    outs = [((cells, z_count), BF16)]
    if place.fold:
        outs += [((channels, channels), F32), ((channels, hidden_units), F32)]
    grad_field, *totals = call(functools.partial(finish_kernel, place), outs, "finish")(
        *pieces, grad_pre, mix_weight
    )
    grad_mix, grad_head = totals if place.fold else sums
    return (
        prediction[None],
        grad_field.reshape(lifted_field.shape),
        grad_spectral,
        grad_mix,
        grad_head,
    )


def solution(mesh):
    return jax.shard_map(
        body,
        mesh=mesh,
        in_specs=(
            P("wide", None, "narrow", None),
            P("wide", "narrow", None, None, None),
            P(),
            P(),
            P(),
            P(),
            P(),
            P("wide", "narrow", None),
        ),
        out_specs=(
            P("wide", "narrow", None),
            P("wide", None, "narrow", None),
            P("wide", "narrow", None, None, None),
            P(),
            P(),
        ),
        check_vma=False,
    )
```

```python
import functools
import math

import jax
import jax.numpy as jnp
import numpy as np
from jax import lax
from jax.experimental import pallas as pl
from jax.experimental.pallas import tpu as pltpu
from jax.sharding import PartitionSpec as P

MX = 16
MY = 16
MZ = 16
F32 = jnp.float32
BF16 = jnp.bfloat16
VMEM_LIMIT = 32 * 1024 * 1024


def signed(indices, count):
    return np.where(indices < count // 2, indices, indices - count)


def wave(positions, frequency, length):
    turned = np.mod(np.multiply.outer(positions, frequency), length)
    angles = turned.astype(np.float32) * np.float32(2.0 * math.pi / length)
    scale = np.float32(1.0 / math.sqrt(length))
    return np.cos(angles) * scale, np.sin(angles) * scale


def pair(cosine, sine, sign):
    return np.stack(
        [np.stack([cosine, -sign * sine], -1), np.stack([sign * sine, cosine], -1)], -2
    )


def y_tables(total_y, rows_y, kz, modes):
    cosine, sine = wave(np.arange(total_y), signed(np.arange(MY), MY), total_y)
    narrow = total_y // rows_y
    same = np.eye(kz, dtype=np.float32)
    forward = pair(cosine, sine, -1.0).reshape(narrow, rows_y, MY // modes, modes, 2, 2)
    inverse = pair(cosine, sine, 1.0).reshape(narrow, rows_y, MY // modes, modes, 2, 2)
    forward = np.einsum("nybjtr,kl->bjtkynlr", forward, same)
    inverse = np.einsum("nybjst,kl->bnyksjtl", inverse, same)
    blocks = MY // modes
    forward = forward.reshape(blocks, modes * 2 * kz, rows_y * narrow * kz * 2)
    inverse = inverse.reshape(blocks, narrow * rows_y * kz * 2, modes * 2 * kz)
    return forward.astype(BF16), inverse.astype(BF16)


def dot(a, b):
    return jnp.dot(a, b, preferred_element_type=F32)


def dot_nt(a, b):
    return lax.dot_general(a, b, (((1,), (1,)), ((), ())), preferred_element_type=F32)


def dot_tn(a, b):
    return lax.dot_general(a, b, (((0,), (0,)), ((), ())), preferred_element_type=F32)


def grid_of(rows, columns):
    shape = (rows, columns)
    return lax.broadcasted_iota(jnp.int32, shape, 0), lax.broadcasted_iota(jnp.int32, shape, 1)


def selector(rows, columns, condition):
    return jnp.where(condition(*grid_of(rows, columns)), 1.0, 0.0).astype(BF16)


def halves(values):
    high = values.astype(BF16)
    return high, (values - high.astype(F32)).astype(BF16)


def stacked(refs, lanes=slice(None)):
    return jnp.concatenate([ref[:, lanes] for ref in refs], axis=0)


def cosine_of(phase, length):
    angles = (phase & (length - 1)).astype(F32) * (2.0 * math.pi / length)
    return jnp.cos(angles) * (1.0 / math.sqrt(length))


class Place:
    def __init__(self, wide, narrow, kz, modes, rows_y, channels, z_count, fold):
        self.wide, self.narrow, self.kz, self.modes = wide, narrow, kz, modes
        self.rows_y, self.channels, self.z_count, self.fold = rows_y, channels, z_count, fold
        self.outer = wide // 2
        self.partners = self.outer * narrow
        self.lanes = rows_y * channels

    def here(self):
        wide = lax.axis_index("wide")
        return wide // 2, wide % 2

    def frequency(self, wide):
        index = (wide * self.modes) // MY
        return jnp.where(index < MX // 2, index, index - MX)

    def z_table(self, doubled):
        row, z = grid_of(2 * MZ, self.z_count)
        frequency = row >> 1
        value = cosine_of(z * frequency + (row & 1) * (self.z_count // 4), self.z_count)
        if doubled:
            value = jnp.where(frequency > 0, 2.0 * value, value)
        return value.astype(BF16)

    def expanded(self, small):
        row, column = grid_of(2 * MZ, small.shape[1])
        same = (row >> 1) == ((column >> 1) & (MZ - 1))
        blocks = []
        for g in range(small.shape[0] // 2):
            value = jnp.where((row & 1) == 0, small[2 * g : 2 * g + 1], small[2 * g + 1 : 2 * g + 2])
            blocks.append(jnp.where(same, value, 0.0))
        return jnp.concatenate(blocks, axis=0)

    def forward_x(self):
        outer, inner = self.here()
        row, column = grid_of(2 * self.outer, 4 * MZ)
        x = 2 * outer + (inner ^ (column // (2 * MZ)))
        frequency = self.frequency(2 * (row >> 1) + inner)
        quarter = self.wide // 4
        small = cosine_of(x * frequency + quarter * ((row & 1) - (column & 1)), self.wide)
        return self.expanded(small)

    def inverse_x(self):
        outer, inner = self.here()
        row, column = grid_of(4, self.outer * 2 * MZ)
        x = 2 * outer + (inner ^ (row >> 1))
        frequency = self.frequency(2 * (column // (2 * MZ)) + inner)
        quarter = self.wide // 4
        small = cosine_of(x * frequency + quarter * ((column & 1) - (row & 1)), self.wide)
        return self.expanded(small).astype(BF16)

    def sum_owner(self, index, inner):
        return ((index // self.narrow) * 2 + inner) * self.narrow + index % self.narrow


def repeat_rows(out_ref, block):
    height = block.shape[0]
    for first in range(0, out_ref.shape[0], height):
        out_ref[first : first + height] = block


def write_pieces(place, send_ref, block, shares):
    step, half = 2 * place.kz, place.lanes // 2
    height = send_ref.shape[0] // place.partners
    for p in range(place.partners):
        own = block[p * step % block.shape[0] :][:step]
        first = p * height
        send_ref[first : first + step] = own[:, :half]
        send_ref[first + step : first + 2 * step] = own[:, half:]
        send_ref[first + 2 * step : first + height] = shares[p * 8 % shares.shape[0] :][:8]


def read_pieces(place, pieces_ref):
    step = 2 * place.kz
    if pieces_ref.shape[1] == place.lanes:
        return pieces_ref[...], None
    height = pieces_ref.shape[0] // place.partners
    blocks, shares = [], []
    for p in range(place.partners):
        first = p * height
        left = pieces_ref[first : first + step]
        right = pieces_ref[first + step : first + 2 * step]
        blocks.append(jnp.concatenate([left, right], axis=1))
        shares.append(pieces_ref[first + 2 * step : first + height].astype(F32))
    return jnp.concatenate(blocks, axis=0), shares


def analysed(place, pieces, y_forward, copies):
    height = 2 * MZ
    turned = sum(
        pieces[first : first + height].astype(F32) for first in range(0, pieces.shape[0], height)
    )
    channels = place.channels
    lines = jnp.concatenate(
        [turned[:, y * channels : (y + 1) * channels] for y in range(place.rows_y)], axis=0
    )
    high, low = halves(jnp.concatenate([lines] * copies, axis=1))
    return dot(y_forward, high) + dot(y_forward, low)


def spread_lines(place, modes, y_inverse):
    lines = dot(y_inverse, modes)
    step = 2 * place.kz
    blocks = []
    for n in range(place.narrow):
        first = n * place.rows_y
        parts = [lines[(first + y) * step : (first + y + 1) * step] for y in range(place.rows_y)]
        blocks.append(jnp.concatenate(parts, axis=1))
    return jnp.concatenate(blocks, axis=0).astype(BF16)


def start_kernel(place, field_ref, field_out_ref, send_ref):
    channels, rows_y = place.channels, place.rows_y
    turn = selector(
        place.lanes,
        place.lanes,
        lambda row, column: (row % channels == column // rows_y)
        & (row // channels == column % rows_y),
    )
    turned = dot(turn, field_ref[...]).astype(BF16)
    field_out_ref[...] = turned
    send_ref[...] = dot_nt(place.z_table(False), turned).astype(BF16)


def weight_kernel(weight_ref, out_ref):
    modes, kz, _, channels, _ = weight_ref.shape
    for j in range(modes):
        both = jnp.concatenate([weight_ref[j, :, 0], weight_ref[j, :, 1]], axis=-1)
        out_ref[j] = both.reshape(kz * channels, 2 * channels).astype(BF16)


def fold_kernel(place, *refs):
    own_ref, got_ref = refs[:2]
    high, low = halves(place.forward_x())
    height = 2 * MZ
    values = jnp.concatenate([own_ref[:height], got_ref[:height]], axis=0)
    partial = (dot(high, values) + dot(low, values)).astype(BF16)
    if got_ref.shape[0] == height:
        refs[2][...] = partial
        return
    sums_ref, send_ref = refs[2:]
    got = got_ref[height:].astype(F32)
    width = sums_ref.shape[1]
    high, low = halves(sums_ref[...] + got[:, :width] + got[:, width:])
    count = place.partners
    place_of = selector(
        8 * count,
        4 * count,
        lambda row, column: (row % 8 == column // count) & (row // 8 == column % count),
    )
    shares = dot(place_of, jnp.concatenate([high, low], axis=0)).astype(BF16)
    write_pieces(place, send_ref, partial, shares)


def mode_kernel(
    place, pieces_ref, y_forward_ref, y_inverse_ref, weight_ref, spectrum_ref, send_ref
):
    kz, channels = place.kz, place.channels
    spectrum = analysed(place, pieces_ref[...], y_forward_ref[...], kz)
    spectrum_ref[...] = spectrum[:, :channels]
    row, lane = grid_of(*spectrum.shape)
    blocked = jnp.where(row % kz == lane // channels, spectrum, 0.0)
    mixed = []
    for j in range(place.modes):
        left = blocked[j * 2 * kz : (j + 1) * 2 * kz].astype(BF16)
        product = dot(left, weight_ref[j])
        real, imag = product[:, :channels], product[:, channels:]
        mixed.append(real[:kz] - imag[kz:])
        mixed.append(imag[:kz] + real[kz:])
    mode = jnp.concatenate(mixed, axis=0).astype(BF16)
    repeat_rows(send_ref, spread_lines(place, mode, y_inverse_ref[...]))


def part_kernel(place, *refs):
    pieces, shares = read_pieces(place, refs[0])
    lines = dot(place.inverse_x(), pieces)
    height = 2 * MZ
    own_ref, send_ref = refs[1:3]
    own_ref[...] = lines[:height]
    if shares is None:
        send_ref[...] = lines[height:].astype(BF16)
        return
    sums_ref = refs[3]
    count = place.partners
    got = jnp.concatenate(shares, axis=0).astype(BF16)

    def chosen(part):
        return dot(
            selector(
                2 * count,
                8 * count,
                lambda row, column: (row // count + 2 * part == column % 8)
                & (row % count == column // 8),
            ),
            got,
        )

    high, low = chosen(0), chosen(1)
    sums_ref[...] = high + low
    send_ref[:height] = lines[height:].astype(BF16)
    send_ref[height:] = jnp.concatenate([high, low], axis=1).astype(BF16)


def normal(values):
    cumulative = 0.5 * (1.0 + lax.erf(values * (1.0 / math.sqrt(2.0))))
    density = jnp.exp(-0.5 * values * values) * (1.0 / math.sqrt(2.0 * math.pi))
    return values * cumulative, cumulative + values * density


def cell_kernel(place, *refs):
    own_ref, got_ref, refs = refs[0], refs[1], refs[2:]
    field_ref, mix_ref, mix_bias_ref, head_ref, head_bias_ref, out_weight_ref, cotangent_ref = refs[:7]
    prediction_ref, grad_pre_ref, send_ref = refs[7:10]
    channels, hidden_units = head_ref.shape
    z_table = place.z_table(True)
    lines = (own_ref[...] + got_ref[...].astype(F32)).astype(BF16)
    branch = dot_tn(lines, z_table)
    mix, head = mix_ref[...], head_ref[...]
    mix_bias, head_bias = mix_bias_ref[...], head_bias_ref[...]
    out_weight = out_weight_ref[...]
    grad_mix = jnp.zeros((channels, channels), F32)
    grad_head = jnp.zeros((channels, hidden_units), F32)
    gradients = []
    for y in range(place.rows_y):
        cells = slice(y * channels, (y + 1) * channels)
        field = field_ref[cells]
        pre_act = branch[cells] + dot_tn(mix, field) + mix_bias
        hidden, pre_slope = normal(pre_act)
        hidden = hidden.astype(BF16)
        head_pre = dot_tn(head, hidden) + head_bias
        active, slope = normal(head_pre)
        active = active.astype(BF16).astype(F32)
        prediction_ref[y : y + 1] = jnp.sum(active * out_weight, axis=0, keepdims=True)
        head_slope = (cotangent_ref[y : y + 1] * out_weight * slope).astype(BF16)
        grad_pre = (dot(head, head_slope) * pre_slope).astype(BF16)
        grad_head += dot_nt(hidden, head_slope)
        grad_mix += dot_nt(field, grad_pre)
        gradients.append(grad_pre)

    gradient = jnp.concatenate(gradients, axis=0)
    grad_pre_ref[...] = gradient
    height = 2 * MZ
    send_ref[:height] = dot_nt(z_table, gradient).astype(BF16)
    if not place.fold:
        refs[-2][...] = grad_mix
        refs[-1][...] = grad_head
        return
    wide_mix = jnp.concatenate(
        [grad_mix, jnp.zeros((channels, hidden_units - channels), F32)], axis=1
    )
    high, low = halves(jnp.concatenate([grad_head, wide_mix], axis=0))
    count = place.partners
    _, inner = place.here()

    def chosen(owner):
        def condition(row, column):
            target = place.sum_owner(row % count, owner)
            return column == (row // count) * channels + target

        picked = selector(2 * count, 2 * channels, condition)
        return dot(picked, high), dot(picked, low)

    refs[10][...] = sum(chosen(inner))
    send_ref[height:] = jnp.concatenate(chosen(1 - inner), axis=1).astype(BF16)


def back_kernel(
    place, pieces_ref, y_forward_ref, y_inverse_ref, weight_ref, adjoint_ref, send_ref
):
    kz, channels = place.kz, place.channels
    pieces, shares = read_pieces(place, pieces_ref)
    adjoint = analysed(place, pieces, y_forward_ref[...], 1)
    adjoint_ref[...] = adjoint
    pulled = []
    for j in range(place.modes):
        real = adjoint[j * 2 * kz : j * 2 * kz + kz]
        imag = adjoint[j * 2 * kz + kz : (j + 1) * 2 * kz]
        left = jnp.concatenate(
            [jnp.concatenate([real, imag], axis=1), jnp.concatenate([imag, -real], axis=1)], axis=0
        )
        pulled.append(dot_nt(left.astype(BF16), weight_ref[j]))
    pulled = jnp.concatenate(pulled, axis=0)
    row, lane = grid_of(*pulled.shape)
    pulled = jnp.where(row % kz == lane // channels, pulled, 0.0).astype(BF16)
    gather = selector(
        kz * channels, channels, lambda row, column: row % channels == column
    )
    modes_back = dot(pulled, gather).astype(BF16)
    block = spread_lines(place, modes_back, y_inverse_ref[...])
    if shares is None:
        repeat_rows(send_ref, block)
        return
    total = sum(shares[1:], shares[0])
    high, low = halves(total[0:2] + total[2:4])
    rest = jnp.zeros((4, total.shape[1]), F32)
    split = jnp.concatenate([high.astype(F32), low.astype(F32), rest], axis=0)
    write_pieces(place, send_ref, block, split.astype(BF16))


def outer_kernel(spectrum_ref, adjoint_ref, out_ref):
    modes, kz = out_ref.shape[:2]
    for j in range(modes):
        columns = jnp.transpose(spectrum_ref[j])
        adjoint = adjoint_ref[j]
        for k in range(kz):
            s_real, s_imag = columns[:, k : k + 1], columns[:, kz + k : kz + k + 1]
            a_real, a_imag = adjoint[k : k + 1], adjoint[kz + k : kz + k + 1]
            out_ref[j, k, 0] = s_real * a_real + s_imag * a_imag
            out_ref[j, k, 1] = s_real * a_imag - s_imag * a_real


def finish_kernel(place, *refs):
    own_ref, got_ref, grad_pre_ref, mix_ref = refs[:4]
    refs = refs[4:]
    height = 2 * MZ
    channels, rows_y = place.channels, place.rows_y
    lines = (own_ref[...] + got_ref[:height].astype(F32)).astype(BF16)
    branch = dot_tn(lines, place.z_table(False))
    parts = []
    for y in range(rows_y):
        cells = slice(y * channels, (y + 1) * channels)
        parts.append((branch[cells] + dot(mix_ref[...], grad_pre_ref[cells])).astype(BF16))
    turn = selector(
        place.lanes,
        place.lanes,
        lambda row, column: (row // rows_y == column % channels)
        & (row % rows_y == column // channels),
    )
    if not place.fold:
        refs[0][...] = dot(turn, jnp.concatenate(parts, axis=0)).astype(BF16)
        return
    sums_ref, grad_field_ref, grad_mix_ref, grad_head_ref = refs
    grad_field_ref[...] = dot(turn, jnp.concatenate(parts, axis=0)).astype(BF16)
    _, inner = place.here()
    count = place.partners
    width = sums_ref.shape[1]
    own_high, own_low = halves(sums_ref[...])
    got = got_ref[height:]

    def picked(kind):
        def choose(owner):
            def condition(row, column):
                target = place.sum_owner(column % count, owner)
                return (column // count == kind) & (target == row)

            return selector(channels, 2 * count, condition)

        own, twin = choose(inner), choose(1 - inner)
        both = dot(twin, got)
        return dot(own, own_high) + dot(own, own_low) + both[:, :width] + both[:, width:]

    grad_head_ref[...] = picked(0)
    grad_mix_ref[...] = picked(1)[:, :channels]


def call(kernel, outs, name):
    return pl.pallas_call(
        kernel,
        out_shape=[jax.ShapeDtypeStruct(shape, dtype) for shape, dtype in outs],
        compiler_params=pltpu.CompilerParams(vmem_limit_bytes=VMEM_LIMIT),
        cost_estimate=pl.CostEstimate(flops=1 << 22, bytes_accessed=1 << 19, transcendentals=0),
        name=name,
    )


def body(
    lifted_field,
    spectral_weight,
    mix_weight,
    mix_bias,
    head_weight,
    head_bias,
    out_weight,
    cotangent,
):
    wide = lax.axis_size("wide")
    narrow = lax.axis_size("narrow")
    devices = wide * narrow
    _, channels, rows_y, z_count = lifted_field.shape
    modes, kz = spectral_weight.shape[:2]
    hidden_units = head_weight.shape[1]
    cells = channels * rows_y
    place = Place(wide, narrow, kz, modes, rows_y, channels, z_count, False)
    place.fold = devices == channels and hidden_units == 128 and place.lanes == 256 and kz % 8 == 0
    height = 2 * MZ
    step = 2 * kz
    partners = place.partners
    mode_lines = modes * 2 * kz

    y_forward, y_inverse = y_tables(rows_y * narrow, rows_y, kz, modes)
    if len(y_forward) > 1:
        block = lax.axis_index("wide") % len(y_forward)
        y_forward = lax.dynamic_index_in_dim(jnp.asarray(y_forward), block, 0, False)
        y_inverse = lax.dynamic_index_in_dim(jnp.asarray(y_inverse), block, 0, False)
    else:
        y_forward, y_inverse = jnp.asarray(y_forward[0]), jnp.asarray(y_inverse[0])

    def to_twin(send):
        pairs = [(p, p ^ narrow) for p in range(devices)]
        return lax.ppermute(send, ("wide", "narrow"), pairs)

    groups = [
        [(2 * outer + inner) * narrow + n for outer in range(wide // 2) for n in range(narrow)]
        for inner in range(2)
    ]

    def exchange(send):
        pieces = send.reshape(partners, -1, send.shape[1])
        got = lax.all_to_all(
            pieces, ("wide", "narrow"), 0, 0, axis_index_groups=groups, tiled=True
        )
        return got.reshape(send.shape)

    plain = ((partners * step, cells), BF16)
    shared = ((partners * (2 * step + 8), cells // 2), BF16) if place.fold else plain
    twin_plain = ((height, cells), BF16)
    twin_shared = ((2 * height, cells), BF16) if place.fold else twin_plain
    sums_shape = ((2 * partners, hidden_units), F32)
    own_lines = ((height, cells), F32)

    field, send = call(
        functools.partial(start_kernel, place),
        [((cells, z_count), BF16), twin_plain],
        "start",
    )(lifted_field.reshape(cells, z_count))
    some = max(1, modes // 4)
    weight = pl.pallas_call(
        weight_kernel,
        grid=(modes // some,),
        in_specs=[pl.BlockSpec((some, kz, 2, channels, channels), lambda j: (j, 0, 0, 0, 0))],
        out_specs=pl.BlockSpec((some, kz * channels, 2 * channels), lambda j: (j, 0, 0)),
        out_shape=jax.ShapeDtypeStruct((modes, kz * channels, 2 * channels), BF16),
        compiler_params=pltpu.CompilerParams(vmem_limit_bytes=VMEM_LIMIT),
        cost_estimate=pl.CostEstimate(flops=1 << 20, bytes_accessed=5 << 20, transcendentals=0),
        name="weights",
    )(spectral_weight)
    (send,) = call(functools.partial(fold_kernel, place), [plain], "fold")(send, to_twin(send))
    spectrum, send = call(
        functools.partial(mode_kernel, place),
        [((mode_lines, channels), F32), plain],
        "mode",
    )(exchange(send), y_forward, y_inverse, weight)
    own, send = call(functools.partial(part_kernel, place), [own_lines, twin_plain], "part")(
        exchange(send)
    )
    outs = [((rows_y, z_count), F32), ((cells, z_count), BF16), twin_shared]
    if place.fold:
        outs += [sums_shape]
    else:
        outs += [((channels, channels), F32), ((channels, hidden_units), F32)]
    prediction, grad_pre, send, *sums = call(functools.partial(cell_kernel, place), outs, "cell")(
        own,
        to_twin(send),
        field,
        mix_weight,
        mix_bias[:, None],
        head_weight,
        head_bias[:, None],
        out_weight.astype(F32)[:, None],
        cotangent[0],
    )
    if not place.fold:
        totals = lax.psum(tuple(sums), ("wide", "narrow"))
        sums = []
    (send,) = call(functools.partial(fold_kernel, place), [shared], "fold")(
        send, to_twin(send), *sums
    )
    adjoint, send = call(
        functools.partial(back_kernel, place),
        [((mode_lines, channels), F32), shared],
        "back",
    )(exchange(send), y_forward, y_inverse, weight)
    outs = [own_lines, twin_shared] + ([sums_shape] if place.fold else [])
    own, send, *sums = call(functools.partial(part_kernel, place), outs, "part")(exchange(send))
    grad_spectral = pl.pallas_call(
        outer_kernel,
        grid=(modes // some,),
        in_specs=[pl.BlockSpec((some, 2 * kz, channels), lambda j: (j, 0, 0))] * 2,
        out_specs=pl.BlockSpec((some, kz, 2, channels, channels), lambda j: (j, 0, 0, 0, 0)),
        out_shape=jax.ShapeDtypeStruct(spectral_weight.shape, F32),
        compiler_params=pltpu.CompilerParams(vmem_limit_bytes=VMEM_LIMIT),
        cost_estimate=pl.CostEstimate(flops=1 << 22, bytes_accessed=5 << 20, transcendentals=0),
        name="outer",
    )(spectrum.reshape(modes, 2 * kz, channels), adjoint.reshape(modes, 2 * kz, channels))
    outs = [((cells, z_count), BF16)]
    if place.fold:
        outs += [((channels, channels), F32), ((channels, hidden_units), F32)]
    grad_field, *summed = call(functools.partial(finish_kernel, place), outs, "finish")(
        own, to_twin(send), grad_pre, mix_weight, *sums
    )
    grad_mix, grad_head = summed if place.fold else totals
    return (
        prediction[None],
        grad_field.reshape(lifted_field.shape),
        grad_spectral,
        grad_mix,
        grad_head,
    )


def solution(mesh):
    return jax.shard_map(
        body,
        mesh=mesh,
        in_specs=(
            P("wide", None, "narrow", None),
            P("wide", "narrow", None, None, None),
            P(),
            P(),
            P(),
            P(),
            P(),
            P("wide", "narrow", None),
        ),
        out_specs=(
            P("wide", "narrow", None),
            P("wide", None, "narrow", None),
            P("wide", "narrow", None, None, None),
            P(),
            P(),
        ),
        check_vma=False,
    )
```

```python
import functools
import math

import jax
import jax.numpy as jnp
import numpy as np
from jax import lax
from jax.experimental import pallas as pl
from jax.experimental.pallas import tpu as pltpu
from jax.sharding import PartitionSpec as P

MX = 16
MY = 16
MZ = 16
F32 = jnp.float32
BF16 = jnp.bfloat16
VMEM_LIMIT = 32 * 1024 * 1024

TAIL_SLOPE = 0.275
TAIL = (
    0.11780925840139389,
    0.04211147502064705,
    0.3339323103427887,
    -0.3309934139251709,
    0.4519987106323242,
    -0.11485832929611206,
)


def signed(indices, count):
    return np.where(indices < count // 2, indices, indices - count)


def wave(positions, frequency, length):
    turned = np.mod(np.multiply.outer(positions, frequency), length)
    angles = turned.astype(np.float32) * np.float32(2.0 * math.pi / length)
    scale = np.float32(1.0 / math.sqrt(length))
    return np.cos(angles) * scale, np.sin(angles) * scale


def pair(cosine, sine, sign):
    return np.stack(
        [np.stack([cosine, -sign * sine], -1), np.stack([sign * sine, cosine], -1)], -2
    )


def y_tables(total_y, rows_y, kz, modes):
    cosine, sine = wave(np.arange(total_y), signed(np.arange(MY), MY), total_y)
    narrow = total_y // rows_y
    same = np.eye(kz, dtype=np.float32)
    forward = pair(cosine, sine, -1.0).reshape(narrow, rows_y, MY // modes, modes, 2, 2)
    inverse = pair(cosine, sine, 1.0).reshape(narrow, rows_y, MY // modes, modes, 2, 2)
    forward = np.einsum("nybjtr,kl->bjtkynlr", forward, same)
    inverse = np.einsum("nybjst,kl->bnyksjtl", inverse, same)
    blocks = MY // modes
    forward = forward.reshape(blocks, modes * 2 * kz, rows_y * narrow * kz * 2)
    inverse = inverse.reshape(blocks, narrow * rows_y * kz * 2, modes * 2 * kz)
    return forward.astype(BF16), inverse.astype(BF16)


def dot(a, b):
    return jnp.dot(a, b, preferred_element_type=F32)


def dot_nt(a, b):
    return lax.dot_general(a, b, (((1,), (1,)), ((), ())), preferred_element_type=F32)


def dot_tn(a, b):
    return lax.dot_general(a, b, (((0,), (0,)), ((), ())), preferred_element_type=F32)


def grid_of(rows, columns):
    shape = (rows, columns)
    return lax.broadcasted_iota(jnp.int32, shape, 0), lax.broadcasted_iota(jnp.int32, shape, 1)


def selector(rows, columns, condition):
    return jnp.where(condition(*grid_of(rows, columns)), 1.0, 0.0).astype(BF16)


def halves(values):
    high = values.astype(BF16)
    return high, (values - high.astype(F32)).astype(BF16)


def stacked(refs, lanes=slice(None)):
    return jnp.concatenate([ref[:, lanes] for ref in refs], axis=0)


def cosine_of(phase, length):
    angles = (phase & (length - 1)).astype(F32) * (2.0 * math.pi / length)
    return jnp.cos(angles) * (1.0 / math.sqrt(length))


class Place:
    def __init__(self, wide, narrow, kz, modes, rows_y, channels, z_count, fold):
        self.wide, self.narrow, self.kz, self.modes = wide, narrow, kz, modes
        self.rows_y, self.channels, self.z_count, self.fold = rows_y, channels, z_count, fold
        self.outer = wide // 2
        self.partners = self.outer * narrow
        self.lanes = rows_y * channels

    def here(self):
        wide = lax.axis_index("wide")
        return wide // 2, wide % 2

    def frequency(self, wide):
        index = (wide * self.modes) // MY
        return jnp.where(index < MX // 2, index, index - MX)

    def z_table(self, doubled):
        row, z = grid_of(2 * MZ, self.z_count)
        frequency = row >> 1
        value = cosine_of(z * frequency + (row & 1) * (self.z_count // 4), self.z_count)
        if doubled:
            value = jnp.where(frequency > 0, 2.0 * value, value)
        return value.astype(BF16)

    def expanded(self, small):
        row, column = grid_of(2 * MZ, small.shape[1])
        same = (row >> 1) == ((column >> 1) & (MZ - 1))
        blocks = []
        for g in range(small.shape[0] // 2):
            value = jnp.where((row & 1) == 0, small[2 * g : 2 * g + 1], small[2 * g + 1 : 2 * g + 2])
            blocks.append(jnp.where(same, value, 0.0))
        return jnp.concatenate(blocks, axis=0)

    def forward_x(self):
        outer, inner = self.here()
        row, column = grid_of(2 * self.outer, 4 * MZ)
        x = 2 * outer + (inner ^ (column // (2 * MZ)))
        frequency = self.frequency(2 * (row >> 1) + inner)
        quarter = self.wide // 4
        small = cosine_of(x * frequency + quarter * ((row & 1) - (column & 1)), self.wide)
        return self.expanded(small)

    def inverse_x(self):
        outer, inner = self.here()
        row, column = grid_of(4, self.outer * 2 * MZ)
        x = 2 * outer + (inner ^ (row >> 1))
        frequency = self.frequency(2 * (column // (2 * MZ)) + inner)
        quarter = self.wide // 4
        small = cosine_of(x * frequency + quarter * ((column & 1) - (row & 1)), self.wide)
        return self.expanded(small).astype(BF16)

    def sum_owner(self, index, inner):
        return ((index // self.narrow) * 2 + inner) * self.narrow + index % self.narrow


def repeat_rows(out_ref, block):
    height = block.shape[0]
    for first in range(0, out_ref.shape[0], height):
        out_ref[first : first + height] = block


def write_pieces(place, send_ref, block, shares):
    step, half = 2 * place.kz, place.lanes // 2
    height = send_ref.shape[0] // place.partners
    for p in range(place.partners):
        own = block[p * step % block.shape[0] :][:step]
        first = p * height
        send_ref[first : first + step] = own[:, :half]
        send_ref[first + step : first + 2 * step] = own[:, half:]
        send_ref[first + 2 * step : first + height] = shares[p * 8 % shares.shape[0] :][:8]


def read_pieces(place, pieces_ref):
    step = 2 * place.kz
    if pieces_ref.shape[1] == place.lanes:
        return pieces_ref[...], None
    height = pieces_ref.shape[0] // place.partners
    blocks, shares = [], []
    for p in range(place.partners):
        first = p * height
        left = pieces_ref[first : first + step]
        right = pieces_ref[first + step : first + 2 * step]
        blocks.append(jnp.concatenate([left, right], axis=1))
        shares.append(pieces_ref[first + 2 * step : first + height].astype(F32))
    return jnp.concatenate(blocks, axis=0), shares


def analysed(place, pieces, y_forward, copies):
    height = 2 * MZ
    turned = sum(
        pieces[first : first + height].astype(F32) for first in range(0, pieces.shape[0], height)
    )
    channels = place.channels
    lines = jnp.concatenate(
        [turned[:, y * channels : (y + 1) * channels] for y in range(place.rows_y)], axis=0
    )
    high, low = halves(jnp.concatenate([lines] * copies, axis=1))
    return dot(y_forward, high) + dot(y_forward, low)


def spread_lines(place, modes, y_inverse):
    lines = dot(y_inverse, modes)
    step = 2 * place.kz
    blocks = []
    for n in range(place.narrow):
        first = n * place.rows_y
        parts = [lines[(first + y) * step : (first + y + 1) * step] for y in range(place.rows_y)]
        blocks.append(jnp.concatenate(parts, axis=1))
    return jnp.concatenate(blocks, axis=0).astype(BF16)


def turn_matrix(place):
    channels, rows_y = place.channels, place.rows_y
    return selector(
        place.lanes,
        place.lanes,
        lambda row, column: (row % channels == column // rows_y)
        & (row // channels == column % rows_y),
    )


def side_by_side(values, count):
    height = values.shape[0] // count
    return jnp.concatenate([values[y * height : (y + 1) * height] for y in range(count)], axis=1)


def one_below_other(values, count):
    width = values.shape[1] // count
    return jnp.concatenate([values[:, y * width : (y + 1) * width] for y in range(count)], axis=0)


def start_kernel(place, field_ref, field_out_ref, send_ref):
    turned = dot(turn_matrix(place), field_ref[...]).astype(BF16)
    field_out_ref[...] = side_by_side(turned, place.rows_y)
    send_ref[...] = dot_nt(place.z_table(False), turned).astype(BF16)


def prepare_kernel(
    place, weight_ref, packed_ref, z_plain_ref, z_doubled_ref, turn_ref, forward_ref, inverse_ref
):
    modes, kz, _, channels, _ = weight_ref.shape
    for q in range(modes // 4):
        parts = [weight_ref[4 * q + j // 2, :, j % 2] for j in range(8)]
        packed = jnp.concatenate(parts, axis=-1).reshape(kz * channels, 8 * channels)
        packed_ref[q] = packed.astype(BF16)
    z_plain_ref[...] = place.z_table(False)
    z_doubled_ref[...] = place.z_table(True)
    turn_ref[...] = turn_matrix(place)
    forward_ref[...] = jnp.concatenate(halves(place.forward_x()), axis=1)
    inverse_ref[...] = place.inverse_x()


def fold_kernel(place, *refs):
    own_ref, got_ref = refs[:2]
    height = 2 * MZ
    values = jnp.concatenate([own_ref[:height], got_ref[:height]], axis=0)
    if len(refs) > 3:
        tables, refs = refs[2][...], refs[:2] + refs[3:]
    else:
        tables = jnp.concatenate(halves(place.forward_x()), axis=1)
    partial = dot(tables, jnp.concatenate([values, values], axis=0)).astype(BF16)
    if got_ref.shape[0] == height:
        refs[2][...] = partial
        return
    sums_ref, send_ref = refs[2:]
    got = got_ref[height:].astype(F32)
    width = sums_ref.shape[1]
    high, low = halves(sums_ref[...] + got[:, :width] + got[:, width:])
    count = place.partners
    place_of = selector(
        8 * count,
        4 * count,
        lambda row, column: (row % 8 == column // count) & (row // 8 == column % count),
    )
    shares = dot(place_of, jnp.concatenate([high, low], axis=0)).astype(BF16)
    write_pieces(place, send_ref, partial, shares)


def mode_kernel(
    place, pieces_ref, y_forward_ref, y_inverse_ref, weight_ref, spectrum_ref, send_ref
):
    kz, channels = place.kz, place.channels
    spectrum = analysed(place, pieces_ref[...], y_forward_ref[...], kz)
    spectrum_ref[...] = spectrum[:, :channels]
    row, lane = grid_of(*spectrum.shape)
    blocked = jnp.where(row % kz == lane // channels, spectrum, 0.0)
    mixed = []
    for q in range(place.modes // 4):
        left = blocked[q * 8 * kz : (q + 1) * 8 * kz].astype(BF16)
        product = dot(left, weight_ref[q])
        for j in range(4):
            own = product[j * 2 * kz : (j + 1) * 2 * kz, j * 2 * channels : (j + 1) * 2 * channels]
            real, imag = own[:, :channels], own[:, channels:]
            mixed.append(real[:kz] - imag[kz:])
            mixed.append(imag[:kz] + real[kz:])
    mode = jnp.concatenate(mixed, axis=0).astype(BF16)
    repeat_rows(send_ref, spread_lines(place, mode, y_inverse_ref[...]))


def part_kernel(place, *refs):
    pieces, shares = read_pieces(place, refs[0])
    lines = dot(refs[1][...], pieces)
    height = 2 * MZ
    refs = refs[3:] if place.fold and shares is not None else refs[2:]
    own_ref, send_ref = refs[:2]
    own_ref[...] = lines[:height]
    if shares is None:
        send_ref[...] = lines[height:].astype(BF16)
        return
    sums_ref = refs[2]
    count = place.partners
    got = jnp.concatenate(shares, axis=0).astype(BF16)

    def chosen(part):
        return dot(
            selector(
                2 * count,
                8 * count,
                lambda row, column: (row // count + 2 * part == column % 8)
                & (row % count == column // 8),
            ),
            got,
        )

    high, low = chosen(0), chosen(1)
    sums_ref[...] = high + low
    send_ref[:height] = lines[height:].astype(BF16)
    send_ref[height:] = jnp.concatenate([high, low], axis=1).astype(BF16)


def normal(values):
    scaled = 1.0 / (1.0 + TAIL_SLOPE * jnp.abs(values))
    decay = jnp.exp(-0.5 * values * values)
    tail = TAIL[-1]
    for factor in TAIL[-2::-1]:
        tail = tail * scaled + factor
    tail = tail * (scaled * decay)
    cumulative = jnp.where(values > 0.0, 1.0 - tail, tail)
    return values * cumulative, cumulative + values * (decay * (1.0 / math.sqrt(2.0 * math.pi)))


def cell_kernel(place, *refs):
    own_ref, got_ref, z_table_ref, refs = refs[0], refs[1], refs[2], refs[3:]
    field_ref, mix_ref, mix_bias_ref, head_ref, head_bias_ref = refs[:5]
    out_row_ref, out_column_ref, cotangent_ref = refs[5:8]
    prediction_ref, grad_pre_ref, send_ref = refs[8:11]
    channels, hidden_units = head_ref.shape
    rows_y, z_count = place.rows_y, place.z_count
    z_table = z_table_ref[...]
    lines = (own_ref[...] + got_ref[...].astype(F32)).astype(BF16)
    branch = side_by_side(dot_tn(lines, z_table), rows_y)
    field, head = field_ref[...], head_ref[...]
    head_turned = jnp.transpose(head.astype(F32)).astype(BF16)
    pre_act = branch + dot_tn(mix_ref[...], field) + mix_bias_ref[...]
    head_bias, out_row, out_column = head_bias_ref[...], out_row_ref[...], out_column_ref[...]
    width = 2 * z_count
    hidden, slopes, head_pre = [], [], []
    for first in range(0, rows_y * z_count, width):
        value, slope = normal(pre_act[:, first : first + width])
        hidden.append(value.astype(BF16))
        slopes.append(slope)
        head_pre.append(dot(head_turned, hidden[-1]))
    head_slopes, gradients = [], []
    for index, first in enumerate(range(0, rows_y, 2)):
        target = jnp.concatenate(
            [cotangent_ref[y : y + 1] for y in range(first, first + 2)], axis=1
        )
        active, slope = normal(head_pre[index] + head_bias)
        predicted = dot(out_row, active.astype(BF16))
        prediction_ref[first : first + 1] = predicted[:, :z_count]
        prediction_ref[first + 1 : first + 2] = predicted[:, z_count:]
        head_slope = (target * out_column * slope).astype(BF16)
        gradients.append((dot(head, head_slope) * slopes[index]).astype(BF16))
        head_slopes.append(head_slope)
    gradient = jnp.concatenate(gradients, axis=1)
    grad_pre_ref[...] = gradient
    height = 2 * MZ
    send_ref[:height] = dot_nt(z_table, one_below_other(gradient, rows_y)).astype(BF16)
    grad_mix = dot_nt(field, gradient)
    grad_head = dot_nt(jnp.concatenate(hidden, axis=1), jnp.concatenate(head_slopes, axis=1))
    if not place.fold:
        refs[-2][...] = grad_mix
        refs[-1][...] = grad_head
        return
    wide_mix = jnp.concatenate(
        [grad_mix, jnp.zeros((channels, hidden_units - channels), F32)], axis=1
    )
    high, low = halves(jnp.concatenate([grad_head, wide_mix], axis=0))
    count = place.partners
    _, inner = place.here()

    def chosen(owner):
        def condition(row, column):
            target = place.sum_owner(row % count, owner)
            return column == (row // count) * channels + target

        picked = selector(2 * count, 2 * channels, condition)
        return dot(picked, high), dot(picked, low)

    refs[11][...] = sum(chosen(inner))
    send_ref[height:] = jnp.concatenate(chosen(1 - inner), axis=1).astype(BF16)


def back_kernel(
    place, pieces_ref, y_forward_ref, y_inverse_ref, weight_ref, adjoint_ref, send_ref
):
    kz, channels = place.kz, place.channels
    pieces, shares = read_pieces(place, pieces_ref)
    adjoint = analysed(place, pieces, y_forward_ref[...], 1)
    adjoint_ref[...] = adjoint
    turned = []
    for first in range(0, adjoint.shape[0], 2 * kz):
        turned += [adjoint[first + kz : first + 2 * kz], -adjoint[first : first + kz]]
    left = jnp.concatenate([adjoint, jnp.concatenate(turned, axis=0)], axis=1)
    left = jnp.concatenate([left] * 4, axis=1)
    row, lane = grid_of(*left.shape)
    same = (row // (2 * kz)) % 4 == lane // (2 * channels)
    left = jnp.where(same, left, 0.0).astype(BF16)
    block = 8 * kz
    pulled = [
        dot_nt(left[q * block : (q + 1) * block], weight_ref[q]) for q in range(place.modes // 4)
    ]
    pulled = jnp.concatenate(pulled, axis=0)
    row, lane = grid_of(*pulled.shape)
    pulled = jnp.where(row % kz == lane // channels, pulled, 0.0).astype(BF16)
    gather = selector(
        kz * channels, channels, lambda row, column: row % channels == column
    )
    modes_back = dot(pulled, gather).astype(BF16)
    block = spread_lines(place, modes_back, y_inverse_ref[...])
    if shares is None:
        repeat_rows(send_ref, block)
        return
    total = sum(shares[1:], shares[0])
    high, low = halves(total[0:2] + total[2:4])
    rest = jnp.zeros((4, total.shape[1]), F32)
    split = jnp.concatenate([high.astype(F32), low.astype(F32), rest], axis=0)
    write_pieces(place, send_ref, block, split.astype(BF16))


def outer_kernel(spectrum_ref, adjoint_ref, out_ref, done_ref):
    done_ref[...] = jnp.zeros(done_ref.shape, F32)
    modes, kz = out_ref.shape[:2]
    for j in range(modes):
        columns = jnp.transpose(spectrum_ref[j])
        adjoint = adjoint_ref[j]
        for k in range(kz):
            s_real, s_imag = columns[:, k : k + 1], columns[:, kz + k : kz + k + 1]
            a_real, a_imag = adjoint[k : k + 1], adjoint[kz + k : kz + k + 1]
            out_ref[j, k, 0] = s_real * a_real + s_imag * a_imag
            out_ref[j, k, 1] = s_real * a_imag - s_imag * a_real


def finish_kernel(place, *refs):
    own_ref, got_ref, z_table_ref, turn_ref, grad_pre_ref, mix_ref = refs[:6]
    refs = refs[6:]
    height = 2 * MZ
    channels, rows_y = place.channels, place.rows_y
    lines = (own_ref[...] + got_ref[:height].astype(F32)).astype(BF16)
    branch = dot_tn(lines, z_table_ref[...])
    pointwise = one_below_other(dot(mix_ref[...], grad_pre_ref[...]), rows_y)
    grad_field = dot_tn(turn_ref[...], (branch + pointwise).astype(BF16)).astype(BF16)
    if not place.fold:
        refs[0][...] = grad_field
        return
    sums_ref, grad_field_ref, grad_mix_ref, grad_head_ref = refs
    grad_field_ref[...] = grad_field
    _, inner = place.here()
    count = place.partners
    width = sums_ref.shape[1]
    own_high, own_low = halves(sums_ref[...])
    got = got_ref[height:]

    def picked(kind):
        def choose(owner):
            def condition(row, column):
                target = place.sum_owner(column % count, owner)
                return (column // count == kind) & (target == row)

            return selector(channels, 2 * count, condition)

        own, twin = choose(inner), choose(1 - inner)
        both = dot(twin, got)
        return dot(own, own_high) + dot(own, own_low) + both[:, :width] + both[:, width:]

    grad_head_ref[...] = picked(0)
    grad_mix_ref[...] = picked(1)[:, :channels]


def call(kernel, outs, name):
    return pl.pallas_call(
        kernel,
        out_shape=[jax.ShapeDtypeStruct(shape, dtype) for shape, dtype in outs],
        compiler_params=pltpu.CompilerParams(vmem_limit_bytes=VMEM_LIMIT),
        cost_estimate=pl.CostEstimate(flops=1 << 22, bytes_accessed=1 << 19, transcendentals=0),
        name=name,
    )


def body(
    lifted_field,
    spectral_weight,
    mix_weight,
    mix_bias,
    head_weight,
    head_bias,
    out_weight,
    cotangent,
):
    wide = lax.axis_size("wide")
    narrow = lax.axis_size("narrow")
    devices = wide * narrow
    _, channels, rows_y, z_count = lifted_field.shape
    modes, kz = spectral_weight.shape[:2]
    hidden_units = head_weight.shape[1]
    cells = channels * rows_y
    place = Place(wide, narrow, kz, modes, rows_y, channels, z_count, False)
    place.fold = devices == channels and hidden_units == 128 and place.lanes == 256 and kz % 8 == 0
    height = 2 * MZ
    step = 2 * kz
    partners = place.partners
    mode_lines = modes * 2 * kz

    y_forward, y_inverse = y_tables(rows_y * narrow, rows_y, kz, modes)
    if len(y_forward) > 1:
        block = lax.axis_index("wide") % len(y_forward)
        y_forward = lax.dynamic_index_in_dim(jnp.asarray(y_forward), block, 0, False)
        y_inverse = lax.dynamic_index_in_dim(jnp.asarray(y_inverse), block, 0, False)
    else:
        y_forward, y_inverse = jnp.asarray(y_forward[0]), jnp.asarray(y_inverse[0])

    def to_twin(send):
        pairs = [(p, p ^ narrow) for p in range(devices)]
        return lax.ppermute(send, ("wide", "narrow"), pairs)

    groups = [
        [(2 * outer + inner) * narrow + n for outer in range(wide // 2) for n in range(narrow)]
        for inner in range(2)
    ]

    def exchange(send):
        pieces = send.reshape(partners, -1, send.shape[1])
        got = lax.all_to_all(
            pieces, ("wide", "narrow"), 0, 0, axis_index_groups=groups, tiled=True
        )
        return got.reshape(send.shape)

    plain = ((partners * step, cells), BF16)
    shared = ((partners * (2 * step + 8), cells // 2), BF16) if place.fold else plain
    twin_plain = ((height, cells), BF16)
    twin_shared = ((2 * height, cells), BF16) if place.fold else twin_plain
    sums_shape = ((2 * partners, hidden_units), F32)
    own_lines = ((height, cells), F32)

    field, send = call(
        functools.partial(start_kernel, place),
        [((channels, rows_y * z_count), BF16), twin_plain],
        "start",
    )(lifted_field.reshape(cells, z_count))
    some = max(1, modes // 4)
    weight, z_plain, z_doubled, turn, forward, inverse = call(
        functools.partial(prepare_kernel, place),
        [
            ((modes // 4, kz * channels, 8 * channels), BF16),
            ((height, z_count), BF16),
            ((height, z_count), BF16),
            ((cells, cells), BF16),
            ((wide // 2 * height, 4 * height), BF16),
            ((2 * height, wide // 2 * height), BF16),
        ],
        "prepare",
    )(spectral_weight)
    (send,) = call(functools.partial(fold_kernel, place), [plain], "fold")(send, to_twin(send))
    spectrum, send = call(
        functools.partial(mode_kernel, place),
        [((mode_lines, channels), F32), plain],
        "mode",
    )(exchange(send), y_forward, y_inverse, weight)
    own, send = call(functools.partial(part_kernel, place), [own_lines, twin_plain], "part")(
        exchange(send), inverse
    )
    outs = [((rows_y, z_count), F32), ((channels, rows_y * z_count), BF16), twin_shared]
    if place.fold:
        outs += [sums_shape]
    else:
        outs += [((channels, channels), F32), ((channels, hidden_units), F32)]
    prediction, grad_pre, send, *sums = call(functools.partial(cell_kernel, place), outs, "cell")(
        own,
        to_twin(send),
        z_doubled,
        field,
        mix_weight,
        mix_bias[:, None],
        head_weight,
        head_bias[:, None],
        out_weight[None],
        out_weight.astype(F32)[:, None],
        cotangent[0],
    )
    if not place.fold:
        totals = lax.psum(tuple(sums), ("wide", "narrow"))
        sums = []
    (send,) = call(functools.partial(fold_kernel, place), [shared], "fold")(
        send, to_twin(send), forward, *sums
    )
    adjoint, send = call(
        functools.partial(back_kernel, place),
        [((mode_lines, channels), F32), shared],
        "back",
    )(exchange(send), y_forward, y_inverse, weight)
    grad_spectral, done = pl.pallas_call(
        outer_kernel,
        grid=(modes // some,),
        in_specs=[pl.BlockSpec((some, 2 * kz, channels), lambda j: (j, 0, 0))] * 2,
        out_specs=[
            pl.BlockSpec((some, kz, 2, channels, channels), lambda j: (j, 0, 0, 0, 0)),
            pl.BlockSpec((8, 128), lambda j: (0, 0)),
        ],
        out_shape=[
            jax.ShapeDtypeStruct(spectral_weight.shape, F32),
            jax.ShapeDtypeStruct((8, 128), F32),
        ],
        compiler_params=pltpu.CompilerParams(vmem_limit_bytes=VMEM_LIMIT),
        cost_estimate=pl.CostEstimate(flops=1 << 22, bytes_accessed=5 << 20, transcendentals=0),
        name="outer",
    )(spectrum.reshape(modes, 2 * kz, channels), adjoint.reshape(modes, 2 * kz, channels))
    pieces = exchange(send)
    outs = [own_lines, twin_shared] + ([sums_shape] if place.fold else [])
    operands = (pieces, inverse, done) if place.fold else (pieces, inverse)
    own, send, *sums = call(functools.partial(part_kernel, place), outs, "part")(*operands)
    outs = [((cells, z_count), BF16)]
    if place.fold:
        outs += [((channels, channels), F32), ((channels, hidden_units), F32)]
    grad_field, *summed = call(functools.partial(finish_kernel, place), outs, "finish")(
        own, to_twin(send), z_plain, turn, grad_pre, mix_weight, *sums
    )
    grad_mix, grad_head = summed if place.fold else totals
    return (
        prediction[None],
        grad_field.reshape(lifted_field.shape),
        grad_spectral,
        grad_mix,
        grad_head,
    )


def solution(mesh):
    return jax.shard_map(
        body,
        mesh=mesh,
        in_specs=(
            P("wide", None, "narrow", None),
            P("wide", "narrow", None, None, None),
            P(),
            P(),
            P(),
            P(),
            P(),
            P("wide", "narrow", None),
        ),
        out_specs=(
            P("wide", "narrow", None),
            P("wide", None, "narrow", None),
            P("wide", "narrow", None, None, None),
            P(),
            P(),
        ),
        check_vma=False,
    )
```

```python
import functools
import math

import jax
import jax.numpy as jnp
import numpy as np
from jax import lax
from jax.experimental import pallas as pl
from jax.experimental.pallas import tpu as pltpu
from jax.sharding import PartitionSpec as P

MX = 16
MY = 16
MZ = 16
F32 = jnp.float32
BF16 = jnp.bfloat16
VMEM_LIMIT = 32 * 1024 * 1024

TAIL_SLOPE = 0.275
TAIL = (
    0.11780925840139389,
    0.04211147502064705,
    0.3339323103427887,
    -0.3309934139251709,
    0.4519987106323242,
    -0.11485832929611206,
)


def signed(indices, count):
    return np.where(indices < count // 2, indices, indices - count)


def wave(positions, frequency, length):
    turned = np.mod(np.multiply.outer(positions, frequency), length)
    angles = turned.astype(np.float32) * np.float32(2.0 * math.pi / length)
    scale = np.float32(1.0 / math.sqrt(length))
    return np.cos(angles) * scale, np.sin(angles) * scale


def pair(cosine, sine, sign):
    return np.stack(
        [np.stack([cosine, -sign * sine], -1), np.stack([sign * sine, cosine], -1)], -2
    )


def y_tables(total_y, rows_y, kz, modes):
    cosine, sine = wave(np.arange(total_y), signed(np.arange(MY), MY), total_y)
    narrow = total_y // rows_y
    same = np.eye(kz, dtype=np.float32)
    forward = pair(cosine, sine, -1.0).reshape(narrow, rows_y, MY // modes, modes, 2, 2)
    inverse = pair(cosine, sine, 1.0).reshape(narrow, rows_y, MY // modes, modes, 2, 2)
    forward = np.einsum("nybjtr,kl->bjtkynlr", forward, same)
    inverse = np.einsum("nybjst,kl->bnyksjtl", inverse, same)
    blocks = MY // modes
    forward = forward.reshape(blocks, modes * 2 * kz, rows_y * narrow * kz * 2)
    inverse = inverse.reshape(blocks, narrow * rows_y * kz * 2, modes * 2 * kz)
    return forward.astype(BF16), inverse.astype(BF16)


def dot(a, b):
    return jnp.dot(a, b, preferred_element_type=F32)


def dot_nt(a, b):
    return lax.dot_general(a, b, (((1,), (1,)), ((), ())), preferred_element_type=F32)


def dot_tn(a, b):
    return lax.dot_general(a, b, (((0,), (0,)), ((), ())), preferred_element_type=F32)


def grid_of(rows, columns):
    shape = (rows, columns)
    return lax.broadcasted_iota(jnp.int32, shape, 0), lax.broadcasted_iota(jnp.int32, shape, 1)


def selector(rows, columns, condition):
    return jnp.where(condition(*grid_of(rows, columns)), 1.0, 0.0).astype(BF16)


def halves(values):
    high = values.astype(BF16)
    return high, (values - high.astype(F32)).astype(BF16)


def stacked(refs, lanes=slice(None)):
    return jnp.concatenate([ref[:, lanes] for ref in refs], axis=0)


def cosine_of(phase, length):
    angles = (phase & (length - 1)).astype(F32) * (2.0 * math.pi / length)
    return jnp.cos(angles) * (1.0 / math.sqrt(length))


class Place:
    def __init__(self, wide, narrow, kz, modes, rows_y, channels, z_count, fold):
        self.wide, self.narrow, self.kz, self.modes = wide, narrow, kz, modes
        self.rows_y, self.channels, self.z_count, self.fold = rows_y, channels, z_count, fold
        self.outer = wide // 2
        self.partners = self.outer * narrow
        self.lanes = rows_y * channels

    def here(self):
        wide = lax.axis_index("wide")
        return wide // 2, wide % 2

    def frequency(self, wide):
        index = (wide * self.modes) // MY
        return jnp.where(index < MX // 2, index, index - MX)

    def z_table(self, doubled):
        row, z = grid_of(2 * MZ, self.z_count)
        frequency = row >> 1
        value = cosine_of(z * frequency + (row & 1) * (self.z_count // 4), self.z_count)
        if doubled:
            value = jnp.where(frequency > 0, 2.0 * value, value)
        return value.astype(BF16)

    def expanded(self, small):
        row, column = grid_of(2 * MZ, small.shape[1])
        same = (row >> 1) == ((column >> 1) & (MZ - 1))
        blocks = []
        for g in range(small.shape[0] // 2):
            value = jnp.where((row & 1) == 0, small[2 * g : 2 * g + 1], small[2 * g + 1 : 2 * g + 2])
            blocks.append(jnp.where(same, value, 0.0))
        return jnp.concatenate(blocks, axis=0)

    def forward_x(self):
        outer, inner = self.here()
        row, column = grid_of(2 * self.outer, 4 * MZ)
        x = 2 * outer + (inner ^ (column // (2 * MZ)))
        frequency = self.frequency(2 * (row >> 1) + inner)
        quarter = self.wide // 4
        small = cosine_of(x * frequency + quarter * ((row & 1) - (column & 1)), self.wide)
        return self.expanded(small)

    def inverse_x(self):
        outer, inner = self.here()
        row, column = grid_of(4, self.outer * 2 * MZ)
        x = 2 * outer + (inner ^ (row >> 1))
        frequency = self.frequency(2 * (column // (2 * MZ)) + inner)
        quarter = self.wide // 4
        small = cosine_of(x * frequency + quarter * ((column & 1) - (row & 1)), self.wide)
        return self.expanded(small).astype(BF16)


def repeat_rows(out_ref, block):
    height = block.shape[0]
    for first in range(0, out_ref.shape[0], height):
        out_ref[first : first + height] = block


def write_pieces(place, send_ref, block, shares):
    step, half = 2 * place.kz, place.lanes // 2
    height = send_ref.shape[0] // place.partners
    for p in range(place.partners):
        own = block[p * step % block.shape[0] :][:step]
        first = p * height
        send_ref[first : first + step] = own[:, :half]
        send_ref[first + step : first + 2 * step] = own[:, half:]
        send_ref[first + 2 * step : first + height] = shares[p * 8 % shares.shape[0] :][:8]


def read_pieces(place, pieces_ref):
    step = 2 * place.kz
    if pieces_ref.shape[1] == place.lanes:
        return pieces_ref[...], None
    height = pieces_ref.shape[0] // place.partners
    blocks, shares = [], []
    for p in range(place.partners):
        first = p * height
        left = pieces_ref[first : first + step]
        right = pieces_ref[first + step : first + 2 * step]
        blocks.append(jnp.concatenate([left, right], axis=1))
        shares.append(pieces_ref[first + 2 * step : first + height].astype(F32))
    return jnp.concatenate(blocks, axis=0), shares


def analysed(place, pieces, y_forward, copies):
    height = 2 * MZ
    turned = sum(
        pieces[first : first + height].astype(F32) for first in range(0, pieces.shape[0], height)
    )
    channels = place.channels
    lines = jnp.concatenate(
        [turned[:, y * channels : (y + 1) * channels] for y in range(place.rows_y)], axis=0
    )
    return dot(y_forward, jnp.concatenate([lines.astype(BF16)] * copies, axis=1))


def spread_lines(place, modes, y_inverse):
    lines = dot(y_inverse, modes)
    step = 2 * place.kz
    blocks = []
    for n in range(place.narrow):
        first = n * place.rows_y
        parts = [lines[(first + y) * step : (first + y + 1) * step] for y in range(place.rows_y)]
        blocks.append(jnp.concatenate(parts, axis=1))
    return jnp.concatenate(blocks, axis=0).astype(BF16)


def turn_matrix(place, forward):
    channels, rows_y = place.channels, place.rows_y

    def same(row, column):
        if forward:
            row, column = column, row
        return (row % channels == column // rows_y) & (row // channels == column % rows_y)

    return selector(place.lanes, place.lanes, same)


def side_by_side(values, count):
    height = values.shape[0] // count
    return jnp.concatenate([values[y * height : (y + 1) * height] for y in range(count)], axis=1)


def one_below_other(values, count):
    width = values.shape[1] // count
    return jnp.concatenate([values[:, y * width : (y + 1) * width] for y in range(count)], axis=0)


def start_kernel(place, field_ref, twin_ref, send_ref):
    fields = jnp.concatenate([field_ref[...], twin_ref[...]], axis=0)
    spectra = dot_nt(place.z_table(False), fields).astype(BF16)
    values = one_below_other(spectra, 2)
    values = dot(values, turn_matrix(place, True)).astype(BF16)
    tables = jnp.concatenate(halves(place.forward_x()), axis=1)
    send_ref[...] = dot(tables, jnp.concatenate([values, values], axis=0)).astype(BF16)


def prepare_kernel(place, weight_ref, field_ref, mix_ref, mix_bias_ref, head_ref, *refs):
    packed_ref, z_plain_ref, z_doubled_ref, turn_ref, forward_ref, inverse_ref = refs[:6]
    field_out_ref, pointwise_ref, head_out_ref, held_ref, arrived = refs[6:]
    modes, kz, _, channels, _ = weight_ref.shape
    copies = []
    for q in range(modes // 4):
        part = pl.ds(4 * q, 4)
        copies.append(
            pltpu.make_async_copy(weight_ref.at[part], held_ref.at[part], arrived.at[q])
        )
        copies[-1].start()
    z_plain_ref[...] = place.z_table(False)
    z_doubled_ref[...] = place.z_table(True)
    turn_ref[...] = turn_matrix(place, False)
    forward_ref[...] = jnp.concatenate(halves(place.forward_x()), axis=1)
    inverse_ref[...] = place.inverse_x()
    field = side_by_side(dot(turn_ref[...], field_ref[...]).astype(BF16), place.rows_y)
    field_out_ref[...] = field
    pointwise_ref[...] = dot_tn(mix_ref[...], field) + mix_bias_ref[...]
    head_out_ref[...] = jnp.transpose(head_ref[...].astype(F32)).astype(BF16)
    for q in range(modes // 4):
        copies[q].wait()
        parts = [held_ref[4 * q + j // 2, :, j % 2] for j in range(8)]
        packed = jnp.concatenate(parts, axis=-1).reshape(kz * channels, 8 * channels)
        packed_ref[q] = packed.astype(BF16)


def fold_kernel(place, own_ref, got_ref, tables_ref, *refs):
    values = jnp.concatenate([own_ref[...], got_ref[...]], axis=0)
    values = jnp.concatenate([values, values], axis=0)
    partial = dot(tables_ref[...], values).astype(BF16)
    if place.fold:
        shares_ref, send_ref = refs
        write_pieces(place, send_ref, partial, shares_ref[...])
    else:
        refs[0][...] = partial


def mode_kernel(
    place, pieces_ref, y_forward_ref, y_inverse_ref, weight_ref, spectrum_ref, send_ref
):
    kz, channels = place.kz, place.channels
    spectrum = analysed(place, pieces_ref[...], y_forward_ref[...], kz)
    spectrum_ref[...] = spectrum[:, :channels]
    row, lane = grid_of(*spectrum.shape)
    blocked = jnp.where(row % kz == lane // channels, spectrum, 0.0)
    mixed = []
    for q in range(place.modes // 4):
        left = blocked[q * 8 * kz : (q + 1) * 8 * kz].astype(BF16)
        product = dot(left, weight_ref[q])
        for j in range(4):
            own = product[j * 2 * kz : (j + 1) * 2 * kz, j * 2 * channels : (j + 1) * 2 * channels]
            real, imag = own[:, :channels], own[:, channels:]
            mixed.append(real[:kz] - imag[kz:])
            mixed.append(imag[:kz] + real[kz:])
    mode = jnp.concatenate(mixed, axis=0).astype(BF16)
    repeat_rows(send_ref, spread_lines(place, mode, y_inverse_ref[...]))


def part_kernel(place, pieces_ref, table_ref, *refs):
    pieces, shares = read_pieces(place, pieces_ref)
    lines = dot(table_ref[...], pieces)
    height = 2 * MZ
    if shares is None:
        own_ref, send_ref = refs
        own_ref[...] = lines[:height]
        send_ref[...] = lines[height:].astype(BF16)
        return
    _, own_ref, send_ref, sums_ref = refs
    own_ref[...] = lines[:height]
    send_ref[:height] = lines[height:].astype(BF16)
    got = jnp.concatenate(shares, axis=0).astype(BF16)
    channels = place.channels

    def chosen(part):
        return dot(
            selector(
                2 * channels,
                got.shape[0],
                lambda row, column: (column // 8 == (row % channels) // 2)
                & (column % 8 == 4 * part + 2 * (row // channels) + row % 2),
            ),
            got,
        )

    high, low = chosen(0), chosen(1)
    sums_ref[...] = high + low
    send_ref[height:] = jnp.concatenate([high, low], axis=1).astype(BF16)


def normal(values):
    scaled = 1.0 / (1.0 + TAIL_SLOPE * jnp.abs(values))
    decay = jnp.exp(-0.5 * values * values)
    tail = TAIL[-1]
    for factor in TAIL[-2::-1]:
        tail = tail * scaled + factor
    tail = tail * (scaled * decay)
    cumulative = jnp.where(values > 0.0, 1.0 - tail, tail)
    return values * cumulative, cumulative + values * (decay * (1.0 / math.sqrt(2.0 * math.pi)))


def cell_kernel(place, *refs):
    own_ref, got_ref, z_table_ref, pointwise_ref, head_ref, head_turned_ref = refs[:6]
    head_bias_ref, out_row_ref, out_column_ref, cotangent_ref = refs[6:10]
    prediction_ref, grad_pre_ref, send_ref, hidden_ref, head_slope_ref = refs[10:]
    rows_y, z_count = place.rows_y, place.z_count
    z_table = z_table_ref[...]
    lines = (own_ref[...] + got_ref[...].astype(F32)).astype(BF16)
    pre_act = side_by_side(dot_tn(lines, z_table), rows_y) + pointwise_ref[...]
    head, head_turned = head_ref[...], head_turned_ref[...]
    head_bias, out_row, out_column = head_bias_ref[...], out_row_ref[...], out_column_ref[...]
    width = 2 * z_count
    slopes, head_pre = [], []
    for first in range(0, rows_y * z_count, width):
        value, slope = normal(pre_act[:, first : first + width])
        hidden = value.astype(BF16)
        hidden_ref[:, first : first + width] = hidden
        slopes.append(slope)
        head_pre.append(dot(head_turned, hidden))
    gradients = []
    for index, first in enumerate(range(0, rows_y, 2)):
        target = jnp.concatenate(
            [cotangent_ref[y : y + 1] for y in range(first, first + 2)], axis=1
        )
        active, slope = normal(head_pre[index] + head_bias)
        predicted = dot(out_row, active.astype(BF16))
        prediction_ref[first : first + 1] = predicted[:, :z_count]
        prediction_ref[first + 1 : first + 2] = predicted[:, z_count:]
        head_slope = (target * out_column * slope).astype(BF16)
        head_slope_ref[:, first * z_count : first * z_count + width] = head_slope
        gradients.append((dot(head, head_slope) * slopes[index]).astype(BF16))
    gradient = jnp.concatenate(gradients, axis=1)
    grad_pre_ref[...] = gradient
    send_ref[...] = dot_nt(z_table, one_below_other(gradient, rows_y)).astype(BF16)


def sums_kernel(place, field_ref, gradient_ref, hidden_ref, head_slope_ref, *refs):
    grad_mix = dot_nt(field_ref[...], gradient_ref[...])
    grad_head = dot_nt(hidden_ref[...], head_slope_ref[...])
    if not place.fold:
        refs[0][...] = grad_mix
        refs[1][...] = grad_head
        return
    channels, hidden_units = grad_head.shape
    rest = jnp.zeros((channels, hidden_units - channels), F32)
    wide_mix = jnp.concatenate([grad_mix, rest], axis=1)
    high, low = halves(jnp.concatenate([grad_head, wide_mix], axis=0))
    split = jnp.concatenate([high, low], axis=0)
    place_of = selector(
        8 * place.partners,
        4 * channels,
        lambda row, column: (column % channels == 2 * (row // 8) + row % 2)
        & (column // channels == (row % 8) // 2),
    )
    refs[0][...] = dot(place_of, split).astype(BF16)


def back_kernel(
    place, pieces_ref, y_forward_ref, y_inverse_ref, weight_ref, adjoint_ref, send_ref
):
    kz, channels = place.kz, place.channels
    pieces, shares = read_pieces(place, pieces_ref)
    adjoint = analysed(place, pieces, y_forward_ref[...], 1)
    adjoint_ref[...] = adjoint
    turned = []
    for first in range(0, adjoint.shape[0], 2 * kz):
        turned += [adjoint[first + kz : first + 2 * kz], -adjoint[first : first + kz]]
    left = jnp.concatenate([adjoint, jnp.concatenate(turned, axis=0)], axis=1)
    left = jnp.concatenate([left] * 4, axis=1)
    row, lane = grid_of(*left.shape)
    same = (row // (2 * kz)) % 4 == lane // (2 * channels)
    left = jnp.where(same, left, 0.0).astype(BF16)
    block = 8 * kz
    pulled = [
        dot_nt(left[q * block : (q + 1) * block], weight_ref[q]) for q in range(place.modes // 4)
    ]
    pulled = jnp.concatenate(pulled, axis=0)
    row, lane = grid_of(*pulled.shape)
    pulled = jnp.where(row % kz == lane // channels, pulled, 0.0).astype(BF16)
    gather = selector(
        kz * channels, channels, lambda row, column: row % channels == column
    )
    modes_back = dot(pulled, gather).astype(BF16)
    block = spread_lines(place, modes_back, y_inverse_ref[...])
    if shares is None:
        repeat_rows(send_ref, block)
        return
    total = sum(shares[1:], shares[0])
    high, low = halves(total[0:4] + total[4:8])
    split = jnp.concatenate([high.astype(F32), low.astype(F32)], axis=0)
    write_pieces(place, send_ref, block, split.astype(BF16))


def outer_kernel(spectrum_ref, adjoint_ref, out_ref, done_ref):
    done_ref[...] = jnp.zeros(done_ref.shape, F32)
    modes, kz = out_ref.shape[:2]
    for j in range(modes):
        columns = jnp.transpose(spectrum_ref[j])
        adjoint = adjoint_ref[j]
        for k in range(kz):
            s_real, s_imag = columns[:, k : k + 1], columns[:, kz + k : kz + k + 1]
            a_real, a_imag = adjoint[k : k + 1], adjoint[kz + k : kz + k + 1]
            out_ref[j, k, 0] = s_real * a_real + s_imag * a_imag
            out_ref[j, k, 1] = s_real * a_imag - s_imag * a_real


def pointwise_kernel(place, mix_ref, gradient_ref, out_ref):
    z_count = place.z_count
    product = dot(mix_ref[...], gradient_ref[...])
    for y in range(place.rows_y):
        out_ref[:, y, :] = product[:, y * z_count : (y + 1) * z_count]


def finish_kernel(place, *refs):
    own_ref, got_ref, z_table_ref, turn_ref, pointwise_ref, prediction_ref = refs[:6]
    refs = refs[6:]
    height = 2 * MZ
    channels = place.channels
    lines = (own_ref[...] + got_ref[:height].astype(F32)).astype(BF16)
    lines = dot(lines, turn_ref[...]).astype(BF16)
    pointwise = pointwise_ref[...].reshape(place.lanes, place.z_count)
    grad_field = (dot_tn(lines, z_table_ref[...]) + pointwise).astype(BF16)
    if not place.fold:
        refs[0][...] = grad_field
        refs[1][...] = prediction_ref[...]
        return
    sums_ref, grad_field_ref, out_ref, grad_mix_ref, grad_head_ref = refs
    grad_field_ref[...] = grad_field
    out_ref[...] = prediction_ref[...]
    got = got_ref[height:].astype(F32)
    width = sums_ref.shape[1]
    total = sums_ref[...] + got[:, :width] + got[:, width:]
    grad_head_ref[...] = total[:channels]
    grad_mix_ref[...] = total[channels:, :channels]


def call(kernel, outs, name, **spec):
    return pl.pallas_call(
        kernel,
        out_shape=[jax.ShapeDtypeStruct(shape, dtype) for shape, dtype in outs],
        compiler_params=pltpu.CompilerParams(vmem_limit_bytes=VMEM_LIMIT),
        cost_estimate=pl.CostEstimate(flops=1 << 22, bytes_accessed=1 << 19, transcendentals=0),
        name=name,
        **spec,
    )


def body(
    lifted_field,
    spectral_weight,
    mix_weight,
    mix_bias,
    head_weight,
    head_bias,
    out_weight,
    cotangent,
):
    wide = lax.axis_size("wide")
    narrow = lax.axis_size("narrow")
    devices = wide * narrow
    _, channels, rows_y, z_count = lifted_field.shape
    modes, kz = spectral_weight.shape[:2]
    hidden_units = head_weight.shape[1]
    cells = channels * rows_y
    place = Place(wide, narrow, kz, modes, rows_y, channels, z_count, False)
    place.fold = 2 * place.partners == channels and hidden_units == 128 and cells == 256 and kz % 8 == 0
    height = 2 * MZ
    step = 2 * kz
    partners = place.partners
    mode_lines = modes * 2 * kz

    y_forward, y_inverse = y_tables(rows_y * narrow, rows_y, kz, modes)
    if len(y_forward) > 1:
        block = lax.axis_index("wide") % len(y_forward)
        y_forward = lax.dynamic_index_in_dim(jnp.asarray(y_forward), block, 0, False)
        y_inverse = lax.dynamic_index_in_dim(jnp.asarray(y_inverse), block, 0, False)
    else:
        y_forward, y_inverse = jnp.asarray(y_forward[0]), jnp.asarray(y_inverse[0])

    def to_twin(send):
        pairs = [(p, p ^ narrow) for p in range(devices)]
        return lax.ppermute(send, ("wide", "narrow"), pairs)

    groups = [
        [(2 * outer + inner) * narrow + n for outer in range(wide // 2) for n in range(narrow)]
        for inner in range(2)
    ]

    def exchange(send):
        pieces = send.reshape(partners, -1, send.shape[1])
        got = lax.all_to_all(
            pieces, ("wide", "narrow"), 0, 0, axis_index_groups=groups, tiled=True
        )
        return got.reshape(send.shape)

    plain = ((partners * step, cells), BF16)
    shared = ((partners * (2 * step + 8), cells // 2), BF16) if place.fold else plain
    twin_plain = ((height, cells), BF16)
    twin_shared = ((height + 2 * channels, cells), BF16) if place.fold else twin_plain
    sums_shape = ((2 * channels, hidden_units), F32)
    own_lines = ((height, cells), F32)
    across = (channels, rows_y * z_count)

    def run(kernel, outs, name, **spec):
        return call(functools.partial(kernel, place), outs, name, **spec)

    flat_field = lifted_field.reshape(cells, z_count)
    (send,) = run(start_kernel, [plain], "start")(flat_field, to_twin(flat_field))
    vmem = pl.BlockSpec(memory_space=pltpu.VMEM)
    weight, z_plain, z_doubled, turn, forward, inverse, field, pointwise, head_turned = run(
        prepare_kernel,
        [
            ((modes // 4, kz * channels, 8 * channels), BF16),
            ((height, z_count), BF16),
            ((height, z_count), BF16),
            ((cells, cells), BF16),
            ((wide // 2 * height, 4 * height), BF16),
            ((2 * height, wide // 2 * height), BF16),
            (across, BF16),
            (across, F32),
            ((hidden_units, channels), BF16),
        ],
        "prepare",
        in_specs=[pl.BlockSpec(memory_space=pltpu.HBM)] + [vmem] * 4,
        scratch_shapes=[
            pltpu.VMEM(spectral_weight.shape, F32),
            pltpu.SemaphoreType.DMA((modes // 4,)),
        ],
    )(spectral_weight, flat_field, mix_weight, mix_bias[:, None], head_weight)
    spectrum, send = run(mode_kernel, [((mode_lines, channels), F32), plain], "mode")(
        exchange(send), y_forward, y_inverse, weight
    )
    own, send = run(part_kernel, [own_lines, twin_plain], "part")(exchange(send), inverse)
    prediction, grad_pre, send, hidden, head_slope = run(
        cell_kernel,
        [
            ((rows_y, z_count), F32),
            (across, BF16),
            twin_plain,
            (across, BF16),
            ((hidden_units, rows_y * z_count), BF16),
        ],
        "cell",
    )(
        own,
        to_twin(send),
        z_doubled,
        pointwise,
        head_weight,
        head_turned,
        head_bias[:, None],
        out_weight[None],
        out_weight.astype(F32)[:, None],
        cotangent[0],
    )
    if place.fold:
        outs = [((8 * partners, hidden_units), BF16)]
    else:
        outs = [((channels, channels), F32), ((channels, hidden_units), F32)]
    sums = run(sums_kernel, outs, "sums")(field, grad_pre, hidden, head_slope)
    if not place.fold:
        totals = lax.psum(tuple(sums), ("wide", "narrow"))
        sums = []
    (send,) = run(fold_kernel, [shared], "fold")(send, to_twin(send), forward, *sums)
    adjoint, send = run(back_kernel, [((mode_lines, channels), F32), shared], "back")(
        exchange(send), y_forward, y_inverse, weight
    )
    some = max(1, modes // 4)
    grad_spectral, done = pl.pallas_call(
        outer_kernel,
        grid=(modes // some,),
        in_specs=[pl.BlockSpec((some, 2 * kz, channels), lambda j: (j, 0, 0))] * 2,
        out_specs=[
            pl.BlockSpec((some, kz, 2, channels, channels), lambda j: (j, 0, 0, 0, 0)),
            pl.BlockSpec((8, 128), lambda j: (0, 0)),
        ],
        out_shape=[
            jax.ShapeDtypeStruct(spectral_weight.shape, F32),
            jax.ShapeDtypeStruct((8, 128), F32),
        ],
        compiler_params=pltpu.CompilerParams(vmem_limit_bytes=VMEM_LIMIT),
        cost_estimate=pl.CostEstimate(flops=1 << 22, bytes_accessed=5 << 20, transcendentals=0),
        name="outer",
    )(spectrum.reshape(modes, 2 * kz, channels), adjoint.reshape(modes, 2 * kz, channels))
    (pointwise,) = run(pointwise_kernel, [((channels, rows_y, z_count), F32)], "pointwise")(
        mix_weight, grad_pre
    )
    outs = [own_lines, twin_shared] + ([sums_shape] if place.fold else [])
    after = (done,) if place.fold else ()
    own, send, *sums = run(part_kernel, outs, "part")(exchange(send), inverse, *after)
    outs = [((cells, z_count), BF16), ((rows_y, z_count), F32)]
    if place.fold:
        outs += [((channels, channels), F32), ((channels, hidden_units), F32)]
    grad_field, prediction, *summed = run(finish_kernel, outs, "finish")(
        own, to_twin(send), z_plain, turn, pointwise, prediction, *sums
    )
    grad_mix, grad_head = summed if place.fold else totals
    return (
        prediction[None],
        grad_field.reshape(lifted_field.shape),
        grad_spectral,
        grad_mix,
        grad_head,
    )


def solution(mesh):
    return jax.shard_map(
        body,
        mesh=mesh,
        in_specs=(
            P("wide", None, "narrow", None),
            P("wide", "narrow", None, None, None),
            P(),
            P(),
            P(),
            P(),
            P(),
            P("wide", "narrow", None),
        ),
        out_specs=(
            P("wide", "narrow", None),
            P("wide", None, "narrow", None),
            P("wide", "narrow", None, None, None),
            P(),
            P(),
        ),
        check_vma=False,
    )
```

```python
import functools
import math

import jax
import jax.numpy as jnp
import numpy as np
from jax import lax
from jax.experimental import pallas as pl
from jax.experimental.pallas import tpu as pltpu
from jax.sharding import PartitionSpec as P

MX = 16
MY = 16
MZ = 16
F32 = jnp.float32
BF16 = jnp.bfloat16
VMEM_LIMIT = 32 * 1024 * 1024

TAIL_SLOPE = 0.275
TAIL = (
    0.11780925840139389,
    0.04211147502064705,
    0.3339323103427887,
    -0.3309934139251709,
    0.4519987106323242,
    -0.11485832929611206,
)


def signed(indices, count):
    return np.where(indices < count // 2, indices, indices - count)


def wave(positions, frequency, length):
    turned = np.mod(np.multiply.outer(positions, frequency), length)
    angles = turned.astype(np.float32) * np.float32(2.0 * math.pi / length)
    scale = np.float32(1.0 / math.sqrt(length))
    return np.cos(angles) * scale, np.sin(angles) * scale


def pair(cosine, sine, sign):
    return np.stack(
        [np.stack([cosine, -sign * sine], -1), np.stack([sign * sine, cosine], -1)], -2
    )


def y_tables(total_y, rows_y, kz, modes):
    cosine, sine = wave(np.arange(total_y), signed(np.arange(MY), MY), total_y)
    narrow = total_y // rows_y
    same = np.eye(kz, dtype=np.float32)
    forward = pair(cosine, sine, -1.0).reshape(narrow, rows_y, MY // modes, modes, 2, 2)
    inverse = pair(cosine, sine, 1.0).reshape(narrow, rows_y, MY // modes, modes, 2, 2)
    forward = np.einsum("nybjtr,kl->bjtkynlr", forward, same)
    inverse = np.einsum("nybjst,kl->bnyksjtl", inverse, same)
    blocks = MY // modes
    forward = forward.reshape(blocks, modes * 2 * kz, rows_y * narrow * kz * 2)
    inverse = inverse.reshape(blocks, narrow * rows_y * kz * 2, modes * 2 * kz)
    return forward.astype(BF16), inverse.astype(BF16)


def dot(a, b):
    return jnp.dot(a, b, preferred_element_type=F32)


def dot_nt(a, b):
    return lax.dot_general(a, b, (((1,), (1,)), ((), ())), preferred_element_type=F32)


def dot_tn(a, b):
    return lax.dot_general(a, b, (((0,), (0,)), ((), ())), preferred_element_type=F32)


def grid_of(rows, columns):
    shape = (rows, columns)
    return lax.broadcasted_iota(jnp.int32, shape, 0), lax.broadcasted_iota(jnp.int32, shape, 1)


def selector(rows, columns, condition):
    return jnp.where(condition(*grid_of(rows, columns)), 1.0, 0.0).astype(BF16)


def halves(values):
    high = values.astype(BF16)
    return high, (values - high.astype(F32)).astype(BF16)


def stacked(refs, lanes=slice(None)):
    return jnp.concatenate([ref[:, lanes] for ref in refs], axis=0)


def cosine_of(phase, length):
    angles = (phase & (length - 1)).astype(F32) * (2.0 * math.pi / length)
    return jnp.cos(angles) * (1.0 / math.sqrt(length))


class Place:
    def __init__(self, wide, narrow, kz, modes, rows_y, channels, z_count, fold):
        self.wide, self.narrow, self.kz, self.modes = wide, narrow, kz, modes
        self.rows_y, self.channels, self.z_count, self.fold = rows_y, channels, z_count, fold
        self.outer = wide // 2
        self.partners = self.outer * narrow
        self.lanes = rows_y * channels

    def here(self):
        wide = lax.axis_index("wide")
        return wide // 2, wide % 2

    def frequency(self, wide):
        index = (wide * self.modes) // MY
        return jnp.where(index < MX // 2, index, index - MX)

    def z_table(self, doubled):
        row, z = grid_of(2 * MZ, self.z_count)
        frequency = row >> 1
        value = cosine_of(z * frequency + (row & 1) * (self.z_count // 4), self.z_count)
        if doubled:
            value = jnp.where(frequency > 0, 2.0 * value, value)
        return value.astype(BF16)

    def expanded(self, small):
        row, column = grid_of(2 * MZ, small.shape[1])
        same = (row >> 1) == ((column >> 1) & (MZ - 1))
        blocks = []
        for g in range(small.shape[0] // 2):
            value = jnp.where((row & 1) == 0, small[2 * g : 2 * g + 1], small[2 * g + 1 : 2 * g + 2])
            blocks.append(jnp.where(same, value, 0.0))
        return jnp.concatenate(blocks, axis=0)

    def forward_x(self):
        outer, inner = self.here()
        row, column = grid_of(2 * self.outer, 4 * MZ)
        x = 2 * outer + (inner ^ (column // (2 * MZ)))
        frequency = self.frequency(2 * (row >> 1) + inner)
        quarter = self.wide // 4
        small = cosine_of(x * frequency + quarter * ((row & 1) - (column & 1)), self.wide)
        return self.expanded(small)

    def inverse_x(self):
        outer, inner = self.here()
        row, column = grid_of(4, self.outer * 2 * MZ)
        x = 2 * outer + (inner ^ (row >> 1))
        frequency = self.frequency(2 * (column // (2 * MZ)) + inner)
        quarter = self.wide // 4
        small = cosine_of(x * frequency + quarter * ((column & 1) - (row & 1)), self.wide)
        return self.expanded(small).astype(BF16)


def repeat_rows(out_ref, block):
    height = block.shape[0]
    for first in range(0, out_ref.shape[0], height):
        out_ref[first : first + height] = block


def write_pieces(place, send_ref, block, shares):
    step, half = 2 * place.kz, place.lanes // 2
    height = send_ref.shape[0] // place.partners
    for p in range(place.partners):
        own = block[p * step % block.shape[0] :][:step]
        first = p * height
        send_ref[first : first + step] = own[:, :half]
        send_ref[first + step : first + 2 * step] = own[:, half:]
        send_ref[first + 2 * step : first + height] = shares[p * 8 % shares.shape[0] :][:8]


def read_pieces(place, pieces_ref):
    step = 2 * place.kz
    if pieces_ref.shape[1] == place.lanes:
        return pieces_ref[...], None
    height = pieces_ref.shape[0] // place.partners
    blocks, shares = [], []
    for p in range(place.partners):
        first = p * height
        left = pieces_ref[first : first + step]
        right = pieces_ref[first + step : first + 2 * step]
        blocks.append(jnp.concatenate([left, right], axis=1))
        shares.append(pieces_ref[first + 2 * step : first + height].astype(F32))
    return jnp.concatenate(blocks, axis=0), shares


def analysed(place, pieces, y_forward, copies):
    height = 2 * MZ
    turned = sum(
        pieces[first : first + height].astype(F32) for first in range(0, pieces.shape[0], height)
    )
    channels = place.channels
    lines = jnp.concatenate(
        [turned[:, y * channels : (y + 1) * channels] for y in range(place.rows_y)], axis=0
    )
    return dot(y_forward, jnp.concatenate([lines.astype(BF16)] * copies, axis=1))


def spread_lines(place, modes, y_inverse):
    lines = dot(y_inverse, modes)
    step = 2 * place.kz
    blocks = []
    for n in range(place.narrow):
        first = n * place.rows_y
        parts = [lines[(first + y) * step : (first + y + 1) * step] for y in range(place.rows_y)]
        blocks.append(jnp.concatenate(parts, axis=1))
    return jnp.concatenate(blocks, axis=0).astype(BF16)


def turn_matrix(place, forward):
    channels, rows_y = place.channels, place.rows_y

    def same(row, column):
        if forward:
            row, column = column, row
        return (row % channels == column // rows_y) & (row // channels == column % rows_y)

    return selector(place.lanes, place.lanes, same)


def side_by_side(values, count):
    height = values.shape[0] // count
    return jnp.concatenate([values[y * height : (y + 1) * height] for y in range(count)], axis=1)


def one_below_other(values, count):
    width = values.shape[1] // count
    return jnp.concatenate([values[:, y * width : (y + 1) * width] for y in range(count)], axis=0)


def own_kernel(place, field_ref, field_out_ref, spectra_ref):
    turned = dot(turn_matrix(place, False), field_ref[...]).astype(BF16)
    field_out_ref[...] = side_by_side(turned, place.rows_y)
    spectra_ref[...] = dot_nt(place.z_table(False), turned).astype(BF16)


def start_kernel(place, spectra_ref, twin_ref, send_ref):
    twin = dot_nt(place.z_table(False), twin_ref[...]).astype(BF16)
    twin = dot(twin, turn_matrix(place, True)).astype(BF16)
    values = jnp.concatenate([spectra_ref[...], twin], axis=0)
    tables = jnp.concatenate(halves(place.forward_x()), axis=1)
    send_ref[...] = dot(tables, jnp.concatenate([values, values], axis=0)).astype(BF16)


def pack_kernel(weight_ref, packed_ref):
    modes, kz, _, channels, _ = weight_ref.shape
    for q in range(modes // 4):
        parts = [weight_ref[4 * q + j // 2, :, j % 2] for j in range(8)]
        packed = jnp.concatenate(parts, axis=-1).reshape(kz * channels, 8 * channels)
        packed_ref[q] = packed.astype(BF16)


def ready_kernel(place, field_ref, mix_ref, mix_bias_ref, head_ref, *refs):
    pointwise_ref, head_out_ref, z_doubled_ref = refs
    pointwise_ref[...] = dot_tn(mix_ref[...], field_ref[...]) + mix_bias_ref[...]
    head_out_ref[...] = jnp.transpose(head_ref[...].astype(F32)).astype(BF16)
    z_doubled_ref[...] = place.z_table(True)


def fold_kernel(place, own_ref, got_ref, tables_ref, *refs):
    values = jnp.concatenate([own_ref[...], got_ref[...]], axis=0)
    values = jnp.concatenate([values, values], axis=0)
    partial = dot(tables_ref[...], values).astype(BF16)
    if place.fold:
        shares_ref, send_ref = refs
        write_pieces(place, send_ref, partial, shares_ref[...])
    else:
        refs[0][...] = partial


def mode_kernel(
    place, pieces_ref, y_forward_ref, y_inverse_ref, weight_ref, spectrum_ref, send_ref
):
    kz, channels = place.kz, place.channels
    spectrum = analysed(place, pieces_ref[...], y_forward_ref[...], kz)
    spectrum_ref[...] = spectrum[:, :channels]
    row, lane = grid_of(*spectrum.shape)
    blocked = jnp.where(row % kz == lane // channels, spectrum, 0.0)
    mixed = []
    for q in range(place.modes // 4):
        left = blocked[q * 8 * kz : (q + 1) * 8 * kz].astype(BF16)
        product = dot(left, weight_ref[q])
        for j in range(4):
            own = product[j * 2 * kz : (j + 1) * 2 * kz, j * 2 * channels : (j + 1) * 2 * channels]
            real, imag = own[:, :channels], own[:, channels:]
            mixed.append(real[:kz] - imag[kz:])
            mixed.append(imag[:kz] + real[kz:])
    mode = jnp.concatenate(mixed, axis=0).astype(BF16)
    repeat_rows(send_ref, spread_lines(place, mode, y_inverse_ref[...]))


def part_kernel(place, pieces_ref, *refs):
    pieces, shares = read_pieces(place, pieces_ref)
    lines = dot(place.inverse_x(), pieces)
    height = 2 * MZ
    if shares is None:
        own_ref, send_ref = refs
        own_ref[...] = lines[:height]
        send_ref[...] = lines[height:].astype(BF16)
        return
    _, own_ref, send_ref, sums_ref = refs
    own_ref[...] = lines[:height]
    send_ref[:height] = lines[height:].astype(BF16)
    got = jnp.concatenate(shares, axis=0).astype(BF16)
    channels = place.channels

    def chosen(part):
        return dot(
            selector(
                2 * channels,
                got.shape[0],
                lambda row, column: (column // 8 == (row % channels) // 2)
                & (column % 8 == 4 * part + 2 * (row // channels) + row % 2),
            ),
            got,
        )

    high, low = chosen(0), chosen(1)
    sums_ref[...] = high + low
    send_ref[height:] = jnp.concatenate([high, low], axis=1).astype(BF16)


def normal(values):
    scaled = 1.0 / (1.0 + TAIL_SLOPE * jnp.abs(values))
    decay = jnp.exp(-0.5 * values * values)
    tail = TAIL[-1]
    for factor in TAIL[-2::-1]:
        tail = tail * scaled + factor
    tail = tail * (scaled * decay)
    cumulative = jnp.where(values > 0.0, 1.0 - tail, tail)
    return values * cumulative, cumulative + values * (decay * (1.0 / math.sqrt(2.0 * math.pi)))


def cell_kernel(place, *refs):
    own_ref, got_ref, z_table_ref, pointwise_ref, head_ref, head_turned_ref = refs[:6]
    head_bias_ref, out_row_ref, out_column_ref, cotangent_ref = refs[6:10]
    prediction_ref, grad_pre_ref, send_ref, hidden_ref, head_slope_ref = refs[10:]
    rows_y, z_count = place.rows_y, place.z_count
    z_table = z_table_ref[...]
    lines = (own_ref[...] + got_ref[...].astype(F32)).astype(BF16)
    pre_act = side_by_side(dot_tn(lines, z_table), rows_y) + pointwise_ref[...]
    head, head_turned = head_ref[...], head_turned_ref[...]
    head_bias, out_row, out_column = head_bias_ref[...], out_row_ref[...], out_column_ref[...]
    width = 2 * z_count
    slopes, head_pre = [], []
    for first in range(0, rows_y * z_count, width):
        value, slope = normal(pre_act[:, first : first + width])
        hidden = value.astype(BF16)
        hidden_ref[:, first : first + width] = hidden
        slopes.append(slope)
        head_pre.append(dot(head_turned, hidden))
    gradients = []
    for index, first in enumerate(range(0, rows_y, 2)):
        target = jnp.concatenate(
            [cotangent_ref[y : y + 1] for y in range(first, first + 2)], axis=1
        )
        active, slope = normal(head_pre[index] + head_bias)
        predicted = dot(out_row, active.astype(BF16))
        prediction_ref[first : first + 1] = predicted[:, :z_count]
        prediction_ref[first + 1 : first + 2] = predicted[:, z_count:]
        head_slope = (target * out_column * slope).astype(BF16)
        head_slope_ref[:, first * z_count : first * z_count + width] = head_slope
        gradients.append((dot(head, head_slope) * slopes[index]).astype(BF16))
    gradient = jnp.concatenate(gradients, axis=1)
    grad_pre_ref[...] = gradient
    send_ref[...] = dot_nt(z_table, one_below_other(gradient, rows_y)).astype(BF16)


def sums_kernel(place, field_ref, gradient_ref, hidden_ref, head_slope_ref, *refs):
    refs[-1][...] = jnp.concatenate(halves(place.forward_x()), axis=1)
    grad_mix = dot_nt(field_ref[...], gradient_ref[...])
    grad_head = dot_nt(hidden_ref[...], head_slope_ref[...])
    if not place.fold:
        refs[0][...] = grad_mix
        refs[1][...] = grad_head
        return
    channels, hidden_units = grad_head.shape
    rest = jnp.zeros((channels, hidden_units - channels), F32)
    wide_mix = jnp.concatenate([grad_mix, rest], axis=1)
    high, low = halves(jnp.concatenate([grad_head, wide_mix], axis=0))
    split = jnp.concatenate([high, low], axis=0)
    place_of = selector(
        8 * place.partners,
        4 * channels,
        lambda row, column: (column % channels == 2 * (row // 8) + row % 2)
        & (column // channels == (row % 8) // 2),
    )
    refs[0][...] = dot(place_of, split).astype(BF16)


def back_kernel(
    place, pieces_ref, y_forward_ref, y_inverse_ref, weight_ref, adjoint_ref, send_ref
):
    kz, channels = place.kz, place.channels
    pieces, shares = read_pieces(place, pieces_ref)
    adjoint = analysed(place, pieces, y_forward_ref[...], 1)
    adjoint_ref[...] = adjoint
    turned = []
    for first in range(0, adjoint.shape[0], 2 * kz):
        turned += [adjoint[first + kz : first + 2 * kz], -adjoint[first : first + kz]]
    left = jnp.concatenate([adjoint, jnp.concatenate(turned, axis=0)], axis=1)
    left = jnp.concatenate([left] * 4, axis=1)
    row, lane = grid_of(*left.shape)
    same = (row // (2 * kz)) % 4 == lane // (2 * channels)
    left = jnp.where(same, left, 0.0).astype(BF16)
    block = 8 * kz
    pulled = [
        dot_nt(left[q * block : (q + 1) * block], weight_ref[q]) for q in range(place.modes // 4)
    ]
    pulled = jnp.concatenate(pulled, axis=0)
    row, lane = grid_of(*pulled.shape)
    pulled = jnp.where(row % kz == lane // channels, pulled, 0.0).astype(BF16)
    gather = selector(
        kz * channels, channels, lambda row, column: row % channels == column
    )
    modes_back = dot(pulled, gather).astype(BF16)
    block = spread_lines(place, modes_back, y_inverse_ref[...])
    if shares is None:
        repeat_rows(send_ref, block)
        return
    total = sum(shares[1:], shares[0])
    high, low = halves(total[0:4] + total[4:8])
    split = jnp.concatenate([high.astype(F32), low.astype(F32)], axis=0)
    write_pieces(place, send_ref, block, split.astype(BF16))


def outer_kernel(spectrum_ref, adjoint_ref, out_ref, done_ref):
    done_ref[...] = jnp.zeros(done_ref.shape, F32)
    modes, kz = out_ref.shape[:2]
    for j in range(modes):
        columns = jnp.transpose(spectrum_ref[j])
        adjoint = adjoint_ref[j]
        for k in range(kz):
            s_real, s_imag = columns[:, k : k + 1], columns[:, kz + k : kz + k + 1]
            a_real, a_imag = adjoint[k : k + 1], adjoint[kz + k : kz + k + 1]
            out_ref[j, k, 0] = s_real * a_real + s_imag * a_imag
            out_ref[j, k, 1] = s_real * a_imag - s_imag * a_real


def pointwise_kernel(place, mix_ref, gradient_ref, out_ref, z_plain_ref, turn_ref):
    z_plain_ref[...] = place.z_table(False)
    turn_ref[...] = turn_matrix(place, False)
    z_count = place.z_count
    product = dot(mix_ref[...], gradient_ref[...])
    for y in range(place.rows_y):
        out_ref[:, y, :] = product[:, y * z_count : (y + 1) * z_count]


def finish_kernel(place, *refs):
    own_ref, got_ref, z_table_ref, turn_ref, pointwise_ref, prediction_ref = refs[:6]
    refs = refs[6:]
    height = 2 * MZ
    channels = place.channels
    lines = (own_ref[...] + got_ref[:height].astype(F32)).astype(BF16)
    lines = dot(lines, turn_ref[...]).astype(BF16)
    pointwise = pointwise_ref[...].reshape(place.lanes, place.z_count)
    grad_field = (dot_tn(lines, z_table_ref[...]) + pointwise).astype(BF16)
    if not place.fold:
        refs[0][...] = grad_field
        refs[1][...] = prediction_ref[...]
        return
    sums_ref, grad_field_ref, out_ref, grad_mix_ref, grad_head_ref = refs
    grad_field_ref[...] = grad_field
    out_ref[...] = prediction_ref[...]
    got = got_ref[height:].astype(F32)
    width = sums_ref.shape[1]
    total = sums_ref[...] + got[:, :width] + got[:, width:]
    grad_head_ref[...] = total[:channels]
    grad_mix_ref[...] = total[channels:, :channels]


def call(kernel, outs, name, **spec):
    return pl.pallas_call(
        kernel,
        out_shape=[jax.ShapeDtypeStruct(shape, dtype) for shape, dtype in outs],
        compiler_params=pltpu.CompilerParams(vmem_limit_bytes=VMEM_LIMIT),
        cost_estimate=pl.CostEstimate(flops=1 << 22, bytes_accessed=1 << 19, transcendentals=0),
        name=name,
        **spec,
    )


def body(
    lifted_field,
    spectral_weight,
    mix_weight,
    mix_bias,
    head_weight,
    head_bias,
    out_weight,
    cotangent,
):
    wide = lax.axis_size("wide")
    narrow = lax.axis_size("narrow")
    devices = wide * narrow
    _, channels, rows_y, z_count = lifted_field.shape
    modes, kz = spectral_weight.shape[:2]
    hidden_units = head_weight.shape[1]
    cells = channels * rows_y
    place = Place(wide, narrow, kz, modes, rows_y, channels, z_count, False)
    place.fold = 2 * place.partners == channels and hidden_units == 128 and cells == 256 and kz % 8 == 0
    height = 2 * MZ
    step = 2 * kz
    partners = place.partners
    mode_lines = modes * 2 * kz

    y_forward, y_inverse = y_tables(rows_y * narrow, rows_y, kz, modes)
    if len(y_forward) > 1:
        block = lax.axis_index("wide") % len(y_forward)
        y_forward = lax.dynamic_index_in_dim(jnp.asarray(y_forward), block, 0, False)
        y_inverse = lax.dynamic_index_in_dim(jnp.asarray(y_inverse), block, 0, False)
    else:
        y_forward, y_inverse = jnp.asarray(y_forward[0]), jnp.asarray(y_inverse[0])

    def to_twin(send):
        pairs = [(p, p ^ narrow) for p in range(devices)]
        return lax.ppermute(send, ("wide", "narrow"), pairs)

    groups = [
        [(2 * outer + inner) * narrow + n for outer in range(wide // 2) for n in range(narrow)]
        for inner in range(2)
    ]

    def exchange(send):
        pieces = send.reshape(partners, -1, send.shape[1])
        got = lax.all_to_all(
            pieces, ("wide", "narrow"), 0, 0, axis_index_groups=groups, tiled=True
        )
        return got.reshape(send.shape)

    plain = ((partners * step, cells), BF16)
    shared = ((partners * (2 * step + 8), cells // 2), BF16) if place.fold else plain
    twin_plain = ((height, cells), BF16)
    twin_shared = ((height + 2 * channels, cells), BF16) if place.fold else twin_plain
    sums_shape = ((2 * channels, hidden_units), F32)
    own_lines = ((height, cells), F32)
    across = (channels, rows_y * z_count)

    def run(kernel, outs, name, **spec):
        return call(functools.partial(kernel, place), outs, name, **spec)

    flat_field = lifted_field.reshape(cells, z_count)
    twin_field = to_twin(flat_field)
    field, spectra = run(own_kernel, [(across, BF16), twin_plain], "own")(flat_field)
    (send,) = run(start_kernel, [plain], "start")(spectra, twin_field)
    packed_shape = ((modes // 4, kz * channels, 8 * channels), BF16)
    (weight,) = call(pack_kernel, [packed_shape], "pack")(spectral_weight)
    spectrum, send = run(mode_kernel, [((mode_lines, channels), F32), plain], "mode")(
        exchange(send), y_forward, y_inverse, weight
    )
    own, send = run(part_kernel, [own_lines, twin_plain], "part")(exchange(send))
    pointwise, head_turned, z_doubled = run(
        ready_kernel,
        [(across, F32), ((hidden_units, channels), BF16), ((height, z_count), BF16)],
        "ready",
    )(field, mix_weight, mix_bias[:, None], head_weight)
    prediction, grad_pre, send, hidden, head_slope = run(
        cell_kernel,
        [
            ((rows_y, z_count), F32),
            (across, BF16),
            twin_plain,
            (across, BF16),
            ((hidden_units, rows_y * z_count), BF16),
        ],
        "cell",
    )(
        own,
        to_twin(send),
        z_doubled,
        pointwise,
        head_weight,
        head_turned,
        head_bias[:, None],
        out_weight[None],
        out_weight.astype(F32)[:, None],
        cotangent[0],
    )
    if place.fold:
        outs = [((8 * partners, hidden_units), BF16)]
    else:
        outs = [((channels, channels), F32), ((channels, hidden_units), F32)]
    outs += [((wide // 2 * height, 4 * height), BF16)]
    *sums, forward = run(sums_kernel, outs, "sums")(field, grad_pre, hidden, head_slope)
    if not place.fold:
        totals = lax.psum(tuple(sums), ("wide", "narrow"))
        sums = []
    (send,) = run(fold_kernel, [shared], "fold")(send, to_twin(send), forward, *sums)
    adjoint, send = run(back_kernel, [((mode_lines, channels), F32), shared], "back")(
        exchange(send), y_forward, y_inverse, weight
    )
    some = max(1, modes // 4)
    grad_spectral, done = pl.pallas_call(
        outer_kernel,
        grid=(modes // some,),
        in_specs=[pl.BlockSpec((some, 2 * kz, channels), lambda j: (j, 0, 0))] * 2,
        out_specs=[
            pl.BlockSpec((some, kz, 2, channels, channels), lambda j: (j, 0, 0, 0, 0)),
            pl.BlockSpec((8, 128), lambda j: (0, 0)),
        ],
        out_shape=[
            jax.ShapeDtypeStruct(spectral_weight.shape, F32),
            jax.ShapeDtypeStruct((8, 128), F32),
        ],
        compiler_params=pltpu.CompilerParams(vmem_limit_bytes=VMEM_LIMIT),
        cost_estimate=pl.CostEstimate(flops=1 << 22, bytes_accessed=5 << 20, transcendentals=0),
        name="outer",
    )(spectrum.reshape(modes, 2 * kz, channels), adjoint.reshape(modes, 2 * kz, channels))
    pointwise, z_plain, turn = run(
        pointwise_kernel,
        [
            ((channels, rows_y, z_count), F32),
            ((height, z_count), BF16),
            ((cells, cells), BF16),
        ],
        "pointwise",
    )(mix_weight, grad_pre)
    outs = [own_lines, twin_shared] + ([sums_shape] if place.fold else [])
    after = (done,) if place.fold else ()
    own, send, *sums = run(part_kernel, outs, "part")(exchange(send), *after)
    outs = [((cells, z_count), BF16), ((rows_y, z_count), F32)]
    if place.fold:
        outs += [((channels, channels), F32), ((channels, hidden_units), F32)]
    grad_field, prediction, *summed = run(finish_kernel, outs, "finish")(
        own, to_twin(send), z_plain, turn, pointwise, prediction, *sums
    )
    grad_mix, grad_head = summed if place.fold else totals
    return (
        prediction[None],
        grad_field.reshape(lifted_field.shape),
        grad_spectral,
        grad_mix,
        grad_head,
    )


def solution(mesh):
    return jax.shard_map(
        body,
        mesh=mesh,
        in_specs=(
            P("wide", None, "narrow", None),
            P("wide", "narrow", None, None, None),
            P(),
            P(),
            P(),
            P(),
            P(),
            P("wide", "narrow", None),
        ),
        out_specs=(
            P("wide", "narrow", None),
            P("wide", None, "narrow", None),
            P("wide", "narrow", None, None, None),
            P(),
            P(),
        ),
        check_vma=False,
    )
```

```python
import functools
import math

import jax
import jax.numpy as jnp
import numpy as np
from jax import lax
from jax.experimental import pallas as pl
from jax.experimental.pallas import tpu as pltpu
from jax.sharding import PartitionSpec as P

MX = 16
MY = 16
MZ = 16
F32 = jnp.float32
BF16 = jnp.bfloat16
VMEM_LIMIT = 32 * 1024 * 1024
FETCH_LIMIT = 52 * 1024 * 1024

TAIL_SLOPE = 0.275
TAIL = (
    0.11780925840139389,
    0.04211147502064705,
    0.3339323103427887,
    -0.3309934139251709,
    0.4519987106323242,
    -0.11485832929611206,
)


def signed(indices, count):
    return np.where(indices < count // 2, indices, indices - count)


def wave(positions, frequency, length):
    turned = np.mod(np.multiply.outer(positions, frequency), length)
    angles = turned.astype(np.float32) * np.float32(2.0 * math.pi / length)
    scale = np.float32(1.0 / math.sqrt(length))
    return np.cos(angles) * scale, np.sin(angles) * scale


def pair(cosine, sine, sign):
    return np.stack(
        [np.stack([cosine, -sign * sine], -1), np.stack([sign * sine, cosine], -1)], -2
    )


def y_tables(total_y, rows_y, kz, modes):
    cosine, sine = wave(np.arange(total_y), signed(np.arange(MY), MY), total_y)
    narrow = total_y // rows_y
    same = np.eye(kz, dtype=np.float32)
    forward = pair(cosine, sine, -1.0).reshape(narrow, rows_y, MY // modes, modes, 2, 2)
    inverse = pair(cosine, sine, 1.0).reshape(narrow, rows_y, MY // modes, modes, 2, 2)
    forward = np.einsum("nybjtr,kl->bjtkynlr", forward, same)
    inverse = np.einsum("nybjst,kl->bnyksjtl", inverse, same)
    blocks = MY // modes
    forward = forward.reshape(blocks, modes * 2 * kz, rows_y * narrow * kz * 2)
    inverse = inverse.reshape(blocks, narrow * rows_y * kz * 2, modes * 2 * kz)
    return forward.astype(BF16), inverse.astype(BF16)


def dot(a, b):
    return jnp.dot(a, b, preferred_element_type=F32)


def dot_nt(a, b):
    return lax.dot_general(a, b, (((1,), (1,)), ((), ())), preferred_element_type=F32)


def dot_tn(a, b):
    return lax.dot_general(a, b, (((0,), (0,)), ((), ())), preferred_element_type=F32)


def grid_of(rows, columns):
    shape = (rows, columns)
    return lax.broadcasted_iota(jnp.int32, shape, 0), lax.broadcasted_iota(jnp.int32, shape, 1)


def selector(rows, columns, condition):
    return jnp.where(condition(*grid_of(rows, columns)), 1.0, 0.0).astype(BF16)


def halves(values):
    high = values.astype(BF16)
    return high, (values - high.astype(F32)).astype(BF16)


def stacked(refs, lanes=slice(None)):
    return jnp.concatenate([ref[:, lanes] for ref in refs], axis=0)


def cosine_of(phase, length):
    angles = (phase & (length - 1)).astype(F32) * (2.0 * math.pi / length)
    return jnp.cos(angles) * (1.0 / math.sqrt(length))


class Place:
    def __init__(self, wide, narrow, kz, modes, rows_y, channels, z_count, fold):
        self.wide, self.narrow, self.kz, self.modes = wide, narrow, kz, modes
        self.rows_y, self.channels, self.z_count, self.fold = rows_y, channels, z_count, fold
        self.outer = wide // 2
        self.partners = self.outer * narrow
        self.lanes = rows_y * channels

    def here(self):
        wide = lax.axis_index("wide")
        return wide // 2, wide % 2

    def frequency(self, wide):
        index = (wide * self.modes) // MY
        return jnp.where(index < MX // 2, index, index - MX)

    def z_table(self, doubled):
        row, z = grid_of(2 * MZ, self.z_count)
        frequency = row >> 1
        value = cosine_of(z * frequency + (row & 1) * (self.z_count // 4), self.z_count)
        if doubled:
            value = jnp.where(frequency > 0, 2.0 * value, value)
        return value.astype(BF16)

    def expanded(self, small):
        row, column = grid_of(2 * MZ, small.shape[1])
        same = (row >> 1) == ((column >> 1) & (MZ - 1))
        blocks = []
        for g in range(small.shape[0] // 2):
            value = jnp.where((row & 1) == 0, small[2 * g : 2 * g + 1], small[2 * g + 1 : 2 * g + 2])
            blocks.append(jnp.where(same, value, 0.0))
        return jnp.concatenate(blocks, axis=0)

    def forward_x(self):
        outer, inner = self.here()
        row, column = grid_of(2 * self.outer, 4 * MZ)
        x = 2 * outer + (inner ^ (column // (2 * MZ)))
        frequency = self.frequency(2 * (row >> 1) + inner)
        quarter = self.wide // 4
        small = cosine_of(x * frequency + quarter * ((row & 1) - (column & 1)), self.wide)
        return self.expanded(small)

    def inverse_x(self):
        outer, inner = self.here()
        row, column = grid_of(4, self.outer * 2 * MZ)
        x = 2 * outer + (inner ^ (row >> 1))
        frequency = self.frequency(2 * (column // (2 * MZ)) + inner)
        quarter = self.wide // 4
        small = cosine_of(x * frequency + quarter * ((column & 1) - (row & 1)), self.wide)
        return self.expanded(small).astype(BF16)


def repeat_rows(out_ref, block):
    height = block.shape[0]
    for first in range(0, out_ref.shape[0], height):
        out_ref[first : first + height] = block


def write_pieces(place, send_ref, block, shares):
    step, half = 2 * place.kz, place.lanes // 2
    height = send_ref.shape[0] // place.partners
    for p in range(place.partners):
        own = block[p * step % block.shape[0] :][:step]
        first = p * height
        send_ref[first : first + step] = own[:, :half]
        send_ref[first + step : first + 2 * step] = own[:, half:]
        send_ref[first + 2 * step : first + height] = shares[p * 8 % shares.shape[0] :][:8]


def read_pieces(place, pieces_ref):
    step = 2 * place.kz
    if pieces_ref.shape[1] == place.lanes:
        return pieces_ref[...], None
    height = pieces_ref.shape[0] // place.partners
    blocks, shares = [], []
    for p in range(place.partners):
        first = p * height
        left = pieces_ref[first : first + step]
        right = pieces_ref[first + step : first + 2 * step]
        blocks.append(jnp.concatenate([left, right], axis=1))
        shares.append(pieces_ref[first + 2 * step : first + height].astype(F32))
    return jnp.concatenate(blocks, axis=0), shares


def analysed(place, pieces, y_forward, copies):
    height = 2 * MZ
    turned = sum(
        pieces[first : first + height].astype(F32) for first in range(0, pieces.shape[0], height)
    )
    channels = place.channels
    lines = jnp.concatenate(
        [turned[:, y * channels : (y + 1) * channels] for y in range(place.rows_y)], axis=0
    )
    return dot(y_forward, jnp.concatenate([lines.astype(BF16)] * copies, axis=1))


def spread_lines(place, modes, y_inverse):
    lines = dot(y_inverse, modes)
    step = 2 * place.kz
    blocks = []
    for n in range(place.narrow):
        first = n * place.rows_y
        parts = [lines[(first + y) * step : (first + y + 1) * step] for y in range(place.rows_y)]
        blocks.append(jnp.concatenate(parts, axis=1))
    return jnp.concatenate(blocks, axis=0).astype(BF16)


def turn_matrix(place, forward):
    channels, rows_y = place.channels, place.rows_y

    def same(row, column):
        if forward:
            row, column = column, row
        return (row % channels == column // rows_y) & (row // channels == column % rows_y)

    return selector(place.lanes, place.lanes, same)


def side_by_side(values, count):
    height = values.shape[0] // count
    return jnp.concatenate([values[y * height : (y + 1) * height] for y in range(count)], axis=1)


def one_below_other(values, count):
    width = values.shape[1] // count
    return jnp.concatenate([values[:, y * width : (y + 1) * width] for y in range(count)], axis=0)


def fetch_kernel(place, weight_ref, *refs):
    packed_ref, z_plain_ref, z_doubled_ref, turn_in_ref, turn_out_ref = refs[:5]
    forward_ref, inverse_ref, held_ref, arrived = refs[5:]
    modes, kz, _, channels, _ = weight_ref.shape
    copies = []
    for q in range(modes // 4):
        part = pl.ds(4 * q, 4)
        copies.append(
            pltpu.make_async_copy(weight_ref.at[part], held_ref.at[part], arrived.at[q])
        )
        copies[-1].start()
    z_plain_ref[...] = place.z_table(False)
    z_doubled_ref[...] = place.z_table(True)
    turn_in_ref[...] = turn_matrix(place, True)
    turn_out_ref[...] = turn_matrix(place, False)
    forward_ref[...] = jnp.concatenate(halves(place.forward_x()), axis=1)
    inverse_ref[...] = place.inverse_x()
    for q in range(modes // 4):
        copies[q].wait()
        parts = [held_ref[4 * q + j // 2, :, j % 2] for j in range(8)]
        packed = jnp.concatenate(parts, axis=-1).reshape(kz * channels, 8 * channels)
        packed_ref[q] = packed.astype(BF16)


def own_kernel(place, field_ref, z_table_ref, turn_ref, field_out_ref, spectra_ref):
    turned = dot(turn_ref[...], field_ref[...]).astype(BF16)
    field_out_ref[...] = side_by_side(turned, place.rows_y)
    spectra_ref[...] = dot_nt(z_table_ref[...], turned).astype(BF16)


def start_kernel(place, spectra_ref, twin_ref, z_table_ref, turn_ref, tables_ref, send_ref):
    twin = dot_nt(z_table_ref[...], twin_ref[...]).astype(BF16)
    twin = dot(twin, turn_ref[...]).astype(BF16)
    values = jnp.concatenate([spectra_ref[...], twin], axis=0)
    send_ref[...] = dot(tables_ref[...], jnp.concatenate([values, values], axis=0)).astype(BF16)


def ready_kernel(place, field_ref, mix_ref, mix_bias_ref, head_ref, *refs):
    pointwise_ref, head_out_ref = refs
    pointwise_ref[...] = dot_tn(mix_ref[...], field_ref[...]) + mix_bias_ref[...]
    head_out_ref[...] = jnp.transpose(head_ref[...].astype(F32)).astype(BF16)


def fold_kernel(place, own_ref, got_ref, tables_ref, *refs):
    values = jnp.concatenate([own_ref[...], got_ref[...]], axis=0)
    values = jnp.concatenate([values, values], axis=0)
    partial = dot(tables_ref[...], values).astype(BF16)
    if place.fold:
        shares_ref, send_ref = refs
        write_pieces(place, send_ref, partial, shares_ref[...])
    else:
        refs[0][...] = partial


def mode_kernel(
    place, pieces_ref, y_forward_ref, y_inverse_ref, weight_ref, spectrum_ref, send_ref
):
    kz, channels = place.kz, place.channels
    spectrum = analysed(place, pieces_ref[...], y_forward_ref[...], kz)
    spectrum_ref[...] = spectrum[:, :channels]
    row, lane = grid_of(*spectrum.shape)
    blocked = jnp.where(row % kz == lane // channels, spectrum, 0.0)
    mixed = []
    for q in range(place.modes // 4):
        left = blocked[q * 8 * kz : (q + 1) * 8 * kz].astype(BF16)
        product = dot(left, weight_ref[q])
        for j in range(4):
            own = product[j * 2 * kz : (j + 1) * 2 * kz, j * 2 * channels : (j + 1) * 2 * channels]
            real, imag = own[:, :channels], own[:, channels:]
            mixed.append(real[:kz] - imag[kz:])
            mixed.append(imag[:kz] + real[kz:])
    mode = jnp.concatenate(mixed, axis=0).astype(BF16)
    repeat_rows(send_ref, spread_lines(place, mode, y_inverse_ref[...]))


def part_kernel(place, pieces_ref, table_ref, *refs):
    pieces, shares = read_pieces(place, pieces_ref)
    lines = dot(table_ref[...], pieces)
    height = 2 * MZ
    if shares is None:
        own_ref, send_ref = refs
        own_ref[...] = lines[:height]
        send_ref[...] = lines[height:].astype(BF16)
        return
    _, own_ref, send_ref, sums_ref = refs
    own_ref[...] = lines[:height]
    send_ref[:height] = lines[height:].astype(BF16)
    got = jnp.concatenate(shares, axis=0).astype(BF16)
    channels = place.channels

    def chosen(part):
        return dot(
            selector(
                2 * channels,
                got.shape[0],
                lambda row, column: (column // 8 == (row % channels) // 2)
                & (column % 8 == 4 * part + 2 * (row // channels) + row % 2),
            ),
            got,
        )

    high, low = chosen(0), chosen(1)
    sums_ref[...] = high + low
    send_ref[height:] = jnp.concatenate([high, low], axis=1).astype(BF16)


def normal(values):
    scaled = 1.0 / (1.0 + TAIL_SLOPE * jnp.abs(values))
    decay = jnp.exp(-0.5 * values * values)
    tail = TAIL[-1]
    for factor in TAIL[-2::-1]:
        tail = tail * scaled + factor
    tail = tail * (scaled * decay)
    cumulative = jnp.where(values > 0.0, 1.0 - tail, tail)
    return values * cumulative, cumulative + values * (decay * (1.0 / math.sqrt(2.0 * math.pi)))


def cell_kernel(place, *refs):
    own_ref, got_ref, z_table_ref, pointwise_ref, head_ref, head_turned_ref = refs[:6]
    head_bias_ref, out_row_ref, out_column_ref, cotangent_ref = refs[6:10]
    prediction_ref, grad_pre_ref, send_ref, hidden_ref, head_slope_ref = refs[10:]
    rows_y, z_count = place.rows_y, place.z_count
    z_table = z_table_ref[...]
    lines = (own_ref[...] + got_ref[...].astype(F32)).astype(BF16)
    pre_act = side_by_side(dot_tn(lines, z_table), rows_y) + pointwise_ref[...]
    head, head_turned = head_ref[...], head_turned_ref[...]
    head_bias, out_row, out_column = head_bias_ref[...], out_row_ref[...], out_column_ref[...]
    width = 2 * z_count
    slopes, head_pre = [], []
    for first in range(0, rows_y * z_count, width):
        value, slope = normal(pre_act[:, first : first + width])
        hidden = value.astype(BF16)
        hidden_ref[:, first : first + width] = hidden
        slopes.append(slope)
        head_pre.append(dot(head_turned, hidden))
    gradients = []
    for index, first in enumerate(range(0, rows_y, 2)):
        target = jnp.concatenate(
            [cotangent_ref[y : y + 1] for y in range(first, first + 2)], axis=1
        )
        active, slope = normal(head_pre[index] + head_bias)
        predicted = dot(out_row, active.astype(BF16))
        prediction_ref[first : first + 1] = predicted[:, :z_count]
        prediction_ref[first + 1 : first + 2] = predicted[:, z_count:]
        head_slope = (target * out_column * slope).astype(BF16)
        head_slope_ref[:, first * z_count : first * z_count + width] = head_slope
        gradients.append((dot(head, head_slope) * slopes[index]).astype(BF16))
    gradient = jnp.concatenate(gradients, axis=1)
    grad_pre_ref[...] = gradient
    send_ref[...] = dot_nt(z_table, one_below_other(gradient, rows_y)).astype(BF16)


def sums_kernel(place, field_ref, gradient_ref, hidden_ref, head_slope_ref, *refs):
    grad_mix = dot_nt(field_ref[...], gradient_ref[...])
    grad_head = dot_nt(hidden_ref[...], head_slope_ref[...])
    if not place.fold:
        refs[0][...] = grad_mix
        refs[1][...] = grad_head
        return
    channels, hidden_units = grad_head.shape
    rest = jnp.zeros((channels, hidden_units - channels), F32)
    wide_mix = jnp.concatenate([grad_mix, rest], axis=1)
    high, low = halves(jnp.concatenate([grad_head, wide_mix], axis=0))
    split = jnp.concatenate([high, low], axis=0)
    place_of = selector(
        8 * place.partners,
        4 * channels,
        lambda row, column: (column % channels == 2 * (row // 8) + row % 2)
        & (column // channels == (row % 8) // 2),
    )
    refs[0][...] = dot(place_of, split).astype(BF16)


def back_kernel(
    place, pieces_ref, y_forward_ref, y_inverse_ref, weight_ref, adjoint_ref, send_ref
):
    kz, channels = place.kz, place.channels
    pieces, shares = read_pieces(place, pieces_ref)
    adjoint = analysed(place, pieces, y_forward_ref[...], 1)
    adjoint_ref[...] = adjoint
    turned = []
    for first in range(0, adjoint.shape[0], 2 * kz):
        turned += [adjoint[first + kz : first + 2 * kz], -adjoint[first : first + kz]]
    left = jnp.concatenate([adjoint, jnp.concatenate(turned, axis=0)], axis=1)
    left = jnp.concatenate([left] * 4, axis=1)
    row, lane = grid_of(*left.shape)
    same = (row // (2 * kz)) % 4 == lane // (2 * channels)
    left = jnp.where(same, left, 0.0).astype(BF16)
    block = 8 * kz
    pulled = [
        dot_nt(left[q * block : (q + 1) * block], weight_ref[q]) for q in range(place.modes // 4)
    ]
    pulled = jnp.concatenate(pulled, axis=0)
    row, lane = grid_of(*pulled.shape)
    pulled = jnp.where(row % kz == lane // channels, pulled, 0.0).astype(BF16)
    gather = selector(
        kz * channels, channels, lambda row, column: row % channels == column
    )
    modes_back = dot(pulled, gather).astype(BF16)
    block = spread_lines(place, modes_back, y_inverse_ref[...])
    if shares is None:
        repeat_rows(send_ref, block)
        return
    total = sum(shares[1:], shares[0])
    high, low = halves(total[0:4] + total[4:8])
    split = jnp.concatenate([high.astype(F32), low.astype(F32)], axis=0)
    write_pieces(place, send_ref, block, split.astype(BF16))


def outer_kernel(spectrum_ref, adjoint_ref, out_ref, done_ref):
    done_ref[...] = jnp.zeros(done_ref.shape, F32)
    modes, kz = out_ref.shape[:2]
    for j in range(modes):
        columns = jnp.transpose(spectrum_ref[j])
        adjoint = adjoint_ref[j]
        for k in range(kz):
            s_real, s_imag = columns[:, k : k + 1], columns[:, kz + k : kz + k + 1]
            a_real, a_imag = adjoint[k : k + 1], adjoint[kz + k : kz + k + 1]
            out_ref[j, k, 0] = s_real * a_real + s_imag * a_imag
            out_ref[j, k, 1] = s_real * a_imag - s_imag * a_real


def pointwise_kernel(place, mix_ref, gradient_ref, out_ref):
    z_count = place.z_count
    product = dot(mix_ref[...], gradient_ref[...])
    for y in range(place.rows_y):
        out_ref[:, y, :] = product[:, y * z_count : (y + 1) * z_count]


def finish_kernel(place, *refs):
    own_ref, got_ref, z_table_ref, turn_ref, pointwise_ref, prediction_ref = refs[:6]
    refs = refs[6:]
    height = 2 * MZ
    channels = place.channels
    lines = (own_ref[...] + got_ref[:height].astype(F32)).astype(BF16)
    lines = dot(lines, turn_ref[...]).astype(BF16)
    pointwise = pointwise_ref[...].reshape(place.lanes, place.z_count)
    grad_field = (dot_tn(lines, z_table_ref[...]) + pointwise).astype(BF16)
    if not place.fold:
        refs[0][...] = grad_field
        refs[1][...] = prediction_ref[...]
        return
    sums_ref, grad_field_ref, out_ref, grad_mix_ref, grad_head_ref = refs
    grad_field_ref[...] = grad_field
    out_ref[...] = prediction_ref[...]
    got = got_ref[height:].astype(F32)
    width = sums_ref.shape[1]
    total = sums_ref[...] + got[:, :width] + got[:, width:]
    grad_head_ref[...] = total[:channels]
    grad_mix_ref[...] = total[channels:, :channels]


def call(kernel, outs, name, limit=VMEM_LIMIT, **spec):
    return pl.pallas_call(
        kernel,
        out_shape=[jax.ShapeDtypeStruct(shape, dtype) for shape, dtype in outs],
        compiler_params=pltpu.CompilerParams(vmem_limit_bytes=limit),
        cost_estimate=pl.CostEstimate(flops=1 << 22, bytes_accessed=1 << 19, transcendentals=0),
        name=name,
        **spec,
    )


def body(
    lifted_field,
    spectral_weight,
    mix_weight,
    mix_bias,
    head_weight,
    head_bias,
    out_weight,
    cotangent,
):
    wide = lax.axis_size("wide")
    narrow = lax.axis_size("narrow")
    devices = wide * narrow
    _, channels, rows_y, z_count = lifted_field.shape
    modes, kz = spectral_weight.shape[:2]
    hidden_units = head_weight.shape[1]
    cells = channels * rows_y
    place = Place(wide, narrow, kz, modes, rows_y, channels, z_count, False)
    place.fold = 2 * place.partners == channels and hidden_units == 128 and cells == 256 and kz % 8 == 0
    height = 2 * MZ
    step = 2 * kz
    partners = place.partners
    mode_lines = modes * 2 * kz

    y_forward, y_inverse = y_tables(rows_y * narrow, rows_y, kz, modes)
    if len(y_forward) > 1:
        block = lax.axis_index("wide") % len(y_forward)
        y_forward = lax.dynamic_index_in_dim(jnp.asarray(y_forward), block, 0, False)
        y_inverse = lax.dynamic_index_in_dim(jnp.asarray(y_inverse), block, 0, False)
    else:
        y_forward, y_inverse = jnp.asarray(y_forward[0]), jnp.asarray(y_inverse[0])

    def to_twin(send):
        pairs = [(p, p ^ narrow) for p in range(devices)]
        return lax.ppermute(send, ("wide", "narrow"), pairs)

    groups = [
        [(2 * outer + inner) * narrow + n for outer in range(wide // 2) for n in range(narrow)]
        for inner in range(2)
    ]

    def exchange(send):
        pieces = send.reshape(partners, -1, send.shape[1])
        got = lax.all_to_all(
            pieces, ("wide", "narrow"), 0, 0, axis_index_groups=groups, tiled=True
        )
        return got.reshape(send.shape)

    plain = ((partners * step, cells), BF16)
    shared = ((partners * (2 * step + 8), cells // 2), BF16) if place.fold else plain
    twin_plain = ((height, cells), BF16)
    twin_shared = ((height + 2 * channels, cells), BF16) if place.fold else twin_plain
    sums_shape = ((2 * channels, hidden_units), F32)
    own_lines = ((height, cells), F32)
    across = (channels, rows_y * z_count)

    def run(kernel, outs, name, **spec):
        return call(functools.partial(kernel, place), outs, name, **spec)

    flat_field = lifted_field.reshape(cells, z_count)
    twin_field = to_twin(flat_field)
    weight, z_plain, z_doubled, turn_in, turn, forward, inverse = run(
        fetch_kernel,
        [
            ((modes // 4, kz * channels, 8 * channels), BF16),
            ((height, z_count), BF16),
            ((height, z_count), BF16),
            ((cells, cells), BF16),
            ((cells, cells), BF16),
            ((wide // 2 * height, 4 * height), BF16),
            ((2 * height, wide // 2 * height), BF16),
        ],
        "fetch",
        limit=FETCH_LIMIT,
        in_specs=[pl.BlockSpec(memory_space=pl.ANY)],
        scratch_shapes=[
            pltpu.VMEM(spectral_weight.shape, F32),
            pltpu.SemaphoreType.DMA((modes // 4,)),
        ],
    )(spectral_weight)
    field, spectra = run(own_kernel, [(across, BF16), twin_plain], "own")(
        flat_field, z_plain, turn
    )
    (send,) = run(start_kernel, [plain], "start")(spectra, twin_field, z_plain, turn_in, forward)
    spectrum, send = run(mode_kernel, [((mode_lines, channels), F32), plain], "mode")(
        exchange(send), y_forward, y_inverse, weight
    )
    own, send = run(part_kernel, [own_lines, twin_plain], "part")(exchange(send), inverse)
    pointwise, head_turned = run(
        ready_kernel, [(across, F32), ((hidden_units, channels), BF16)], "ready"
    )(field, mix_weight, mix_bias[:, None], head_weight)
    prediction, grad_pre, send, hidden, head_slope = run(
        cell_kernel,
        [
            ((rows_y, z_count), F32),
            (across, BF16),
            twin_plain,
            (across, BF16),
            ((hidden_units, rows_y * z_count), BF16),
        ],
        "cell",
    )(
        own,
        to_twin(send),
        z_doubled,
        pointwise,
        head_weight,
        head_turned,
        head_bias[:, None],
        out_weight[None],
        out_weight.astype(F32)[:, None],
        cotangent[0],
    )
    if place.fold:
        outs = [((8 * partners, hidden_units), BF16)]
    else:
        outs = [((channels, channels), F32), ((channels, hidden_units), F32)]
    sums = run(sums_kernel, outs, "sums")(field, grad_pre, hidden, head_slope)
    if not place.fold:
        totals = lax.psum(tuple(sums), ("wide", "narrow"))
        sums = []
    (send,) = run(fold_kernel, [shared], "fold")(send, to_twin(send), forward, *sums)
    adjoint, send = run(back_kernel, [((mode_lines, channels), F32), shared], "back")(
        exchange(send), y_forward, y_inverse, weight
    )
    some = max(1, modes // 4)
    grad_spectral, done = pl.pallas_call(
        outer_kernel,
        grid=(modes // some,),
        in_specs=[pl.BlockSpec((some, 2 * kz, channels), lambda j: (j, 0, 0))] * 2,
        out_specs=[
            pl.BlockSpec((some, kz, 2, channels, channels), lambda j: (j, 0, 0, 0, 0)),
            pl.BlockSpec((8, 128), lambda j: (0, 0)),
        ],
        out_shape=[
            jax.ShapeDtypeStruct(spectral_weight.shape, F32),
            jax.ShapeDtypeStruct((8, 128), F32),
        ],
        compiler_params=pltpu.CompilerParams(vmem_limit_bytes=VMEM_LIMIT),
        cost_estimate=pl.CostEstimate(flops=1 << 22, bytes_accessed=5 << 20, transcendentals=0),
        name="outer",
    )(spectrum.reshape(modes, 2 * kz, channels), adjoint.reshape(modes, 2 * kz, channels))
    (pointwise,) = run(pointwise_kernel, [((channels, rows_y, z_count), F32)], "pointwise")(
        mix_weight, grad_pre
    )
    outs = [own_lines, twin_shared] + ([sums_shape] if place.fold else [])
    after = (done,) if place.fold else ()
    own, send, *sums = run(part_kernel, outs, "part")(exchange(send), inverse, *after)
    outs = [((cells, z_count), BF16), ((rows_y, z_count), F32)]
    if place.fold:
        outs += [((channels, channels), F32), ((channels, hidden_units), F32)]
    grad_field, prediction, *summed = run(finish_kernel, outs, "finish")(
        own, to_twin(send), z_plain, turn, pointwise, prediction, *sums
    )
    grad_mix, grad_head = summed if place.fold else totals
    return (
        prediction[None],
        grad_field.reshape(lifted_field.shape),
        grad_spectral,
        grad_mix,
        grad_head,
    )


def solution(mesh):
    return jax.shard_map(
        body,
        mesh=mesh,
        in_specs=(
            P("wide", None, "narrow", None),
            P("wide", "narrow", None, None, None),
            P(),
            P(),
            P(),
            P(),
            P(),
            P("wide", "narrow", None),
        ),
        out_specs=(
            P("wide", "narrow", None),
            P("wide", None, "narrow", None),
            P("wide", "narrow", None, None, None),
            P(),
            P(),
        ),
        check_vma=False,
    )
```

```python
import functools
import math

import jax
import jax.numpy as jnp
import numpy as np
from jax import lax
from jax.experimental import pallas as pl
from jax.experimental.pallas import tpu as pltpu
from jax.sharding import PartitionSpec as P

MX = 16
MY = 16
MZ = 16
F32 = jnp.float32
BF16 = jnp.bfloat16
VMEM_LIMIT = 32 * 1024 * 1024
FIRST = 2

TAIL_SLOPE = 0.275
TAIL = (
    0.11780925840139389,
    0.04211147502064705,
    0.3339323103427887,
    -0.3309934139251709,
    0.4519987106323242,
    -0.11485832929611206,
)


def signed(indices, count):
    return np.where(indices < count // 2, indices, indices - count)


def wave(positions, frequency, length):
    turned = np.mod(np.multiply.outer(positions, frequency), length)
    angles = turned.astype(np.float32) * np.float32(2.0 * math.pi / length)
    scale = np.float32(1.0 / math.sqrt(length))
    return np.cos(angles) * scale, np.sin(angles) * scale


def pair(cosine, sine, sign):
    return np.stack(
        [np.stack([cosine, -sign * sine], -1), np.stack([sign * sine, cosine], -1)], -2
    )


def y_tables(total_y, rows_y, kz, modes):
    cosine, sine = wave(np.arange(total_y), signed(np.arange(MY), MY), total_y)
    narrow = total_y // rows_y
    same = np.eye(kz, dtype=np.float32)
    forward = pair(cosine, sine, -1.0).reshape(narrow, rows_y, MY // modes, modes, 2, 2)
    inverse = pair(cosine, sine, 1.0).reshape(narrow, rows_y, MY // modes, modes, 2, 2)
    forward = np.einsum("nybjtr,kl->bjtkynlr", forward, same)
    inverse = np.einsum("nybjst,kl->bnyksjtl", inverse, same)
    blocks = MY // modes
    forward = forward.reshape(blocks, modes * 2 * kz, rows_y * narrow * kz * 2)
    inverse = inverse.reshape(blocks, narrow * rows_y * kz * 2, modes * 2 * kz)
    return forward.astype(BF16), inverse.astype(BF16)


def dot(a, b):
    return jnp.dot(a, b, preferred_element_type=F32)


def dot_nt(a, b):
    return lax.dot_general(a, b, (((1,), (1,)), ((), ())), preferred_element_type=F32)


def dot_tn(a, b):
    return lax.dot_general(a, b, (((0,), (0,)), ((), ())), preferred_element_type=F32)


def grid_of(rows, columns):
    shape = (rows, columns)
    return lax.broadcasted_iota(jnp.int32, shape, 0), lax.broadcasted_iota(jnp.int32, shape, 1)


def selector(rows, columns, condition):
    return jnp.where(condition(*grid_of(rows, columns)), 1.0, 0.0).astype(BF16)


def halves(values):
    high = values.astype(BF16)
    return high, (values - high.astype(F32)).astype(BF16)


def stacked(refs, lanes=slice(None)):
    return jnp.concatenate([ref[:, lanes] for ref in refs], axis=0)


def cosine_of(phase, length):
    angles = (phase & (length - 1)).astype(F32) * (2.0 * math.pi / length)
    return jnp.cos(angles) * (1.0 / math.sqrt(length))


class Place:
    def __init__(self, wide, narrow, kz, modes, rows_y, channels, z_count, fold):
        self.wide, self.narrow, self.kz, self.modes = wide, narrow, kz, modes
        self.rows_y, self.channels, self.z_count, self.fold = rows_y, channels, z_count, fold
        self.outer = wide // 2
        self.partners = self.outer * narrow
        self.lanes = rows_y * channels

    def here(self):
        wide = lax.axis_index("wide")
        return wide // 2, wide % 2

    def frequency(self, wide):
        index = (wide * self.modes) // MY
        return jnp.where(index < MX // 2, index, index - MX)

    def z_table(self, doubled):
        row, z = grid_of(2 * MZ, self.z_count)
        frequency = row >> 1
        value = cosine_of(z * frequency + (row & 1) * (self.z_count // 4), self.z_count)
        if doubled:
            value = jnp.where(frequency > 0, 2.0 * value, value)
        return value.astype(BF16)

    def expanded(self, small):
        row, column = grid_of(2 * MZ, small.shape[1])
        same = (row >> 1) == ((column >> 1) & (MZ - 1))
        blocks = []
        for g in range(small.shape[0] // 2):
            value = jnp.where((row & 1) == 0, small[2 * g : 2 * g + 1], small[2 * g + 1 : 2 * g + 2])
            blocks.append(jnp.where(same, value, 0.0))
        return jnp.concatenate(blocks, axis=0)

    def forward_x(self):
        outer, inner = self.here()
        row, column = grid_of(2 * self.outer, 4 * MZ)
        x = 2 * outer + (inner ^ (column // (2 * MZ)))
        frequency = self.frequency(2 * ((row >> 1) ^ FIRST) + inner)
        quarter = self.wide // 4
        small = cosine_of(x * frequency + quarter * ((row & 1) - (column & 1)), self.wide)
        return self.expanded(small)

    def inverse_x(self):
        outer, inner = self.here()
        row, column = grid_of(4, self.outer * 2 * MZ)
        x = 2 * outer + (inner ^ (row >> 1))
        frequency = self.frequency(2 * ((column // (2 * MZ)) ^ FIRST) + inner)
        quarter = self.wide // 4
        small = cosine_of(x * frequency + quarter * ((column & 1) - (row & 1)), self.wide)
        return self.expanded(small).astype(BF16)


def repeat_rows(out_ref, block):
    height = block.shape[0]
    for first in range(0, out_ref.shape[0], height):
        out_ref[first : first + height] = block


def write_pieces(place, send_ref, block, shares):
    step, half = 2 * place.kz, place.lanes // 2
    height = send_ref.shape[0] // place.partners
    for p in range(place.partners):
        own = block[p * step % block.shape[0] :][:step]
        first = p * height
        send_ref[first : first + step] = own[:, :half]
        send_ref[first + step : first + 2 * step] = own[:, half:]
        send_ref[first + 2 * step : first + height] = shares[p * 8 % shares.shape[0] :][:8]


def read_pieces(place, pieces_ref):
    step = 2 * place.kz
    if pieces_ref.shape[1] == place.lanes:
        return pieces_ref[...], None
    height = pieces_ref.shape[0] // place.partners
    blocks, shares = [], []
    for p in range(place.partners):
        first = p * height
        left = pieces_ref[first : first + step]
        right = pieces_ref[first + step : first + 2 * step]
        blocks.append(jnp.concatenate([left, right], axis=1))
        shares.append(pieces_ref[first + 2 * step : first + height].astype(F32))
    return jnp.concatenate(blocks, axis=0), shares


def analysed(place, pieces, y_forward, copies):
    height = 2 * MZ
    turned = sum(
        pieces[first : first + height].astype(F32) for first in range(0, pieces.shape[0], height)
    )
    channels = place.channels
    lines = jnp.concatenate(
        [turned[:, y * channels : (y + 1) * channels] for y in range(place.rows_y)], axis=0
    )
    return dot(y_forward, jnp.concatenate([lines.astype(BF16)] * copies, axis=1))


def spread_lines(place, modes, y_inverse):
    lines = dot(y_inverse, modes)
    step = 2 * place.kz
    blocks = []
    for n in range(place.narrow):
        first = n * place.rows_y
        parts = [lines[(first + y) * step : (first + y + 1) * step] for y in range(place.rows_y)]
        blocks.append(jnp.concatenate(parts, axis=1))
    return jnp.concatenate(blocks, axis=0).astype(BF16)


def turn_matrix(place, forward):
    channels, rows_y = place.channels, place.rows_y

    def same(row, column):
        if forward:
            row, column = column, row
        return (row % channels == column // rows_y) & (row // channels == column % rows_y)

    return selector(place.lanes, place.lanes, same)


def side_by_side(values, count):
    height = values.shape[0] // count
    return jnp.concatenate([values[y * height : (y + 1) * height] for y in range(count)], axis=1)


def one_below_other(values, count):
    width = values.shape[1] // count
    return jnp.concatenate([values[:, y * width : (y + 1) * width] for y in range(count)], axis=0)


def own_kernel(place, field_ref, field_out_ref, spectra_ref):
    turned = dot(turn_matrix(place, False), field_ref[...]).astype(BF16)
    field_out_ref[...] = side_by_side(turned, place.rows_y)
    spectra_ref[...] = dot_nt(place.z_table(False), turned).astype(BF16)


def start_kernel(place, spectra_ref, twin_ref, send_ref):
    twin = dot_nt(place.z_table(False), twin_ref[...]).astype(BF16)
    twin = dot(twin, turn_matrix(place, True)).astype(BF16)
    values = jnp.concatenate([spectra_ref[...], twin], axis=0)
    tables = jnp.concatenate(halves(place.forward_x()), axis=1)
    send_ref[...] = dot(tables, jnp.concatenate([values, values], axis=0)).astype(BF16)


def pack_kernel(weight_ref, packed_ref):
    modes, kz, _, channels, _ = weight_ref.shape
    for q in range(modes // 4):
        parts = [weight_ref[4 * q + j // 2, :, j % 2] for j in range(8)]
        packed = jnp.concatenate(parts, axis=-1).reshape(kz * channels, 8 * channels)
        packed_ref[q] = packed.astype(BF16)


def ready_kernel(place, field_ref, mix_ref, mix_bias_ref, head_ref, *refs):
    pointwise_ref, head_out_ref, z_doubled_ref = refs
    pointwise_ref[...] = dot_tn(mix_ref[...], field_ref[...]) + mix_bias_ref[...]
    head_out_ref[...] = jnp.transpose(head_ref[...].astype(F32)).astype(BF16)
    z_doubled_ref[...] = place.z_table(True)


def fold_kernel(place, own_ref, got_ref, tables_ref, *refs):
    values = jnp.concatenate([own_ref[...], got_ref[...]], axis=0)
    values = jnp.concatenate([values, values], axis=0)
    partial = dot(tables_ref[...], values).astype(BF16)
    if place.fold:
        shares_ref, send_ref = refs
        write_pieces(place, send_ref, partial, shares_ref[...])
    else:
        refs[0][...] = partial


def mode_kernel(
    place, pieces_ref, y_forward_ref, y_inverse_ref, weight_ref, spectrum_ref, send_ref
):
    kz, channels = place.kz, place.channels
    spectrum = analysed(place, pieces_ref[...], y_forward_ref[...], kz)
    spectrum_ref[...] = spectrum[:, :channels]
    row, lane = grid_of(*spectrum.shape)
    blocked = jnp.where(row % kz == lane // channels, spectrum, 0.0)
    mixed = []
    for q in range(place.modes // 4):
        left = blocked[q * 8 * kz : (q + 1) * 8 * kz].astype(BF16)
        product = dot(left, weight_ref[q])
        for j in range(4):
            own = product[j * 2 * kz : (j + 1) * 2 * kz, j * 2 * channels : (j + 1) * 2 * channels]
            real, imag = own[:, :channels], own[:, channels:]
            mixed.append(real[:kz] - imag[kz:])
            mixed.append(imag[:kz] + real[kz:])
    mode = jnp.concatenate(mixed, axis=0).astype(BF16)
    repeat_rows(send_ref, spread_lines(place, mode, y_inverse_ref[...]))


def part_kernel(place, pieces_ref, *refs):
    pieces, shares = read_pieces(place, pieces_ref)
    lines = dot(place.inverse_x(), pieces)
    height = 2 * MZ
    if shares is None:
        own_ref, send_ref = refs
        own_ref[...] = lines[:height]
        send_ref[...] = lines[height:].astype(BF16)
        return
    _, own_ref, send_ref, sums_ref = refs
    own_ref[...] = lines[:height]
    send_ref[:height] = lines[height:].astype(BF16)
    got = jnp.concatenate(shares, axis=0).astype(BF16)
    channels = place.channels

    def chosen(part):
        return dot(
            selector(
                2 * channels,
                got.shape[0],
                lambda row, column: (column // 8 == (row % channels) // 2)
                & (column % 8 == 4 * part + 2 * (row // channels) + row % 2),
            ),
            got,
        )

    high, low = chosen(0), chosen(1)
    sums_ref[...] = high + low
    send_ref[height:] = jnp.concatenate([high, low], axis=1).astype(BF16)


def normal(values):
    scaled = 1.0 / (1.0 + TAIL_SLOPE * jnp.abs(values))
    decay = jnp.exp(-0.5 * values * values)
    tail = TAIL[-1]
    for factor in TAIL[-2::-1]:
        tail = tail * scaled + factor
    tail = tail * (scaled * decay)
    cumulative = jnp.where(values > 0.0, 1.0 - tail, tail)
    return values * cumulative, cumulative + values * (decay * (1.0 / math.sqrt(2.0 * math.pi)))


def cell_kernel(place, *refs):
    own_ref, got_ref, z_table_ref, pointwise_ref, head_ref, head_turned_ref = refs[:6]
    head_bias_ref, out_row_ref, out_column_ref, cotangent_ref = refs[6:10]
    prediction_ref, grad_pre_ref, send_ref, hidden_ref, head_slope_ref = refs[10:]
    rows_y, z_count = place.rows_y, place.z_count
    z_table = z_table_ref[...]
    lines = (own_ref[...] + got_ref[...].astype(F32)).astype(BF16)
    pre_act = side_by_side(dot_tn(lines, z_table), rows_y) + pointwise_ref[...]
    head, head_turned = head_ref[...], head_turned_ref[...]
    head_bias, out_row, out_column = head_bias_ref[...], out_row_ref[...], out_column_ref[...]
    width = 2 * z_count
    slopes, head_pre = [], []
    for first in range(0, rows_y * z_count, width):
        value, slope = normal(pre_act[:, first : first + width])
        hidden = value.astype(BF16)
        hidden_ref[:, first : first + width] = hidden
        slopes.append(slope)
        head_pre.append(dot(head_turned, hidden))
    gradients = []
    for index, first in enumerate(range(0, rows_y, 2)):
        target = jnp.concatenate(
            [cotangent_ref[y : y + 1] for y in range(first, first + 2)], axis=1
        )
        active, slope = normal(head_pre[index] + head_bias)
        predicted = dot(out_row, active.astype(BF16))
        prediction_ref[first : first + 1] = predicted[:, :z_count]
        prediction_ref[first + 1 : first + 2] = predicted[:, z_count:]
        head_slope = (target * out_column * slope).astype(BF16)
        head_slope_ref[:, first * z_count : first * z_count + width] = head_slope
        gradients.append((dot(head, head_slope) * slopes[index]).astype(BF16))
    gradient = jnp.concatenate(gradients, axis=1)
    grad_pre_ref[...] = gradient
    send_ref[...] = dot_nt(z_table, one_below_other(gradient, rows_y)).astype(BF16)


def sums_kernel(place, field_ref, gradient_ref, hidden_ref, head_slope_ref, *refs):
    refs[-1][...] = jnp.concatenate(halves(place.forward_x()), axis=1)
    grad_mix = dot_nt(field_ref[...], gradient_ref[...])
    grad_head = dot_nt(hidden_ref[...], head_slope_ref[...])
    if not place.fold:
        refs[0][...] = grad_mix
        refs[1][...] = grad_head
        return
    channels, hidden_units = grad_head.shape
    rest = jnp.zeros((channels, hidden_units - channels), F32)
    wide_mix = jnp.concatenate([grad_mix, rest], axis=1)
    high, low = halves(jnp.concatenate([grad_head, wide_mix], axis=0))
    split = jnp.concatenate([high, low], axis=0)
    place_of = selector(
        8 * place.partners,
        4 * channels,
        lambda row, column: (column % channels == 2 * (row // 8) + row % 2)
        & (column // channels == (row % 8) // 2),
    )
    refs[0][...] = dot(place_of, split).astype(BF16)


def back_kernel(
    place, pieces_ref, y_forward_ref, y_inverse_ref, weight_ref, adjoint_ref, send_ref
):
    kz, channels = place.kz, place.channels
    pieces, shares = read_pieces(place, pieces_ref)
    adjoint = analysed(place, pieces, y_forward_ref[...], 1)
    adjoint_ref[...] = adjoint
    turned = []
    for first in range(0, adjoint.shape[0], 2 * kz):
        turned += [adjoint[first + kz : first + 2 * kz], -adjoint[first : first + kz]]
    left = jnp.concatenate([adjoint, jnp.concatenate(turned, axis=0)], axis=1)
    left = jnp.concatenate([left] * 4, axis=1)
    row, lane = grid_of(*left.shape)
    same = (row // (2 * kz)) % 4 == lane // (2 * channels)
    left = jnp.where(same, left, 0.0).astype(BF16)
    block = 8 * kz
    pulled = [
        dot_nt(left[q * block : (q + 1) * block], weight_ref[q]) for q in range(place.modes // 4)
    ]
    pulled = jnp.concatenate(pulled, axis=0)
    row, lane = grid_of(*pulled.shape)
    pulled = jnp.where(row % kz == lane // channels, pulled, 0.0).astype(BF16)
    gather = selector(
        kz * channels, channels, lambda row, column: row % channels == column
    )
    modes_back = dot(pulled, gather).astype(BF16)
    block = spread_lines(place, modes_back, y_inverse_ref[...])
    if shares is None:
        repeat_rows(send_ref, block)
        return
    total = sum(shares[1:], shares[0])
    high, low = halves(total[0:4] + total[4:8])
    split = jnp.concatenate([high.astype(F32), low.astype(F32)], axis=0)
    write_pieces(place, send_ref, block, split.astype(BF16))


def outer_kernel(spectrum_ref, adjoint_ref, out_ref, done_ref):
    done_ref[...] = jnp.zeros(done_ref.shape, F32)
    modes, kz = out_ref.shape[:2]
    for j in range(modes):
        columns = jnp.transpose(spectrum_ref[j])
        adjoint = adjoint_ref[j]
        for k in range(kz):
            s_real, s_imag = columns[:, k : k + 1], columns[:, kz + k : kz + k + 1]
            a_real, a_imag = adjoint[k : k + 1], adjoint[kz + k : kz + k + 1]
            out_ref[j, k, 0] = s_real * a_real + s_imag * a_imag
            out_ref[j, k, 1] = s_real * a_imag - s_imag * a_real


def pointwise_kernel(place, mix_ref, gradient_ref, out_ref, z_plain_ref, turn_ref):
    z_plain_ref[...] = place.z_table(False)
    turn_ref[...] = turn_matrix(place, False)
    z_count = place.z_count
    product = dot(mix_ref[...], gradient_ref[...])
    for y in range(place.rows_y):
        out_ref[:, y, :] = product[:, y * z_count : (y + 1) * z_count]


def finish_kernel(place, *refs):
    own_ref, got_ref, z_table_ref, turn_ref, pointwise_ref, prediction_ref = refs[:6]
    refs = refs[6:]
    height = 2 * MZ
    channels = place.channels
    lines = (own_ref[...] + got_ref[:height].astype(F32)).astype(BF16)
    lines = dot(lines, turn_ref[...]).astype(BF16)
    pointwise = pointwise_ref[...].reshape(place.lanes, place.z_count)
    grad_field = (dot_tn(lines, z_table_ref[...]) + pointwise).astype(BF16)
    if not place.fold:
        refs[0][...] = grad_field
        refs[1][...] = prediction_ref[...]
        return
    sums_ref, grad_field_ref, out_ref, grad_mix_ref, grad_head_ref = refs
    grad_field_ref[...] = grad_field
    out_ref[...] = prediction_ref[...]
    got = got_ref[height:].astype(F32)
    width = sums_ref.shape[1]
    total = sums_ref[...] + got[:, :width] + got[:, width:]
    grad_head_ref[...] = total[:channels]
    grad_mix_ref[...] = total[channels:, :channels]


def call(kernel, outs, name, **spec):
    return pl.pallas_call(
        kernel,
        out_shape=[jax.ShapeDtypeStruct(shape, dtype) for shape, dtype in outs],
        compiler_params=pltpu.CompilerParams(vmem_limit_bytes=VMEM_LIMIT),
        cost_estimate=pl.CostEstimate(flops=1 << 22, bytes_accessed=1 << 19, transcendentals=0),
        name=name,
        **spec,
    )


def body(
    lifted_field,
    spectral_weight,
    mix_weight,
    mix_bias,
    head_weight,
    head_bias,
    out_weight,
    cotangent,
):
    wide = lax.axis_size("wide")
    narrow = lax.axis_size("narrow")
    devices = wide * narrow
    _, channels, rows_y, z_count = lifted_field.shape
    modes, kz = spectral_weight.shape[:2]
    hidden_units = head_weight.shape[1]
    cells = channels * rows_y
    place = Place(wide, narrow, kz, modes, rows_y, channels, z_count, False)
    place.fold = 2 * place.partners == channels and hidden_units == 128 and cells == 256 and kz % 8 == 0
    height = 2 * MZ
    step = 2 * kz
    partners = place.partners
    mode_lines = modes * 2 * kz

    y_forward, y_inverse = y_tables(rows_y * narrow, rows_y, kz, modes)
    if len(y_forward) > 1:
        block = lax.axis_index("wide") % len(y_forward)
        y_forward = lax.dynamic_index_in_dim(jnp.asarray(y_forward), block, 0, False)
        y_inverse = lax.dynamic_index_in_dim(jnp.asarray(y_inverse), block, 0, False)
    else:
        y_forward, y_inverse = jnp.asarray(y_forward[0]), jnp.asarray(y_inverse[0])

    def to_twin(send):
        pairs = [(p, p ^ narrow) for p in range(devices)]
        return lax.ppermute(send, ("wide", "narrow"), pairs)

    groups = [
        [
            (2 * (outer ^ FIRST) + inner) * narrow + n
            for outer in range(wide // 2)
            for n in range(narrow)
        ]
        for inner in range(2)
    ]

    def exchange(send):
        pieces = send.reshape(partners, -1, send.shape[1])
        got = lax.all_to_all(
            pieces, ("wide", "narrow"), 0, 0, axis_index_groups=groups, tiled=True
        )
        return got.reshape(send.shape)

    plain = ((partners * step, cells), BF16)
    shared = ((partners * (2 * step + 8), cells // 2), BF16) if place.fold else plain
    twin_plain = ((height, cells), BF16)
    twin_shared = ((height + 2 * channels, cells), BF16) if place.fold else twin_plain
    sums_shape = ((2 * channels, hidden_units), F32)
    own_lines = ((height, cells), F32)
    across = (channels, rows_y * z_count)

    def run(kernel, outs, name, **spec):
        return call(functools.partial(kernel, place), outs, name, **spec)

    flat_field = lifted_field.reshape(cells, z_count)
    twin_field = to_twin(flat_field)
    field, spectra = run(own_kernel, [(across, BF16), twin_plain], "own")(flat_field)
    (send,) = run(start_kernel, [plain], "start")(spectra, twin_field)
    packed_shape = ((modes // 4, kz * channels, 8 * channels), BF16)
    (weight,) = call(pack_kernel, [packed_shape], "pack")(spectral_weight)
    spectrum, send = run(mode_kernel, [((mode_lines, channels), F32), plain], "mode")(
        exchange(send), y_forward, y_inverse, weight
    )
    own, send = run(part_kernel, [own_lines, twin_plain], "part")(exchange(send))
    pointwise, head_turned, z_doubled = run(
        ready_kernel,
        [(across, F32), ((hidden_units, channels), BF16), ((height, z_count), BF16)],
        "ready",
    )(field, mix_weight, mix_bias[:, None], head_weight)
    prediction, grad_pre, send, hidden, head_slope = run(
        cell_kernel,
        [
            ((rows_y, z_count), F32),
            (across, BF16),
            twin_plain,
            (across, BF16),
            ((hidden_units, rows_y * z_count), BF16),
        ],
        "cell",
    )(
        own,
        to_twin(send),
        z_doubled,
        pointwise,
        head_weight,
        head_turned,
        head_bias[:, None],
        out_weight[None],
        out_weight.astype(F32)[:, None],
        cotangent[0],
    )
    if place.fold:
        outs = [((8 * partners, hidden_units), BF16)]
    else:
        outs = [((channels, channels), F32), ((channels, hidden_units), F32)]
    outs += [((wide // 2 * height, 4 * height), BF16)]
    *sums, forward = run(sums_kernel, outs, "sums")(field, grad_pre, hidden, head_slope)
    if not place.fold:
        totals = lax.psum(tuple(sums), ("wide", "narrow"))
        sums = []
    (send,) = run(fold_kernel, [shared], "fold")(send, to_twin(send), forward, *sums)
    adjoint, send = run(back_kernel, [((mode_lines, channels), F32), shared], "back")(
        exchange(send), y_forward, y_inverse, weight
    )
    some = max(1, modes // 4)
    grad_spectral, done = pl.pallas_call(
        outer_kernel,
        grid=(modes // some,),
        in_specs=[pl.BlockSpec((some, 2 * kz, channels), lambda j: (j, 0, 0))] * 2,
        out_specs=[
            pl.BlockSpec((some, kz, 2, channels, channels), lambda j: (j, 0, 0, 0, 0)),
            pl.BlockSpec((8, 128), lambda j: (0, 0)),
        ],
        out_shape=[
            jax.ShapeDtypeStruct(spectral_weight.shape, F32),
            jax.ShapeDtypeStruct((8, 128), F32),
        ],
        compiler_params=pltpu.CompilerParams(vmem_limit_bytes=VMEM_LIMIT),
        cost_estimate=pl.CostEstimate(flops=1 << 22, bytes_accessed=5 << 20, transcendentals=0),
        name="outer",
    )(spectrum.reshape(modes, 2 * kz, channels), adjoint.reshape(modes, 2 * kz, channels))
    pointwise, z_plain, turn = run(
        pointwise_kernel,
        [
            ((channels, rows_y, z_count), F32),
            ((height, z_count), BF16),
            ((cells, cells), BF16),
        ],
        "pointwise",
    )(mix_weight, grad_pre)
    outs = [own_lines, twin_shared] + ([sums_shape] if place.fold else [])
    after = (done,) if place.fold else ()
    own, send, *sums = run(part_kernel, outs, "part")(exchange(send), *after)
    outs = [((cells, z_count), BF16), ((rows_y, z_count), F32)]
    if place.fold:
        outs += [((channels, channels), F32), ((channels, hidden_units), F32)]
    grad_field, prediction, *summed = run(finish_kernel, outs, "finish")(
        own, to_twin(send), z_plain, turn, pointwise, prediction, *sums
    )
    grad_mix, grad_head = summed if place.fold else totals
    return (
        prediction[None],
        grad_field.reshape(lifted_field.shape),
        grad_spectral,
        grad_mix,
        grad_head,
    )


def solution(mesh):
    return jax.shard_map(
        body,
        mesh=mesh,
        in_specs=(
            P("wide", None, "narrow", None),
            P("wide", "narrow", None, None, None),
            P(),
            P(),
            P(),
            P(),
            P(),
            P("wide", "narrow", None),
        ),
        out_specs=(
            P("wide", "narrow", None),
            P("wide", None, "narrow", None),
            P("wide", "narrow", None, None, None),
            P(),
            P(),
        ),
        check_vma=False,
    )
```

```python
import functools
import math

import jax
import jax.numpy as jnp
import numpy as np
from jax import lax
from jax.experimental import pallas as pl
from jax.experimental.pallas import tpu as pltpu
from jax.sharding import PartitionSpec as P

MX = 16
MY = 16
MZ = 16
F32 = jnp.float32
BF16 = jnp.bfloat16
VMEM_LIMIT = 32 * 1024 * 1024
FIRST = 2

TAIL_SLOPE = 0.275
TAIL = (
    0.11780925840139389,
    0.04211147502064705,
    0.3339323103427887,
    -0.3309934139251709,
    0.4519987106323242,
    -0.11485832929611206,
)


def signed(indices, count):
    return np.where(indices < count // 2, indices, indices - count)


def wave(positions, frequency, length):
    turned = np.mod(np.multiply.outer(positions, frequency), length)
    angles = turned.astype(np.float32) * np.float32(2.0 * math.pi / length)
    scale = np.float32(1.0 / math.sqrt(length))
    return np.cos(angles) * scale, np.sin(angles) * scale


def pair(cosine, sine, sign):
    return np.stack(
        [np.stack([cosine, -sign * sine], -1), np.stack([sign * sine, cosine], -1)], -2
    )


def y_tables(total_y, rows_y, kz, modes):
    cosine, sine = wave(np.arange(total_y), signed(np.arange(MY), MY), total_y)
    narrow = total_y // rows_y
    same = np.eye(kz, dtype=np.float32)
    forward = pair(cosine, sine, -1.0).reshape(narrow, rows_y, MY // modes, modes, 2, 2)
    inverse = pair(cosine, sine, 1.0).reshape(narrow, rows_y, MY // modes, modes, 2, 2)
    forward = np.einsum("nybjtr,kl->bjtkynlr", forward, same)
    inverse = np.einsum("nybjst,kl->bnyksjtl", inverse, same)
    blocks = MY // modes
    forward = forward.reshape(blocks, modes * 2 * kz, rows_y * narrow * kz * 2)
    inverse = inverse.reshape(blocks, narrow * rows_y * kz * 2, modes * 2 * kz)
    return forward.astype(BF16), inverse.astype(BF16)


def dot(a, b):
    return jnp.dot(a, b, preferred_element_type=F32)


def dot_nt(a, b):
    return lax.dot_general(a, b, (((1,), (1,)), ((), ())), preferred_element_type=F32)


def dot_tn(a, b):
    return lax.dot_general(a, b, (((0,), (0,)), ((), ())), preferred_element_type=F32)


def grid_of(rows, columns):
    shape = (rows, columns)
    return lax.broadcasted_iota(jnp.int32, shape, 0), lax.broadcasted_iota(jnp.int32, shape, 1)


def selector(rows, columns, condition):
    return jnp.where(condition(*grid_of(rows, columns)), 1.0, 0.0).astype(BF16)


def halves(values):
    high = values.astype(BF16)
    return high, (values - high.astype(F32)).astype(BF16)


def stacked(refs, lanes=slice(None)):
    return jnp.concatenate([ref[:, lanes] for ref in refs], axis=0)


def cosine_of(phase, length):
    angles = (phase & (length - 1)).astype(F32) * (2.0 * math.pi / length)
    return jnp.cos(angles) * (1.0 / math.sqrt(length))


class Place:
    def __init__(self, wide, narrow, kz, modes, rows_y, channels, z_count, fold):
        self.wide, self.narrow, self.kz, self.modes = wide, narrow, kz, modes
        self.rows_y, self.channels, self.z_count, self.fold = rows_y, channels, z_count, fold
        self.outer = wide // 2
        self.partners = self.outer * narrow
        self.lanes = rows_y * channels

    def here(self):
        wide = lax.axis_index("wide")
        return wide // 2, wide % 2

    def partner(self, outer, inner, other):
        half = self.outer // 2
        return 2 * other + (inner ^ (outer // half) ^ (other // half))

    def frequency(self, wide):
        index = (wide * self.modes) // MY
        return jnp.where(index < MX // 2, index, index - MX)

    def z_table(self, doubled):
        row, z = grid_of(2 * MZ, self.z_count)
        frequency = row >> 1
        value = cosine_of(z * frequency + (row & 1) * (self.z_count // 4), self.z_count)
        if doubled:
            value = jnp.where(frequency > 0, 2.0 * value, value)
        return value.astype(BF16)

    def expanded(self, small):
        row, column = grid_of(2 * MZ, small.shape[1])
        same = (row >> 1) == ((column >> 1) & (MZ - 1))
        blocks = []
        for g in range(small.shape[0] // 2):
            value = jnp.where((row & 1) == 0, small[2 * g : 2 * g + 1], small[2 * g + 1 : 2 * g + 2])
            blocks.append(jnp.where(same, value, 0.0))
        return jnp.concatenate(blocks, axis=0)

    def forward_x(self):
        outer, inner = self.here()
        row, column = grid_of(2 * self.outer, 4 * MZ)
        x = 2 * outer + (inner ^ (column // (2 * MZ)))
        frequency = self.frequency(self.partner(outer, inner, (row >> 1) ^ FIRST))
        quarter = self.wide // 4
        small = cosine_of(x * frequency + quarter * ((row & 1) - (column & 1)), self.wide)
        return self.expanded(small)

    def inverse_x(self):
        outer, inner = self.here()
        row, column = grid_of(4, self.outer * 2 * MZ)
        x = 2 * outer + (inner ^ (row >> 1))
        frequency = self.frequency(self.partner(outer, inner, (column // (2 * MZ)) ^ FIRST))
        quarter = self.wide // 4
        small = cosine_of(x * frequency + quarter * ((column & 1) - (row & 1)), self.wide)
        return self.expanded(small).astype(BF16)


def repeat_rows(out_ref, block):
    height = block.shape[0]
    for first in range(0, out_ref.shape[0], height):
        out_ref[first : first + height] = block


def write_pieces(place, send_ref, block, shares):
    step, half = 2 * place.kz, place.lanes // 2
    height = send_ref.shape[0] // place.partners
    for p in range(place.partners):
        own = block[p * step % block.shape[0] :][:step]
        first = p * height
        send_ref[first : first + step] = own[:, :half]
        send_ref[first + step : first + 2 * step] = own[:, half:]
        send_ref[first + 2 * step : first + height] = shares[p * 8 % shares.shape[0] :][:8]


def read_pieces(place, pieces_ref):
    step = 2 * place.kz
    if pieces_ref.shape[1] == place.lanes:
        return pieces_ref[...], None
    height = pieces_ref.shape[0] // place.partners
    blocks, shares = [], []
    for p in range(place.partners):
        first = p * height
        left = pieces_ref[first : first + step]
        right = pieces_ref[first + step : first + 2 * step]
        blocks.append(jnp.concatenate([left, right], axis=1))
        shares.append(pieces_ref[first + 2 * step : first + height].astype(F32))
    return jnp.concatenate(blocks, axis=0), shares


def analysed(place, pieces, y_forward, copies):
    height = 2 * MZ
    turned = sum(
        pieces[first : first + height].astype(F32) for first in range(0, pieces.shape[0], height)
    )
    channels = place.channels
    lines = jnp.concatenate(
        [turned[:, y * channels : (y + 1) * channels] for y in range(place.rows_y)], axis=0
    )
    return dot(y_forward, jnp.concatenate([lines.astype(BF16)] * copies, axis=1))


def spread_lines(place, modes, y_inverse):
    lines = dot(y_inverse, modes)
    step = 2 * place.kz
    blocks = []
    for n in range(place.narrow):
        first = n * place.rows_y
        parts = [lines[(first + y) * step : (first + y + 1) * step] for y in range(place.rows_y)]
        blocks.append(jnp.concatenate(parts, axis=1))
    return jnp.concatenate(blocks, axis=0).astype(BF16)


def turn_matrix(place, forward):
    channels, rows_y = place.channels, place.rows_y

    def same(row, column):
        if forward:
            row, column = column, row
        return (row % channels == column // rows_y) & (row // channels == column % rows_y)

    return selector(place.lanes, place.lanes, same)


def side_by_side(values, count):
    height = values.shape[0] // count
    return jnp.concatenate([values[y * height : (y + 1) * height] for y in range(count)], axis=1)


def one_below_other(values, count):
    width = values.shape[1] // count
    return jnp.concatenate([values[:, y * width : (y + 1) * width] for y in range(count)], axis=0)


def own_kernel(place, field_ref, field_out_ref, spectra_ref):
    turned = dot(turn_matrix(place, False), field_ref[...]).astype(BF16)
    field_out_ref[...] = side_by_side(turned, place.rows_y)
    spectra_ref[...] = dot_nt(place.z_table(False), turned).astype(BF16)


def start_kernel(place, spectra_ref, twin_ref, send_ref):
    twin = dot_nt(place.z_table(False), twin_ref[...]).astype(BF16)
    twin = dot(twin, turn_matrix(place, True)).astype(BF16)
    values = jnp.concatenate([spectra_ref[...], twin], axis=0)
    tables = jnp.concatenate(halves(place.forward_x()), axis=1)
    send_ref[...] = dot(tables, jnp.concatenate([values, values], axis=0)).astype(BF16)


def pack_kernel(weight_ref, packed_ref):
    modes, kz, _, channels, _ = weight_ref.shape
    for q in range(modes // 4):
        parts = [weight_ref[4 * q + j // 2, :, j % 2] for j in range(8)]
        packed = jnp.concatenate(parts, axis=-1).reshape(kz * channels, 8 * channels)
        packed_ref[q] = packed.astype(BF16)


def ready_kernel(place, field_ref, mix_ref, mix_bias_ref, head_ref, *refs):
    pointwise_ref, head_out_ref, z_doubled_ref = refs
    pointwise_ref[...] = dot_tn(mix_ref[...], field_ref[...]) + mix_bias_ref[...]
    head_out_ref[...] = jnp.transpose(head_ref[...].astype(F32)).astype(BF16)
    z_doubled_ref[...] = place.z_table(True)


def fold_kernel(place, own_ref, got_ref, tables_ref, *refs):
    values = jnp.concatenate([own_ref[...], got_ref[...]], axis=0)
    values = jnp.concatenate([values, values], axis=0)
    partial = dot(tables_ref[...], values).astype(BF16)
    if place.fold:
        shares_ref, send_ref = refs
        write_pieces(place, send_ref, partial, shares_ref[...])
    else:
        refs[0][...] = partial


def mode_kernel(
    place, pieces_ref, y_forward_ref, y_inverse_ref, weight_ref, spectrum_ref, send_ref
):
    kz, channels = place.kz, place.channels
    spectrum = analysed(place, pieces_ref[...], y_forward_ref[...], kz)
    spectrum_ref[...] = spectrum[:, :channels]
    row, lane = grid_of(*spectrum.shape)
    blocked = jnp.where(row % kz == lane // channels, spectrum, 0.0)
    mixed = []
    for q in range(place.modes // 4):
        left = blocked[q * 8 * kz : (q + 1) * 8 * kz].astype(BF16)
        product = dot(left, weight_ref[q])
        for j in range(4):
            own = product[j * 2 * kz : (j + 1) * 2 * kz, j * 2 * channels : (j + 1) * 2 * channels]
            real, imag = own[:, :channels], own[:, channels:]
            mixed.append(real[:kz] - imag[kz:])
            mixed.append(imag[:kz] + real[kz:])
    mode = jnp.concatenate(mixed, axis=0).astype(BF16)
    repeat_rows(send_ref, spread_lines(place, mode, y_inverse_ref[...]))


def part_kernel(place, pieces_ref, *refs):
    pieces, shares = read_pieces(place, pieces_ref)
    lines = dot(place.inverse_x(), pieces)
    height = 2 * MZ
    if shares is None:
        own_ref, send_ref = refs
        own_ref[...] = lines[:height]
        send_ref[...] = lines[height:].astype(BF16)
        return
    _, own_ref, send_ref, sums_ref = refs
    own_ref[...] = lines[:height]
    send_ref[:height] = lines[height:].astype(BF16)
    got = jnp.concatenate(shares, axis=0).astype(BF16)
    channels = place.channels

    def chosen(part):
        return dot(
            selector(
                2 * channels,
                got.shape[0],
                lambda row, column: (column // 8 == (row % channels) // 2)
                & (column % 8 == 4 * part + 2 * (row // channels) + row % 2),
            ),
            got,
        )

    high, low = chosen(0), chosen(1)
    sums_ref[...] = high + low
    send_ref[height:] = jnp.concatenate([high, low], axis=1).astype(BF16)


def normal(values):
    scaled = 1.0 / (1.0 + TAIL_SLOPE * jnp.abs(values))
    decay = jnp.exp(-0.5 * values * values)
    tail = TAIL[-1]
    for factor in TAIL[-2::-1]:
        tail = tail * scaled + factor
    tail = tail * (scaled * decay)
    cumulative = jnp.where(values > 0.0, 1.0 - tail, tail)
    return values * cumulative, cumulative + values * (decay * (1.0 / math.sqrt(2.0 * math.pi)))


def cell_kernel(place, *refs):
    own_ref, got_ref, z_table_ref, pointwise_ref, head_ref, head_turned_ref = refs[:6]
    head_bias_ref, out_row_ref, out_column_ref, cotangent_ref = refs[6:10]
    prediction_ref, grad_pre_ref, send_ref, hidden_ref, head_slope_ref = refs[10:]
    rows_y, z_count = place.rows_y, place.z_count
    z_table = z_table_ref[...]
    lines = (own_ref[...] + got_ref[...].astype(F32)).astype(BF16)
    pre_act = side_by_side(dot_tn(lines, z_table), rows_y) + pointwise_ref[...]
    head, head_turned = head_ref[...], head_turned_ref[...]
    head_bias, out_row, out_column = head_bias_ref[...], out_row_ref[...], out_column_ref[...]
    width = 2 * z_count
    slopes, head_pre = [], []
    for first in range(0, rows_y * z_count, width):
        value, slope = normal(pre_act[:, first : first + width])
        hidden = value.astype(BF16)
        hidden_ref[:, first : first + width] = hidden
        slopes.append(slope)
        head_pre.append(dot(head_turned, hidden))
    gradients = []
    for index, first in enumerate(range(0, rows_y, 2)):
        target = jnp.concatenate(
            [cotangent_ref[y : y + 1] for y in range(first, first + 2)], axis=1
        )
        active, slope = normal(head_pre[index] + head_bias)
        predicted = dot(out_row, active.astype(BF16))
        prediction_ref[first : first + 1] = predicted[:, :z_count]
        prediction_ref[first + 1 : first + 2] = predicted[:, z_count:]
        head_slope = (target * out_column * slope).astype(BF16)
        head_slope_ref[:, first * z_count : first * z_count + width] = head_slope
        gradients.append((dot(head, head_slope) * slopes[index]).astype(BF16))
    gradient = jnp.concatenate(gradients, axis=1)
    grad_pre_ref[...] = gradient
    send_ref[...] = dot_nt(z_table, one_below_other(gradient, rows_y)).astype(BF16)


def sums_kernel(place, field_ref, gradient_ref, hidden_ref, head_slope_ref, *refs):
    refs[-1][...] = jnp.concatenate(halves(place.forward_x()), axis=1)
    grad_mix = dot_nt(field_ref[...], gradient_ref[...])
    grad_head = dot_nt(hidden_ref[...], head_slope_ref[...])
    if not place.fold:
        refs[0][...] = grad_mix
        refs[1][...] = grad_head
        return
    channels, hidden_units = grad_head.shape
    rest = jnp.zeros((channels, hidden_units - channels), F32)
    wide_mix = jnp.concatenate([grad_mix, rest], axis=1)
    high, low = halves(jnp.concatenate([grad_head, wide_mix], axis=0))
    split = jnp.concatenate([high, low], axis=0)
    place_of = selector(
        8 * place.partners,
        4 * channels,
        lambda row, column: (column % channels == 2 * (row // 8) + row % 2)
        & (column // channels == (row % 8) // 2),
    )
    refs[0][...] = dot(place_of, split).astype(BF16)


def back_kernel(
    place, pieces_ref, y_forward_ref, y_inverse_ref, weight_ref, adjoint_ref, send_ref
):
    kz, channels = place.kz, place.channels
    pieces, shares = read_pieces(place, pieces_ref)
    adjoint = analysed(place, pieces, y_forward_ref[...], 1)
    adjoint_ref[...] = adjoint
    turned = []
    for first in range(0, adjoint.shape[0], 2 * kz):
        turned += [adjoint[first + kz : first + 2 * kz], -adjoint[first : first + kz]]
    left = jnp.concatenate([adjoint, jnp.concatenate(turned, axis=0)], axis=1)
    left = jnp.concatenate([left] * 4, axis=1)
    row, lane = grid_of(*left.shape)
    same = (row // (2 * kz)) % 4 == lane // (2 * channels)
    left = jnp.where(same, left, 0.0).astype(BF16)
    block = 8 * kz
    pulled = [
        dot_nt(left[q * block : (q + 1) * block], weight_ref[q]) for q in range(place.modes // 4)
    ]
    pulled = jnp.concatenate(pulled, axis=0)
    row, lane = grid_of(*pulled.shape)
    pulled = jnp.where(row % kz == lane // channels, pulled, 0.0).astype(BF16)
    gather = selector(
        kz * channels, channels, lambda row, column: row % channels == column
    )
    modes_back = dot(pulled, gather).astype(BF16)
    block = spread_lines(place, modes_back, y_inverse_ref[...])
    if shares is None:
        repeat_rows(send_ref, block)
        return
    total = sum(shares[1:], shares[0])
    high, low = halves(total[0:4] + total[4:8])
    split = jnp.concatenate([high.astype(F32), low.astype(F32)], axis=0)
    write_pieces(place, send_ref, block, split.astype(BF16))


def outer_kernel(spectrum_ref, adjoint_ref, out_ref, done_ref):
    done_ref[...] = jnp.zeros(done_ref.shape, F32)
    modes, kz = out_ref.shape[:2]
    for j in range(modes):
        columns = jnp.transpose(spectrum_ref[j])
        adjoint = adjoint_ref[j]
        for k in range(kz):
            s_real, s_imag = columns[:, k : k + 1], columns[:, kz + k : kz + k + 1]
            a_real, a_imag = adjoint[k : k + 1], adjoint[kz + k : kz + k + 1]
            out_ref[j, k, 0] = s_real * a_real + s_imag * a_imag
            out_ref[j, k, 1] = s_real * a_imag - s_imag * a_real


def pointwise_kernel(place, mix_ref, gradient_ref, out_ref, z_plain_ref, turn_ref):
    z_plain_ref[...] = place.z_table(False)
    turn_ref[...] = turn_matrix(place, False)
    z_count = place.z_count
    product = dot(mix_ref[...], gradient_ref[...])
    for y in range(place.rows_y):
        out_ref[:, y, :] = product[:, y * z_count : (y + 1) * z_count]


def finish_kernel(place, *refs):
    own_ref, got_ref, z_table_ref, turn_ref, pointwise_ref, prediction_ref = refs[:6]
    refs = refs[6:]
    height = 2 * MZ
    channels = place.channels
    lines = (own_ref[...] + got_ref[:height].astype(F32)).astype(BF16)
    lines = dot(lines, turn_ref[...]).astype(BF16)
    pointwise = pointwise_ref[...].reshape(place.lanes, place.z_count)
    grad_field = (dot_tn(lines, z_table_ref[...]) + pointwise).astype(BF16)
    if not place.fold:
        refs[0][...] = grad_field
        refs[1][...] = prediction_ref[...]
        return
    sums_ref, grad_field_ref, out_ref, grad_mix_ref, grad_head_ref = refs
    grad_field_ref[...] = grad_field
    out_ref[...] = prediction_ref[...]
    got = got_ref[height:].astype(F32)
    width = sums_ref.shape[1]
    total = sums_ref[...] + got[:, :width] + got[:, width:]
    grad_head_ref[...] = total[:channels]
    grad_mix_ref[...] = total[channels:, :channels]


def call(kernel, outs, name, **spec):
    return pl.pallas_call(
        kernel,
        out_shape=[jax.ShapeDtypeStruct(shape, dtype) for shape, dtype in outs],
        compiler_params=pltpu.CompilerParams(vmem_limit_bytes=VMEM_LIMIT),
        cost_estimate=pl.CostEstimate(flops=1 << 22, bytes_accessed=1 << 19, transcendentals=0),
        name=name,
        **spec,
    )


def body(
    lifted_field,
    spectral_weight,
    mix_weight,
    mix_bias,
    head_weight,
    head_bias,
    out_weight,
    cotangent,
):
    wide = lax.axis_size("wide")
    narrow = lax.axis_size("narrow")
    devices = wide * narrow
    _, channels, rows_y, z_count = lifted_field.shape
    modes, kz = spectral_weight.shape[:2]
    hidden_units = head_weight.shape[1]
    cells = channels * rows_y
    place = Place(wide, narrow, kz, modes, rows_y, channels, z_count, False)
    place.fold = 2 * place.partners == channels and hidden_units == 128 and cells == 256 and kz % 8 == 0
    height = 2 * MZ
    step = 2 * kz
    partners = place.partners
    mode_lines = modes * 2 * kz

    y_forward, y_inverse = y_tables(rows_y * narrow, rows_y, kz, modes)
    if len(y_forward) > 1:
        block = lax.axis_index("wide") % len(y_forward)
        y_forward = lax.dynamic_index_in_dim(jnp.asarray(y_forward), block, 0, False)
        y_inverse = lax.dynamic_index_in_dim(jnp.asarray(y_inverse), block, 0, False)
    else:
        y_forward, y_inverse = jnp.asarray(y_forward[0]), jnp.asarray(y_inverse[0])

    def to_twin(send):
        pairs = [(p, p ^ narrow) for p in range(devices)]
        return lax.ppermute(send, ("wide", "narrow"), pairs)

    groups = [
        [
            place.partner(0, inner, outer ^ FIRST) * narrow + n
            for outer in range(wide // 2)
            for n in range(narrow)
        ]
        for inner in range(2)
    ]

    def exchange(send):
        pieces = send.reshape(partners, -1, send.shape[1])
        got = lax.all_to_all(
            pieces, ("wide", "narrow"), 0, 0, axis_index_groups=groups, tiled=True
        )
        return got.reshape(send.shape)

    plain = ((partners * step, cells), BF16)
    shared = ((partners * (2 * step + 8), cells // 2), BF16) if place.fold else plain
    twin_plain = ((height, cells), BF16)
    twin_shared = ((height + 2 * channels, cells), BF16) if place.fold else twin_plain
    sums_shape = ((2 * channels, hidden_units), F32)
    own_lines = ((height, cells), F32)
    across = (channels, rows_y * z_count)

    def run(kernel, outs, name, **spec):
        return call(functools.partial(kernel, place), outs, name, **spec)

    flat_field = lifted_field.reshape(cells, z_count)
    twin_field = to_twin(flat_field)
    field, spectra = run(own_kernel, [(across, BF16), twin_plain], "own")(flat_field)
    (send,) = run(start_kernel, [plain], "start")(spectra, twin_field)
    packed_shape = ((modes // 4, kz * channels, 8 * channels), BF16)
    (weight,) = call(pack_kernel, [packed_shape], "pack")(spectral_weight)
    spectrum, send = run(mode_kernel, [((mode_lines, channels), F32), plain], "mode")(
        exchange(send), y_forward, y_inverse, weight
    )
    own, send = run(part_kernel, [own_lines, twin_plain], "part")(exchange(send))
    pointwise, head_turned, z_doubled = run(
        ready_kernel,
        [(across, F32), ((hidden_units, channels), BF16), ((height, z_count), BF16)],
        "ready",
    )(field, mix_weight, mix_bias[:, None], head_weight)
    prediction, grad_pre, send, hidden, head_slope = run(
        cell_kernel,
        [
            ((rows_y, z_count), F32),
            (across, BF16),
            twin_plain,
            (across, BF16),
            ((hidden_units, rows_y * z_count), BF16),
        ],
        "cell",
    )(
        own,
        to_twin(send),
        z_doubled,
        pointwise,
        head_weight,
        head_turned,
        head_bias[:, None],
        out_weight[None],
        out_weight.astype(F32)[:, None],
        cotangent[0],
    )
    if place.fold:
        outs = [((8 * partners, hidden_units), BF16)]
    else:
        outs = [((channels, channels), F32), ((channels, hidden_units), F32)]
    outs += [((wide // 2 * height, 4 * height), BF16)]
    *sums, forward = run(sums_kernel, outs, "sums")(field, grad_pre, hidden, head_slope)
    if not place.fold:
        totals = lax.psum(tuple(sums), ("wide", "narrow"))
        sums = []
    (send,) = run(fold_kernel, [shared], "fold")(send, to_twin(send), forward, *sums)
    adjoint, send = run(back_kernel, [((mode_lines, channels), F32), shared], "back")(
        exchange(send), y_forward, y_inverse, weight
    )
    some = max(1, modes // 4)
    grad_spectral, done = pl.pallas_call(
        outer_kernel,
        grid=(modes // some,),
        in_specs=[pl.BlockSpec((some, 2 * kz, channels), lambda j: (j, 0, 0))] * 2,
        out_specs=[
            pl.BlockSpec((some, kz, 2, channels, channels), lambda j: (j, 0, 0, 0, 0)),
            pl.BlockSpec((8, 128), lambda j: (0, 0)),
        ],
        out_shape=[
            jax.ShapeDtypeStruct(spectral_weight.shape, F32),
            jax.ShapeDtypeStruct((8, 128), F32),
        ],
        compiler_params=pltpu.CompilerParams(vmem_limit_bytes=VMEM_LIMIT),
        cost_estimate=pl.CostEstimate(flops=1 << 22, bytes_accessed=5 << 20, transcendentals=0),
        name="outer",
    )(spectrum.reshape(modes, 2 * kz, channels), adjoint.reshape(modes, 2 * kz, channels))
    pointwise, z_plain, turn = run(
        pointwise_kernel,
        [
            ((channels, rows_y, z_count), F32),
            ((height, z_count), BF16),
            ((cells, cells), BF16),
        ],
        "pointwise",
    )(mix_weight, grad_pre)
    outs = [own_lines, twin_shared] + ([sums_shape] if place.fold else [])
    after = (done,) if place.fold else ()
    own, send, *sums = run(part_kernel, outs, "part")(exchange(send), *after)
    outs = [((cells, z_count), BF16), ((rows_y, z_count), F32)]
    if place.fold:
        outs += [((channels, channels), F32), ((channels, hidden_units), F32)]
    grad_field, prediction, *summed = run(finish_kernel, outs, "finish")(
        own, to_twin(send), z_plain, turn, pointwise, prediction, *sums
    )
    grad_mix, grad_head = summed if place.fold else totals
    return (
        prediction[None],
        grad_field.reshape(lifted_field.shape),
        grad_spectral,
        grad_mix,
        grad_head,
    )


def solution(mesh):
    return jax.shard_map(
        body,
        mesh=mesh,
        in_specs=(
            P("wide", None, "narrow", None),
            P("wide", "narrow", None, None, None),
            P(),
            P(),
            P(),
            P(),
            P(),
            P("wide", "narrow", None),
        ),
        out_specs=(
            P("wide", "narrow", None),
            P("wide", None, "narrow", None),
            P("wide", "narrow", None, None, None),
            P(),
            P(),
        ),
        check_vma=False,
    )
```

```python
import functools
import math

import jax
import jax.numpy as jnp
import numpy as np
from jax import lax
from jax.experimental import pallas as pl
from jax.experimental.pallas import tpu as pltpu
from jax.sharding import PartitionSpec as P

MX = 16
MY = 16
MZ = 16
F32 = jnp.float32
BF16 = jnp.bfloat16
VMEM_LIMIT = 32 * 1024 * 1024
FIRST = 4

TAIL_SLOPE = 0.275
TAIL = (
    0.11780925840139389,
    0.04211147502064705,
    0.3339323103427887,
    -0.3309934139251709,
    0.4519987106323242,
    -0.11485832929611206,
)


def signed(indices, count):
    return np.where(indices < count // 2, indices, indices - count)


def wave(positions, frequency, length):
    turned = np.mod(np.multiply.outer(positions, frequency), length)
    angles = turned.astype(np.float32) * np.float32(2.0 * math.pi / length)
    scale = np.float32(1.0 / math.sqrt(length))
    return np.cos(angles) * scale, np.sin(angles) * scale


def pair(cosine, sine, sign):
    return np.stack(
        [np.stack([cosine, -sign * sine], -1), np.stack([sign * sine, cosine], -1)], -2
    )


def y_tables(total_y, rows_y, kz, modes):
    cosine, sine = wave(np.arange(total_y), signed(np.arange(MY), MY), total_y)
    narrow = total_y // rows_y
    same = np.eye(kz, dtype=np.float32)
    forward = pair(cosine, sine, -1.0).reshape(narrow, rows_y, MY // modes, modes, 2, 2)
    inverse = pair(cosine, sine, 1.0).reshape(narrow, rows_y, MY // modes, modes, 2, 2)
    forward = np.einsum("nybjtr,kl->bjtkynlr", forward, same)
    inverse = np.einsum("nybjst,kl->bnyksjtl", inverse, same)
    blocks = MY // modes
    forward = forward.reshape(blocks, modes * 2 * kz, rows_y * narrow * kz * 2)
    inverse = inverse.reshape(blocks, narrow * rows_y * kz * 2, modes * 2 * kz)
    return forward.astype(BF16), inverse.astype(BF16)


def dot(a, b):
    return jnp.dot(a, b, preferred_element_type=F32)


def dot_nt(a, b):
    return lax.dot_general(a, b, (((1,), (1,)), ((), ())), preferred_element_type=F32)


def dot_tn(a, b):
    return lax.dot_general(a, b, (((0,), (0,)), ((), ())), preferred_element_type=F32)


def grid_of(rows, columns):
    shape = (rows, columns)
    return lax.broadcasted_iota(jnp.int32, shape, 0), lax.broadcasted_iota(jnp.int32, shape, 1)


def selector(rows, columns, condition):
    return jnp.where(condition(*grid_of(rows, columns)), 1.0, 0.0).astype(BF16)


def halves(values):
    high = values.astype(BF16)
    return high, (values - high.astype(F32)).astype(BF16)


def stacked(refs, lanes=slice(None)):
    return jnp.concatenate([ref[:, lanes] for ref in refs], axis=0)


def cosine_of(phase, length):
    angles = (phase & (length - 1)).astype(F32) * (2.0 * math.pi / length)
    return jnp.cos(angles) * (1.0 / math.sqrt(length))


class Place:
    def __init__(self, wide, narrow, kz, modes, rows_y, channels, z_count, fold):
        self.wide, self.narrow, self.kz, self.modes = wide, narrow, kz, modes
        self.rows_y, self.channels, self.z_count, self.fold = rows_y, channels, z_count, fold
        self.outer = wide // 2
        self.partners = self.outer * narrow
        self.lanes = rows_y * channels

    def here(self):
        wide = lax.axis_index("wide")
        return wide // 2, wide % 2

    def frequency(self, wide):
        index = (wide * self.modes) // MY
        return jnp.where(index < MX // 2, index, index - MX)

    def z_table(self, doubled):
        row, z = grid_of(2 * MZ, self.z_count)
        frequency = row >> 1
        value = cosine_of(z * frequency + (row & 1) * (self.z_count // 4), self.z_count)
        if doubled:
            value = jnp.where(frequency > 0, 2.0 * value, value)
        return value.astype(BF16)

    def expanded(self, small):
        row, column = grid_of(2 * MZ, small.shape[1])
        same = (row >> 1) == ((column >> 1) & (MZ - 1))
        blocks = []
        for g in range(small.shape[0] // 2):
            value = jnp.where((row & 1) == 0, small[2 * g : 2 * g + 1], small[2 * g + 1 : 2 * g + 2])
            blocks.append(jnp.where(same, value, 0.0))
        return jnp.concatenate(blocks, axis=0)

    def forward_x(self):
        outer, inner = self.here()
        row, column = grid_of(2 * self.outer, 4 * MZ)
        x = 2 * outer + (inner ^ (column // (2 * MZ)))
        frequency = self.frequency(2 * ((row >> 1) ^ FIRST) + inner)
        quarter = self.wide // 4
        small = cosine_of(x * frequency + quarter * ((row & 1) - (column & 1)), self.wide)
        return self.expanded(small)

    def inverse_x(self):
        outer, inner = self.here()
        row, column = grid_of(4, self.outer * 2 * MZ)
        x = 2 * outer + (inner ^ (row >> 1))
        frequency = self.frequency(2 * ((column // (2 * MZ)) ^ FIRST) + inner)
        quarter = self.wide // 4
        small = cosine_of(x * frequency + quarter * ((column & 1) - (row & 1)), self.wide)
        return self.expanded(small).astype(BF16)


def repeat_rows(out_ref, block):
    height = block.shape[0]
    for first in range(0, out_ref.shape[0], height):
        out_ref[first : first + height] = block


def write_pieces(place, send_ref, block, shares):
    step, half = 2 * place.kz, place.lanes // 2
    height = send_ref.shape[0] // place.partners
    for p in range(place.partners):
        own = block[p * step % block.shape[0] :][:step]
        first = p * height
        send_ref[first : first + step] = own[:, :half]
        send_ref[first + step : first + 2 * step] = own[:, half:]
        send_ref[first + 2 * step : first + height] = shares[p * 8 % shares.shape[0] :][:8]


def read_pieces(place, pieces_ref):
    step = 2 * place.kz
    if pieces_ref.shape[1] == place.lanes:
        return pieces_ref[...], None
    height = pieces_ref.shape[0] // place.partners
    blocks, shares = [], []
    for p in range(place.partners):
        first = p * height
        left = pieces_ref[first : first + step]
        right = pieces_ref[first + step : first + 2 * step]
        blocks.append(jnp.concatenate([left, right], axis=1))
        shares.append(pieces_ref[first + 2 * step : first + height].astype(F32))
    return jnp.concatenate(blocks, axis=0), shares


def analysed(place, pieces, y_forward, copies):
    height = 2 * MZ
    turned = sum(
        pieces[first : first + height].astype(F32) for first in range(0, pieces.shape[0], height)
    )
    channels = place.channels
    lines = jnp.concatenate(
        [turned[:, y * channels : (y + 1) * channels] for y in range(place.rows_y)], axis=0
    )
    return dot(y_forward, jnp.concatenate([lines.astype(BF16)] * copies, axis=1))


def spread_lines(place, modes, y_inverse):
    lines = dot(y_inverse, modes)
    step = 2 * place.kz
    blocks = []
    for n in range(place.narrow):
        first = n * place.rows_y
        parts = [lines[(first + y) * step : (first + y + 1) * step] for y in range(place.rows_y)]
        blocks.append(jnp.concatenate(parts, axis=1))
    return jnp.concatenate(blocks, axis=0).astype(BF16)


def turn_matrix(place, forward):
    channels, rows_y = place.channels, place.rows_y

    def same(row, column):
        if forward:
            row, column = column, row
        return (row % channels == column // rows_y) & (row // channels == column % rows_y)

    return selector(place.lanes, place.lanes, same)


def side_by_side(values, count):
    height = values.shape[0] // count
    return jnp.concatenate([values[y * height : (y + 1) * height] for y in range(count)], axis=1)


def one_below_other(values, count):
    width = values.shape[1] // count
    return jnp.concatenate([values[:, y * width : (y + 1) * width] for y in range(count)], axis=0)


def own_kernel(place, field_ref, field_out_ref, spectra_ref):
    turned = dot(turn_matrix(place, False), field_ref[...]).astype(BF16)
    field_out_ref[...] = side_by_side(turned, place.rows_y)
    spectra_ref[...] = dot_nt(place.z_table(False), turned).astype(BF16)


def start_kernel(place, spectra_ref, twin_ref, send_ref):
    twin = dot_nt(place.z_table(False), twin_ref[...]).astype(BF16)
    twin = dot(twin, turn_matrix(place, True)).astype(BF16)
    values = jnp.concatenate([spectra_ref[...], twin], axis=0)
    tables = jnp.concatenate(halves(place.forward_x()), axis=1)
    send_ref[...] = dot(tables, jnp.concatenate([values, values], axis=0)).astype(BF16)


def pack_kernel(weight_ref, packed_ref):
    modes, kz, _, channels, _ = weight_ref.shape
    for q in range(modes // 4):
        parts = [weight_ref[4 * q + j // 2, :, j % 2] for j in range(8)]
        packed = jnp.concatenate(parts, axis=-1).reshape(kz * channels, 8 * channels)
        packed_ref[q] = packed.astype(BF16)


def ready_kernel(place, field_ref, mix_ref, mix_bias_ref, head_ref, *refs):
    pointwise_ref, head_out_ref, z_doubled_ref = refs
    pointwise_ref[...] = dot_tn(mix_ref[...], field_ref[...]) + mix_bias_ref[...]
    head_out_ref[...] = jnp.transpose(head_ref[...].astype(F32)).astype(BF16)
    z_doubled_ref[...] = place.z_table(True)


def fold_kernel(place, own_ref, got_ref, tables_ref, *refs):
    values = jnp.concatenate([own_ref[...], got_ref[...]], axis=0)
    values = jnp.concatenate([values, values], axis=0)
    partial = dot(tables_ref[...], values).astype(BF16)
    if place.fold:
        shares_ref, send_ref = refs
        write_pieces(place, send_ref, partial, shares_ref[...])
    else:
        refs[0][...] = partial


def mode_kernel(
    place, pieces_ref, y_forward_ref, y_inverse_ref, weight_ref, spectrum_ref, send_ref
):
    kz, channels = place.kz, place.channels
    spectrum = analysed(place, pieces_ref[...], y_forward_ref[...], kz)
    spectrum_ref[...] = spectrum[:, :channels]
    row, lane = grid_of(*spectrum.shape)
    blocked = jnp.where(row % kz == lane // channels, spectrum, 0.0)
    mixed = []
    for q in range(place.modes // 4):
        left = blocked[q * 8 * kz : (q + 1) * 8 * kz].astype(BF16)
        product = dot(left, weight_ref[q])
        for j in range(4):
            own = product[j * 2 * kz : (j + 1) * 2 * kz, j * 2 * channels : (j + 1) * 2 * channels]
            real, imag = own[:, :channels], own[:, channels:]
            mixed.append(real[:kz] - imag[kz:])
            mixed.append(imag[:kz] + real[kz:])
    mode = jnp.concatenate(mixed, axis=0).astype(BF16)
    repeat_rows(send_ref, spread_lines(place, mode, y_inverse_ref[...]))


def part_kernel(place, pieces_ref, *refs):
    pieces, shares = read_pieces(place, pieces_ref)
    lines = dot(place.inverse_x(), pieces)
    height = 2 * MZ
    if shares is None:
        own_ref, send_ref = refs
        own_ref[...] = lines[:height]
        send_ref[...] = lines[height:].astype(BF16)
        return
    _, own_ref, send_ref, sums_ref = refs
    own_ref[...] = lines[:height]
    send_ref[:height] = lines[height:].astype(BF16)
    got = jnp.concatenate(shares, axis=0).astype(BF16)
    channels = place.channels

    def chosen(part):
        return dot(
            selector(
                2 * channels,
                got.shape[0],
                lambda row, column: (column // 8 == (row % channels) // 2)
                & (column % 8 == 4 * part + 2 * (row // channels) + row % 2),
            ),
            got,
        )

    high, low = chosen(0), chosen(1)
    sums_ref[...] = high + low
    send_ref[height:] = jnp.concatenate([high, low], axis=1).astype(BF16)


def normal(values):
    scaled = 1.0 / (1.0 + TAIL_SLOPE * jnp.abs(values))
    decay = jnp.exp(-0.5 * values * values)
    tail = TAIL[-1]
    for factor in TAIL[-2::-1]:
        tail = tail * scaled + factor
    tail = tail * (scaled * decay)
    cumulative = jnp.where(values > 0.0, 1.0 - tail, tail)
    return values * cumulative, cumulative + values * (decay * (1.0 / math.sqrt(2.0 * math.pi)))


def cell_kernel(place, *refs):
    own_ref, got_ref, z_table_ref, pointwise_ref, head_ref, head_turned_ref = refs[:6]
    head_bias_ref, out_row_ref, out_column_ref, cotangent_ref = refs[6:10]
    prediction_ref, grad_pre_ref, send_ref, hidden_ref, head_slope_ref = refs[10:]
    rows_y, z_count = place.rows_y, place.z_count
    z_table = z_table_ref[...]
    lines = (own_ref[...] + got_ref[...].astype(F32)).astype(BF16)
    pre_act = side_by_side(dot_tn(lines, z_table), rows_y) + pointwise_ref[...]
    head, head_turned = head_ref[...], head_turned_ref[...]
    head_bias, out_row, out_column = head_bias_ref[...], out_row_ref[...], out_column_ref[...]
    width = 2 * z_count
    slopes, head_pre = [], []
    for first in range(0, rows_y * z_count, width):
        value, slope = normal(pre_act[:, first : first + width])
        hidden = value.astype(BF16)
        hidden_ref[:, first : first + width] = hidden
        slopes.append(slope)
        head_pre.append(dot(head_turned, hidden))
    gradients = []
    for index, first in enumerate(range(0, rows_y, 2)):
        target = jnp.concatenate(
            [cotangent_ref[y : y + 1] for y in range(first, first + 2)], axis=1
        )
        active, slope = normal(head_pre[index] + head_bias)
        predicted = dot(out_row, active.astype(BF16))
        prediction_ref[first : first + 1] = predicted[:, :z_count]
        prediction_ref[first + 1 : first + 2] = predicted[:, z_count:]
        head_slope = (target * out_column * slope).astype(BF16)
        head_slope_ref[:, first * z_count : first * z_count + width] = head_slope
        gradients.append((dot(head, head_slope) * slopes[index]).astype(BF16))
    gradient = jnp.concatenate(gradients, axis=1)
    grad_pre_ref[...] = gradient
    send_ref[...] = dot_nt(z_table, one_below_other(gradient, rows_y)).astype(BF16)


def sums_kernel(place, field_ref, gradient_ref, hidden_ref, head_slope_ref, *refs):
    refs[-1][...] = jnp.concatenate(halves(place.forward_x()), axis=1)
    grad_mix = dot_nt(field_ref[...], gradient_ref[...])
    grad_head = dot_nt(hidden_ref[...], head_slope_ref[...])
    if not place.fold:
        refs[0][...] = grad_mix
        refs[1][...] = grad_head
        return
    channels, hidden_units = grad_head.shape
    rest = jnp.zeros((channels, hidden_units - channels), F32)
    wide_mix = jnp.concatenate([grad_mix, rest], axis=1)
    high, low = halves(jnp.concatenate([grad_head, wide_mix], axis=0))
    split = jnp.concatenate([high, low], axis=0)
    place_of = selector(
        8 * place.partners,
        4 * channels,
        lambda row, column: (column % channels == 2 * (row // 8) + row % 2)
        & (column // channels == (row % 8) // 2),
    )
    refs[0][...] = dot(place_of, split).astype(BF16)


def back_kernel(
    place, pieces_ref, y_forward_ref, y_inverse_ref, weight_ref, adjoint_ref, send_ref
):
    kz, channels = place.kz, place.channels
    pieces, shares = read_pieces(place, pieces_ref)
    adjoint = analysed(place, pieces, y_forward_ref[...], 1)
    adjoint_ref[...] = adjoint
    turned = []
    for first in range(0, adjoint.shape[0], 2 * kz):
        turned += [adjoint[first + kz : first + 2 * kz], -adjoint[first : first + kz]]
    left = jnp.concatenate([adjoint, jnp.concatenate(turned, axis=0)], axis=1)
    left = jnp.concatenate([left] * 4, axis=1)
    row, lane = grid_of(*left.shape)
    same = (row // (2 * kz)) % 4 == lane // (2 * channels)
    left = jnp.where(same, left, 0.0).astype(BF16)
    block = 8 * kz
    pulled = [
        dot_nt(left[q * block : (q + 1) * block], weight_ref[q]) for q in range(place.modes // 4)
    ]
    pulled = jnp.concatenate(pulled, axis=0)
    row, lane = grid_of(*pulled.shape)
    pulled = jnp.where(row % kz == lane // channels, pulled, 0.0).astype(BF16)
    gather = selector(
        kz * channels, channels, lambda row, column: row % channels == column
    )
    modes_back = dot(pulled, gather).astype(BF16)
    block = spread_lines(place, modes_back, y_inverse_ref[...])
    if shares is None:
        repeat_rows(send_ref, block)
        return
    total = sum(shares[1:], shares[0])
    high, low = halves(total[0:4] + total[4:8])
    split = jnp.concatenate([high.astype(F32), low.astype(F32)], axis=0)
    write_pieces(place, send_ref, block, split.astype(BF16))


def outer_kernel(spectrum_ref, adjoint_ref, out_ref, done_ref):
    done_ref[...] = jnp.zeros(done_ref.shape, F32)
    modes, kz = out_ref.shape[:2]
    for j in range(modes):
        columns = jnp.transpose(spectrum_ref[j])
        adjoint = adjoint_ref[j]
        for k in range(kz):
            s_real, s_imag = columns[:, k : k + 1], columns[:, kz + k : kz + k + 1]
            a_real, a_imag = adjoint[k : k + 1], adjoint[kz + k : kz + k + 1]
            out_ref[j, k, 0] = s_real * a_real + s_imag * a_imag
            out_ref[j, k, 1] = s_real * a_imag - s_imag * a_real


def pointwise_kernel(place, mix_ref, gradient_ref, out_ref, z_plain_ref, turn_ref):
    z_plain_ref[...] = place.z_table(False)
    turn_ref[...] = turn_matrix(place, False)
    z_count = place.z_count
    product = dot(mix_ref[...], gradient_ref[...])
    for y in range(place.rows_y):
        out_ref[:, y, :] = product[:, y * z_count : (y + 1) * z_count]


def finish_kernel(place, *refs):
    own_ref, got_ref, z_table_ref, turn_ref, pointwise_ref, prediction_ref = refs[:6]
    refs = refs[6:]
    height = 2 * MZ
    channels = place.channels
    lines = (own_ref[...] + got_ref[:height].astype(F32)).astype(BF16)
    lines = dot(lines, turn_ref[...]).astype(BF16)
    pointwise = pointwise_ref[...].reshape(place.lanes, place.z_count)
    grad_field = (dot_tn(lines, z_table_ref[...]) + pointwise).astype(BF16)
    if not place.fold:
        refs[0][...] = grad_field
        refs[1][...] = prediction_ref[...]
        return
    sums_ref, grad_field_ref, out_ref, grad_mix_ref, grad_head_ref = refs
    grad_field_ref[...] = grad_field
    out_ref[...] = prediction_ref[...]
    got = got_ref[height:].astype(F32)
    width = sums_ref.shape[1]
    total = sums_ref[...] + got[:, :width] + got[:, width:]
    grad_head_ref[...] = total[:channels]
    grad_mix_ref[...] = total[channels:, :channels]


def call(kernel, outs, name, **spec):
    return pl.pallas_call(
        kernel,
        out_shape=[jax.ShapeDtypeStruct(shape, dtype) for shape, dtype in outs],
        compiler_params=pltpu.CompilerParams(vmem_limit_bytes=VMEM_LIMIT),
        cost_estimate=pl.CostEstimate(flops=1 << 22, bytes_accessed=1 << 19, transcendentals=0),
        name=name,
        **spec,
    )


def body(
    lifted_field,
    spectral_weight,
    mix_weight,
    mix_bias,
    head_weight,
    head_bias,
    out_weight,
    cotangent,
):
    wide = lax.axis_size("wide")
    narrow = lax.axis_size("narrow")
    devices = wide * narrow
    _, channels, rows_y, z_count = lifted_field.shape
    modes, kz = spectral_weight.shape[:2]
    hidden_units = head_weight.shape[1]
    cells = channels * rows_y
    place = Place(wide, narrow, kz, modes, rows_y, channels, z_count, False)
    place.fold = 2 * place.partners == channels and hidden_units == 128 and cells == 256 and kz % 8 == 0
    height = 2 * MZ
    step = 2 * kz
    partners = place.partners
    mode_lines = modes * 2 * kz

    y_forward, y_inverse = y_tables(rows_y * narrow, rows_y, kz, modes)
    if len(y_forward) > 1:
        block = lax.axis_index("wide") % len(y_forward)
        y_forward = lax.dynamic_index_in_dim(jnp.asarray(y_forward), block, 0, False)
        y_inverse = lax.dynamic_index_in_dim(jnp.asarray(y_inverse), block, 0, False)
    else:
        y_forward, y_inverse = jnp.asarray(y_forward[0]), jnp.asarray(y_inverse[0])

    def to_twin(send):
        pairs = [(p, p ^ narrow) for p in range(devices)]
        return lax.ppermute(send, ("wide", "narrow"), pairs)

    groups = [
        [
            (2 * (outer ^ FIRST) + inner) * narrow + n
            for outer in range(wide // 2)
            for n in range(narrow)
        ]
        for inner in range(2)
    ]

    def exchange(send):
        pieces = send.reshape(partners, -1, send.shape[1])
        got = lax.all_to_all(
            pieces, ("wide", "narrow"), 0, 0, axis_index_groups=groups, tiled=True
        )
        return got.reshape(send.shape)

    plain = ((partners * step, cells), BF16)
    shared = ((partners * (2 * step + 8), cells // 2), BF16) if place.fold else plain
    twin_plain = ((height, cells), BF16)
    twin_shared = ((height + 2 * channels, cells), BF16) if place.fold else twin_plain
    sums_shape = ((2 * channels, hidden_units), F32)
    own_lines = ((height, cells), F32)
    across = (channels, rows_y * z_count)

    def run(kernel, outs, name, **spec):
        return call(functools.partial(kernel, place), outs, name, **spec)

    flat_field = lifted_field.reshape(cells, z_count)
    twin_field = to_twin(flat_field)
    field, spectra = run(own_kernel, [(across, BF16), twin_plain], "own")(flat_field)
    (send,) = run(start_kernel, [plain], "start")(spectra, twin_field)
    packed_shape = ((modes // 4, kz * channels, 8 * channels), BF16)
    (weight,) = call(pack_kernel, [packed_shape], "pack")(spectral_weight)
    spectrum, send = run(mode_kernel, [((mode_lines, channels), F32), plain], "mode")(
        exchange(send), y_forward, y_inverse, weight
    )
    own, send = run(part_kernel, [own_lines, twin_plain], "part")(exchange(send))
    pointwise, head_turned, z_doubled = run(
        ready_kernel,
        [(across, F32), ((hidden_units, channels), BF16), ((height, z_count), BF16)],
        "ready",
    )(field, mix_weight, mix_bias[:, None], head_weight)
    prediction, grad_pre, send, hidden, head_slope = run(
        cell_kernel,
        [
            ((rows_y, z_count), F32),
            (across, BF16),
            twin_plain,
            (across, BF16),
            ((hidden_units, rows_y * z_count), BF16),
        ],
        "cell",
    )(
        own,
        to_twin(send),
        z_doubled,
        pointwise,
        head_weight,
        head_turned,
        head_bias[:, None],
        out_weight[None],
        out_weight.astype(F32)[:, None],
        cotangent[0],
    )
    if place.fold:
        outs = [((8 * partners, hidden_units), BF16)]
    else:
        outs = [((channels, channels), F32), ((channels, hidden_units), F32)]
    outs += [((wide // 2 * height, 4 * height), BF16)]
    *sums, forward = run(sums_kernel, outs, "sums")(field, grad_pre, hidden, head_slope)
    if not place.fold:
        totals = lax.psum(tuple(sums), ("wide", "narrow"))
        sums = []
    (send,) = run(fold_kernel, [shared], "fold")(send, to_twin(send), forward, *sums)
    adjoint, send = run(back_kernel, [((mode_lines, channels), F32), shared], "back")(
        exchange(send), y_forward, y_inverse, weight
    )
    some = max(1, modes // 4)
    grad_spectral, done = pl.pallas_call(
        outer_kernel,
        grid=(modes // some,),
        in_specs=[pl.BlockSpec((some, 2 * kz, channels), lambda j: (j, 0, 0))] * 2,
        out_specs=[
            pl.BlockSpec((some, kz, 2, channels, channels), lambda j: (j, 0, 0, 0, 0)),
            pl.BlockSpec((8, 128), lambda j: (0, 0)),
        ],
        out_shape=[
            jax.ShapeDtypeStruct(spectral_weight.shape, F32),
            jax.ShapeDtypeStruct((8, 128), F32),
        ],
        compiler_params=pltpu.CompilerParams(vmem_limit_bytes=VMEM_LIMIT),
        cost_estimate=pl.CostEstimate(flops=1 << 22, bytes_accessed=5 << 20, transcendentals=0),
        name="outer",
    )(spectrum.reshape(modes, 2 * kz, channels), adjoint.reshape(modes, 2 * kz, channels))
    pointwise, z_plain, turn = run(
        pointwise_kernel,
        [
            ((channels, rows_y, z_count), F32),
            ((height, z_count), BF16),
            ((cells, cells), BF16),
        ],
        "pointwise",
    )(mix_weight, grad_pre)
    outs = [own_lines, twin_shared] + ([sums_shape] if place.fold else [])
    after = (done,) if place.fold else ()
    own, send, *sums = run(part_kernel, outs, "part")(exchange(send), *after)
    outs = [((cells, z_count), BF16), ((rows_y, z_count), F32)]
    if place.fold:
        outs += [((channels, channels), F32), ((channels, hidden_units), F32)]
    grad_field, prediction, *summed = run(finish_kernel, outs, "finish")(
        own, to_twin(send), z_plain, turn, pointwise, prediction, *sums
    )
    grad_mix, grad_head = summed if place.fold else totals
    return (
        prediction[None],
        grad_field.reshape(lifted_field.shape),
        grad_spectral,
        grad_mix,
        grad_head,
    )


def solution(mesh):
    return jax.shard_map(
        body,
        mesh=mesh,
        in_specs=(
            P("wide", None, "narrow", None),
            P("wide", "narrow", None, None, None),
            P(),
            P(),
            P(),
            P(),
            P(),
            P("wide", "narrow", None),
        ),
        out_specs=(
            P("wide", "narrow", None),
            P("wide", None, "narrow", None),
            P("wide", "narrow", None, None, None),
            P(),
            P(),
        ),
        check_vma=False,
    )
```

```python
import functools
import math

import jax
import jax.numpy as jnp
import numpy as np
from jax import lax
from jax.experimental import pallas as pl
from jax.experimental.pallas import tpu as pltpu
from jax.sharding import PartitionSpec as P

MX = 16
MY = 16
MZ = 16
F32 = jnp.float32
BF16 = jnp.bfloat16
VMEM_LIMIT = 32 * 1024 * 1024

TAIL_SLOPE = 0.275
TAIL = (
    0.11780925840139389,
    0.04211147502064705,
    0.3339323103427887,
    -0.3309934139251709,
    0.4519987106323242,
    -0.11485832929611206,
)


def signed(indices, count):
    return np.where(indices < count // 2, indices, indices - count)


def wave(positions, frequency, length):
    turned = np.mod(np.multiply.outer(positions, frequency), length)
    angles = turned.astype(np.float32) * np.float32(2.0 * math.pi / length)
    scale = np.float32(1.0 / math.sqrt(length))
    return np.cos(angles) * scale, np.sin(angles) * scale


def pair(cosine, sine, sign):
    return np.stack(
        [np.stack([cosine, -sign * sine], -1), np.stack([sign * sine, cosine], -1)], -2
    )


def y_tables(total_y, rows_y, kz, modes):
    cosine, sine = wave(np.arange(total_y), signed(np.arange(MY), MY), total_y)
    narrow = total_y // rows_y
    same = np.eye(kz, dtype=np.float32)
    forward = pair(cosine, sine, -1.0).reshape(narrow, rows_y, MY // modes, modes, 2, 2)
    inverse = pair(cosine, sine, 1.0).reshape(narrow, rows_y, MY // modes, modes, 2, 2)
    forward = np.einsum("nybjtr,kl->bjtkynlr", forward, same)
    inverse = np.einsum("nybjst,kl->bnyksjtl", inverse, same)
    blocks = MY // modes
    forward = forward.reshape(blocks, modes * 2 * kz, rows_y * narrow * kz * 2)
    inverse = inverse.reshape(blocks, narrow * rows_y * kz * 2, modes * 2 * kz)
    return forward.astype(BF16), inverse.astype(BF16)


def dot(a, b):
    return jnp.dot(a, b, preferred_element_type=F32)


def dot_nt(a, b):
    return lax.dot_general(a, b, (((1,), (1,)), ((), ())), preferred_element_type=F32)


def dot_tn(a, b):
    return lax.dot_general(a, b, (((0,), (0,)), ((), ())), preferred_element_type=F32)


def grid_of(rows, columns):
    shape = (rows, columns)
    return lax.broadcasted_iota(jnp.int32, shape, 0), lax.broadcasted_iota(jnp.int32, shape, 1)


def selector(rows, columns, condition):
    return jnp.where(condition(*grid_of(rows, columns)), 1.0, 0.0).astype(BF16)


def halves(values):
    high = values.astype(BF16)
    return high, (values - high.astype(F32)).astype(BF16)


def stacked(refs, lanes=slice(None)):
    return jnp.concatenate([ref[:, lanes] for ref in refs], axis=0)


def cosine_of(phase, length):
    angles = (phase & (length - 1)).astype(F32) * (2.0 * math.pi / length)
    return jnp.cos(angles) * (1.0 / math.sqrt(length))


class Place:
    def __init__(self, wide, narrow, kz, modes, rows_y, channels, z_count, fold):
        self.wide, self.narrow, self.kz, self.modes = wide, narrow, kz, modes
        self.rows_y, self.channels, self.z_count, self.fold = rows_y, channels, z_count, fold
        self.outer = wide // 2
        self.partners = self.outer * narrow
        self.lanes = rows_y * channels

    def here(self):
        wide = lax.axis_index("wide")
        return wide // 2, wide % 2

    def listed(self, position):
        lines = self.outer // 2
        return ((lines // 2 - position // 2) & (lines - 1)) * 2 + position % 2

    def frequency(self, wide):
        index = (wide * self.modes) // MY
        return jnp.where(index < MX // 2, index, index - MX)

    def z_table(self, doubled):
        row, z = grid_of(2 * MZ, self.z_count)
        frequency = row >> 1
        value = cosine_of(z * frequency + (row & 1) * (self.z_count // 4), self.z_count)
        if doubled:
            value = jnp.where(frequency > 0, 2.0 * value, value)
        return value.astype(BF16)

    def expanded(self, small):
        row, column = grid_of(2 * MZ, small.shape[1])
        same = (row >> 1) == ((column >> 1) & (MZ - 1))
        blocks = []
        for g in range(small.shape[0] // 2):
            value = jnp.where((row & 1) == 0, small[2 * g : 2 * g + 1], small[2 * g + 1 : 2 * g + 2])
            blocks.append(jnp.where(same, value, 0.0))
        return jnp.concatenate(blocks, axis=0)

    def forward_x(self):
        outer, inner = self.here()
        row, column = grid_of(2 * self.outer, 4 * MZ)
        x = 2 * outer + (inner ^ (column // (2 * MZ)))
        frequency = self.frequency(2 * self.listed(row >> 1) + inner)
        quarter = self.wide // 4
        small = cosine_of(x * frequency + quarter * ((row & 1) - (column & 1)), self.wide)
        return self.expanded(small)

    def inverse_x(self):
        outer, inner = self.here()
        row, column = grid_of(4, self.outer * 2 * MZ)
        x = 2 * outer + (inner ^ (row >> 1))
        frequency = self.frequency(2 * self.listed(column // (2 * MZ)) + inner)
        quarter = self.wide // 4
        small = cosine_of(x * frequency + quarter * ((column & 1) - (row & 1)), self.wide)
        return self.expanded(small).astype(BF16)


def repeat_rows(out_ref, block):
    height = block.shape[0]
    for first in range(0, out_ref.shape[0], height):
        out_ref[first : first + height] = block


def write_pieces(place, send_ref, block, shares):
    step, half = 2 * place.kz, place.lanes // 2
    height = send_ref.shape[0] // place.partners
    for p in range(place.partners):
        own = block[p * step % block.shape[0] :][:step]
        first = p * height
        send_ref[first : first + step] = own[:, :half]
        send_ref[first + step : first + 2 * step] = own[:, half:]
        send_ref[first + 2 * step : first + height] = shares[p * 8 % shares.shape[0] :][:8]


def read_pieces(place, pieces_ref):
    step = 2 * place.kz
    if pieces_ref.shape[1] == place.lanes:
        return pieces_ref[...], None
    height = pieces_ref.shape[0] // place.partners
    blocks, shares = [], []
    for p in range(place.partners):
        first = p * height
        left = pieces_ref[first : first + step]
        right = pieces_ref[first + step : first + 2 * step]
        blocks.append(jnp.concatenate([left, right], axis=1))
        shares.append(pieces_ref[first + 2 * step : first + height].astype(F32))
    return jnp.concatenate(blocks, axis=0), shares


def analysed(place, pieces, y_forward, copies):
    height = 2 * MZ
    turned = sum(
        pieces[first : first + height].astype(F32) for first in range(0, pieces.shape[0], height)
    )
    channels = place.channels
    lines = jnp.concatenate(
        [turned[:, y * channels : (y + 1) * channels] for y in range(place.rows_y)], axis=0
    )
    return dot(y_forward, jnp.concatenate([lines.astype(BF16)] * copies, axis=1))


def spread_lines(place, modes, y_inverse):
    lines = dot(y_inverse, modes)
    step = 2 * place.kz
    blocks = []
    for n in range(place.narrow):
        first = n * place.rows_y
        parts = [lines[(first + y) * step : (first + y + 1) * step] for y in range(place.rows_y)]
        blocks.append(jnp.concatenate(parts, axis=1))
    return jnp.concatenate(blocks, axis=0).astype(BF16)


def turn_matrix(place, forward):
    channels, rows_y = place.channels, place.rows_y

    def same(row, column):
        if forward:
            row, column = column, row
        return (row % channels == column // rows_y) & (row // channels == column % rows_y)

    return selector(place.lanes, place.lanes, same)


def side_by_side(values, count):
    height = values.shape[0] // count
    return jnp.concatenate([values[y * height : (y + 1) * height] for y in range(count)], axis=1)


def one_below_other(values, count):
    width = values.shape[1] // count
    return jnp.concatenate([values[:, y * width : (y + 1) * width] for y in range(count)], axis=0)


def own_kernel(place, field_ref, field_out_ref, spectra_ref):
    turned = dot(turn_matrix(place, False), field_ref[...]).astype(BF16)
    field_out_ref[...] = side_by_side(turned, place.rows_y)
    spectra_ref[...] = dot_nt(place.z_table(False), turned).astype(BF16)


def start_kernel(place, spectra_ref, twin_ref, send_ref):
    twin = dot_nt(place.z_table(False), twin_ref[...]).astype(BF16)
    twin = dot(twin, turn_matrix(place, True)).astype(BF16)
    values = jnp.concatenate([spectra_ref[...], twin], axis=0)
    tables = jnp.concatenate(halves(place.forward_x()), axis=1)
    send_ref[...] = dot(tables, jnp.concatenate([values, values], axis=0)).astype(BF16)


def pack_kernel(weight_ref, packed_ref):
    modes, kz, _, channels, _ = weight_ref.shape
    for q in range(modes // 4):
        parts = [weight_ref[4 * q + j // 2, :, j % 2] for j in range(8)]
        packed = jnp.concatenate(parts, axis=-1).reshape(kz * channels, 8 * channels)
        packed_ref[q] = packed.astype(BF16)


def ready_kernel(place, field_ref, mix_ref, mix_bias_ref, head_ref, *refs):
    pointwise_ref, head_out_ref, z_doubled_ref = refs
    pointwise_ref[...] = dot_tn(mix_ref[...], field_ref[...]) + mix_bias_ref[...]
    head_out_ref[...] = jnp.transpose(head_ref[...].astype(F32)).astype(BF16)
    z_doubled_ref[...] = place.z_table(True)


def fold_kernel(place, own_ref, got_ref, tables_ref, *refs):
    values = jnp.concatenate([own_ref[...], got_ref[...]], axis=0)
    values = jnp.concatenate([values, values], axis=0)
    partial = dot(tables_ref[...], values).astype(BF16)
    if place.fold:
        shares_ref, send_ref = refs
        write_pieces(place, send_ref, partial, shares_ref[...])
    else:
        refs[0][...] = partial


def mode_kernel(
    place, pieces_ref, y_forward_ref, y_inverse_ref, weight_ref, spectrum_ref, send_ref
):
    kz, channels = place.kz, place.channels
    spectrum = analysed(place, pieces_ref[...], y_forward_ref[...], kz)
    spectrum_ref[...] = spectrum[:, :channels]
    row, lane = grid_of(*spectrum.shape)
    blocked = jnp.where(row % kz == lane // channels, spectrum, 0.0)
    mixed = []
    for q in range(place.modes // 4):
        left = blocked[q * 8 * kz : (q + 1) * 8 * kz].astype(BF16)
        product = dot(left, weight_ref[q])
        for j in range(4):
            own = product[j * 2 * kz : (j + 1) * 2 * kz, j * 2 * channels : (j + 1) * 2 * channels]
            real, imag = own[:, :channels], own[:, channels:]
            mixed.append(real[:kz] - imag[kz:])
            mixed.append(imag[:kz] + real[kz:])
    mode = jnp.concatenate(mixed, axis=0).astype(BF16)
    repeat_rows(send_ref, spread_lines(place, mode, y_inverse_ref[...]))


def part_kernel(place, pieces_ref, *refs):
    pieces, shares = read_pieces(place, pieces_ref)
    lines = dot(place.inverse_x(), pieces)
    height = 2 * MZ
    if shares is None:
        own_ref, send_ref = refs
        own_ref[...] = lines[:height]
        send_ref[...] = lines[height:].astype(BF16)
        return
    _, own_ref, send_ref, sums_ref = refs
    own_ref[...] = lines[:height]
    send_ref[:height] = lines[height:].astype(BF16)
    got = jnp.concatenate(shares, axis=0).astype(BF16)
    channels = place.channels

    def chosen(part):
        return dot(
            selector(
                2 * channels,
                got.shape[0],
                lambda row, column: (column // 8 == (row % channels) // 2)
                & (column % 8 == 4 * part + 2 * (row // channels) + row % 2),
            ),
            got,
        )

    high, low = chosen(0), chosen(1)
    sums_ref[...] = high + low
    send_ref[height:] = jnp.concatenate([high, low], axis=1).astype(BF16)


def normal(values):
    scaled = 1.0 / (1.0 + TAIL_SLOPE * jnp.abs(values))
    decay = jnp.exp(-0.5 * values * values)
    tail = TAIL[-1]
    for factor in TAIL[-2::-1]:
        tail = tail * scaled + factor
    tail = tail * (scaled * decay)
    cumulative = jnp.where(values > 0.0, 1.0 - tail, tail)
    return values * cumulative, cumulative + values * (decay * (1.0 / math.sqrt(2.0 * math.pi)))


def cell_kernel(place, *refs):
    own_ref, got_ref, z_table_ref, pointwise_ref, head_ref, head_turned_ref = refs[:6]
    head_bias_ref, out_row_ref, out_column_ref, cotangent_ref = refs[6:10]
    prediction_ref, grad_pre_ref, send_ref, hidden_ref, head_slope_ref = refs[10:]
    rows_y, z_count = place.rows_y, place.z_count
    z_table = z_table_ref[...]
    lines = (own_ref[...] + got_ref[...].astype(F32)).astype(BF16)
    pre_act = side_by_side(dot_tn(lines, z_table), rows_y) + pointwise_ref[...]
    head, head_turned = head_ref[...], head_turned_ref[...]
    head_bias, out_row, out_column = head_bias_ref[...], out_row_ref[...], out_column_ref[...]
    width = 2 * z_count
    slopes, head_pre = [], []
    for first in range(0, rows_y * z_count, width):
        value, slope = normal(pre_act[:, first : first + width])
        hidden = value.astype(BF16)
        hidden_ref[:, first : first + width] = hidden
        slopes.append(slope)
        head_pre.append(dot(head_turned, hidden))
    gradients = []
    for index, first in enumerate(range(0, rows_y, 2)):
        target = jnp.concatenate(
            [cotangent_ref[y : y + 1] for y in range(first, first + 2)], axis=1
        )
        active, slope = normal(head_pre[index] + head_bias)
        predicted = dot(out_row, active.astype(BF16))
        prediction_ref[first : first + 1] = predicted[:, :z_count]
        prediction_ref[first + 1 : first + 2] = predicted[:, z_count:]
        head_slope = (target * out_column * slope).astype(BF16)
        head_slope_ref[:, first * z_count : first * z_count + width] = head_slope
        gradients.append((dot(head, head_slope) * slopes[index]).astype(BF16))
    gradient = jnp.concatenate(gradients, axis=1)
    grad_pre_ref[...] = gradient
    send_ref[...] = dot_nt(z_table, one_below_other(gradient, rows_y)).astype(BF16)


def sums_kernel(place, field_ref, gradient_ref, hidden_ref, head_slope_ref, *refs):
    refs[-1][...] = jnp.concatenate(halves(place.forward_x()), axis=1)
    grad_mix = dot_nt(field_ref[...], gradient_ref[...])
    grad_head = dot_nt(hidden_ref[...], head_slope_ref[...])
    if not place.fold:
        refs[0][...] = grad_mix
        refs[1][...] = grad_head
        return
    channels, hidden_units = grad_head.shape
    rest = jnp.zeros((channels, hidden_units - channels), F32)
    wide_mix = jnp.concatenate([grad_mix, rest], axis=1)
    high, low = halves(jnp.concatenate([grad_head, wide_mix], axis=0))
    split = jnp.concatenate([high, low], axis=0)
    place_of = selector(
        8 * place.partners,
        4 * channels,
        lambda row, column: (column % channels == 2 * (row // 8) + row % 2)
        & (column // channels == (row % 8) // 2),
    )
    refs[0][...] = dot(place_of, split).astype(BF16)


def back_kernel(
    place, pieces_ref, y_forward_ref, y_inverse_ref, weight_ref, adjoint_ref, send_ref
):
    kz, channels = place.kz, place.channels
    pieces, shares = read_pieces(place, pieces_ref)
    adjoint = analysed(place, pieces, y_forward_ref[...], 1)
    adjoint_ref[...] = adjoint
    turned = []
    for first in range(0, adjoint.shape[0], 2 * kz):
        turned += [adjoint[first + kz : first + 2 * kz], -adjoint[first : first + kz]]
    left = jnp.concatenate([adjoint, jnp.concatenate(turned, axis=0)], axis=1)
    left = jnp.concatenate([left] * 4, axis=1)
    row, lane = grid_of(*left.shape)
    same = (row // (2 * kz)) % 4 == lane // (2 * channels)
    left = jnp.where(same, left, 0.0).astype(BF16)
    block = 8 * kz
    pulled = [
        dot_nt(left[q * block : (q + 1) * block], weight_ref[q]) for q in range(place.modes // 4)
    ]
    pulled = jnp.concatenate(pulled, axis=0)
    row, lane = grid_of(*pulled.shape)
    pulled = jnp.where(row % kz == lane // channels, pulled, 0.0).astype(BF16)
    gather = selector(
        kz * channels, channels, lambda row, column: row % channels == column
    )
    modes_back = dot(pulled, gather).astype(BF16)
    block = spread_lines(place, modes_back, y_inverse_ref[...])
    if shares is None:
        repeat_rows(send_ref, block)
        return
    total = sum(shares[1:], shares[0])
    high, low = halves(total[0:4] + total[4:8])
    split = jnp.concatenate([high.astype(F32), low.astype(F32)], axis=0)
    write_pieces(place, send_ref, block, split.astype(BF16))


def outer_kernel(spectrum_ref, adjoint_ref, out_ref, done_ref):
    done_ref[...] = jnp.zeros(done_ref.shape, F32)
    modes, kz = out_ref.shape[:2]
    for j in range(modes):
        columns = jnp.transpose(spectrum_ref[j])
        adjoint = adjoint_ref[j]
        for k in range(kz):
            s_real, s_imag = columns[:, k : k + 1], columns[:, kz + k : kz + k + 1]
            a_real, a_imag = adjoint[k : k + 1], adjoint[kz + k : kz + k + 1]
            out_ref[j, k, 0] = s_real * a_real + s_imag * a_imag
            out_ref[j, k, 1] = s_real * a_imag - s_imag * a_real


def pointwise_kernel(place, mix_ref, gradient_ref, out_ref, z_plain_ref, turn_ref):
    z_plain_ref[...] = place.z_table(False)
    turn_ref[...] = turn_matrix(place, False)
    z_count = place.z_count
    product = dot(mix_ref[...], gradient_ref[...])
    for y in range(place.rows_y):
        out_ref[:, y, :] = product[:, y * z_count : (y + 1) * z_count]


def finish_kernel(place, *refs):
    own_ref, got_ref, z_table_ref, turn_ref, pointwise_ref, prediction_ref = refs[:6]
    refs = refs[6:]
    height = 2 * MZ
    channels = place.channels
    lines = (own_ref[...] + got_ref[:height].astype(F32)).astype(BF16)
    lines = dot(lines, turn_ref[...]).astype(BF16)
    pointwise = pointwise_ref[...].reshape(place.lanes, place.z_count)
    grad_field = (dot_tn(lines, z_table_ref[...]) + pointwise).astype(BF16)
    if not place.fold:
        refs[0][...] = grad_field
        refs[1][...] = prediction_ref[...]
        return
    sums_ref, grad_field_ref, out_ref, grad_mix_ref, grad_head_ref = refs
    grad_field_ref[...] = grad_field
    out_ref[...] = prediction_ref[...]
    got = got_ref[height:].astype(F32)
    width = sums_ref.shape[1]
    total = sums_ref[...] + got[:, :width] + got[:, width:]
    grad_head_ref[...] = total[:channels]
    grad_mix_ref[...] = total[channels:, :channels]


def call(kernel, outs, name, **spec):
    return pl.pallas_call(
        kernel,
        out_shape=[jax.ShapeDtypeStruct(shape, dtype) for shape, dtype in outs],
        compiler_params=pltpu.CompilerParams(vmem_limit_bytes=VMEM_LIMIT),
        cost_estimate=pl.CostEstimate(flops=1 << 22, bytes_accessed=1 << 19, transcendentals=0),
        name=name,
        **spec,
    )


def body(
    lifted_field,
    spectral_weight,
    mix_weight,
    mix_bias,
    head_weight,
    head_bias,
    out_weight,
    cotangent,
):
    wide = lax.axis_size("wide")
    narrow = lax.axis_size("narrow")
    devices = wide * narrow
    _, channels, rows_y, z_count = lifted_field.shape
    modes, kz = spectral_weight.shape[:2]
    hidden_units = head_weight.shape[1]
    cells = channels * rows_y
    place = Place(wide, narrow, kz, modes, rows_y, channels, z_count, False)
    place.fold = 2 * place.partners == channels and hidden_units == 128 and cells == 256 and kz % 8 == 0
    height = 2 * MZ
    step = 2 * kz
    partners = place.partners
    mode_lines = modes * 2 * kz

    y_forward, y_inverse = y_tables(rows_y * narrow, rows_y, kz, modes)
    if len(y_forward) > 1:
        block = lax.axis_index("wide") % len(y_forward)
        y_forward = lax.dynamic_index_in_dim(jnp.asarray(y_forward), block, 0, False)
        y_inverse = lax.dynamic_index_in_dim(jnp.asarray(y_inverse), block, 0, False)
    else:
        y_forward, y_inverse = jnp.asarray(y_forward[0]), jnp.asarray(y_inverse[0])

    def to_twin(send):
        pairs = [(p, p ^ narrow) for p in range(devices)]
        return lax.ppermute(send, ("wide", "narrow"), pairs)

    groups = [
        [
            (2 * place.listed(outer) + inner) * narrow + n
            for outer in range(place.outer)
            for n in range(narrow)
        ]
        for inner in range(2)
    ]

    def exchange(send):
        pieces = send.reshape(partners, -1, send.shape[1])
        got = lax.all_to_all(
            pieces, ("wide", "narrow"), 0, 0, axis_index_groups=groups, tiled=True
        )
        return got.reshape(send.shape)

    plain = ((partners * step, cells), BF16)
    shared = ((partners * (2 * step + 8), cells // 2), BF16) if place.fold else plain
    twin_plain = ((height, cells), BF16)
    twin_shared = ((height + 2 * channels, cells), BF16) if place.fold else twin_plain
    sums_shape = ((2 * channels, hidden_units), F32)
    own_lines = ((height, cells), F32)
    across = (channels, rows_y * z_count)

    def run(kernel, outs, name, **spec):
        return call(functools.partial(kernel, place), outs, name, **spec)

    flat_field = lifted_field.reshape(cells, z_count)
    twin_field = to_twin(flat_field)
    field, spectra = run(own_kernel, [(across, BF16), twin_plain], "own")(flat_field)
    (send,) = run(start_kernel, [plain], "start")(spectra, twin_field)
    packed_shape = ((modes // 4, kz * channels, 8 * channels), BF16)
    (weight,) = call(pack_kernel, [packed_shape], "pack")(spectral_weight)
    spectrum, send = run(mode_kernel, [((mode_lines, channels), F32), plain], "mode")(
        exchange(send), y_forward, y_inverse, weight
    )
    own, send = run(part_kernel, [own_lines, twin_plain], "part")(exchange(send))
    pointwise, head_turned, z_doubled = run(
        ready_kernel,
        [(across, F32), ((hidden_units, channels), BF16), ((height, z_count), BF16)],
        "ready",
    )(field, mix_weight, mix_bias[:, None], head_weight)
    prediction, grad_pre, send, hidden, head_slope = run(
        cell_kernel,
        [
            ((rows_y, z_count), F32),
            (across, BF16),
            twin_plain,
            (across, BF16),
            ((hidden_units, rows_y * z_count), BF16),
        ],
        "cell",
    )(
        own,
        to_twin(send),
        z_doubled,
        pointwise,
        head_weight,
        head_turned,
        head_bias[:, None],
        out_weight[None],
        out_weight.astype(F32)[:, None],
        cotangent[0],
    )
    if place.fold:
        outs = [((8 * partners, hidden_units), BF16)]
    else:
        outs = [((channels, channels), F32), ((channels, hidden_units), F32)]
    outs += [((wide // 2 * height, 4 * height), BF16)]
    *sums, forward = run(sums_kernel, outs, "sums")(field, grad_pre, hidden, head_slope)
    if not place.fold:
        totals = lax.psum(tuple(sums), ("wide", "narrow"))
        sums = []
    (send,) = run(fold_kernel, [shared], "fold")(send, to_twin(send), forward, *sums)
    adjoint, send = run(back_kernel, [((mode_lines, channels), F32), shared], "back")(
        exchange(send), y_forward, y_inverse, weight
    )
    some = max(1, modes // 4)
    grad_spectral, done = pl.pallas_call(
        outer_kernel,
        grid=(modes // some,),
        in_specs=[pl.BlockSpec((some, 2 * kz, channels), lambda j: (j, 0, 0))] * 2,
        out_specs=[
            pl.BlockSpec((some, kz, 2, channels, channels), lambda j: (j, 0, 0, 0, 0)),
            pl.BlockSpec((8, 128), lambda j: (0, 0)),
        ],
        out_shape=[
            jax.ShapeDtypeStruct(spectral_weight.shape, F32),
            jax.ShapeDtypeStruct((8, 128), F32),
        ],
        compiler_params=pltpu.CompilerParams(vmem_limit_bytes=VMEM_LIMIT),
        cost_estimate=pl.CostEstimate(flops=1 << 22, bytes_accessed=5 << 20, transcendentals=0),
        name="outer",
    )(spectrum.reshape(modes, 2 * kz, channels), adjoint.reshape(modes, 2 * kz, channels))
    pointwise, z_plain, turn = run(
        pointwise_kernel,
        [
            ((channels, rows_y, z_count), F32),
            ((height, z_count), BF16),
            ((cells, cells), BF16),
        ],
        "pointwise",
    )(mix_weight, grad_pre)
    outs = [own_lines, twin_shared] + ([sums_shape] if place.fold else [])
    after = (done,) if place.fold else ()
    own, send, *sums = run(part_kernel, outs, "part")(exchange(send), *after)
    outs = [((cells, z_count), BF16), ((rows_y, z_count), F32)]
    if place.fold:
        outs += [((channels, channels), F32), ((channels, hidden_units), F32)]
    grad_field, prediction, *summed = run(finish_kernel, outs, "finish")(
        own, to_twin(send), z_plain, turn, pointwise, prediction, *sums
    )
    grad_mix, grad_head = summed if place.fold else totals
    return (
        prediction[None],
        grad_field.reshape(lifted_field.shape),
        grad_spectral,
        grad_mix,
        grad_head,
    )


def solution(mesh):
    return jax.shard_map(
        body,
        mesh=mesh,
        in_specs=(
            P("wide", None, "narrow", None),
            P("wide", "narrow", None, None, None),
            P(),
            P(),
            P(),
            P(),
            P(),
            P("wide", "narrow", None),
        ),
        out_specs=(
            P("wide", "narrow", None),
            P("wide", None, "narrow", None),
            P("wide", "narrow", None, None, None),
            P(),
            P(),
        ),
        check_vma=False,
    )
```

```python
import functools
import math

import jax
import jax.numpy as jnp
import numpy as np
from jax import lax
from jax.experimental import pallas as pl
from jax.experimental.pallas import tpu as pltpu
from jax.sharding import PartitionSpec as P

MX = 16
MY = 16
MZ = 16
F32 = jnp.float32
BF16 = jnp.bfloat16
VMEM_LIMIT = 32 * 1024 * 1024

TAIL_SLOPE = 0.275
TAIL = (
    0.11780925840139389,
    0.04211147502064705,
    0.3339323103427887,
    -0.3309934139251709,
    0.4519987106323242,
    -0.11485832929611206,
)


def signed(indices, count):
    return np.where(indices < count // 2, indices, indices - count)


def wave(positions, frequency, length):
    turned = np.mod(np.multiply.outer(positions, frequency), length)
    angles = turned.astype(np.float32) * np.float32(2.0 * math.pi / length)
    scale = np.float32(1.0 / math.sqrt(length))
    return np.cos(angles) * scale, np.sin(angles) * scale


def pair(cosine, sine, sign):
    return np.stack(
        [np.stack([cosine, -sign * sine], -1), np.stack([sign * sine, cosine], -1)], -2
    )


def y_tables(total_y, rows_y, kz, modes):
    cosine, sine = wave(np.arange(total_y), signed(np.arange(MY), MY), total_y)
    narrow = total_y // rows_y
    same = np.eye(kz, dtype=np.float32)
    forward = pair(cosine, sine, -1.0).reshape(narrow, rows_y, MY // modes, modes, 2, 2)
    inverse = pair(cosine, sine, 1.0).reshape(narrow, rows_y, MY // modes, modes, 2, 2)
    forward = np.einsum("nybjtr,kl->bjtkynlr", forward, same)
    inverse = np.einsum("nybjst,kl->bnyksjtl", inverse, same)
    blocks = MY // modes
    forward = forward.reshape(blocks, modes * 2 * kz, rows_y * narrow * kz * 2)
    inverse = inverse.reshape(blocks, narrow * rows_y * kz * 2, modes * 2 * kz)
    return forward.astype(BF16), inverse.astype(BF16)


def dot(a, b):
    return jnp.dot(a, b, preferred_element_type=F32)


def dot_nt(a, b):
    return lax.dot_general(a, b, (((1,), (1,)), ((), ())), preferred_element_type=F32)


def dot_tn(a, b):
    return lax.dot_general(a, b, (((0,), (0,)), ((), ())), preferred_element_type=F32)


def grid_of(rows, columns):
    shape = (rows, columns)
    return lax.broadcasted_iota(jnp.int32, shape, 0), lax.broadcasted_iota(jnp.int32, shape, 1)


def selector(rows, columns, condition):
    return jnp.where(condition(*grid_of(rows, columns)), 1.0, 0.0).astype(BF16)


def halves(values):
    high = values.astype(BF16)
    return high, (values - high.astype(F32)).astype(BF16)


def stacked(refs, lanes=slice(None)):
    return jnp.concatenate([ref[:, lanes] for ref in refs], axis=0)


def cosine_of(phase, length):
    angles = (phase & (length - 1)).astype(F32) * (2.0 * math.pi / length)
    return jnp.cos(angles) * (1.0 / math.sqrt(length))


class Place:
    def __init__(self, wide, narrow, kz, modes, rows_y, channels, z_count, fold):
        self.wide, self.narrow, self.kz, self.modes = wide, narrow, kz, modes
        self.rows_y, self.channels, self.z_count, self.fold = rows_y, channels, z_count, fold
        self.outer = wide // 2
        self.partners = self.outer * narrow
        self.lanes = rows_y * channels
        middle, last = self.outer // 4, self.outer // 2 - 1
        self.firsts = (last, middle, middle, last)

    def here(self):
        wide = lax.axis_index("wide")
        return wide // 2, wide % 2

    def listed(self, position, first):
        lines = self.outer // 2
        return ((first + position // 2) & (lines - 1)) * 2 + position % 2

    def frequency(self, wide):
        index = (wide * self.modes) // MY
        return jnp.where(index < MX // 2, index, index - MX)

    def z_table(self, doubled):
        row, z = grid_of(2 * MZ, self.z_count)
        frequency = row >> 1
        value = cosine_of(z * frequency + (row & 1) * (self.z_count // 4), self.z_count)
        if doubled:
            value = jnp.where(frequency > 0, 2.0 * value, value)
        return value.astype(BF16)

    def expanded(self, small):
        row, column = grid_of(2 * MZ, small.shape[1])
        same = (row >> 1) == ((column >> 1) & (MZ - 1))
        blocks = []
        for g in range(small.shape[0] // 2):
            value = jnp.where((row & 1) == 0, small[2 * g : 2 * g + 1], small[2 * g + 1 : 2 * g + 2])
            blocks.append(jnp.where(same, value, 0.0))
        return jnp.concatenate(blocks, axis=0)

    def forward_x(self, first):
        outer, inner = self.here()
        row, column = grid_of(2 * self.outer, 4 * MZ)
        x = 2 * outer + (inner ^ (column // (2 * MZ)))
        frequency = self.frequency(2 * self.listed(row >> 1, first) + inner)
        quarter = self.wide // 4
        small = cosine_of(x * frequency + quarter * ((row & 1) - (column & 1)), self.wide)
        return self.expanded(small)

    def inverse_x(self, first):
        outer, inner = self.here()
        row, column = grid_of(4, self.outer * 2 * MZ)
        x = 2 * outer + (inner ^ (row >> 1))
        frequency = self.frequency(2 * self.listed(column // (2 * MZ), first) + inner)
        quarter = self.wide // 4
        small = cosine_of(x * frequency + quarter * ((column & 1) - (row & 1)), self.wide)
        return self.expanded(small).astype(BF16)


def repeat_rows(out_ref, block):
    height = block.shape[0]
    for first in range(0, out_ref.shape[0], height):
        out_ref[first : first + height] = block


def write_pieces(place, send_ref, block, shares):
    step, half = 2 * place.kz, place.lanes // 2
    height = send_ref.shape[0] // place.partners
    for p in range(place.partners):
        own = block[p * step % block.shape[0] :][:step]
        first = p * height
        send_ref[first : first + step] = own[:, :half]
        send_ref[first + step : first + 2 * step] = own[:, half:]
        send_ref[first + 2 * step : first + height] = shares[p * 8 % shares.shape[0] :][:8]


def read_pieces(place, pieces_ref):
    step = 2 * place.kz
    if pieces_ref.shape[1] == place.lanes:
        return pieces_ref[...], None
    height = pieces_ref.shape[0] // place.partners
    blocks, shares = [], []
    for p in range(place.partners):
        first = p * height
        left = pieces_ref[first : first + step]
        right = pieces_ref[first + step : first + 2 * step]
        blocks.append(jnp.concatenate([left, right], axis=1))
        shares.append(pieces_ref[first + 2 * step : first + height].astype(F32))
    return jnp.concatenate(blocks, axis=0), shares


def analysed(place, pieces, y_forward, copies):
    height = 2 * MZ
    turned = sum(
        pieces[first : first + height].astype(F32) for first in range(0, pieces.shape[0], height)
    )
    channels = place.channels
    lines = jnp.concatenate(
        [turned[:, y * channels : (y + 1) * channels] for y in range(place.rows_y)], axis=0
    )
    return dot(y_forward, jnp.concatenate([lines.astype(BF16)] * copies, axis=1))


def spread_lines(place, modes, y_inverse):
    lines = dot(y_inverse, modes)
    step = 2 * place.kz
    blocks = []
    for n in range(place.narrow):
        first = n * place.rows_y
        parts = [lines[(first + y) * step : (first + y + 1) * step] for y in range(place.rows_y)]
        blocks.append(jnp.concatenate(parts, axis=1))
    return jnp.concatenate(blocks, axis=0).astype(BF16)


def turn_matrix(place, forward):
    channels, rows_y = place.channels, place.rows_y

    def same(row, column):
        if forward:
            row, column = column, row
        return (row % channels == column // rows_y) & (row // channels == column % rows_y)

    return selector(place.lanes, place.lanes, same)


def side_by_side(values, count):
    height = values.shape[0] // count
    return jnp.concatenate([values[y * height : (y + 1) * height] for y in range(count)], axis=1)


def one_below_other(values, count):
    width = values.shape[1] // count
    return jnp.concatenate([values[:, y * width : (y + 1) * width] for y in range(count)], axis=0)


def own_kernel(place, field_ref, field_out_ref, spectra_ref):
    turned = dot(turn_matrix(place, False), field_ref[...]).astype(BF16)
    field_out_ref[...] = side_by_side(turned, place.rows_y)
    spectra_ref[...] = dot_nt(place.z_table(False), turned).astype(BF16)


def start_kernel(place, spectra_ref, twin_ref, send_ref):
    twin = dot_nt(place.z_table(False), twin_ref[...]).astype(BF16)
    twin = dot(twin, turn_matrix(place, True)).astype(BF16)
    values = jnp.concatenate([spectra_ref[...], twin], axis=0)
    tables = jnp.concatenate(halves(place.forward_x(place.firsts[0])), axis=1)
    send_ref[...] = dot(tables, jnp.concatenate([values, values], axis=0)).astype(BF16)


def pack_kernel(weight_ref, packed_ref):
    modes, kz, _, channels, _ = weight_ref.shape
    for q in range(modes // 4):
        parts = [weight_ref[4 * q + j // 2, :, j % 2] for j in range(8)]
        packed = jnp.concatenate(parts, axis=-1).reshape(kz * channels, 8 * channels)
        packed_ref[q] = packed.astype(BF16)


def ready_kernel(place, field_ref, mix_ref, mix_bias_ref, head_ref, *refs):
    pointwise_ref, head_out_ref, z_doubled_ref = refs
    pointwise_ref[...] = dot_tn(mix_ref[...], field_ref[...]) + mix_bias_ref[...]
    head_out_ref[...] = jnp.transpose(head_ref[...].astype(F32)).astype(BF16)
    z_doubled_ref[...] = place.z_table(True)


def fold_kernel(place, own_ref, got_ref, tables_ref, *refs):
    values = jnp.concatenate([own_ref[...], got_ref[...]], axis=0)
    values = jnp.concatenate([values, values], axis=0)
    partial = dot(tables_ref[...], values).astype(BF16)
    if place.fold:
        shares_ref, send_ref = refs
        write_pieces(place, send_ref, partial, shares_ref[...])
    else:
        refs[0][...] = partial


def mode_kernel(
    place, pieces_ref, y_forward_ref, y_inverse_ref, weight_ref, spectrum_ref, send_ref
):
    kz, channels = place.kz, place.channels
    spectrum = analysed(place, pieces_ref[...], y_forward_ref[...], kz)
    spectrum_ref[...] = spectrum[:, :channels]
    row, lane = grid_of(*spectrum.shape)
    blocked = jnp.where(row % kz == lane // channels, spectrum, 0.0)
    mixed = []
    for q in range(place.modes // 4):
        left = blocked[q * 8 * kz : (q + 1) * 8 * kz].astype(BF16)
        product = dot(left, weight_ref[q])
        for j in range(4):
            own = product[j * 2 * kz : (j + 1) * 2 * kz, j * 2 * channels : (j + 1) * 2 * channels]
            real, imag = own[:, :channels], own[:, channels:]
            mixed.append(real[:kz] - imag[kz:])
            mixed.append(imag[:kz] + real[kz:])
    mode = jnp.concatenate(mixed, axis=0).astype(BF16)
    repeat_rows(send_ref, spread_lines(place, mode, y_inverse_ref[...]))


def part_kernel(place, first, pieces_ref, *refs):
    pieces, shares = read_pieces(place, pieces_ref)
    lines = dot(place.inverse_x(first), pieces)
    height = 2 * MZ
    if shares is None:
        own_ref, send_ref = refs
        own_ref[...] = lines[:height]
        send_ref[...] = lines[height:].astype(BF16)
        return
    _, own_ref, send_ref, sums_ref = refs
    own_ref[...] = lines[:height]
    send_ref[:height] = lines[height:].astype(BF16)
    got = jnp.concatenate(shares, axis=0).astype(BF16)
    channels, narrow = place.channels, place.narrow

    def chosen(part):
        def condition(row, column):
            owner, source = (row % channels) // 2, column // 8
            return (
                (place.listed(owner // narrow, place.firsts[2]) == place.listed(source // narrow, first))
                & (owner % narrow == source % narrow)
                & (column % 8 == 4 * part + 2 * (row // channels) + row % 2)
            )

        return dot(selector(2 * channels, got.shape[0], condition), got)

    high, low = chosen(0), chosen(1)
    sums_ref[...] = high + low
    send_ref[height:] = jnp.concatenate([high, low], axis=1).astype(BF16)


def normal(values):
    scaled = 1.0 / (1.0 + TAIL_SLOPE * jnp.abs(values))
    decay = jnp.exp(-0.5 * values * values)
    tail = TAIL[-1]
    for factor in TAIL[-2::-1]:
        tail = tail * scaled + factor
    tail = tail * (scaled * decay)
    cumulative = jnp.where(values > 0.0, 1.0 - tail, tail)
    return values * cumulative, cumulative + values * (decay * (1.0 / math.sqrt(2.0 * math.pi)))


def cell_kernel(place, *refs):
    own_ref, got_ref, z_table_ref, pointwise_ref, head_ref, head_turned_ref = refs[:6]
    head_bias_ref, out_row_ref, out_column_ref, cotangent_ref = refs[6:10]
    prediction_ref, grad_pre_ref, send_ref, hidden_ref, head_slope_ref = refs[10:]
    rows_y, z_count = place.rows_y, place.z_count
    z_table = z_table_ref[...]
    lines = (own_ref[...] + got_ref[...].astype(F32)).astype(BF16)
    pre_act = side_by_side(dot_tn(lines, z_table), rows_y) + pointwise_ref[...]
    head, head_turned = head_ref[...], head_turned_ref[...]
    head_bias, out_row, out_column = head_bias_ref[...], out_row_ref[...], out_column_ref[...]
    width = 2 * z_count
    slopes, head_pre = [], []
    for first in range(0, rows_y * z_count, width):
        value, slope = normal(pre_act[:, first : first + width])
        hidden = value.astype(BF16)
        hidden_ref[:, first : first + width] = hidden
        slopes.append(slope)
        head_pre.append(dot(head_turned, hidden))
    gradients = []
    for index, first in enumerate(range(0, rows_y, 2)):
        target = jnp.concatenate(
            [cotangent_ref[y : y + 1] for y in range(first, first + 2)], axis=1
        )
        active, slope = normal(head_pre[index] + head_bias)
        predicted = dot(out_row, active.astype(BF16))
        prediction_ref[first : first + 1] = predicted[:, :z_count]
        prediction_ref[first + 1 : first + 2] = predicted[:, z_count:]
        head_slope = (target * out_column * slope).astype(BF16)
        head_slope_ref[:, first * z_count : first * z_count + width] = head_slope
        gradients.append((dot(head, head_slope) * slopes[index]).astype(BF16))
    gradient = jnp.concatenate(gradients, axis=1)
    grad_pre_ref[...] = gradient
    send_ref[...] = dot_nt(z_table, one_below_other(gradient, rows_y)).astype(BF16)


def sums_kernel(place, field_ref, gradient_ref, hidden_ref, head_slope_ref, *refs):
    refs[-1][...] = jnp.concatenate(halves(place.forward_x(place.firsts[2])), axis=1)
    grad_mix = dot_nt(field_ref[...], gradient_ref[...])
    grad_head = dot_nt(hidden_ref[...], head_slope_ref[...])
    if not place.fold:
        refs[0][...] = grad_mix
        refs[1][...] = grad_head
        return
    channels, hidden_units = grad_head.shape
    rest = jnp.zeros((channels, hidden_units - channels), F32)
    wide_mix = jnp.concatenate([grad_mix, rest], axis=1)
    high, low = halves(jnp.concatenate([grad_head, wide_mix], axis=0))
    split = jnp.concatenate([high, low], axis=0)
    place_of = selector(
        8 * place.partners,
        4 * channels,
        lambda row, column: (column % channels == 2 * (row // 8) + row % 2)
        & (column // channels == (row % 8) // 2),
    )
    refs[0][...] = dot(place_of, split).astype(BF16)


def back_kernel(
    place, pieces_ref, y_forward_ref, y_inverse_ref, weight_ref, adjoint_ref, send_ref
):
    kz, channels = place.kz, place.channels
    pieces, shares = read_pieces(place, pieces_ref)
    adjoint = analysed(place, pieces, y_forward_ref[...], 1)
    adjoint_ref[...] = adjoint
    turned = []
    for first in range(0, adjoint.shape[0], 2 * kz):
        turned += [adjoint[first + kz : first + 2 * kz], -adjoint[first : first + kz]]
    left = jnp.concatenate([adjoint, jnp.concatenate(turned, axis=0)], axis=1)
    left = jnp.concatenate([left] * 4, axis=1)
    row, lane = grid_of(*left.shape)
    same = (row // (2 * kz)) % 4 == lane // (2 * channels)
    left = jnp.where(same, left, 0.0).astype(BF16)
    block = 8 * kz
    pulled = [
        dot_nt(left[q * block : (q + 1) * block], weight_ref[q]) for q in range(place.modes // 4)
    ]
    pulled = jnp.concatenate(pulled, axis=0)
    row, lane = grid_of(*pulled.shape)
    pulled = jnp.where(row % kz == lane // channels, pulled, 0.0).astype(BF16)
    gather = selector(
        kz * channels, channels, lambda row, column: row % channels == column
    )
    modes_back = dot(pulled, gather).astype(BF16)
    block = spread_lines(place, modes_back, y_inverse_ref[...])
    if shares is None:
        repeat_rows(send_ref, block)
        return
    total = sum(shares[1:], shares[0])
    high, low = halves(total[0:4] + total[4:8])
    split = jnp.concatenate([high.astype(F32), low.astype(F32)], axis=0)
    write_pieces(place, send_ref, block, split.astype(BF16))


def outer_kernel(spectrum_ref, adjoint_ref, out_ref, done_ref):
    done_ref[...] = jnp.zeros(done_ref.shape, F32)
    modes, kz = out_ref.shape[:2]
    for j in range(modes):
        columns = jnp.transpose(spectrum_ref[j])
        adjoint = adjoint_ref[j]
        for k in range(kz):
            s_real, s_imag = columns[:, k : k + 1], columns[:, kz + k : kz + k + 1]
            a_real, a_imag = adjoint[k : k + 1], adjoint[kz + k : kz + k + 1]
            out_ref[j, k, 0] = s_real * a_real + s_imag * a_imag
            out_ref[j, k, 1] = s_real * a_imag - s_imag * a_real


def pointwise_kernel(place, mix_ref, gradient_ref, out_ref, z_plain_ref, turn_ref):
    z_plain_ref[...] = place.z_table(False)
    turn_ref[...] = turn_matrix(place, False)
    z_count = place.z_count
    product = dot(mix_ref[...], gradient_ref[...])
    for y in range(place.rows_y):
        out_ref[:, y, :] = product[:, y * z_count : (y + 1) * z_count]


def finish_kernel(place, *refs):
    own_ref, got_ref, z_table_ref, turn_ref, pointwise_ref, prediction_ref = refs[:6]
    refs = refs[6:]
    height = 2 * MZ
    channels = place.channels
    lines = (own_ref[...] + got_ref[:height].astype(F32)).astype(BF16)
    lines = dot(lines, turn_ref[...]).astype(BF16)
    pointwise = pointwise_ref[...].reshape(place.lanes, place.z_count)
    grad_field = (dot_tn(lines, z_table_ref[...]) + pointwise).astype(BF16)
    if not place.fold:
        refs[0][...] = grad_field
        refs[1][...] = prediction_ref[...]
        return
    sums_ref, grad_field_ref, out_ref, grad_mix_ref, grad_head_ref = refs
    grad_field_ref[...] = grad_field
    out_ref[...] = prediction_ref[...]
    got = got_ref[height:].astype(F32)
    width = sums_ref.shape[1]
    total = sums_ref[...] + got[:, :width] + got[:, width:]
    grad_head_ref[...] = total[:channels]
    grad_mix_ref[...] = total[channels:, :channels]


def call(kernel, outs, name, **spec):
    return pl.pallas_call(
        kernel,
        out_shape=[jax.ShapeDtypeStruct(shape, dtype) for shape, dtype in outs],
        compiler_params=pltpu.CompilerParams(vmem_limit_bytes=VMEM_LIMIT),
        cost_estimate=pl.CostEstimate(flops=1 << 22, bytes_accessed=1 << 19, transcendentals=0),
        name=name,
        **spec,
    )


def body(
    lifted_field,
    spectral_weight,
    mix_weight,
    mix_bias,
    head_weight,
    head_bias,
    out_weight,
    cotangent,
):
    wide = lax.axis_size("wide")
    narrow = lax.axis_size("narrow")
    devices = wide * narrow
    _, channels, rows_y, z_count = lifted_field.shape
    modes, kz = spectral_weight.shape[:2]
    hidden_units = head_weight.shape[1]
    cells = channels * rows_y
    place = Place(wide, narrow, kz, modes, rows_y, channels, z_count, False)
    place.fold = 2 * place.partners == channels and hidden_units == 128 and cells == 256 and kz % 8 == 0
    height = 2 * MZ
    step = 2 * kz
    partners = place.partners
    mode_lines = modes * 2 * kz

    y_forward, y_inverse = y_tables(rows_y * narrow, rows_y, kz, modes)
    if len(y_forward) > 1:
        block = lax.axis_index("wide") % len(y_forward)
        y_forward = lax.dynamic_index_in_dim(jnp.asarray(y_forward), block, 0, False)
        y_inverse = lax.dynamic_index_in_dim(jnp.asarray(y_inverse), block, 0, False)
    else:
        y_forward, y_inverse = jnp.asarray(y_forward[0]), jnp.asarray(y_inverse[0])

    def to_twin(send):
        pairs = [(p, p ^ narrow) for p in range(devices)]
        return lax.ppermute(send, ("wide", "narrow"), pairs)

    def exchange(send, transform):
        first = place.firsts[transform]
        groups = [
            [
                (2 * place.listed(outer, first) + inner) * narrow + n
                for outer in range(place.outer)
                for n in range(narrow)
            ]
            for inner in range(2)
        ]
        pieces = send.reshape(partners, -1, send.shape[1])
        got = lax.all_to_all(
            pieces, ("wide", "narrow"), 0, 0, axis_index_groups=groups, tiled=True
        )
        return got.reshape(send.shape)

    plain = ((partners * step, cells), BF16)
    shared = ((partners * (2 * step + 8), cells // 2), BF16) if place.fold else plain
    twin_plain = ((height, cells), BF16)
    twin_shared = ((height + 2 * channels, cells), BF16) if place.fold else twin_plain
    sums_shape = ((2 * channels, hidden_units), F32)
    own_lines = ((height, cells), F32)
    across = (channels, rows_y * z_count)

    def run(kernel, outs, name, **spec):
        return call(functools.partial(kernel, place), outs, name, **spec)

    flat_field = lifted_field.reshape(cells, z_count)
    twin_field = to_twin(flat_field)
    field, spectra = run(own_kernel, [(across, BF16), twin_plain], "own")(flat_field)
    (send,) = run(start_kernel, [plain], "start")(spectra, twin_field)
    packed_shape = ((modes // 4, kz * channels, 8 * channels), BF16)
    (weight,) = call(pack_kernel, [packed_shape], "pack")(spectral_weight)
    spectrum, send = run(mode_kernel, [((mode_lines, channels), F32), plain], "mode")(
        exchange(send, 0), y_forward, y_inverse, weight
    )
    part = functools.partial(part_kernel, place, place.firsts[1])
    own, send = call(part, [own_lines, twin_plain], "part")(exchange(send, 1))
    pointwise, head_turned, z_doubled = run(
        ready_kernel,
        [(across, F32), ((hidden_units, channels), BF16), ((height, z_count), BF16)],
        "ready",
    )(field, mix_weight, mix_bias[:, None], head_weight)
    prediction, grad_pre, send, hidden, head_slope = run(
        cell_kernel,
        [
            ((rows_y, z_count), F32),
            (across, BF16),
            twin_plain,
            (across, BF16),
            ((hidden_units, rows_y * z_count), BF16),
        ],
        "cell",
    )(
        own,
        to_twin(send),
        z_doubled,
        pointwise,
        head_weight,
        head_turned,
        head_bias[:, None],
        out_weight[None],
        out_weight.astype(F32)[:, None],
        cotangent[0],
    )
    if place.fold:
        outs = [((8 * partners, hidden_units), BF16)]
    else:
        outs = [((channels, channels), F32), ((channels, hidden_units), F32)]
    outs += [((wide // 2 * height, 4 * height), BF16)]
    *sums, forward = run(sums_kernel, outs, "sums")(field, grad_pre, hidden, head_slope)
    if not place.fold:
        totals = lax.psum(tuple(sums), ("wide", "narrow"))
        sums = []
    (send,) = run(fold_kernel, [shared], "fold")(send, to_twin(send), forward, *sums)
    adjoint, send = run(back_kernel, [((mode_lines, channels), F32), shared], "back")(
        exchange(send, 2), y_forward, y_inverse, weight
    )
    some = max(1, modes // 4)
    grad_spectral, done = pl.pallas_call(
        outer_kernel,
        grid=(modes // some,),
        in_specs=[pl.BlockSpec((some, 2 * kz, channels), lambda j: (j, 0, 0))] * 2,
        out_specs=[
            pl.BlockSpec((some, kz, 2, channels, channels), lambda j: (j, 0, 0, 0, 0)),
            pl.BlockSpec((8, 128), lambda j: (0, 0)),
        ],
        out_shape=[
            jax.ShapeDtypeStruct(spectral_weight.shape, F32),
            jax.ShapeDtypeStruct((8, 128), F32),
        ],
        compiler_params=pltpu.CompilerParams(vmem_limit_bytes=VMEM_LIMIT),
        cost_estimate=pl.CostEstimate(flops=1 << 22, bytes_accessed=5 << 20, transcendentals=0),
        name="outer",
    )(spectrum.reshape(modes, 2 * kz, channels), adjoint.reshape(modes, 2 * kz, channels))
    pointwise, z_plain, turn = run(
        pointwise_kernel,
        [
            ((channels, rows_y, z_count), F32),
            ((height, z_count), BF16),
            ((cells, cells), BF16),
        ],
        "pointwise",
    )(mix_weight, grad_pre)
    outs = [own_lines, twin_shared] + ([sums_shape] if place.fold else [])
    after = (done,) if place.fold else ()
    part = functools.partial(part_kernel, place, place.firsts[3])
    own, send, *sums = call(part, outs, "part")(exchange(send, 3), *after)
    outs = [((cells, z_count), BF16), ((rows_y, z_count), F32)]
    if place.fold:
        outs += [((channels, channels), F32), ((channels, hidden_units), F32)]
    grad_field, prediction, *summed = run(finish_kernel, outs, "finish")(
        own, to_twin(send), z_plain, turn, pointwise, prediction, *sums
    )
    grad_mix, grad_head = summed if place.fold else totals
    return (
        prediction[None],
        grad_field.reshape(lifted_field.shape),
        grad_spectral,
        grad_mix,
        grad_head,
    )


def solution(mesh):
    return jax.shard_map(
        body,
        mesh=mesh,
        in_specs=(
            P("wide", None, "narrow", None),
            P("wide", "narrow", None, None, None),
            P(),
            P(),
            P(),
            P(),
            P(),
            P("wide", "narrow", None),
        ),
        out_specs=(
            P("wide", "narrow", None),
            P("wide", None, "narrow", None),
            P("wide", "narrow", None, None, None),
            P(),
            P(),
        ),
        check_vma=False,
    )
```

```python
import functools
import math

import jax
import jax.numpy as jnp
import numpy as np
from jax import lax
from jax.experimental import pallas as pl
from jax.experimental.pallas import tpu as pltpu
from jax.sharding import PartitionSpec as P

MX = 16
MY = 16
MZ = 16
F32 = jnp.float32
BF16 = jnp.bfloat16
VMEM_LIMIT = 32 * 1024 * 1024

TAIL_SLOPE = 0.275
TAIL = (
    0.11780925840139389,
    0.04211147502064705,
    0.3339323103427887,
    -0.3309934139251709,
    0.4519987106323242,
    -0.11485832929611206,
)


def signed(indices, count):
    return np.where(indices < count // 2, indices, indices - count)


def wave(positions, frequency, length):
    turned = np.mod(np.multiply.outer(positions, frequency), length)
    angles = turned.astype(np.float32) * np.float32(2.0 * math.pi / length)
    scale = np.float32(1.0 / math.sqrt(length))
    return np.cos(angles) * scale, np.sin(angles) * scale


def pair(cosine, sine, sign):
    return np.stack(
        [np.stack([cosine, -sign * sine], -1), np.stack([sign * sine, cosine], -1)], -2
    )


def y_tables(total_y, rows_y, kz, modes):
    cosine, sine = wave(np.arange(total_y), signed(np.arange(MY), MY), total_y)
    narrow = total_y // rows_y
    same = np.eye(kz, dtype=np.float32)
    forward = pair(cosine, sine, -1.0).reshape(narrow, rows_y, MY // modes, modes, 2, 2)
    inverse = pair(cosine, sine, 1.0).reshape(narrow, rows_y, MY // modes, modes, 2, 2)
    forward = np.einsum("nybjtr,kl->bjtkynlr", forward, same)
    inverse = np.einsum("nybjst,kl->bnyksjtl", inverse, same)
    blocks = MY // modes
    forward = forward.reshape(blocks, modes * 2 * kz, rows_y * narrow * kz * 2)
    inverse = inverse.reshape(blocks, narrow * rows_y * kz * 2, modes * 2 * kz)
    return forward.astype(BF16), inverse.astype(BF16)


def dot(a, b):
    return jnp.dot(a, b, preferred_element_type=F32)


def dot_nt(a, b):
    return lax.dot_general(a, b, (((1,), (1,)), ((), ())), preferred_element_type=F32)


def dot_tn(a, b):
    return lax.dot_general(a, b, (((0,), (0,)), ((), ())), preferred_element_type=F32)


def grid_of(rows, columns):
    shape = (rows, columns)
    return lax.broadcasted_iota(jnp.int32, shape, 0), lax.broadcasted_iota(jnp.int32, shape, 1)


def selector(rows, columns, condition):
    return jnp.where(condition(*grid_of(rows, columns)), 1.0, 0.0).astype(BF16)


def halves(values):
    high = values.astype(BF16)
    return high, (values - high.astype(F32)).astype(BF16)


def stacked(refs, lanes=slice(None)):
    return jnp.concatenate([ref[:, lanes] for ref in refs], axis=0)


def cosine_of(phase, length):
    angles = (phase & (length - 1)).astype(F32) * (2.0 * math.pi / length)
    return jnp.cos(angles) * (1.0 / math.sqrt(length))


class Place:
    def __init__(self, wide, narrow, kz, modes, rows_y, channels, z_count, fold):
        self.wide, self.narrow, self.kz, self.modes = wide, narrow, kz, modes
        self.rows_y, self.channels, self.z_count, self.fold = rows_y, channels, z_count, fold
        self.outer = wide // 2
        self.partners = self.outer * narrow
        self.lanes = rows_y * channels
        middle, last = self.outer // 4, self.outer // 2 - 1
        self.firsts = (last, middle, middle, middle)

    def here(self):
        wide = lax.axis_index("wide")
        return wide // 2, wide % 2

    def listed(self, position, first):
        lines = self.outer // 2
        return ((first + position // 2) & (lines - 1)) * 2 + position % 2

    def frequency(self, wide):
        index = (wide * self.modes) // MY
        return jnp.where(index < MX // 2, index, index - MX)

    def z_table(self, doubled):
        row, z = grid_of(2 * MZ, self.z_count)
        frequency = row >> 1
        value = cosine_of(z * frequency + (row & 1) * (self.z_count // 4), self.z_count)
        if doubled:
            value = jnp.where(frequency > 0, 2.0 * value, value)
        return value.astype(BF16)

    def expanded(self, small):
        row, column = grid_of(2 * MZ, small.shape[1])
        same = (row >> 1) == ((column >> 1) & (MZ - 1))
        blocks = []
        for g in range(small.shape[0] // 2):
            value = jnp.where((row & 1) == 0, small[2 * g : 2 * g + 1], small[2 * g + 1 : 2 * g + 2])
            blocks.append(jnp.where(same, value, 0.0))
        return jnp.concatenate(blocks, axis=0)

    def forward_x(self, first):
        outer, inner = self.here()
        row, column = grid_of(2 * self.outer, 4 * MZ)
        x = 2 * outer + (inner ^ (column // (2 * MZ)))
        frequency = self.frequency(2 * self.listed(row >> 1, first) + inner)
        quarter = self.wide // 4
        small = cosine_of(x * frequency + quarter * ((row & 1) - (column & 1)), self.wide)
        return self.expanded(small)

    def inverse_x(self, first):
        outer, inner = self.here()
        row, column = grid_of(4, self.outer * 2 * MZ)
        x = 2 * outer + (inner ^ (row >> 1))
        frequency = self.frequency(2 * self.listed(column // (2 * MZ), first) + inner)
        quarter = self.wide // 4
        small = cosine_of(x * frequency + quarter * ((column & 1) - (row & 1)), self.wide)
        return self.expanded(small).astype(BF16)


def repeat_rows(out_ref, block):
    height = block.shape[0]
    for first in range(0, out_ref.shape[0], height):
        out_ref[first : first + height] = block


def write_pieces(place, send_ref, block, shares):
    step, half = 2 * place.kz, place.lanes // 2
    height = send_ref.shape[0] // place.partners
    for p in range(place.partners):
        own = block[p * step % block.shape[0] :][:step]
        first = p * height
        send_ref[first : first + step] = own[:, :half]
        send_ref[first + step : first + 2 * step] = own[:, half:]
        send_ref[first + 2 * step : first + height] = shares[p * 8 % shares.shape[0] :][:8]


def read_pieces(place, pieces_ref):
    step = 2 * place.kz
    if pieces_ref.shape[1] == place.lanes:
        return pieces_ref[...], None
    height = pieces_ref.shape[0] // place.partners
    blocks, shares = [], []
    for p in range(place.partners):
        first = p * height
        left = pieces_ref[first : first + step]
        right = pieces_ref[first + step : first + 2 * step]
        blocks.append(jnp.concatenate([left, right], axis=1))
        shares.append(pieces_ref[first + 2 * step : first + height].astype(F32))
    return jnp.concatenate(blocks, axis=0), shares


def analysed(place, pieces, y_forward, copies):
    height = 2 * MZ
    turned = sum(
        pieces[first : first + height].astype(F32) for first in range(0, pieces.shape[0], height)
    )
    channels = place.channels
    lines = jnp.concatenate(
        [turned[:, y * channels : (y + 1) * channels] for y in range(place.rows_y)], axis=0
    )
    return dot(y_forward, jnp.concatenate([lines.astype(BF16)] * copies, axis=1))


def spread_lines(place, modes, y_inverse):
    lines = dot(y_inverse, modes)
    step = 2 * place.kz
    blocks = []
    for n in range(place.narrow):
        first = n * place.rows_y
        parts = [lines[(first + y) * step : (first + y + 1) * step] for y in range(place.rows_y)]
        blocks.append(jnp.concatenate(parts, axis=1))
    return jnp.concatenate(blocks, axis=0).astype(BF16)


def turn_matrix(place, forward):
    channels, rows_y = place.channels, place.rows_y

    def same(row, column):
        if forward:
            row, column = column, row
        return (row % channels == column // rows_y) & (row // channels == column % rows_y)

    return selector(place.lanes, place.lanes, same)


def side_by_side(values, count):
    height = values.shape[0] // count
    return jnp.concatenate([values[y * height : (y + 1) * height] for y in range(count)], axis=1)


def one_below_other(values, count):
    width = values.shape[1] // count
    return jnp.concatenate([values[:, y * width : (y + 1) * width] for y in range(count)], axis=0)


def own_kernel(place, field_ref, field_out_ref, spectra_ref):
    turned = dot(turn_matrix(place, False), field_ref[...]).astype(BF16)
    field_out_ref[...] = side_by_side(turned, place.rows_y)
    spectra_ref[...] = dot_nt(place.z_table(False), turned).astype(BF16)


def start_kernel(place, spectra_ref, twin_ref, send_ref):
    twin = dot_nt(place.z_table(False), twin_ref[...]).astype(BF16)
    twin = dot(twin, turn_matrix(place, True)).astype(BF16)
    values = jnp.concatenate([spectra_ref[...], twin], axis=0)
    tables = jnp.concatenate(halves(place.forward_x(place.firsts[0])), axis=1)
    send_ref[...] = dot(tables, jnp.concatenate([values, values], axis=0)).astype(BF16)


def pack_kernel(weight_ref, packed_ref):
    modes, kz, _, channels, _ = weight_ref.shape
    for q in range(modes // 4):
        parts = [weight_ref[4 * q + j // 2, :, j % 2] for j in range(8)]
        packed = jnp.concatenate(parts, axis=-1).reshape(kz * channels, 8 * channels)
        packed_ref[q] = packed.astype(BF16)


def ready_kernel(place, field_ref, mix_ref, mix_bias_ref, head_ref, *refs):
    pointwise_ref, head_out_ref, z_doubled_ref = refs
    pointwise_ref[...] = dot_tn(mix_ref[...], field_ref[...]) + mix_bias_ref[...]
    head_out_ref[...] = jnp.transpose(head_ref[...].astype(F32)).astype(BF16)
    z_doubled_ref[...] = place.z_table(True)


def fold_kernel(place, own_ref, got_ref, tables_ref, *refs):
    values = jnp.concatenate([own_ref[...], got_ref[...]], axis=0)
    values = jnp.concatenate([values, values], axis=0)
    partial = dot(tables_ref[...], values).astype(BF16)
    if place.fold:
        shares_ref, send_ref = refs
        write_pieces(place, send_ref, partial, shares_ref[...])
    else:
        refs[0][...] = partial


def mode_kernel(
    place, pieces_ref, y_forward_ref, y_inverse_ref, weight_ref, spectrum_ref, send_ref
):
    kz, channels = place.kz, place.channels
    spectrum = analysed(place, pieces_ref[...], y_forward_ref[...], kz)
    spectrum_ref[...] = spectrum[:, :channels]
    row, lane = grid_of(*spectrum.shape)
    blocked = jnp.where(row % kz == lane // channels, spectrum, 0.0)
    mixed = []
    for q in range(place.modes // 4):
        left = blocked[q * 8 * kz : (q + 1) * 8 * kz].astype(BF16)
        product = dot(left, weight_ref[q])
        for j in range(4):
            own = product[j * 2 * kz : (j + 1) * 2 * kz, j * 2 * channels : (j + 1) * 2 * channels]
            real, imag = own[:, :channels], own[:, channels:]
            mixed.append(real[:kz] - imag[kz:])
            mixed.append(imag[:kz] + real[kz:])
    mode = jnp.concatenate(mixed, axis=0).astype(BF16)
    repeat_rows(send_ref, spread_lines(place, mode, y_inverse_ref[...]))


def part_kernel(place, first, pieces_ref, *refs):
    pieces, shares = read_pieces(place, pieces_ref)
    lines = dot(place.inverse_x(first), pieces)
    height = 2 * MZ
    if shares is None:
        own_ref, send_ref = refs
        own_ref[...] = lines[:height]
        send_ref[...] = lines[height:].astype(BF16)
        return
    _, own_ref, send_ref, sums_ref = refs
    own_ref[...] = lines[:height]
    send_ref[:height] = lines[height:].astype(BF16)
    got = jnp.concatenate(shares, axis=0).astype(BF16)
    channels, narrow = place.channels, place.narrow

    def chosen(part):
        def condition(row, column):
            owner, source = (row % channels) // 2, column // 8
            return (
                (place.listed(owner // narrow, place.firsts[2]) == place.listed(source // narrow, first))
                & (owner % narrow == source % narrow)
                & (column % 8 == 4 * part + 2 * (row // channels) + row % 2)
            )

        return dot(selector(2 * channels, got.shape[0], condition), got)

    high, low = chosen(0), chosen(1)
    sums_ref[...] = high + low
    send_ref[height:] = jnp.concatenate([high, low], axis=1).astype(BF16)


def normal(values):
    scaled = 1.0 / (1.0 + TAIL_SLOPE * jnp.abs(values))
    decay = jnp.exp(-0.5 * values * values)
    tail = TAIL[-1]
    for factor in TAIL[-2::-1]:
        tail = tail * scaled + factor
    tail = tail * (scaled * decay)
    cumulative = jnp.where(values > 0.0, 1.0 - tail, tail)
    return values * cumulative, cumulative + values * (decay * (1.0 / math.sqrt(2.0 * math.pi)))


def cell_kernel(place, *refs):
    own_ref, got_ref, z_table_ref, pointwise_ref, head_ref, head_turned_ref = refs[:6]
    head_bias_ref, out_row_ref, out_column_ref, cotangent_ref = refs[6:10]
    prediction_ref, grad_pre_ref, send_ref, hidden_ref, head_slope_ref = refs[10:]
    rows_y, z_count = place.rows_y, place.z_count
    z_table = z_table_ref[...]
    lines = (own_ref[...] + got_ref[...].astype(F32)).astype(BF16)
    pre_act = side_by_side(dot_tn(lines, z_table), rows_y) + pointwise_ref[...]
    head, head_turned = head_ref[...], head_turned_ref[...]
    head_bias, out_row, out_column = head_bias_ref[...], out_row_ref[...], out_column_ref[...]
    width = 2 * z_count
    slopes, head_pre = [], []
    for first in range(0, rows_y * z_count, width):
        value, slope = normal(pre_act[:, first : first + width])
        hidden = value.astype(BF16)
        hidden_ref[:, first : first + width] = hidden
        slopes.append(slope)
        head_pre.append(dot(head_turned, hidden))
    gradients = []
    for index, first in enumerate(range(0, rows_y, 2)):
        target = jnp.concatenate(
            [cotangent_ref[y : y + 1] for y in range(first, first + 2)], axis=1
        )
        active, slope = normal(head_pre[index] + head_bias)
        predicted = dot(out_row, active.astype(BF16))
        prediction_ref[first : first + 1] = predicted[:, :z_count]
        prediction_ref[first + 1 : first + 2] = predicted[:, z_count:]
        head_slope = (target * out_column * slope).astype(BF16)
        head_slope_ref[:, first * z_count : first * z_count + width] = head_slope
        gradients.append((dot(head, head_slope) * slopes[index]).astype(BF16))
    gradient = jnp.concatenate(gradients, axis=1)
    grad_pre_ref[...] = gradient
    send_ref[...] = dot_nt(z_table, one_below_other(gradient, rows_y)).astype(BF16)


def sums_kernel(place, field_ref, gradient_ref, hidden_ref, head_slope_ref, *refs):
    refs[-1][...] = jnp.concatenate(halves(place.forward_x(place.firsts[2])), axis=1)
    grad_mix = dot_nt(field_ref[...], gradient_ref[...])
    grad_head = dot_nt(hidden_ref[...], head_slope_ref[...])
    if not place.fold:
        refs[0][...] = grad_mix
        refs[1][...] = grad_head
        return
    channels, hidden_units = grad_head.shape
    rest = jnp.zeros((channels, hidden_units - channels), F32)
    wide_mix = jnp.concatenate([grad_mix, rest], axis=1)
    high, low = halves(jnp.concatenate([grad_head, wide_mix], axis=0))
    split = jnp.concatenate([high, low], axis=0)
    place_of = selector(
        8 * place.partners,
        4 * channels,
        lambda row, column: (column % channels == 2 * (row // 8) + row % 2)
        & (column // channels == (row % 8) // 2),
    )
    refs[0][...] = dot(place_of, split).astype(BF16)


def back_kernel(
    place, pieces_ref, y_forward_ref, y_inverse_ref, weight_ref, adjoint_ref, send_ref
):
    kz, channels = place.kz, place.channels
    pieces, shares = read_pieces(place, pieces_ref)
    adjoint = analysed(place, pieces, y_forward_ref[...], 1)
    adjoint_ref[...] = adjoint
    turned = []
    for first in range(0, adjoint.shape[0], 2 * kz):
        turned += [adjoint[first + kz : first + 2 * kz], -adjoint[first : first + kz]]
    left = jnp.concatenate([adjoint, jnp.concatenate(turned, axis=0)], axis=1)
    left = jnp.concatenate([left] * 4, axis=1)
    row, lane = grid_of(*left.shape)
    same = (row // (2 * kz)) % 4 == lane // (2 * channels)
    left = jnp.where(same, left, 0.0).astype(BF16)
    block = 8 * kz
    pulled = [
        dot_nt(left[q * block : (q + 1) * block], weight_ref[q]) for q in range(place.modes // 4)
    ]
    pulled = jnp.concatenate(pulled, axis=0)
    row, lane = grid_of(*pulled.shape)
    pulled = jnp.where(row % kz == lane // channels, pulled, 0.0).astype(BF16)
    gather = selector(
        kz * channels, channels, lambda row, column: row % channels == column
    )
    modes_back = dot(pulled, gather).astype(BF16)
    block = spread_lines(place, modes_back, y_inverse_ref[...])
    if shares is None:
        repeat_rows(send_ref, block)
        return
    total = sum(shares[1:], shares[0])
    high, low = halves(total[0:4] + total[4:8])
    split = jnp.concatenate([high.astype(F32), low.astype(F32)], axis=0)
    write_pieces(place, send_ref, block, split.astype(BF16))


def outer_kernel(spectrum_ref, adjoint_ref, out_ref, done_ref):
    done_ref[...] = jnp.zeros(done_ref.shape, F32)
    modes, kz = out_ref.shape[:2]
    for j in range(modes):
        columns = jnp.transpose(spectrum_ref[j])
        adjoint = adjoint_ref[j]
        for k in range(kz):
            s_real, s_imag = columns[:, k : k + 1], columns[:, kz + k : kz + k + 1]
            a_real, a_imag = adjoint[k : k + 1], adjoint[kz + k : kz + k + 1]
            out_ref[j, k, 0] = s_real * a_real + s_imag * a_imag
            out_ref[j, k, 1] = s_real * a_imag - s_imag * a_real


def pointwise_kernel(place, mix_ref, gradient_ref, out_ref, z_plain_ref, turn_ref):
    z_plain_ref[...] = place.z_table(False)
    turn_ref[...] = turn_matrix(place, False)
    z_count = place.z_count
    product = dot(mix_ref[...], gradient_ref[...])
    for y in range(place.rows_y):
        out_ref[:, y, :] = product[:, y * z_count : (y + 1) * z_count]


def finish_kernel(place, *refs):
    own_ref, got_ref, z_table_ref, turn_ref, pointwise_ref, prediction_ref = refs[:6]
    refs = refs[6:]
    height = 2 * MZ
    channels = place.channels
    lines = (own_ref[...] + got_ref[:height].astype(F32)).astype(BF16)
    lines = dot(lines, turn_ref[...]).astype(BF16)
    pointwise = pointwise_ref[...].reshape(place.lanes, place.z_count)
    grad_field = (dot_tn(lines, z_table_ref[...]) + pointwise).astype(BF16)
    if not place.fold:
        refs[0][...] = grad_field
        refs[1][...] = prediction_ref[...]
        return
    sums_ref, grad_field_ref, out_ref, grad_mix_ref, grad_head_ref = refs
    grad_field_ref[...] = grad_field
    out_ref[...] = prediction_ref[...]
    got = got_ref[height:].astype(F32)
    width = sums_ref.shape[1]
    total = sums_ref[...] + got[:, :width] + got[:, width:]
    grad_head_ref[...] = total[:channels]
    grad_mix_ref[...] = total[channels:, :channels]


def call(kernel, outs, name, **spec):
    return pl.pallas_call(
        kernel,
        out_shape=[jax.ShapeDtypeStruct(shape, dtype) for shape, dtype in outs],
        compiler_params=pltpu.CompilerParams(vmem_limit_bytes=VMEM_LIMIT),
        cost_estimate=pl.CostEstimate(flops=1 << 22, bytes_accessed=1 << 19, transcendentals=0),
        name=name,
        **spec,
    )


def body(
    lifted_field,
    spectral_weight,
    mix_weight,
    mix_bias,
    head_weight,
    head_bias,
    out_weight,
    cotangent,
):
    wide = lax.axis_size("wide")
    narrow = lax.axis_size("narrow")
    devices = wide * narrow
    _, channels, rows_y, z_count = lifted_field.shape
    modes, kz = spectral_weight.shape[:2]
    hidden_units = head_weight.shape[1]
    cells = channels * rows_y
    place = Place(wide, narrow, kz, modes, rows_y, channels, z_count, False)
    place.fold = 2 * place.partners == channels and hidden_units == 128 and cells == 256 and kz % 8 == 0
    height = 2 * MZ
    step = 2 * kz
    partners = place.partners
    mode_lines = modes * 2 * kz

    y_forward, y_inverse = y_tables(rows_y * narrow, rows_y, kz, modes)
    if len(y_forward) > 1:
        block = lax.axis_index("wide") % len(y_forward)
        y_forward = lax.dynamic_index_in_dim(jnp.asarray(y_forward), block, 0, False)
        y_inverse = lax.dynamic_index_in_dim(jnp.asarray(y_inverse), block, 0, False)
    else:
        y_forward, y_inverse = jnp.asarray(y_forward[0]), jnp.asarray(y_inverse[0])

    def to_twin(send):
        pairs = [(p, p ^ narrow) for p in range(devices)]
        return lax.ppermute(send, ("wide", "narrow"), pairs)

    def exchange(send, transform):
        first = place.firsts[transform]
        groups = [
            [
                (2 * place.listed(outer, first) + inner) * narrow + n
                for outer in range(place.outer)
                for n in range(narrow)
            ]
            for inner in range(2)
        ]
        pieces = send.reshape(partners, -1, send.shape[1])
        got = lax.all_to_all(
            pieces, ("wide", "narrow"), 0, 0, axis_index_groups=groups, tiled=True
        )
        return got.reshape(send.shape)

    plain = ((partners * step, cells), BF16)
    shared = ((partners * (2 * step + 8), cells // 2), BF16) if place.fold else plain
    twin_plain = ((height, cells), BF16)
    twin_shared = ((height + 2 * channels, cells), BF16) if place.fold else twin_plain
    sums_shape = ((2 * channels, hidden_units), F32)
    own_lines = ((height, cells), F32)
    across = (channels, rows_y * z_count)

    def run(kernel, outs, name, **spec):
        return call(functools.partial(kernel, place), outs, name, **spec)

    flat_field = lifted_field.reshape(cells, z_count)
    twin_field = to_twin(flat_field)
    field, spectra = run(own_kernel, [(across, BF16), twin_plain], "own")(flat_field)
    (send,) = run(start_kernel, [plain], "start")(spectra, twin_field)
    packed_shape = ((modes // 4, kz * channels, 8 * channels), BF16)
    (weight,) = call(pack_kernel, [packed_shape], "pack")(spectral_weight)
    spectrum, send = run(mode_kernel, [((mode_lines, channels), F32), plain], "mode")(
        exchange(send, 0), y_forward, y_inverse, weight
    )
    part = functools.partial(part_kernel, place, place.firsts[1])
    own, send = call(part, [own_lines, twin_plain], "part")(exchange(send, 1))
    pointwise, head_turned, z_doubled = run(
        ready_kernel,
        [(across, F32), ((hidden_units, channels), BF16), ((height, z_count), BF16)],
        "ready",
    )(field, mix_weight, mix_bias[:, None], head_weight)
    prediction, grad_pre, send, hidden, head_slope = run(
        cell_kernel,
        [
            ((rows_y, z_count), F32),
            (across, BF16),
            twin_plain,
            (across, BF16),
            ((hidden_units, rows_y * z_count), BF16),
        ],
        "cell",
    )(
        own,
        to_twin(send),
        z_doubled,
        pointwise,
        head_weight,
        head_turned,
        head_bias[:, None],
        out_weight[None],
        out_weight.astype(F32)[:, None],
        cotangent[0],
    )
    if place.fold:
        outs = [((8 * partners, hidden_units), BF16)]
    else:
        outs = [((channels, channels), F32), ((channels, hidden_units), F32)]
    outs += [((wide // 2 * height, 4 * height), BF16)]
    *sums, forward = run(sums_kernel, outs, "sums")(field, grad_pre, hidden, head_slope)
    if not place.fold:
        totals = lax.psum(tuple(sums), ("wide", "narrow"))
        sums = []
    (send,) = run(fold_kernel, [shared], "fold")(send, to_twin(send), forward, *sums)
    adjoint, send = run(back_kernel, [((mode_lines, channels), F32), shared], "back")(
        exchange(send, 2), y_forward, y_inverse, weight
    )
    some = max(1, modes // 4)
    grad_spectral, done = pl.pallas_call(
        outer_kernel,
        grid=(modes // some,),
        in_specs=[pl.BlockSpec((some, 2 * kz, channels), lambda j: (j, 0, 0))] * 2,
        out_specs=[
            pl.BlockSpec((some, kz, 2, channels, channels), lambda j: (j, 0, 0, 0, 0)),
            pl.BlockSpec((8, 128), lambda j: (0, 0)),
        ],
        out_shape=[
            jax.ShapeDtypeStruct(spectral_weight.shape, F32),
            jax.ShapeDtypeStruct((8, 128), F32),
        ],
        compiler_params=pltpu.CompilerParams(vmem_limit_bytes=VMEM_LIMIT),
        cost_estimate=pl.CostEstimate(flops=1 << 22, bytes_accessed=5 << 20, transcendentals=0),
        name="outer",
    )(spectrum.reshape(modes, 2 * kz, channels), adjoint.reshape(modes, 2 * kz, channels))
    pointwise, z_plain, turn = run(
        pointwise_kernel,
        [
            ((channels, rows_y, z_count), F32),
            ((height, z_count), BF16),
            ((cells, cells), BF16),
        ],
        "pointwise",
    )(mix_weight, grad_pre)
    outs = [own_lines, twin_shared] + ([sums_shape] if place.fold else [])
    after = (done,) if place.fold else ()
    part = functools.partial(part_kernel, place, place.firsts[3])
    own, send, *sums = call(part, outs, "part")(exchange(send, 3), *after)
    outs = [((cells, z_count), BF16), ((rows_y, z_count), F32)]
    if place.fold:
        outs += [((channels, channels), F32), ((channels, hidden_units), F32)]
    grad_field, prediction, *summed = run(finish_kernel, outs, "finish")(
        own, to_twin(send), z_plain, turn, pointwise, prediction, *sums
    )
    grad_mix, grad_head = summed if place.fold else totals
    return (
        prediction[None],
        grad_field.reshape(lifted_field.shape),
        grad_spectral,
        grad_mix,
        grad_head,
    )


def solution(mesh):
    return jax.shard_map(
        body,
        mesh=mesh,
        in_specs=(
            P("wide", None, "narrow", None),
            P("wide", "narrow", None, None, None),
            P(),
            P(),
            P(),
            P(),
            P(),
            P("wide", "narrow", None),
        ),
        out_specs=(
            P("wide", "narrow", None),
            P("wide", None, "narrow", None),
            P("wide", "narrow", None, None, None),
            P(),
            P(),
        ),
        check_vma=False,
    )
```

```python
import functools
import math

import jax
import jax.numpy as jnp
import numpy as np
from jax import lax
from jax.experimental import pallas as pl
from jax.experimental.pallas import tpu as pltpu
from jax.sharding import PartitionSpec as P

MX = 16
MY = 16
MZ = 16
F32 = jnp.float32
BF16 = jnp.bfloat16
VMEM_LIMIT = 32 * 1024 * 1024

TAIL_SLOPE = 0.275
TAIL = (
    0.11780925840139389,
    0.04211147502064705,
    0.3339323103427887,
    -0.3309934139251709,
    0.4519987106323242,
    -0.11485832929611206,
)


def signed(indices, count):
    return np.where(indices < count // 2, indices, indices - count)


def wave(positions, frequency, length):
    turned = np.mod(np.multiply.outer(positions, frequency), length)
    angles = turned.astype(np.float32) * np.float32(2.0 * math.pi / length)
    scale = np.float32(1.0 / math.sqrt(length))
    return np.cos(angles) * scale, np.sin(angles) * scale


def pair(cosine, sine, sign):
    return np.stack(
        [np.stack([cosine, -sign * sine], -1), np.stack([sign * sine, cosine], -1)], -2
    )


def y_tables(total_y, rows_y, kz, modes):
    cosine, sine = wave(np.arange(total_y), signed(np.arange(MY), MY), total_y)
    narrow = total_y // rows_y
    same = np.eye(kz, dtype=np.float32)
    forward = pair(cosine, sine, -1.0).reshape(narrow, rows_y, MY // modes, modes, 2, 2)
    inverse = pair(cosine, sine, 1.0).reshape(narrow, rows_y, MY // modes, modes, 2, 2)
    forward = np.einsum("nybjtr,kl->bjtkynlr", forward, same)
    inverse = np.einsum("nybjst,kl->bnyksjtl", inverse, same)
    blocks = MY // modes
    forward = forward.reshape(blocks, modes * 2 * kz, rows_y * narrow * kz * 2)
    inverse = inverse.reshape(blocks, narrow * rows_y * kz * 2, modes * 2 * kz)
    return forward.astype(BF16), inverse.astype(BF16)


def dot(a, b):
    return jnp.dot(a, b, preferred_element_type=F32)


def dot_nt(a, b):
    return lax.dot_general(a, b, (((1,), (1,)), ((), ())), preferred_element_type=F32)


def dot_tn(a, b):
    return lax.dot_general(a, b, (((0,), (0,)), ((), ())), preferred_element_type=F32)


def grid_of(rows, columns):
    shape = (rows, columns)
    return lax.broadcasted_iota(jnp.int32, shape, 0), lax.broadcasted_iota(jnp.int32, shape, 1)


def selector(rows, columns, condition):
    return jnp.where(condition(*grid_of(rows, columns)), 1.0, 0.0).astype(BF16)


def halves(values):
    high = values.astype(BF16)
    return high, (values - high.astype(F32)).astype(BF16)


def stacked(refs, lanes=slice(None)):
    return jnp.concatenate([ref[:, lanes] for ref in refs], axis=0)


def cosine_of(phase, length):
    angles = (phase & (length - 1)).astype(F32) * (2.0 * math.pi / length)
    return jnp.cos(angles) * (1.0 / math.sqrt(length))


class Place:
    def __init__(self, wide, narrow, kz, modes, rows_y, channels, z_count, fold):
        self.wide, self.narrow, self.kz, self.modes = wide, narrow, kz, modes
        self.rows_y, self.channels, self.z_count, self.fold = rows_y, channels, z_count, fold
        self.outer = wide // 2
        self.partners = self.outer * narrow
        self.lanes = rows_y * channels
        middle, last = self.outer // 4, self.outer // 2 - 1
        self.lists = ((last, 1), (middle, 0), (middle, 0), (middle, 1))

    def here(self):
        wide = lax.axis_index("wide")
        return wide // 2, wide % 2

    def listed(self, position, transform):
        lines = self.outer // 2
        first, far = self.lists[transform]
        return ((first + position // 2) & (lines - 1)) * 2 + (position % 2 ^ far)

    def turned_narrow(self, transform):
        return self.lists[transform][1] * (self.narrow - 1)

    def in_list_order(self, blocks, transform):
        return blocks[::-1] if self.lists[transform][1] else blocks

    def frequency(self, wide):
        index = (wide * self.modes) // MY
        return jnp.where(index < MX // 2, index, index - MX)

    def z_table(self, doubled):
        row, z = grid_of(2 * MZ, self.z_count)
        frequency = row >> 1
        value = cosine_of(z * frequency + (row & 1) * (self.z_count // 4), self.z_count)
        if doubled:
            value = jnp.where(frequency > 0, 2.0 * value, value)
        return value.astype(BF16)

    def expanded(self, small, transform):
        row, column = grid_of(2 * MZ, small.shape[1])
        turned = self.turned_narrow(transform) * self.kz
        same = ((row >> 1) ^ turned) == ((column >> 1) & (MZ - 1))
        blocks = []
        for g in range(small.shape[0] // 2):
            value = jnp.where((row & 1) == 0, small[2 * g : 2 * g + 1], small[2 * g + 1 : 2 * g + 2])
            blocks.append(jnp.where(same, value, 0.0))
        return jnp.concatenate(blocks, axis=0)

    def forward_x(self, transform):
        outer, inner = self.here()
        row, column = grid_of(2 * self.outer, 4 * MZ)
        x = 2 * outer + (inner ^ (column // (2 * MZ)))
        frequency = self.frequency(2 * self.listed(row >> 1, transform) + inner)
        quarter = self.wide // 4
        small = cosine_of(x * frequency + quarter * ((row & 1) - (column & 1)), self.wide)
        return self.expanded(small, transform)

    def inverse_x(self, transform):
        outer, inner = self.here()
        row, column = grid_of(4, self.outer * 2 * MZ)
        x = 2 * outer + (inner ^ (row >> 1))
        frequency = self.frequency(2 * self.listed(column // (2 * MZ), transform) + inner)
        quarter = self.wide // 4
        small = cosine_of(x * frequency + quarter * ((column & 1) - (row & 1)), self.wide)
        return self.expanded(small, transform).astype(BF16)


def repeat_rows(out_ref, block):
    height = block.shape[0]
    for first in range(0, out_ref.shape[0], height):
        out_ref[first : first + height] = block


def write_pieces(place, send_ref, block, shares):
    step, half = 2 * place.kz, place.lanes // 2
    height = send_ref.shape[0] // place.partners
    for p in range(place.partners):
        own = block[p * step % block.shape[0] :][:step]
        first = p * height
        send_ref[first : first + step] = own[:, :half]
        send_ref[first + step : first + 2 * step] = own[:, half:]
        send_ref[first + 2 * step : first + height] = shares[p * 8 % shares.shape[0] :][:8]


def read_pieces(place, pieces_ref):
    step = 2 * place.kz
    if pieces_ref.shape[1] == place.lanes:
        return pieces_ref[...], None
    height = pieces_ref.shape[0] // place.partners
    blocks, shares = [], []
    for p in range(place.partners):
        first = p * height
        left = pieces_ref[first : first + step]
        right = pieces_ref[first + step : first + 2 * step]
        blocks.append(jnp.concatenate([left, right], axis=1))
        shares.append(pieces_ref[first + 2 * step : first + height].astype(F32))
    return jnp.concatenate(blocks, axis=0), shares


def analysed(place, pieces, y_forward, copies, transform):
    height = 2 * MZ
    turned = sum(
        pieces[first : first + height].astype(F32) for first in range(0, pieces.shape[0], height)
    )
    step = 2 * place.kz
    turned = jnp.concatenate(
        place.in_list_order(
            [turned[first : first + step] for first in range(0, height, step)], transform
        ),
        axis=0,
    )
    channels = place.channels
    lines = jnp.concatenate(
        [turned[:, y * channels : (y + 1) * channels] for y in range(place.rows_y)], axis=0
    )
    return dot(y_forward, jnp.concatenate([lines.astype(BF16)] * copies, axis=1))


def spread_lines(place, modes, y_inverse, transform):
    lines = dot(y_inverse, modes)
    step = 2 * place.kz
    blocks = []
    for n in range(place.narrow):
        first = n * place.rows_y
        parts = [lines[(first + y) * step : (first + y + 1) * step] for y in range(place.rows_y)]
        blocks.append(jnp.concatenate(parts, axis=1))
    return jnp.concatenate(place.in_list_order(blocks, transform), axis=0).astype(BF16)


def turn_matrix(place, forward):
    channels, rows_y = place.channels, place.rows_y

    def same(row, column):
        if forward:
            row, column = column, row
        return (row % channels == column // rows_y) & (row // channels == column % rows_y)

    return selector(place.lanes, place.lanes, same)


def side_by_side(values, count):
    height = values.shape[0] // count
    return jnp.concatenate([values[y * height : (y + 1) * height] for y in range(count)], axis=1)


def one_below_other(values, count):
    width = values.shape[1] // count
    return jnp.concatenate([values[:, y * width : (y + 1) * width] for y in range(count)], axis=0)


def own_kernel(place, field_ref, field_out_ref, spectra_ref):
    turned = dot(turn_matrix(place, False), field_ref[...]).astype(BF16)
    field_out_ref[...] = side_by_side(turned, place.rows_y)
    spectra_ref[...] = dot_nt(place.z_table(False), turned).astype(BF16)


def start_kernel(place, spectra_ref, twin_ref, send_ref):
    twin = dot_nt(place.z_table(False), twin_ref[...]).astype(BF16)
    twin = dot(twin, turn_matrix(place, True)).astype(BF16)
    values = jnp.concatenate([spectra_ref[...], twin], axis=0)
    tables = jnp.concatenate(halves(place.forward_x(0)), axis=1)
    send_ref[...] = dot(tables, jnp.concatenate([values, values], axis=0)).astype(BF16)


def pack_kernel(weight_ref, packed_ref):
    modes, kz, _, channels, _ = weight_ref.shape
    for q in range(modes // 4):
        parts = [weight_ref[4 * q + j // 2, :, j % 2] for j in range(8)]
        packed = jnp.concatenate(parts, axis=-1).reshape(kz * channels, 8 * channels)
        packed_ref[q] = packed.astype(BF16)


def ready_kernel(place, field_ref, mix_ref, mix_bias_ref, head_ref, *refs):
    pointwise_ref, head_out_ref, z_doubled_ref = refs
    pointwise_ref[...] = dot_tn(mix_ref[...], field_ref[...]) + mix_bias_ref[...]
    head_out_ref[...] = jnp.transpose(head_ref[...].astype(F32)).astype(BF16)
    z_doubled_ref[...] = place.z_table(True)


def fold_kernel(place, own_ref, got_ref, tables_ref, *refs):
    values = jnp.concatenate([own_ref[...], got_ref[...]], axis=0)
    values = jnp.concatenate([values, values], axis=0)
    partial = dot(tables_ref[...], values).astype(BF16)
    if place.fold:
        shares_ref, send_ref = refs
        write_pieces(place, send_ref, partial, shares_ref[...])
    else:
        refs[0][...] = partial


def mode_kernel(
    place, pieces_ref, y_forward_ref, y_inverse_ref, weight_ref, spectrum_ref, send_ref
):
    kz, channels = place.kz, place.channels
    spectrum = analysed(place, pieces_ref[...], y_forward_ref[...], kz, 0)
    spectrum_ref[...] = spectrum[:, :channels]
    row, lane = grid_of(*spectrum.shape)
    blocked = jnp.where(row % kz == lane // channels, spectrum, 0.0)
    mixed = []
    for q in range(place.modes // 4):
        left = blocked[q * 8 * kz : (q + 1) * 8 * kz].astype(BF16)
        product = dot(left, weight_ref[q])
        for j in range(4):
            own = product[j * 2 * kz : (j + 1) * 2 * kz, j * 2 * channels : (j + 1) * 2 * channels]
            real, imag = own[:, :channels], own[:, channels:]
            mixed.append(real[:kz] - imag[kz:])
            mixed.append(imag[:kz] + real[kz:])
    mode = jnp.concatenate(mixed, axis=0).astype(BF16)
    repeat_rows(send_ref, spread_lines(place, mode, y_inverse_ref[...], 1))


def part_kernel(place, transform, pieces_ref, *refs):
    pieces, shares = read_pieces(place, pieces_ref)
    lines = dot(place.inverse_x(transform), pieces)
    height = 2 * MZ
    if shares is None:
        own_ref, send_ref = refs
        own_ref[...] = lines[:height]
        send_ref[...] = lines[height:].astype(BF16)
        return
    _, own_ref, send_ref, sums_ref = refs
    own_ref[...] = lines[:height]
    send_ref[:height] = lines[height:].astype(BF16)
    got = jnp.concatenate(shares, axis=0).astype(BF16)
    channels, narrow = place.channels, place.narrow

    def chosen(part):
        def condition(row, column):
            owner, source = (row % channels) // 2, column // 8
            turned = place.turned_narrow(2) ^ place.turned_narrow(transform)
            return (
                (place.listed(owner // narrow, 2) == place.listed(source // narrow, transform))
                & (owner % narrow == (source % narrow) ^ turned)
                & (column % 8 == 4 * part + 2 * (row // channels) + row % 2)
            )

        return dot(selector(2 * channels, got.shape[0], condition), got)

    high, low = chosen(0), chosen(1)
    sums_ref[...] = high + low
    send_ref[height:] = jnp.concatenate([high, low], axis=1).astype(BF16)


def normal(values):
    scaled = 1.0 / (1.0 + TAIL_SLOPE * jnp.abs(values))
    decay = jnp.exp(-0.5 * values * values)
    tail = TAIL[-1]
    for factor in TAIL[-2::-1]:
        tail = tail * scaled + factor
    tail = tail * (scaled * decay)
    cumulative = jnp.where(values > 0.0, 1.0 - tail, tail)
    return values * cumulative, cumulative + values * (decay * (1.0 / math.sqrt(2.0 * math.pi)))


def cell_kernel(place, *refs):
    own_ref, got_ref, z_table_ref, pointwise_ref, head_ref, head_turned_ref = refs[:6]
    head_bias_ref, out_row_ref, out_column_ref, cotangent_ref = refs[6:10]
    prediction_ref, grad_pre_ref, send_ref, hidden_ref, head_slope_ref = refs[10:]
    rows_y, z_count = place.rows_y, place.z_count
    z_table = z_table_ref[...]
    lines = (own_ref[...] + got_ref[...].astype(F32)).astype(BF16)
    pre_act = side_by_side(dot_tn(lines, z_table), rows_y) + pointwise_ref[...]
    head, head_turned = head_ref[...], head_turned_ref[...]
    head_bias, out_row, out_column = head_bias_ref[...], out_row_ref[...], out_column_ref[...]
    width = 2 * z_count
    slopes, head_pre = [], []
    for first in range(0, rows_y * z_count, width):
        value, slope = normal(pre_act[:, first : first + width])
        hidden = value.astype(BF16)
        hidden_ref[:, first : first + width] = hidden
        slopes.append(slope)
        head_pre.append(dot(head_turned, hidden))
    gradients = []
    for index, first in enumerate(range(0, rows_y, 2)):
        target = jnp.concatenate(
            [cotangent_ref[y : y + 1] for y in range(first, first + 2)], axis=1
        )
        active, slope = normal(head_pre[index] + head_bias)
        predicted = dot(out_row, active.astype(BF16))
        prediction_ref[first : first + 1] = predicted[:, :z_count]
        prediction_ref[first + 1 : first + 2] = predicted[:, z_count:]
        head_slope = (target * out_column * slope).astype(BF16)
        head_slope_ref[:, first * z_count : first * z_count + width] = head_slope
        gradients.append((dot(head, head_slope) * slopes[index]).astype(BF16))
    gradient = jnp.concatenate(gradients, axis=1)
    grad_pre_ref[...] = gradient
    send_ref[...] = dot_nt(z_table, one_below_other(gradient, rows_y)).astype(BF16)


def sums_kernel(place, field_ref, gradient_ref, hidden_ref, head_slope_ref, *refs):
    refs[-1][...] = jnp.concatenate(halves(place.forward_x(2)), axis=1)
    grad_mix = dot_nt(field_ref[...], gradient_ref[...])
    grad_head = dot_nt(hidden_ref[...], head_slope_ref[...])
    if not place.fold:
        refs[0][...] = grad_mix
        refs[1][...] = grad_head
        return
    channels, hidden_units = grad_head.shape
    rest = jnp.zeros((channels, hidden_units - channels), F32)
    wide_mix = jnp.concatenate([grad_mix, rest], axis=1)
    high, low = halves(jnp.concatenate([grad_head, wide_mix], axis=0))
    split = jnp.concatenate([high, low], axis=0)
    place_of = selector(
        8 * place.partners,
        4 * channels,
        lambda row, column: (column % channels == 2 * (row // 8) + row % 2)
        & (column // channels == (row % 8) // 2),
    )
    refs[0][...] = dot(place_of, split).astype(BF16)


def back_kernel(
    place, pieces_ref, y_forward_ref, y_inverse_ref, weight_ref, adjoint_ref, send_ref
):
    kz, channels = place.kz, place.channels
    pieces, shares = read_pieces(place, pieces_ref)
    adjoint = analysed(place, pieces, y_forward_ref[...], 1, 2)
    adjoint_ref[...] = adjoint
    turned = []
    for first in range(0, adjoint.shape[0], 2 * kz):
        turned += [adjoint[first + kz : first + 2 * kz], -adjoint[first : first + kz]]
    left = jnp.concatenate([adjoint, jnp.concatenate(turned, axis=0)], axis=1)
    left = jnp.concatenate([left] * 4, axis=1)
    row, lane = grid_of(*left.shape)
    same = (row // (2 * kz)) % 4 == lane // (2 * channels)
    left = jnp.where(same, left, 0.0).astype(BF16)
    block = 8 * kz
    pulled = [
        dot_nt(left[q * block : (q + 1) * block], weight_ref[q]) for q in range(place.modes // 4)
    ]
    pulled = jnp.concatenate(pulled, axis=0)
    row, lane = grid_of(*pulled.shape)
    pulled = jnp.where(row % kz == lane // channels, pulled, 0.0).astype(BF16)
    gather = selector(
        kz * channels, channels, lambda row, column: row % channels == column
    )
    modes_back = dot(pulled, gather).astype(BF16)
    block = spread_lines(place, modes_back, y_inverse_ref[...], 3)
    if shares is None:
        repeat_rows(send_ref, block)
        return
    total = sum(shares[1:], shares[0])
    high, low = halves(total[0:4] + total[4:8])
    split = jnp.concatenate([high.astype(F32), low.astype(F32)], axis=0)
    write_pieces(place, send_ref, block, split.astype(BF16))


def outer_kernel(spectrum_ref, adjoint_ref, out_ref, done_ref):
    done_ref[...] = jnp.zeros(done_ref.shape, F32)
    modes, kz = out_ref.shape[:2]
    for j in range(modes):
        columns = jnp.transpose(spectrum_ref[j])
        adjoint = adjoint_ref[j]
        for k in range(kz):
            s_real, s_imag = columns[:, k : k + 1], columns[:, kz + k : kz + k + 1]
            a_real, a_imag = adjoint[k : k + 1], adjoint[kz + k : kz + k + 1]
            out_ref[j, k, 0] = s_real * a_real + s_imag * a_imag
            out_ref[j, k, 1] = s_real * a_imag - s_imag * a_real


def pointwise_kernel(place, mix_ref, gradient_ref, out_ref, z_plain_ref, turn_ref):
    z_plain_ref[...] = place.z_table(False)
    turn_ref[...] = turn_matrix(place, False)
    z_count = place.z_count
    product = dot(mix_ref[...], gradient_ref[...])
    for y in range(place.rows_y):
        out_ref[:, y, :] = product[:, y * z_count : (y + 1) * z_count]


def finish_kernel(place, *refs):
    own_ref, got_ref, z_table_ref, turn_ref, pointwise_ref, prediction_ref = refs[:6]
    refs = refs[6:]
    height = 2 * MZ
    channels = place.channels
    lines = (own_ref[...] + got_ref[:height].astype(F32)).astype(BF16)
    lines = dot(lines, turn_ref[...]).astype(BF16)
    pointwise = pointwise_ref[...].reshape(place.lanes, place.z_count)
    grad_field = (dot_tn(lines, z_table_ref[...]) + pointwise).astype(BF16)
    if not place.fold:
        refs[0][...] = grad_field
        refs[1][...] = prediction_ref[...]
        return
    sums_ref, grad_field_ref, out_ref, grad_mix_ref, grad_head_ref = refs
    grad_field_ref[...] = grad_field
    out_ref[...] = prediction_ref[...]
    got = got_ref[height:].astype(F32)
    width = sums_ref.shape[1]
    total = sums_ref[...] + got[:, :width] + got[:, width:]
    grad_head_ref[...] = total[:channels]
    grad_mix_ref[...] = total[channels:, :channels]


def call(kernel, outs, name, **spec):
    return pl.pallas_call(
        kernel,
        out_shape=[jax.ShapeDtypeStruct(shape, dtype) for shape, dtype in outs],
        compiler_params=pltpu.CompilerParams(vmem_limit_bytes=VMEM_LIMIT),
        cost_estimate=pl.CostEstimate(flops=1 << 22, bytes_accessed=1 << 19, transcendentals=0),
        name=name,
        **spec,
    )


def body(
    lifted_field,
    spectral_weight,
    mix_weight,
    mix_bias,
    head_weight,
    head_bias,
    out_weight,
    cotangent,
):
    wide = lax.axis_size("wide")
    narrow = lax.axis_size("narrow")
    devices = wide * narrow
    _, channels, rows_y, z_count = lifted_field.shape
    modes, kz = spectral_weight.shape[:2]
    hidden_units = head_weight.shape[1]
    cells = channels * rows_y
    place = Place(wide, narrow, kz, modes, rows_y, channels, z_count, False)
    place.fold = 2 * place.partners == channels and hidden_units == 128 and cells == 256 and kz % 8 == 0
    height = 2 * MZ
    step = 2 * kz
    partners = place.partners
    mode_lines = modes * 2 * kz

    y_forward, y_inverse = y_tables(rows_y * narrow, rows_y, kz, modes)
    if len(y_forward) > 1:
        block = lax.axis_index("wide") % len(y_forward)
        y_forward = lax.dynamic_index_in_dim(jnp.asarray(y_forward), block, 0, False)
        y_inverse = lax.dynamic_index_in_dim(jnp.asarray(y_inverse), block, 0, False)
    else:
        y_forward, y_inverse = jnp.asarray(y_forward[0]), jnp.asarray(y_inverse[0])

    def to_twin(send):
        pairs = [(p, p ^ narrow) for p in range(devices)]
        return lax.ppermute(send, ("wide", "narrow"), pairs)

    def exchange(send, transform):
        turned = place.turned_narrow(transform)
        groups = [
            [
                (2 * place.listed(outer, transform) + inner) * narrow + (n ^ turned)
                for outer in range(place.outer)
                for n in range(narrow)
            ]
            for inner in range(2)
        ]
        pieces = send.reshape(partners, -1, send.shape[1])
        got = lax.all_to_all(
            pieces, ("wide", "narrow"), 0, 0, axis_index_groups=groups, tiled=True
        )
        return got.reshape(send.shape)

    plain = ((partners * step, cells), BF16)
    shared = ((partners * (2 * step + 8), cells // 2), BF16) if place.fold else plain
    twin_plain = ((height, cells), BF16)
    twin_shared = ((height + 2 * channels, cells), BF16) if place.fold else twin_plain
    sums_shape = ((2 * channels, hidden_units), F32)
    own_lines = ((height, cells), F32)
    across = (channels, rows_y * z_count)

    def run(kernel, outs, name, **spec):
        return call(functools.partial(kernel, place), outs, name, **spec)

    flat_field = lifted_field.reshape(cells, z_count)
    twin_field = to_twin(flat_field)
    field, spectra = run(own_kernel, [(across, BF16), twin_plain], "own")(flat_field)
    (send,) = run(start_kernel, [plain], "start")(spectra, twin_field)
    packed_shape = ((modes // 4, kz * channels, 8 * channels), BF16)
    (weight,) = call(pack_kernel, [packed_shape], "pack")(spectral_weight)
    spectrum, send = run(mode_kernel, [((mode_lines, channels), F32), plain], "mode")(
        exchange(send, 0), y_forward, y_inverse, weight
    )
    part = functools.partial(part_kernel, place, 1)
    own, send = call(part, [own_lines, twin_plain], "part")(exchange(send, 1))
    pointwise, head_turned, z_doubled = run(
        ready_kernel,
        [(across, F32), ((hidden_units, channels), BF16), ((height, z_count), BF16)],
        "ready",
    )(field, mix_weight, mix_bias[:, None], head_weight)
    prediction, grad_pre, send, hidden, head_slope = run(
        cell_kernel,
        [
            ((rows_y, z_count), F32),
            (across, BF16),
            twin_plain,
            (across, BF16),
            ((hidden_units, rows_y * z_count), BF16),
        ],
        "cell",
    )(
        own,
        to_twin(send),
        z_doubled,
        pointwise,
        head_weight,
        head_turned,
        head_bias[:, None],
        out_weight[None],
        out_weight.astype(F32)[:, None],
        cotangent[0],
    )
    if place.fold:
        outs = [((8 * partners, hidden_units), BF16)]
    else:
        outs = [((channels, channels), F32), ((channels, hidden_units), F32)]
    outs += [((wide // 2 * height, 4 * height), BF16)]
    *sums, forward = run(sums_kernel, outs, "sums")(field, grad_pre, hidden, head_slope)
    if not place.fold:
        totals = lax.psum(tuple(sums), ("wide", "narrow"))
        sums = []
    (send,) = run(fold_kernel, [shared], "fold")(send, to_twin(send), forward, *sums)
    adjoint, send = run(back_kernel, [((mode_lines, channels), F32), shared], "back")(
        exchange(send, 2), y_forward, y_inverse, weight
    )
    some = max(1, modes // 4)
    grad_spectral, done = pl.pallas_call(
        outer_kernel,
        grid=(modes // some,),
        in_specs=[pl.BlockSpec((some, 2 * kz, channels), lambda j: (j, 0, 0))] * 2,
        out_specs=[
            pl.BlockSpec((some, kz, 2, channels, channels), lambda j: (j, 0, 0, 0, 0)),
            pl.BlockSpec((8, 128), lambda j: (0, 0)),
        ],
        out_shape=[
            jax.ShapeDtypeStruct(spectral_weight.shape, F32),
            jax.ShapeDtypeStruct((8, 128), F32),
        ],
        compiler_params=pltpu.CompilerParams(vmem_limit_bytes=VMEM_LIMIT),
        cost_estimate=pl.CostEstimate(flops=1 << 22, bytes_accessed=5 << 20, transcendentals=0),
        name="outer",
    )(spectrum.reshape(modes, 2 * kz, channels), adjoint.reshape(modes, 2 * kz, channels))
    pointwise, z_plain, turn = run(
        pointwise_kernel,
        [
            ((channels, rows_y, z_count), F32),
            ((height, z_count), BF16),
            ((cells, cells), BF16),
        ],
        "pointwise",
    )(mix_weight, grad_pre)
    outs = [own_lines, twin_shared] + ([sums_shape] if place.fold else [])
    after = (done,) if place.fold else ()
    part = functools.partial(part_kernel, place, 3)
    own, send, *sums = call(part, outs, "part")(exchange(send, 3), *after)
    outs = [((cells, z_count), BF16), ((rows_y, z_count), F32)]
    if place.fold:
        outs += [((channels, channels), F32), ((channels, hidden_units), F32)]
    grad_field, prediction, *summed = run(finish_kernel, outs, "finish")(
        own, to_twin(send), z_plain, turn, pointwise, prediction, *sums
    )
    grad_mix, grad_head = summed if place.fold else totals
    return (
        prediction[None],
        grad_field.reshape(lifted_field.shape),
        grad_spectral,
        grad_mix,
        grad_head,
    )


def solution(mesh):
    return jax.shard_map(
        body,
        mesh=mesh,
        in_specs=(
            P("wide", None, "narrow", None),
            P("wide", "narrow", None, None, None),
            P(),
            P(),
            P(),
            P(),
            P(),
            P("wide", "narrow", None),
        ),
        out_specs=(
            P("wide", "narrow", None),
            P("wide", None, "narrow", None),
            P("wide", "narrow", None, None, None),
            P(),
            P(),
        ),
        check_vma=False,
    )
```

```python
import functools
import math

import jax
import jax.numpy as jnp
import numpy as np
from jax import lax
from jax.experimental import pallas as pl
from jax.experimental.pallas import tpu as pltpu
from jax.sharding import PartitionSpec as P

MX = 16
MY = 16
MZ = 16
F32 = jnp.float32
BF16 = jnp.bfloat16
VMEM_LIMIT = 32 * 1024 * 1024

TAIL_SLOPE = 0.275
TAIL = (
    0.11780925840139389,
    0.04211147502064705,
    0.3339323103427887,
    -0.3309934139251709,
    0.4519987106323242,
    -0.11485832929611206,
)


def signed(indices, count):
    return np.where(indices < count // 2, indices, indices - count)


def wave(positions, frequency, length):
    turned = np.mod(np.multiply.outer(positions, frequency), length)
    angles = turned.astype(np.float32) * np.float32(2.0 * math.pi / length)
    scale = np.float32(1.0 / math.sqrt(length))
    return np.cos(angles) * scale, np.sin(angles) * scale


def pair(cosine, sine, sign):
    return np.stack(
        [np.stack([cosine, -sign * sine], -1), np.stack([sign * sine, cosine], -1)], -2
    )


def y_tables(total_y, rows_y, kz, modes):
    cosine, sine = wave(np.arange(total_y), signed(np.arange(MY), MY), total_y)
    narrow = total_y // rows_y
    same = np.eye(kz, dtype=np.float32)
    forward = pair(cosine, sine, -1.0).reshape(narrow, rows_y, MY // modes, modes, 2, 2)
    inverse = pair(cosine, sine, 1.0).reshape(narrow, rows_y, MY // modes, modes, 2, 2)
    forward = np.einsum("nybjtr,kl->bjtkynlr", forward, same)
    inverse = np.einsum("nybjst,kl->bnyksjtl", inverse, same)
    blocks = MY // modes
    forward = forward.reshape(blocks, modes * 2 * kz, rows_y * narrow * kz * 2)
    inverse = inverse.reshape(blocks, narrow * rows_y * kz * 2, modes * 2 * kz)
    return forward.astype(BF16), inverse.astype(BF16)


def dot(a, b):
    return jnp.dot(a, b, preferred_element_type=F32)


def dot_nt(a, b):
    return lax.dot_general(a, b, (((1,), (1,)), ((), ())), preferred_element_type=F32)


def dot_tn(a, b):
    return lax.dot_general(a, b, (((0,), (0,)), ((), ())), preferred_element_type=F32)


def grid_of(rows, columns):
    shape = (rows, columns)
    return lax.broadcasted_iota(jnp.int32, shape, 0), lax.broadcasted_iota(jnp.int32, shape, 1)


def selector(rows, columns, condition):
    return jnp.where(condition(*grid_of(rows, columns)), 1.0, 0.0).astype(BF16)


def halves(values):
    high = values.astype(BF16)
    return high, (values - high.astype(F32)).astype(BF16)


def stacked(refs, lanes=slice(None)):
    return jnp.concatenate([ref[:, lanes] for ref in refs], axis=0)


def cosine_of(phase, length):
    angles = (phase & (length - 1)).astype(F32) * (2.0 * math.pi / length)
    return jnp.cos(angles) * (1.0 / math.sqrt(length))


class Place:
    def __init__(self, wide, narrow, kz, modes, rows_y, channels, z_count, fold):
        self.wide, self.narrow, self.kz, self.modes = wide, narrow, kz, modes
        self.rows_y, self.channels, self.z_count, self.fold = rows_y, channels, z_count, fold
        self.outer = wide // 2
        self.partners = self.outer * narrow
        self.lanes = rows_y * channels
        self.along = kz % 8 == 0
        middle, last = self.outer // 4, self.outer // 2 - 1
        self.firsts = (last, middle, middle, middle)

    def here(self):
        wide = lax.axis_index("wide")
        return wide // 2, wide % 2

    def listed(self, position, first):
        lines = self.outer // 2
        if self.along:
            line, rest = position % lines, position // lines
            return ((first + line) & (lines - 1)) * 2 + rest // self.narrow, rest % self.narrow
        line, rest = position // (2 * self.narrow), position % (2 * self.narrow)
        return ((first + line) & (lines - 1)) * 2 + rest // self.narrow, rest % self.narrow

    def frequency(self, wide):
        index = (wide * self.modes) // MY
        return jnp.where(index < MX // 2, index, index - MX)

    def z_table(self, doubled):
        row, z = grid_of(2 * MZ, self.z_count)
        frequency = row >> 1
        value = cosine_of(z * frequency + (row & 1) * (self.z_count // 4), self.z_count)
        if doubled:
            value = jnp.where(frequency > 0, 2.0 * value, value)
        return value.astype(BF16)

    def forward_x(self, first):
        outer, inner = self.here()
        step, quarter = 2 * self.kz, self.wide // 4
        row, column = grid_of(2 * self.partners, 4 * MZ)
        x = 2 * outer + (inner ^ (column // (2 * MZ)))
        frequency = self.frequency(2 * self.listed(row >> 1, first)[0] + inner)
        small = cosine_of(x * frequency + quarter * ((row & 1) - (column & 1)), self.wide)
        row, column = grid_of(step, 4 * MZ)
        blocks = []
        for p in range(self.partners):
            _, narrow = self.listed(p, first)
            same = narrow * self.kz + (row >> 1) == ((column >> 1) & (MZ - 1))
            value = jnp.where((row & 1) == 0, small[2 * p : 2 * p + 1], small[2 * p + 1 : 2 * p + 2])
            blocks.append(jnp.where(same, value, 0.0))
        return jnp.concatenate(blocks, axis=0)

    def inverse_x(self, first):
        outer, inner = self.here()
        step, quarter = 2 * self.kz, self.wide // 4
        row, column = grid_of(4, self.partners * step)
        x = 2 * outer + (inner ^ (row >> 1))
        frequency = self.frequency(2 * self.listed(column // step, first)[0] + inner)
        small = cosine_of(x * frequency + quarter * ((column & 1) - (row & 1)), self.wide)
        row, column = grid_of(2 * MZ, self.partners * step)
        narrow = self.listed(column // step, first)[1]
        same = (row >> 1) == narrow * self.kz + (column >> 1) % self.kz
        blocks = []
        for g in range(2):
            value = jnp.where((row & 1) == 0, small[2 * g : 2 * g + 1], small[2 * g + 1 : 2 * g + 2])
            blocks.append(jnp.where(same, value, 0.0))
        return jnp.concatenate(blocks, axis=0).astype(BF16)


def repeat_rows(place, out_ref, block, first):
    step, height = 2 * place.kz, block.shape[0]
    if not place.along:
        for start in range(0, out_ref.shape[0], height):
            out_ref[start : start + height] = block
        return
    for p in range(place.partners):
        _, narrow = place.listed(p, first)
        out_ref[p * step : (p + 1) * step] = block[narrow * step : (narrow + 1) * step]


def write_pieces(place, send_ref, block, shares, first=None):
    step, half = 2 * place.kz, place.lanes // 2
    height = send_ref.shape[0] // place.partners
    for p in range(place.partners):
        index = p if first is None else place.listed(p, first)[1]
        own = block[index * step : (index + 1) * step]
        start = p * height
        send_ref[start : start + step] = own[:, :half]
        send_ref[start + step : start + 2 * step] = own[:, half:]
        send_ref[start + 2 * step : start + height] = shares[p * 8 % shares.shape[0] :][:8]


def read_pieces(place, pieces_ref):
    step = 2 * place.kz
    if pieces_ref.shape[1] == place.lanes:
        return pieces_ref[...], None
    height = pieces_ref.shape[0] // place.partners
    blocks, shares = [], []
    for p in range(place.partners):
        first = p * height
        left = pieces_ref[first : first + step]
        right = pieces_ref[first + step : first + 2 * step]
        blocks.append(jnp.concatenate([left, right], axis=1))
        shares.append(pieces_ref[first + 2 * step : first + height].astype(F32))
    return jnp.concatenate(blocks, axis=0), shares


def analysed(place, pieces, y_forward, copies, first):
    if place.along:
        step = 2 * place.kz
        halves_of = [[] for _ in range(place.narrow)]
        for p in range(place.partners):
            part = pieces[p * step : (p + 1) * step].astype(F32)
            halves_of[place.listed(p, first)[1]].append(part)
        turned = jnp.concatenate([sum(parts[1:], parts[0]) for parts in halves_of], axis=0)
    else:
        height = 2 * MZ
        turned = sum(
            pieces[start : start + height].astype(F32) for start in range(0, pieces.shape[0], height)
        )
    channels = place.channels
    lines = jnp.concatenate(
        [turned[:, y * channels : (y + 1) * channels] for y in range(place.rows_y)], axis=0
    )
    return dot(y_forward, jnp.concatenate([lines.astype(BF16)] * copies, axis=1))


def spread_lines(place, modes, y_inverse):
    lines = dot(y_inverse, modes)
    step = 2 * place.kz
    blocks = []
    for n in range(place.narrow):
        first = n * place.rows_y
        parts = [lines[(first + y) * step : (first + y + 1) * step] for y in range(place.rows_y)]
        blocks.append(jnp.concatenate(parts, axis=1))
    return jnp.concatenate(blocks, axis=0).astype(BF16)


def turn_matrix(place, forward):
    channels, rows_y = place.channels, place.rows_y

    def same(row, column):
        if forward:
            row, column = column, row
        return (row % channels == column // rows_y) & (row // channels == column % rows_y)

    return selector(place.lanes, place.lanes, same)


def side_by_side(values, count):
    height = values.shape[0] // count
    return jnp.concatenate([values[y * height : (y + 1) * height] for y in range(count)], axis=1)


def one_below_other(values, count):
    width = values.shape[1] // count
    return jnp.concatenate([values[:, y * width : (y + 1) * width] for y in range(count)], axis=0)


def own_kernel(place, field_ref, field_out_ref, spectra_ref):
    turned = dot(turn_matrix(place, False), field_ref[...]).astype(BF16)
    field_out_ref[...] = side_by_side(turned, place.rows_y)
    spectra_ref[...] = dot_nt(place.z_table(False), turned).astype(BF16)


def start_kernel(place, spectra_ref, twin_ref, send_ref):
    twin = dot_nt(place.z_table(False), twin_ref[...]).astype(BF16)
    twin = dot(twin, turn_matrix(place, True)).astype(BF16)
    values = jnp.concatenate([spectra_ref[...], twin], axis=0)
    tables = jnp.concatenate(halves(place.forward_x(place.firsts[0])), axis=1)
    send_ref[...] = dot(tables, jnp.concatenate([values, values], axis=0)).astype(BF16)


def pack_kernel(weight_ref, packed_ref):
    modes, kz, _, channels, _ = weight_ref.shape
    for q in range(modes // 4):
        parts = [weight_ref[4 * q + j // 2, :, j % 2] for j in range(8)]
        packed = jnp.concatenate(parts, axis=-1).reshape(kz * channels, 8 * channels)
        packed_ref[q] = packed.astype(BF16)


def ready_kernel(place, field_ref, mix_ref, mix_bias_ref, head_ref, *refs):
    pointwise_ref, head_out_ref, z_doubled_ref = refs
    pointwise_ref[...] = dot_tn(mix_ref[...], field_ref[...]) + mix_bias_ref[...]
    head_out_ref[...] = jnp.transpose(head_ref[...].astype(F32)).astype(BF16)
    z_doubled_ref[...] = place.z_table(True)


def fold_kernel(place, own_ref, got_ref, tables_ref, *refs):
    values = jnp.concatenate([own_ref[...], got_ref[...]], axis=0)
    values = jnp.concatenate([values, values], axis=0)
    partial = dot(tables_ref[...], values).astype(BF16)
    if place.fold:
        shares_ref, send_ref = refs
        write_pieces(place, send_ref, partial, shares_ref[...])
    else:
        refs[0][...] = partial


def mode_kernel(
    place, pieces_ref, y_forward_ref, y_inverse_ref, weight_ref, spectrum_ref, send_ref
):
    kz, channels = place.kz, place.channels
    spectrum = analysed(place, pieces_ref[...], y_forward_ref[...], kz, place.firsts[0])
    spectrum_ref[...] = spectrum[:, :channels]
    row, lane = grid_of(*spectrum.shape)
    blocked = jnp.where(row % kz == lane // channels, spectrum, 0.0)
    mixed = []
    for q in range(place.modes // 4):
        left = blocked[q * 8 * kz : (q + 1) * 8 * kz].astype(BF16)
        product = dot(left, weight_ref[q])
        for j in range(4):
            own = product[j * 2 * kz : (j + 1) * 2 * kz, j * 2 * channels : (j + 1) * 2 * channels]
            real, imag = own[:, :channels], own[:, channels:]
            mixed.append(real[:kz] - imag[kz:])
            mixed.append(imag[:kz] + real[kz:])
    mode = jnp.concatenate(mixed, axis=0).astype(BF16)
    repeat_rows(place, send_ref, spread_lines(place, mode, y_inverse_ref[...]), place.firsts[1])


def part_kernel(place, first, pieces_ref, *refs):
    pieces, shares = read_pieces(place, pieces_ref)
    lines = dot(place.inverse_x(first), pieces)
    height = 2 * MZ
    if shares is None:
        own_ref, send_ref = refs
        own_ref[...] = lines[:height]
        send_ref[...] = lines[height:].astype(BF16)
        return
    _, own_ref, send_ref, sums_ref = refs
    own_ref[...] = lines[:height]
    send_ref[:height] = lines[height:].astype(BF16)
    got = jnp.concatenate(shares, axis=0).astype(BF16)
    channels = place.channels

    def chosen(part):
        def condition(row, column):
            owner = place.listed((row % channels) // 2, place.firsts[2])
            source = place.listed(column // 8, first)
            return (
                (owner[0] == source[0])
                & (owner[1] == source[1])
                & (column % 8 == 4 * part + 2 * (row // channels) + row % 2)
            )

        return dot(selector(2 * channels, got.shape[0], condition), got)

    high, low = chosen(0), chosen(1)
    sums_ref[...] = high + low
    send_ref[height:] = jnp.concatenate([high, low], axis=1).astype(BF16)


def normal(values):
    scaled = 1.0 / (1.0 + TAIL_SLOPE * jnp.abs(values))
    decay = jnp.exp(-0.5 * values * values)
    tail = TAIL[-1]
    for factor in TAIL[-2::-1]:
        tail = tail * scaled + factor
    tail = tail * (scaled * decay)
    cumulative = jnp.where(values > 0.0, 1.0 - tail, tail)
    return values * cumulative, cumulative + values * (decay * (1.0 / math.sqrt(2.0 * math.pi)))


def cell_kernel(place, *refs):
    own_ref, got_ref, z_table_ref, pointwise_ref, head_ref, head_turned_ref = refs[:6]
    head_bias_ref, out_row_ref, out_column_ref, cotangent_ref = refs[6:10]
    prediction_ref, grad_pre_ref, send_ref, hidden_ref, head_slope_ref = refs[10:]
    rows_y, z_count = place.rows_y, place.z_count
    z_table = z_table_ref[...]
    lines = (own_ref[...] + got_ref[...].astype(F32)).astype(BF16)
    pre_act = side_by_side(dot_tn(lines, z_table), rows_y) + pointwise_ref[...]
    head, head_turned = head_ref[...], head_turned_ref[...]
    head_bias, out_row, out_column = head_bias_ref[...], out_row_ref[...], out_column_ref[...]
    width = 2 * z_count
    slopes, head_pre = [], []
    for first in range(0, rows_y * z_count, width):
        value, slope = normal(pre_act[:, first : first + width])
        hidden = value.astype(BF16)
        hidden_ref[:, first : first + width] = hidden
        slopes.append(slope)
        head_pre.append(dot(head_turned, hidden))
    gradients = []
    for index, first in enumerate(range(0, rows_y, 2)):
        target = jnp.concatenate(
            [cotangent_ref[y : y + 1] for y in range(first, first + 2)], axis=1
        )
        active, slope = normal(head_pre[index] + head_bias)
        predicted = dot(out_row, active.astype(BF16))
        prediction_ref[first : first + 1] = predicted[:, :z_count]
        prediction_ref[first + 1 : first + 2] = predicted[:, z_count:]
        head_slope = (target * out_column * slope).astype(BF16)
        head_slope_ref[:, first * z_count : first * z_count + width] = head_slope
        gradients.append((dot(head, head_slope) * slopes[index]).astype(BF16))
    gradient = jnp.concatenate(gradients, axis=1)
    grad_pre_ref[...] = gradient
    send_ref[...] = dot_nt(z_table, one_below_other(gradient, rows_y)).astype(BF16)


def sums_kernel(place, field_ref, gradient_ref, hidden_ref, head_slope_ref, *refs):
    refs[-1][...] = jnp.concatenate(halves(place.forward_x(place.firsts[2])), axis=1)
    grad_mix = dot_nt(field_ref[...], gradient_ref[...])
    grad_head = dot_nt(hidden_ref[...], head_slope_ref[...])
    if not place.fold:
        refs[0][...] = grad_mix
        refs[1][...] = grad_head
        return
    channels, hidden_units = grad_head.shape
    rest = jnp.zeros((channels, hidden_units - channels), F32)
    wide_mix = jnp.concatenate([grad_mix, rest], axis=1)
    high, low = halves(jnp.concatenate([grad_head, wide_mix], axis=0))
    split = jnp.concatenate([high, low], axis=0)
    place_of = selector(
        8 * place.partners,
        4 * channels,
        lambda row, column: (column % channels == 2 * (row // 8) + row % 2)
        & (column // channels == (row % 8) // 2),
    )
    refs[0][...] = dot(place_of, split).astype(BF16)


def back_kernel(
    place, pieces_ref, y_forward_ref, y_inverse_ref, weight_ref, adjoint_ref, send_ref
):
    kz, channels = place.kz, place.channels
    pieces, shares = read_pieces(place, pieces_ref)
    adjoint = analysed(place, pieces, y_forward_ref[...], 1, place.firsts[2])
    adjoint_ref[...] = adjoint
    turned = []
    for first in range(0, adjoint.shape[0], 2 * kz):
        turned += [adjoint[first + kz : first + 2 * kz], -adjoint[first : first + kz]]
    left = jnp.concatenate([adjoint, jnp.concatenate(turned, axis=0)], axis=1)
    left = jnp.concatenate([left] * 4, axis=1)
    row, lane = grid_of(*left.shape)
    same = (row // (2 * kz)) % 4 == lane // (2 * channels)
    left = jnp.where(same, left, 0.0).astype(BF16)
    block = 8 * kz
    pulled = [
        dot_nt(left[q * block : (q + 1) * block], weight_ref[q]) for q in range(place.modes // 4)
    ]
    pulled = jnp.concatenate(pulled, axis=0)
    row, lane = grid_of(*pulled.shape)
    pulled = jnp.where(row % kz == lane // channels, pulled, 0.0).astype(BF16)
    gather = selector(
        kz * channels, channels, lambda row, column: row % channels == column
    )
    modes_back = dot(pulled, gather).astype(BF16)
    block = spread_lines(place, modes_back, y_inverse_ref[...])
    if shares is None:
        repeat_rows(place, send_ref, block, place.firsts[3])
        return
    total = sum(shares[1:], shares[0])
    high, low = halves(total[0:4] + total[4:8])
    split = jnp.concatenate([high.astype(F32), low.astype(F32)], axis=0)
    write_pieces(place, send_ref, block, split.astype(BF16), place.firsts[3])


def outer_kernel(spectrum_ref, adjoint_ref, out_ref, done_ref):
    done_ref[...] = jnp.zeros(done_ref.shape, F32)
    modes, kz = out_ref.shape[:2]
    for j in range(modes):
        columns = jnp.transpose(spectrum_ref[j])
        adjoint = adjoint_ref[j]
        for k in range(kz):
            s_real, s_imag = columns[:, k : k + 1], columns[:, kz + k : kz + k + 1]
            a_real, a_imag = adjoint[k : k + 1], adjoint[kz + k : kz + k + 1]
            out_ref[j, k, 0] = s_real * a_real + s_imag * a_imag
            out_ref[j, k, 1] = s_real * a_imag - s_imag * a_real


def pointwise_kernel(place, mix_ref, gradient_ref, out_ref, z_plain_ref, turn_ref):
    z_plain_ref[...] = place.z_table(False)
    turn_ref[...] = turn_matrix(place, False)
    z_count = place.z_count
    product = dot(mix_ref[...], gradient_ref[...])
    for y in range(place.rows_y):
        out_ref[:, y, :] = product[:, y * z_count : (y + 1) * z_count]


def finish_kernel(place, *refs):
    own_ref, got_ref, z_table_ref, turn_ref, pointwise_ref, prediction_ref = refs[:6]
    refs = refs[6:]
    height = 2 * MZ
    channels = place.channels
    lines = (own_ref[...] + got_ref[:height].astype(F32)).astype(BF16)
    lines = dot(lines, turn_ref[...]).astype(BF16)
    pointwise = pointwise_ref[...].reshape(place.lanes, place.z_count)
    grad_field = (dot_tn(lines, z_table_ref[...]) + pointwise).astype(BF16)
    if not place.fold:
        refs[0][...] = grad_field
        refs[1][...] = prediction_ref[...]
        return
    sums_ref, grad_field_ref, out_ref, grad_mix_ref, grad_head_ref = refs
    grad_field_ref[...] = grad_field
    out_ref[...] = prediction_ref[...]
    got = got_ref[height:].astype(F32)
    width = sums_ref.shape[1]
    total = sums_ref[...] + got[:, :width] + got[:, width:]
    grad_head_ref[...] = total[:channels]
    grad_mix_ref[...] = total[channels:, :channels]


def call(kernel, outs, name, **spec):
    return pl.pallas_call(
        kernel,
        out_shape=[jax.ShapeDtypeStruct(shape, dtype) for shape, dtype in outs],
        compiler_params=pltpu.CompilerParams(vmem_limit_bytes=VMEM_LIMIT),
        cost_estimate=pl.CostEstimate(flops=1 << 22, bytes_accessed=1 << 19, transcendentals=0),
        name=name,
        **spec,
    )


def body(
    lifted_field,
    spectral_weight,
    mix_weight,
    mix_bias,
    head_weight,
    head_bias,
    out_weight,
    cotangent,
):
    wide = lax.axis_size("wide")
    narrow = lax.axis_size("narrow")
    devices = wide * narrow
    _, channels, rows_y, z_count = lifted_field.shape
    modes, kz = spectral_weight.shape[:2]
    hidden_units = head_weight.shape[1]
    cells = channels * rows_y
    place = Place(wide, narrow, kz, modes, rows_y, channels, z_count, False)
    place.fold = 2 * place.partners == channels and hidden_units == 128 and cells == 256 and kz % 8 == 0
    height = 2 * MZ
    step = 2 * kz
    partners = place.partners
    mode_lines = modes * 2 * kz

    y_forward, y_inverse = y_tables(rows_y * narrow, rows_y, kz, modes)
    if len(y_forward) > 1:
        block = lax.axis_index("wide") % len(y_forward)
        y_forward = lax.dynamic_index_in_dim(jnp.asarray(y_forward), block, 0, False)
        y_inverse = lax.dynamic_index_in_dim(jnp.asarray(y_inverse), block, 0, False)
    else:
        y_forward, y_inverse = jnp.asarray(y_forward[0]), jnp.asarray(y_inverse[0])

    def to_twin(send):
        pairs = [(p, p ^ narrow) for p in range(devices)]
        return lax.ppermute(send, ("wide", "narrow"), pairs)

    def exchange(send, transform):
        first = place.firsts[transform]
        listed = [place.listed(p, first) for p in range(partners)]
        groups = [[(2 * outer + inner) * narrow + n for outer, n in listed] for inner in range(2)]
        pieces = send.reshape(partners, -1, send.shape[1])
        got = lax.all_to_all(
            pieces, ("wide", "narrow"), 0, 0, axis_index_groups=groups, tiled=True
        )
        return got.reshape(send.shape)

    plain = ((partners * step, cells), BF16)
    shared = ((partners * (2 * step + 8), cells // 2), BF16) if place.fold else plain
    twin_plain = ((height, cells), BF16)
    twin_shared = ((height + 2 * channels, cells), BF16) if place.fold else twin_plain
    sums_shape = ((2 * channels, hidden_units), F32)
    own_lines = ((height, cells), F32)
    across = (channels, rows_y * z_count)

    def run(kernel, outs, name, **spec):
        return call(functools.partial(kernel, place), outs, name, **spec)

    flat_field = lifted_field.reshape(cells, z_count)
    twin_field = to_twin(flat_field)
    field, spectra = run(own_kernel, [(across, BF16), twin_plain], "own")(flat_field)
    (send,) = run(start_kernel, [plain], "start")(spectra, twin_field)
    packed_shape = ((modes // 4, kz * channels, 8 * channels), BF16)
    (weight,) = call(pack_kernel, [packed_shape], "pack")(spectral_weight)
    spectrum, send = run(mode_kernel, [((mode_lines, channels), F32), plain], "mode")(
        exchange(send, 0), y_forward, y_inverse, weight
    )
    part = functools.partial(part_kernel, place, place.firsts[1])
    own, send = call(part, [own_lines, twin_plain], "part")(exchange(send, 1))
    pointwise, head_turned, z_doubled = run(
        ready_kernel,
        [(across, F32), ((hidden_units, channels), BF16), ((height, z_count), BF16)],
        "ready",
    )(field, mix_weight, mix_bias[:, None], head_weight)
    prediction, grad_pre, send, hidden, head_slope = run(
        cell_kernel,
        [
            ((rows_y, z_count), F32),
            (across, BF16),
            twin_plain,
            (across, BF16),
            ((hidden_units, rows_y * z_count), BF16),
        ],
        "cell",
    )(
        own,
        to_twin(send),
        z_doubled,
        pointwise,
        head_weight,
        head_turned,
        head_bias[:, None],
        out_weight[None],
        out_weight.astype(F32)[:, None],
        cotangent[0],
    )
    if place.fold:
        outs = [((8 * partners, hidden_units), BF16)]
    else:
        outs = [((channels, channels), F32), ((channels, hidden_units), F32)]
    outs += [((wide // 2 * height, 4 * height), BF16)]
    *sums, forward = run(sums_kernel, outs, "sums")(field, grad_pre, hidden, head_slope)
    if not place.fold:
        totals = lax.psum(tuple(sums), ("wide", "narrow"))
        sums = []
    (send,) = run(fold_kernel, [shared], "fold")(send, to_twin(send), forward, *sums)
    adjoint, send = run(back_kernel, [((mode_lines, channels), F32), shared], "back")(
        exchange(send, 2), y_forward, y_inverse, weight
    )
    some = max(1, modes // 4)
    grad_spectral, done = pl.pallas_call(
        outer_kernel,
        grid=(modes // some,),
        in_specs=[pl.BlockSpec((some, 2 * kz, channels), lambda j: (j, 0, 0))] * 2,
        out_specs=[
            pl.BlockSpec((some, kz, 2, channels, channels), lambda j: (j, 0, 0, 0, 0)),
            pl.BlockSpec((8, 128), lambda j: (0, 0)),
        ],
        out_shape=[
            jax.ShapeDtypeStruct(spectral_weight.shape, F32),
            jax.ShapeDtypeStruct((8, 128), F32),
        ],
        compiler_params=pltpu.CompilerParams(vmem_limit_bytes=VMEM_LIMIT),
        cost_estimate=pl.CostEstimate(flops=1 << 22, bytes_accessed=5 << 20, transcendentals=0),
        name="outer",
    )(spectrum.reshape(modes, 2 * kz, channels), adjoint.reshape(modes, 2 * kz, channels))
    pointwise, z_plain, turn = run(
        pointwise_kernel,
        [
            ((channels, rows_y, z_count), F32),
            ((height, z_count), BF16),
            ((cells, cells), BF16),
        ],
        "pointwise",
    )(mix_weight, grad_pre)
    outs = [own_lines, twin_shared] + ([sums_shape] if place.fold else [])
    after = (done,) if place.fold else ()
    part = functools.partial(part_kernel, place, place.firsts[3])
    own, send, *sums = call(part, outs, "part")(exchange(send, 3), *after)
    outs = [((cells, z_count), BF16), ((rows_y, z_count), F32)]
    if place.fold:
        outs += [((channels, channels), F32), ((channels, hidden_units), F32)]
    grad_field, prediction, *summed = run(finish_kernel, outs, "finish")(
        own, to_twin(send), z_plain, turn, pointwise, prediction, *sums
    )
    grad_mix, grad_head = summed if place.fold else totals
    return (
        prediction[None],
        grad_field.reshape(lifted_field.shape),
        grad_spectral,
        grad_mix,
        grad_head,
    )


def solution(mesh):
    return jax.shard_map(
        body,
        mesh=mesh,
        in_specs=(
            P("wide", None, "narrow", None),
            P("wide", "narrow", None, None, None),
            P(),
            P(),
            P(),
            P(),
            P(),
            P("wide", "narrow", None),
        ),
        out_specs=(
            P("wide", "narrow", None),
            P("wide", None, "narrow", None),
            P("wide", "narrow", None, None, None),
            P(),
            P(),
        ),
        check_vma=False,
    )
```

```python
import functools
import math

import jax
import jax.numpy as jnp
import numpy as np
from jax import lax
from jax.experimental import pallas as pl
from jax.experimental.pallas import tpu as pltpu
from jax.sharding import PartitionSpec as P

MX = 16
MY = 16
MZ = 16
F32 = jnp.float32
BF16 = jnp.bfloat16
VMEM_LIMIT = 32 * 1024 * 1024

TAIL_SLOPE = 0.275
TAIL = (
    0.11780925840139389,
    0.04211147502064705,
    0.3339323103427887,
    -0.3309934139251709,
    0.4519987106323242,
    -0.11485832929611206,
)


def signed(indices, count):
    return np.where(indices < count // 2, indices, indices - count)


def wave(positions, frequency, length):
    turned = np.mod(np.multiply.outer(positions, frequency), length)
    angles = turned.astype(np.float32) * np.float32(2.0 * math.pi / length)
    scale = np.float32(1.0 / math.sqrt(length))
    return np.cos(angles) * scale, np.sin(angles) * scale


def pair(cosine, sine, sign):
    return np.stack(
        [np.stack([cosine, -sign * sine], -1), np.stack([sign * sine, cosine], -1)], -2
    )


def y_tables(total_y, rows_y, kz, modes):
    cosine, sine = wave(np.arange(total_y), signed(np.arange(MY), MY), total_y)
    narrow = total_y // rows_y
    same = np.eye(kz, dtype=np.float32)
    forward = pair(cosine, sine, -1.0).reshape(narrow, rows_y, MY // modes, modes, 2, 2)
    inverse = pair(cosine, sine, 1.0).reshape(narrow, rows_y, MY // modes, modes, 2, 2)
    forward = np.einsum("nybjtr,kl->bjtkynlr", forward, same)
    inverse = np.einsum("nybjst,kl->bnyksjtl", inverse, same)
    blocks = MY // modes
    forward = forward.reshape(blocks, modes * 2 * kz, rows_y * narrow * kz * 2)
    inverse = inverse.reshape(blocks, narrow * rows_y * kz * 2, modes * 2 * kz)
    return forward.astype(BF16), inverse.astype(BF16)


def dot(a, b):
    return jnp.dot(a, b, preferred_element_type=F32)


def dot_nt(a, b):
    return lax.dot_general(a, b, (((1,), (1,)), ((), ())), preferred_element_type=F32)


def dot_tn(a, b):
    return lax.dot_general(a, b, (((0,), (0,)), ((), ())), preferred_element_type=F32)


def grid_of(rows, columns):
    shape = (rows, columns)
    return lax.broadcasted_iota(jnp.int32, shape, 0), lax.broadcasted_iota(jnp.int32, shape, 1)


def selector(rows, columns, condition):
    return jnp.where(condition(*grid_of(rows, columns)), 1.0, 0.0).astype(BF16)


def halves(values):
    high = values.astype(BF16)
    return high, (values - high.astype(F32)).astype(BF16)


def stacked(refs, lanes=slice(None)):
    return jnp.concatenate([ref[:, lanes] for ref in refs], axis=0)


def cosine_of(phase, length):
    angles = (phase & (length - 1)).astype(F32) * (2.0 * math.pi / length)
    return jnp.cos(angles) * (1.0 / math.sqrt(length))


class Place:
    def __init__(self, wide, narrow, kz, modes, rows_y, channels, z_count, fold):
        self.wide, self.narrow, self.kz, self.modes = wide, narrow, kz, modes
        self.rows_y, self.channels, self.z_count, self.fold = rows_y, channels, z_count, fold
        self.outer = wide // 2
        self.partners = self.outer * narrow
        self.lanes = rows_y * channels
        middle, last = self.outer // 4, self.outer // 2 - 1
        self.firsts = (last, middle, middle, middle)

    def here(self):
        wide = lax.axis_index("wide")
        return wide // 2, wide % 2

    def listed(self, position, first):
        lines = self.outer // 2
        return ((first + position // 2) & (lines - 1)) * 2 + position % 2

    def frequency(self, wide):
        index = (wide * self.modes) // MY
        return jnp.where(index < MX // 2, index, index - MX)

    def z_table(self, doubled):
        row, z = grid_of(2 * MZ, self.z_count)
        frequency = row >> 1
        value = cosine_of(z * frequency + (row & 1) * (self.z_count // 4), self.z_count)
        if doubled:
            value = jnp.where(frequency > 0, 2.0 * value, value)
        return value.astype(BF16)

    def expanded(self, small):
        row, column = grid_of(2 * MZ, small.shape[1])
        same = (row >> 1) == ((column >> 1) & (MZ - 1))
        blocks = []
        for g in range(small.shape[0] // 2):
            value = jnp.where((row & 1) == 0, small[2 * g : 2 * g + 1], small[2 * g + 1 : 2 * g + 2])
            blocks.append(jnp.where(same, value, 0.0))
        return jnp.concatenate(blocks, axis=0)

    def forward_x(self, first):
        outer, inner = self.here()
        row, column = grid_of(2 * self.outer, 4 * MZ)
        x = 2 * outer + (inner ^ (column // (2 * MZ)))
        frequency = self.frequency(2 * self.listed(row >> 1, first) + inner)
        quarter = self.wide // 4
        small = cosine_of(x * frequency + quarter * ((row & 1) - (column & 1)), self.wide)
        return self.expanded(small)

    def inverse_x(self, first):
        outer, inner = self.here()
        row, column = grid_of(4, self.outer * 2 * MZ)
        x = 2 * outer + (inner ^ (row >> 1))
        frequency = self.frequency(2 * self.listed(column // (2 * MZ), first) + inner)
        quarter = self.wide // 4
        small = cosine_of(x * frequency + quarter * ((column & 1) - (row & 1)), self.wide)
        return self.expanded(small).astype(BF16)


def repeat_rows(out_ref, block):
    height = block.shape[0]
    for first in range(0, out_ref.shape[0], height):
        out_ref[first : first + height] = block


def write_pieces(place, send_ref, block, shares):
    step, half = 2 * place.kz, place.lanes // 2
    height = send_ref.shape[0] // place.partners
    for p in range(place.partners):
        own = block[p * step % block.shape[0] :][:step]
        first = p * height
        send_ref[first : first + step] = own[:, :half]
        send_ref[first + step : first + 2 * step] = own[:, half:]
        send_ref[first + 2 * step : first + height] = shares[p * 8 % shares.shape[0] :][:8]


def read_pieces(place, pieces_ref):
    step = 2 * place.kz
    if pieces_ref.shape[1] == place.lanes:
        return pieces_ref[...], None
    height = pieces_ref.shape[0] // place.partners
    blocks, shares = [], []
    for p in range(place.partners):
        first = p * height
        left = pieces_ref[first : first + step]
        right = pieces_ref[first + step : first + 2 * step]
        blocks.append(jnp.concatenate([left, right], axis=1))
        shares.append(pieces_ref[first + 2 * step : first + height].astype(F32))
    return jnp.concatenate(blocks, axis=0), shares


def lane_sum(values, width):
    while values.shape[1] > 128:
        half = values.shape[1] // 2
        values = values[:, :half] + values[:, half:]
    if values.shape[1] < 128:
        blocks = range(0, values.shape[1], width)
        return sum(values[:, first : first + width] for first in blocks)
    shift = 64
    while shift >= width:
        values = values + pltpu.roll(values, shift, 1)
        shift //= 2
    return values[:, :width]


def analysed(place, pieces, y_forward, copies):
    height = 2 * MZ
    turned = sum(
        pieces[first : first + height].astype(F32) for first in range(0, pieces.shape[0], height)
    )
    channels = place.channels
    lines = jnp.concatenate(
        [turned[:, y * channels : (y + 1) * channels] for y in range(place.rows_y)], axis=0
    )
    return dot(y_forward, jnp.concatenate([lines.astype(BF16)] * copies, axis=1))


def spread_lines(place, modes, y_inverse):
    lines = dot(y_inverse, modes)
    step = 2 * place.kz
    blocks = []
    for n in range(place.narrow):
        first = n * place.rows_y
        parts = [lines[(first + y) * step : (first + y + 1) * step] for y in range(place.rows_y)]
        blocks.append(jnp.concatenate(parts, axis=1))
    return jnp.concatenate(blocks, axis=0).astype(BF16)


def turn_matrix(place, forward):
    channels, rows_y = place.channels, place.rows_y

    def same(row, column):
        if forward:
            row, column = column, row
        return (row % channels == column // rows_y) & (row // channels == column % rows_y)

    return selector(place.lanes, place.lanes, same)


def side_by_side(values, count):
    height = values.shape[0] // count
    return jnp.concatenate([values[y * height : (y + 1) * height] for y in range(count)], axis=1)


def one_below_other(values, count):
    width = values.shape[1] // count
    return jnp.concatenate([values[:, y * width : (y + 1) * width] for y in range(count)], axis=0)


def own_kernel(place, field_ref, field_out_ref, spectra_ref):
    turned = dot(turn_matrix(place, False), field_ref[...]).astype(BF16)
    field_out_ref[...] = side_by_side(turned, place.rows_y)
    spectra_ref[...] = dot_nt(place.z_table(False), turned).astype(BF16)


def start_kernel(place, spectra_ref, twin_ref, send_ref):
    twin = dot_nt(place.z_table(False), twin_ref[...]).astype(BF16)
    twin = dot(twin, turn_matrix(place, True)).astype(BF16)
    values = jnp.concatenate([spectra_ref[...], twin], axis=0)
    tables = jnp.concatenate(halves(place.forward_x(place.firsts[0])), axis=1)
    send_ref[...] = dot(tables, jnp.concatenate([values, values], axis=0)).astype(BF16)


def pack_kernel(place, weight_ref, packed_ref, inverse_ref):
    inverse_ref[...] = place.inverse_x(place.firsts[1])
    modes, kz, _, channels, _ = weight_ref.shape
    for q in range(modes // 4):
        parts = [weight_ref[4 * q + j // 2, :, j % 2] for j in range(8)]
        packed = jnp.concatenate(parts, axis=-1).reshape(kz * channels, 8 * channels)
        packed_ref[q] = packed.astype(BF16)


def ready_kernel(place, field_ref, mix_ref, mix_bias_ref, head_ref, *refs):
    pointwise_ref, head_out_ref, z_doubled_ref = refs
    pointwise_ref[...] = dot_tn(mix_ref[...], field_ref[...]) + mix_bias_ref[...]
    head_out_ref[...] = jnp.transpose(head_ref[...].astype(F32)).astype(BF16)
    z_doubled_ref[...] = place.z_table(True)


def fold_kernel(place, own_ref, got_ref, tables_ref, *refs):
    values = jnp.concatenate([own_ref[...], got_ref[...]], axis=0)
    values = jnp.concatenate([values, values], axis=0)
    partial = dot(tables_ref[...], values).astype(BF16)
    if place.fold:
        shares_ref, send_ref = refs
        write_pieces(place, send_ref, partial, shares_ref[...])
    else:
        refs[0][...] = partial


def mode_kernel(
    place, pieces_ref, y_forward_ref, y_inverse_ref, weight_ref, spectrum_ref, send_ref
):
    kz, channels = place.kz, place.channels
    spectrum = analysed(place, pieces_ref[...], y_forward_ref[...], kz)
    spectrum_ref[...] = spectrum[:, :channels]
    row, lane = grid_of(*spectrum.shape)
    blocked = jnp.where(row % kz == lane // channels, spectrum, 0.0)
    mixed = []
    for q in range(place.modes // 4):
        left = blocked[q * 8 * kz : (q + 1) * 8 * kz].astype(BF16)
        product = dot(left, weight_ref[q])
        for j in range(4):
            own = product[j * 2 * kz : (j + 1) * 2 * kz, j * 2 * channels : (j + 1) * 2 * channels]
            real, imag = own[:, :channels], own[:, channels:]
            mixed.append(real[:kz] - imag[kz:])
            mixed.append(imag[:kz] + real[kz:])
    mode = jnp.concatenate(mixed, axis=0).astype(BF16)
    repeat_rows(send_ref, spread_lines(place, mode, y_inverse_ref[...]))


def part_kernel(place, pieces_ref, table_ref, *refs):
    pieces, shares = read_pieces(place, pieces_ref)
    lines = dot(table_ref[...], pieces)
    height = 2 * MZ
    if shares is None:
        own_ref, send_ref = refs
        own_ref[...] = lines[:height]
        send_ref[...] = lines[height:].astype(BF16)
        return
    _, own_ref, send_ref, sums_ref = refs
    own_ref[...] = lines[:height]
    send_ref[:height] = lines[height:].astype(BF16)
    got = jnp.concatenate(shares, axis=0).astype(BF16)
    channels = place.channels

    def chosen(part):
        def condition(row, column):
            owner, source = (row % channels) // 2, column // 8
            return (
                (owner == source)
                & (column % 8 == 4 * part + 2 * (row // channels) + row % 2)
            )

        return dot(selector(2 * channels, got.shape[0], condition), got)

    high, low = chosen(0), chosen(1)
    sums_ref[...] = high + low
    send_ref[height:] = jnp.concatenate([high, low], axis=1).astype(BF16)


def normal(values):
    scaled = pl.reciprocal(1.0 + jnp.abs(TAIL_SLOPE * values), approx=True)
    decay = jnp.exp2(values * values * (-0.5 / math.log(2.0)))
    tail = TAIL[-1]
    for factor in TAIL[-2::-1]:
        tail = tail * scaled + factor
    tail = tail * (scaled * decay)
    cumulative = jnp.where(values > 0.0, 1.0 - tail, tail)
    return values * cumulative, cumulative + values * (decay * (1.0 / math.sqrt(2.0 * math.pi)))


def cell_kernel(place, *refs):
    own_ref, got_ref, z_table_ref, pointwise_ref, head_ref, head_turned_ref = refs[:6]
    head_bias_ref, out_row_ref, out_column_ref, cotangent_ref = refs[6:10]
    prediction_ref, grad_pre_ref, send_ref, hidden_ref, head_slope_ref = refs[10:]
    rows_y, z_count = place.rows_y, place.z_count
    z_table = z_table_ref[...]
    lines = (own_ref[...] + got_ref[...].astype(F32)).astype(BF16)
    pre_act = side_by_side(dot_tn(lines, z_table), rows_y) + pointwise_ref[...]
    head, head_turned = head_ref[...], head_turned_ref[...]
    head_bias, out_row, out_column = head_bias_ref[...], out_row_ref[...], out_column_ref[...]
    width = 2 * z_count
    slopes, head_pre = [], []
    for first in range(0, rows_y * z_count, width):
        value, slope = normal(pre_act[:, first : first + width])
        hidden = value.astype(BF16)
        hidden_ref[:, first : first + width] = hidden
        slopes.append(slope)
        head_pre.append(dot(head_turned, hidden))
    gradients = []
    for index, first in enumerate(range(0, rows_y, 2)):
        target = jnp.concatenate(
            [cotangent_ref[y : y + 1] for y in range(first, first + 2)], axis=1
        )
        active, slope = normal(head_pre[index] + head_bias)
        predicted = dot(out_row, active.astype(BF16))
        prediction_ref[first : first + 1] = predicted[:, :z_count]
        prediction_ref[first + 1 : first + 2] = predicted[:, z_count:]
        head_slope = (target * out_column * slope).astype(BF16)
        head_slope_ref[:, first * z_count : first * z_count + width] = head_slope
        gradients.append((dot(head, head_slope) * slopes[index]).astype(BF16))
    gradient = jnp.concatenate(gradients, axis=1)
    grad_pre_ref[...] = gradient
    send_ref[...] = dot_nt(z_table, one_below_other(gradient, rows_y)).astype(BF16)


def sums_kernel(place, field_ref, gradient_ref, hidden_ref, head_slope_ref, *refs):
    refs[-1][...] = jnp.concatenate(halves(place.forward_x(place.firsts[2])), axis=1)
    grad_mix = dot_nt(field_ref[...], gradient_ref[...])
    grad_head = dot_nt(hidden_ref[...], head_slope_ref[...])
    if not place.fold:
        refs[0][...] = grad_mix
        refs[1][...] = grad_head
        return
    channels, hidden_units = grad_head.shape
    rest = jnp.zeros((channels, hidden_units - channels), F32)
    wide_mix = jnp.concatenate([grad_mix, rest], axis=1)
    high, low = halves(jnp.concatenate([grad_head, wide_mix], axis=0))
    split = jnp.concatenate([high, low], axis=0)
    place_of = selector(
        8 * place.partners,
        4 * channels,
        lambda row, column: (column % channels == 2 * (row // 8) + row % 2)
        & (column // channels == (row % 8) // 2),
    )
    refs[0][...] = dot(place_of, split).astype(BF16)


def back_kernel(
    place, pieces_ref, y_forward_ref, y_inverse_ref, weight_ref, adjoint_ref, send_ref
):
    kz, channels = place.kz, place.channels
    pieces, shares = read_pieces(place, pieces_ref)
    adjoint = analysed(place, pieces, y_forward_ref[...], 1)
    adjoint_ref[...] = adjoint
    turned = []
    for first in range(0, adjoint.shape[0], 2 * kz):
        turned += [adjoint[first + kz : first + 2 * kz], -adjoint[first : first + kz]]
    left = jnp.concatenate([adjoint, jnp.concatenate(turned, axis=0)], axis=1)
    left = jnp.concatenate([left] * 4, axis=1)
    row, lane = grid_of(*left.shape)
    same = (row // (2 * kz)) % 4 == lane // (2 * channels)
    left = jnp.where(same, left, 0.0).astype(BF16)
    block = 8 * kz
    pulled = [
        dot_nt(left[q * block : (q + 1) * block], weight_ref[q]) for q in range(place.modes // 4)
    ]
    pulled = jnp.concatenate(pulled, axis=0)
    row, lane = grid_of(*pulled.shape)
    pulled = jnp.where(row % kz == lane // channels, pulled, 0.0)
    modes_back = lane_sum(pulled, channels).astype(BF16)
    block = spread_lines(place, modes_back, y_inverse_ref[...])
    if shares is None:
        repeat_rows(send_ref, block)
        return
    total = sum(shares[1:], shares[0])
    high, low = halves(total[0:4] + total[4:8])
    split = jnp.concatenate([high.astype(F32), low.astype(F32)], axis=0)
    write_pieces(place, send_ref, block, split.astype(BF16))


def outer_kernel(spectrum_ref, adjoint_ref, out_ref, done_ref):
    done_ref[...] = jnp.zeros(done_ref.shape, F32)
    modes, kz = out_ref.shape[:2]
    for j in range(modes):
        columns = jnp.transpose(spectrum_ref[j])
        adjoint = adjoint_ref[j]
        for k in range(kz):
            s_real, s_imag = columns[:, k : k + 1], columns[:, kz + k : kz + k + 1]
            a_real, a_imag = adjoint[k : k + 1], adjoint[kz + k : kz + k + 1]
            out_ref[j, k, 0] = s_real * a_real + s_imag * a_imag
            out_ref[j, k, 1] = s_real * a_imag - s_imag * a_real


def pointwise_kernel(place, mix_ref, gradient_ref, out_ref, z_plain_ref, turn_ref):
    z_plain_ref[...] = place.z_table(False)
    turn_ref[...] = turn_matrix(place, False)
    z_count = place.z_count
    product = dot(mix_ref[...], gradient_ref[...])
    for y in range(place.rows_y):
        out_ref[:, y, :] = product[:, y * z_count : (y + 1) * z_count]


def finish_kernel(place, *refs):
    own_ref, got_ref, z_table_ref, turn_ref, pointwise_ref, prediction_ref = refs[:6]
    refs = refs[6:]
    height = 2 * MZ
    channels = place.channels
    lines = (own_ref[...] + got_ref[:height].astype(F32)).astype(BF16)
    lines = dot(lines, turn_ref[...]).astype(BF16)
    pointwise = pointwise_ref[...].reshape(place.lanes, place.z_count)
    grad_field = (dot_tn(lines, z_table_ref[...]) + pointwise).astype(BF16)
    if not place.fold:
        refs[0][...] = grad_field
        refs[1][...] = prediction_ref[...]
        return
    sums_ref, grad_field_ref, out_ref, grad_mix_ref, grad_head_ref = refs
    grad_field_ref[...] = grad_field
    out_ref[...] = prediction_ref[...]
    got = got_ref[height:].astype(F32)
    width = sums_ref.shape[1]
    total = sums_ref[...] + got[:, :width] + got[:, width:]
    grad_head_ref[...] = total[:channels]
    grad_mix_ref[...] = total[channels:, :channels]


def call(kernel, outs, name, **spec):
    return pl.pallas_call(
        kernel,
        out_shape=[jax.ShapeDtypeStruct(shape, dtype) for shape, dtype in outs],
        compiler_params=pltpu.CompilerParams(vmem_limit_bytes=VMEM_LIMIT),
        cost_estimate=pl.CostEstimate(flops=1 << 22, bytes_accessed=1 << 19, transcendentals=0),
        name=name,
        **spec,
    )


def body(
    lifted_field,
    spectral_weight,
    mix_weight,
    mix_bias,
    head_weight,
    head_bias,
    out_weight,
    cotangent,
):
    wide = lax.axis_size("wide")
    narrow = lax.axis_size("narrow")
    devices = wide * narrow
    _, channels, rows_y, z_count = lifted_field.shape
    modes, kz = spectral_weight.shape[:2]
    hidden_units = head_weight.shape[1]
    cells = channels * rows_y
    place = Place(wide, narrow, kz, modes, rows_y, channels, z_count, False)
    place.fold = 2 * place.partners == channels and hidden_units == 128 and cells == 256 and kz % 8 == 0
    height = 2 * MZ
    step = 2 * kz
    partners = place.partners
    mode_lines = modes * 2 * kz

    y_forward, y_inverse = y_tables(rows_y * narrow, rows_y, kz, modes)
    if len(y_forward) > 1:
        block = lax.axis_index("wide") % len(y_forward)
        y_forward = lax.dynamic_index_in_dim(jnp.asarray(y_forward), block, 0, False)
        y_inverse = lax.dynamic_index_in_dim(jnp.asarray(y_inverse), block, 0, False)
    else:
        y_forward, y_inverse = jnp.asarray(y_forward[0]), jnp.asarray(y_inverse[0])

    def to_twin(send):
        pairs = [(p, p ^ narrow) for p in range(devices)]
        return lax.ppermute(send, ("wide", "narrow"), pairs)

    def exchange(send, transform):
        first = place.firsts[transform]
        groups = [
            [
                (2 * place.listed(outer, first) + inner) * narrow + n
                for outer in range(place.outer)
                for n in range(narrow)
            ]
            for inner in range(2)
        ]
        pieces = send.reshape(partners, -1, send.shape[1])
        got = lax.all_to_all(
            pieces, ("wide", "narrow"), 0, 0, axis_index_groups=groups, tiled=True
        )
        return got.reshape(send.shape)

    plain = ((partners * step, cells), BF16)
    shared = ((partners * (2 * step + 8), cells // 2), BF16) if place.fold else plain
    twin_plain = ((height, cells), BF16)
    twin_shared = ((height + 2 * channels, cells), BF16) if place.fold else twin_plain
    sums_shape = ((2 * channels, hidden_units), F32)
    own_lines = ((height, cells), F32)
    across = (channels, rows_y * z_count)

    def run(kernel, outs, name, **spec):
        return call(functools.partial(kernel, place), outs, name, **spec)

    flat_field = lifted_field.reshape(cells, z_count)
    twin_field = to_twin(flat_field)
    field, spectra = run(own_kernel, [(across, BF16), twin_plain], "own")(flat_field)
    (send,) = run(start_kernel, [plain], "start")(spectra, twin_field)
    packed_shape = ((modes // 4, kz * channels, 8 * channels), BF16)
    inverse_shape = ((2 * height, wide // 2 * height), BF16)
    weight, inverse = run(pack_kernel, [packed_shape, inverse_shape], "pack")(spectral_weight)
    spectrum, send = run(mode_kernel, [((mode_lines, channels), F32), plain], "mode")(
        exchange(send, 0), y_forward, y_inverse, weight
    )
    own, send = run(part_kernel, [own_lines, twin_plain], "part")(exchange(send, 1), inverse)
    pointwise, head_turned, z_doubled = run(
        ready_kernel,
        [(across, F32), ((hidden_units, channels), BF16), ((height, z_count), BF16)],
        "ready",
    )(field, mix_weight, mix_bias[:, None], head_weight)
    prediction, grad_pre, send, hidden, head_slope = run(
        cell_kernel,
        [
            ((rows_y, z_count), F32),
            (across, BF16),
            twin_plain,
            (across, BF16),
            ((hidden_units, rows_y * z_count), BF16),
        ],
        "cell",
    )(
        own,
        to_twin(send),
        z_doubled,
        pointwise,
        head_weight,
        head_turned,
        head_bias[:, None],
        out_weight[None],
        out_weight.astype(F32)[:, None],
        cotangent[0],
    )
    if place.fold:
        outs = [((8 * partners, hidden_units), BF16)]
    else:
        outs = [((channels, channels), F32), ((channels, hidden_units), F32)]
    outs += [((wide // 2 * height, 4 * height), BF16)]
    *sums, forward = run(sums_kernel, outs, "sums")(field, grad_pre, hidden, head_slope)
    if not place.fold:
        totals = lax.psum(tuple(sums), ("wide", "narrow"))
        sums = []
    (send,) = run(fold_kernel, [shared], "fold")(send, to_twin(send), forward, *sums)
    adjoint, send = run(back_kernel, [((mode_lines, channels), F32), shared], "back")(
        exchange(send, 2), y_forward, y_inverse, weight
    )
    some = max(1, modes // 4)
    grad_spectral, done = pl.pallas_call(
        outer_kernel,
        grid=(modes // some,),
        in_specs=[pl.BlockSpec((some, 2 * kz, channels), lambda j: (j, 0, 0))] * 2,
        out_specs=[
            pl.BlockSpec((some, kz, 2, channels, channels), lambda j: (j, 0, 0, 0, 0)),
            pl.BlockSpec((8, 128), lambda j: (0, 0)),
        ],
        out_shape=[
            jax.ShapeDtypeStruct(spectral_weight.shape, F32),
            jax.ShapeDtypeStruct((8, 128), F32),
        ],
        compiler_params=pltpu.CompilerParams(vmem_limit_bytes=VMEM_LIMIT),
        cost_estimate=pl.CostEstimate(flops=1 << 22, bytes_accessed=5 << 20, transcendentals=0),
        name="outer",
    )(spectrum.reshape(modes, 2 * kz, channels), adjoint.reshape(modes, 2 * kz, channels))
    pointwise, z_plain, turn = run(
        pointwise_kernel,
        [
            ((channels, rows_y, z_count), F32),
            ((height, z_count), BF16),
            ((cells, cells), BF16),
        ],
        "pointwise",
    )(mix_weight, grad_pre)
    outs = [own_lines, twin_shared] + ([sums_shape] if place.fold else [])
    after = (done,) if place.fold else ()
    own, send, *sums = run(part_kernel, outs, "part")(exchange(send, 3), inverse, *after)
    outs = [((cells, z_count), BF16), ((rows_y, z_count), F32)]
    if place.fold:
        outs += [((channels, channels), F32), ((channels, hidden_units), F32)]
    grad_field, prediction, *summed = run(finish_kernel, outs, "finish")(
        own, to_twin(send), z_plain, turn, pointwise, prediction, *sums
    )
    grad_mix, grad_head = summed if place.fold else totals
    return (
        prediction[None],
        grad_field.reshape(lifted_field.shape),
        grad_spectral,
        grad_mix,
        grad_head,
    )


def solution(mesh):
    return jax.shard_map(
        body,
        mesh=mesh,
        in_specs=(
            P("wide", None, "narrow", None),
            P("wide", "narrow", None, None, None),
            P(),
            P(),
            P(),
            P(),
            P(),
            P("wide", "narrow", None),
        ),
        out_specs=(
            P("wide", "narrow", None),
            P("wide", None, "narrow", None),
            P("wide", "narrow", None, None, None),
            P(),
            P(),
        ),
        check_vma=False,
    )
```

```python
import functools
import math

import jax
import jax.numpy as jnp
import numpy as np
from jax import lax
from jax.experimental import pallas as pl
from jax.experimental.pallas import tpu as pltpu
from jax.sharding import PartitionSpec as P

MX = 16
MY = 16
MZ = 16
F32 = jnp.float32
BF16 = jnp.bfloat16
VMEM_LIMIT = 32 * 1024 * 1024

TAIL_SLOPE = 0.275
TAIL = (
    0.11780925840139389,
    0.04211147502064705,
    0.3339323103427887,
    -0.3309934139251709,
    0.4519987106323242,
    -0.11485832929611206,
)


def signed(indices, count):
    return np.where(indices < count // 2, indices, indices - count)


def wave(positions, frequency, length):
    turned = np.mod(np.multiply.outer(positions, frequency), length)
    angles = turned.astype(np.float32) * np.float32(2.0 * math.pi / length)
    scale = np.float32(1.0 / math.sqrt(length))
    return np.cos(angles) * scale, np.sin(angles) * scale


def pair(cosine, sine, sign):
    return np.stack(
        [np.stack([cosine, -sign * sine], -1), np.stack([sign * sine, cosine], -1)], -2
    )


def y_tables(total_y, rows_y, kz, modes):
    cosine, sine = wave(np.arange(total_y), signed(np.arange(MY), MY), total_y)
    narrow = total_y // rows_y
    same = np.eye(kz, dtype=np.float32)
    forward = pair(cosine, sine, -1.0).reshape(narrow, rows_y, MY // modes, modes, 2, 2)
    inverse = pair(cosine, sine, 1.0).reshape(narrow, rows_y, MY // modes, modes, 2, 2)
    forward = np.einsum("nybjtr,kl->bjtkynlr", forward, same)
    inverse = np.einsum("nybjst,kl->bnyksjtl", inverse, same)
    blocks = MY // modes
    forward = forward.reshape(blocks, modes * 2 * kz, rows_y * narrow * kz * 2)
    inverse = inverse.reshape(blocks, narrow * rows_y * kz * 2, modes * 2 * kz)
    return forward.astype(BF16), inverse.astype(BF16)


def dot(a, b):
    return jnp.dot(a, b, preferred_element_type=F32)


def dot_nt(a, b):
    return lax.dot_general(a, b, (((1,), (1,)), ((), ())), preferred_element_type=F32)


def dot_tn(a, b):
    return lax.dot_general(a, b, (((0,), (0,)), ((), ())), preferred_element_type=F32)


def grid_of(rows, columns):
    shape = (rows, columns)
    return lax.broadcasted_iota(jnp.int32, shape, 0), lax.broadcasted_iota(jnp.int32, shape, 1)


def selector(rows, columns, condition):
    return jnp.where(condition(*grid_of(rows, columns)), 1.0, 0.0).astype(BF16)


def halves(values):
    high = values.astype(BF16)
    return high, (values - high.astype(F32)).astype(BF16)


def stacked(refs, lanes=slice(None)):
    return jnp.concatenate([ref[:, lanes] for ref in refs], axis=0)


def cosine_of(phase, length):
    angles = (phase & (length - 1)).astype(F32) * (2.0 * math.pi / length)
    return jnp.cos(angles) * (1.0 / math.sqrt(length))


class Place:
    def __init__(self, wide, narrow, kz, modes, rows_y, channels, z_count, fold):
        self.wide, self.narrow, self.kz, self.modes = wide, narrow, kz, modes
        self.rows_y, self.channels, self.z_count, self.fold = rows_y, channels, z_count, fold
        self.outer = wide // 2
        self.partners = self.outer * narrow
        self.lanes = rows_y * channels
        middle, last = self.outer // 4, self.outer // 2 - 1
        self.firsts = ((last, last), (middle, 0), (middle, 0), (middle, 0))

    def here(self):
        wide = lax.axis_index("wide")
        return wide // 2, wide % 2

    def listed(self, position, firsts, inner):
        lines = self.outer // 2
        first = firsts[0] + (firsts[1] - firsts[0]) * inner
        return ((first + position // 2) & (lines - 1)) * 2 + position % 2

    def frequency(self, wide):
        index = (wide * self.modes) // MY
        return jnp.where(index < MX // 2, index, index - MX)

    def z_table(self, doubled):
        row, z = grid_of(2 * MZ, self.z_count)
        frequency = row >> 1
        value = cosine_of(z * frequency + (row & 1) * (self.z_count // 4), self.z_count)
        if doubled:
            value = jnp.where(frequency > 0, 2.0 * value, value)
        return value.astype(BF16)

    def expanded(self, small):
        row, column = grid_of(2 * MZ, small.shape[1])
        same = (row >> 1) == ((column >> 1) & (MZ - 1))
        blocks = []
        for g in range(small.shape[0] // 2):
            value = jnp.where((row & 1) == 0, small[2 * g : 2 * g + 1], small[2 * g + 1 : 2 * g + 2])
            blocks.append(jnp.where(same, value, 0.0))
        return jnp.concatenate(blocks, axis=0)

    def forward_x(self, firsts):
        outer, inner = self.here()
        row, column = grid_of(2 * self.outer, 4 * MZ)
        x = 2 * outer + (inner ^ (column // (2 * MZ)))
        frequency = self.frequency(2 * self.listed(row >> 1, firsts, inner) + inner)
        quarter = self.wide // 4
        small = cosine_of(x * frequency + quarter * ((row & 1) - (column & 1)), self.wide)
        return self.expanded(small)

    def inverse_x(self, firsts):
        outer, inner = self.here()
        row, column = grid_of(4, self.outer * 2 * MZ)
        x = 2 * outer + (inner ^ (row >> 1))
        frequency = self.frequency(2 * self.listed(column // (2 * MZ), firsts, inner) + inner)
        quarter = self.wide // 4
        small = cosine_of(x * frequency + quarter * ((column & 1) - (row & 1)), self.wide)
        return self.expanded(small).astype(BF16)


def repeat_rows(out_ref, block):
    height = block.shape[0]
    for first in range(0, out_ref.shape[0], height):
        out_ref[first : first + height] = block


def write_pieces(place, send_ref, block, shares):
    step, half = 2 * place.kz, place.lanes // 2
    height = send_ref.shape[0] // place.partners
    for p in range(place.partners):
        own = block[p * step % block.shape[0] :][:step]
        first = p * height
        send_ref[first : first + step] = own[:, :half]
        send_ref[first + step : first + 2 * step] = own[:, half:]
        send_ref[first + 2 * step : first + height] = shares[p * 8 % shares.shape[0] :][:8]


def read_pieces(place, pieces_ref):
    step = 2 * place.kz
    if pieces_ref.shape[1] == place.lanes:
        return pieces_ref[...], None
    height = pieces_ref.shape[0] // place.partners
    blocks, shares = [], []
    for p in range(place.partners):
        first = p * height
        left = pieces_ref[first : first + step]
        right = pieces_ref[first + step : first + 2 * step]
        blocks.append(jnp.concatenate([left, right], axis=1))
        shares.append(pieces_ref[first + 2 * step : first + height].astype(F32))
    return jnp.concatenate(blocks, axis=0), shares


def lane_sum(values, width):
    while values.shape[1] > 128:
        half = values.shape[1] // 2
        values = values[:, :half] + values[:, half:]
    if values.shape[1] < 128:
        blocks = range(0, values.shape[1], width)
        return sum(values[:, first : first + width] for first in blocks)
    shift = 64
    while shift >= width:
        values = values + pltpu.roll(values, shift, 1)
        shift //= 2
    return values[:, :width]


def analysed(place, pieces, y_forward, copies):
    height = 2 * MZ
    turned = sum(
        pieces[first : first + height].astype(F32) for first in range(0, pieces.shape[0], height)
    )
    channels = place.channels
    lines = jnp.concatenate(
        [turned[:, y * channels : (y + 1) * channels] for y in range(place.rows_y)], axis=0
    )
    return dot(y_forward, jnp.concatenate([lines.astype(BF16)] * copies, axis=1))


def spread_lines(place, modes, y_inverse):
    lines = dot(y_inverse, modes)
    step = 2 * place.kz
    blocks = []
    for n in range(place.narrow):
        first = n * place.rows_y
        parts = [lines[(first + y) * step : (first + y + 1) * step] for y in range(place.rows_y)]
        blocks.append(jnp.concatenate(parts, axis=1))
    return jnp.concatenate(blocks, axis=0).astype(BF16)


def turn_matrix(place, forward):
    channels, rows_y = place.channels, place.rows_y

    def same(row, column):
        if forward:
            row, column = column, row
        return (row % channels == column // rows_y) & (row // channels == column % rows_y)

    return selector(place.lanes, place.lanes, same)


def side_by_side(values, count):
    height = values.shape[0] // count
    return jnp.concatenate([values[y * height : (y + 1) * height] for y in range(count)], axis=1)


def one_below_other(values, count):
    width = values.shape[1] // count
    return jnp.concatenate([values[:, y * width : (y + 1) * width] for y in range(count)], axis=0)


def own_kernel(place, field_ref, field_out_ref, spectra_ref):
    turned = dot(turn_matrix(place, False), field_ref[...]).astype(BF16)
    field_out_ref[...] = side_by_side(turned, place.rows_y)
    spectra_ref[...] = dot_nt(place.z_table(False), turned).astype(BF16)


def start_kernel(place, spectra_ref, twin_ref, send_ref):
    twin = dot_nt(place.z_table(False), twin_ref[...]).astype(BF16)
    twin = dot(twin, turn_matrix(place, True)).astype(BF16)
    values = jnp.concatenate([spectra_ref[...], twin], axis=0)
    tables = jnp.concatenate(halves(place.forward_x(place.firsts[0])), axis=1)
    send_ref[...] = dot(tables, jnp.concatenate([values, values], axis=0)).astype(BF16)


def pack_kernel(place, weight_ref, packed_ref, inverse_ref):
    inverse_ref[...] = place.inverse_x(place.firsts[1])
    modes, kz, _, channels, _ = weight_ref.shape
    for q in range(modes // 4):
        parts = [weight_ref[4 * q + j // 2, :, j % 2] for j in range(8)]
        packed = jnp.concatenate(parts, axis=-1).reshape(kz * channels, 8 * channels)
        packed_ref[q] = packed.astype(BF16)


def ready_kernel(place, field_ref, mix_ref, mix_bias_ref, head_ref, *refs):
    pointwise_ref, head_out_ref, z_doubled_ref = refs
    pointwise_ref[...] = dot_tn(mix_ref[...], field_ref[...]) + mix_bias_ref[...]
    head_out_ref[...] = jnp.transpose(head_ref[...].astype(F32)).astype(BF16)
    z_doubled_ref[...] = place.z_table(True)


def fold_kernel(place, own_ref, got_ref, tables_ref, *refs):
    values = jnp.concatenate([own_ref[...], got_ref[...]], axis=0)
    values = jnp.concatenate([values, values], axis=0)
    partial = dot(tables_ref[...], values).astype(BF16)
    if place.fold:
        shares_ref, send_ref = refs
        write_pieces(place, send_ref, partial, shares_ref[...])
    else:
        refs[0][...] = partial


def mode_kernel(
    place, pieces_ref, y_forward_ref, y_inverse_ref, weight_ref, spectrum_ref, send_ref
):
    kz, channels = place.kz, place.channels
    spectrum = analysed(place, pieces_ref[...], y_forward_ref[...], kz)
    spectrum_ref[...] = spectrum[:, :channels]
    row, lane = grid_of(*spectrum.shape)
    blocked = jnp.where(row % kz == lane // channels, spectrum, 0.0)
    mixed = []
    for q in range(place.modes // 4):
        left = blocked[q * 8 * kz : (q + 1) * 8 * kz].astype(BF16)
        product = dot(left, weight_ref[q])
        for j in range(4):
            own = product[j * 2 * kz : (j + 1) * 2 * kz, j * 2 * channels : (j + 1) * 2 * channels]
            real, imag = own[:, :channels], own[:, channels:]
            mixed.append(real[:kz] - imag[kz:])
            mixed.append(imag[:kz] + real[kz:])
    mode = jnp.concatenate(mixed, axis=0).astype(BF16)
    repeat_rows(send_ref, spread_lines(place, mode, y_inverse_ref[...]))


def part_kernel(place, pieces_ref, table_ref, *refs):
    pieces, shares = read_pieces(place, pieces_ref)
    lines = dot(table_ref[...], pieces)
    height = 2 * MZ
    if shares is None:
        own_ref, send_ref = refs
        own_ref[...] = lines[:height]
        send_ref[...] = lines[height:].astype(BF16)
        return
    _, own_ref, send_ref, sums_ref = refs
    own_ref[...] = lines[:height]
    send_ref[:height] = lines[height:].astype(BF16)
    got = jnp.concatenate(shares, axis=0).astype(BF16)
    channels = place.channels

    def chosen(part):
        def condition(row, column):
            owner, source = (row % channels) // 2, column // 8
            return (
                (owner == source)
                & (column % 8 == 4 * part + 2 * (row // channels) + row % 2)
            )

        return dot(selector(2 * channels, got.shape[0], condition), got)

    high, low = chosen(0), chosen(1)
    sums_ref[...] = high + low
    send_ref[height:] = jnp.concatenate([high, low], axis=1).astype(BF16)


def normal(values):
    scaled = pl.reciprocal(1.0 + jnp.abs(TAIL_SLOPE * values), approx=True)
    decay = jnp.exp2(values * values * (-0.5 / math.log(2.0)))
    tail = TAIL[-1]
    for factor in TAIL[-2::-1]:
        tail = tail * scaled + factor
    tail = tail * (scaled * decay)
    cumulative = jnp.where(values > 0.0, 1.0 - tail, tail)
    return values * cumulative, cumulative + values * (decay * (1.0 / math.sqrt(2.0 * math.pi)))


def cell_kernel(place, *refs):
    own_ref, got_ref, z_table_ref, pointwise_ref, head_ref, head_turned_ref = refs[:6]
    head_bias_ref, out_row_ref, out_column_ref, cotangent_ref = refs[6:10]
    prediction_ref, grad_pre_ref, send_ref, hidden_ref, head_slope_ref = refs[10:]
    rows_y, z_count = place.rows_y, place.z_count
    z_table = z_table_ref[...]
    lines = (own_ref[...] + got_ref[...].astype(F32)).astype(BF16)
    pre_act = side_by_side(dot_tn(lines, z_table), rows_y) + pointwise_ref[...]
    head, head_turned = head_ref[...], head_turned_ref[...]
    head_bias, out_row, out_column = head_bias_ref[...], out_row_ref[...], out_column_ref[...]
    width = 2 * z_count
    slopes, head_pre = [], []
    for first in range(0, rows_y * z_count, width):
        value, slope = normal(pre_act[:, first : first + width])
        hidden = value.astype(BF16)
        hidden_ref[:, first : first + width] = hidden
        slopes.append(slope)
        head_pre.append(dot(head_turned, hidden))
    gradients = []
    for index, first in enumerate(range(0, rows_y, 2)):
        target = jnp.concatenate(
            [cotangent_ref[y : y + 1] for y in range(first, first + 2)], axis=1
        )
        active, slope = normal(head_pre[index] + head_bias)
        predicted = dot(out_row, active.astype(BF16))
        prediction_ref[first : first + 1] = predicted[:, :z_count]
        prediction_ref[first + 1 : first + 2] = predicted[:, z_count:]
        head_slope = (target * out_column * slope).astype(BF16)
        head_slope_ref[:, first * z_count : first * z_count + width] = head_slope
        gradients.append((dot(head, head_slope) * slopes[index]).astype(BF16))
    gradient = jnp.concatenate(gradients, axis=1)
    grad_pre_ref[...] = gradient
    send_ref[...] = dot_nt(z_table, one_below_other(gradient, rows_y)).astype(BF16)


def sums_kernel(place, field_ref, gradient_ref, hidden_ref, head_slope_ref, *refs):
    refs[-1][...] = jnp.concatenate(halves(place.forward_x(place.firsts[2])), axis=1)
    grad_mix = dot_nt(field_ref[...], gradient_ref[...])
    grad_head = dot_nt(hidden_ref[...], head_slope_ref[...])
    if not place.fold:
        refs[0][...] = grad_mix
        refs[1][...] = grad_head
        return
    channels, hidden_units = grad_head.shape
    rest = jnp.zeros((channels, hidden_units - channels), F32)
    wide_mix = jnp.concatenate([grad_mix, rest], axis=1)
    high, low = halves(jnp.concatenate([grad_head, wide_mix], axis=0))
    split = jnp.concatenate([high, low], axis=0)
    place_of = selector(
        8 * place.partners,
        4 * channels,
        lambda row, column: (column % channels == 2 * (row // 8) + row % 2)
        & (column // channels == (row % 8) // 2),
    )
    refs[0][...] = dot(place_of, split).astype(BF16)


def back_kernel(
    place, pieces_ref, y_forward_ref, y_inverse_ref, weight_ref, adjoint_ref, send_ref
):
    kz, channels = place.kz, place.channels
    pieces, shares = read_pieces(place, pieces_ref)
    adjoint = analysed(place, pieces, y_forward_ref[...], 1)
    adjoint_ref[...] = adjoint
    turned = []
    for first in range(0, adjoint.shape[0], 2 * kz):
        turned += [adjoint[first + kz : first + 2 * kz], -adjoint[first : first + kz]]
    left = jnp.concatenate([adjoint, jnp.concatenate(turned, axis=0)], axis=1)
    left = jnp.concatenate([left] * 4, axis=1)
    row, lane = grid_of(*left.shape)
    same = (row // (2 * kz)) % 4 == lane // (2 * channels)
    left = jnp.where(same, left, 0.0).astype(BF16)
    block = 8 * kz
    pulled = [
        dot_nt(left[q * block : (q + 1) * block], weight_ref[q]) for q in range(place.modes // 4)
    ]
    pulled = jnp.concatenate(pulled, axis=0)
    row, lane = grid_of(*pulled.shape)
    pulled = jnp.where(row % kz == lane // channels, pulled, 0.0)
    modes_back = lane_sum(pulled, channels).astype(BF16)
    block = spread_lines(place, modes_back, y_inverse_ref[...])
    if shares is None:
        repeat_rows(send_ref, block)
        return
    total = sum(shares[1:], shares[0])
    high, low = halves(total[0:4] + total[4:8])
    split = jnp.concatenate([high.astype(F32), low.astype(F32)], axis=0)
    write_pieces(place, send_ref, block, split.astype(BF16))


def outer_kernel(spectrum_ref, adjoint_ref, out_ref, done_ref):
    done_ref[...] = jnp.zeros(done_ref.shape, F32)
    modes, kz = out_ref.shape[:2]
    for j in range(modes):
        columns = jnp.transpose(spectrum_ref[j])
        adjoint = adjoint_ref[j]
        for k in range(kz):
            s_real, s_imag = columns[:, k : k + 1], columns[:, kz + k : kz + k + 1]
            a_real, a_imag = adjoint[k : k + 1], adjoint[kz + k : kz + k + 1]
            out_ref[j, k, 0] = s_real * a_real + s_imag * a_imag
            out_ref[j, k, 1] = s_real * a_imag - s_imag * a_real


def pointwise_kernel(place, mix_ref, gradient_ref, out_ref, z_plain_ref, turn_ref):
    z_plain_ref[...] = place.z_table(False)
    turn_ref[...] = turn_matrix(place, False)
    z_count = place.z_count
    product = dot(mix_ref[...], gradient_ref[...])
    for y in range(place.rows_y):
        out_ref[:, y, :] = product[:, y * z_count : (y + 1) * z_count]


def finish_kernel(place, *refs):
    own_ref, got_ref, z_table_ref, turn_ref, pointwise_ref, prediction_ref = refs[:6]
    refs = refs[6:]
    height = 2 * MZ
    channels = place.channels
    lines = (own_ref[...] + got_ref[:height].astype(F32)).astype(BF16)
    lines = dot(lines, turn_ref[...]).astype(BF16)
    pointwise = pointwise_ref[...].reshape(place.lanes, place.z_count)
    grad_field = (dot_tn(lines, z_table_ref[...]) + pointwise).astype(BF16)
    if not place.fold:
        refs[0][...] = grad_field
        refs[1][...] = prediction_ref[...]
        return
    sums_ref, grad_field_ref, out_ref, grad_mix_ref, grad_head_ref = refs
    grad_field_ref[...] = grad_field
    out_ref[...] = prediction_ref[...]
    got = got_ref[height:].astype(F32)
    width = sums_ref.shape[1]
    total = sums_ref[...] + got[:, :width] + got[:, width:]
    grad_head_ref[...] = total[:channels]
    grad_mix_ref[...] = total[channels:, :channels]


def call(kernel, outs, name, **spec):
    return pl.pallas_call(
        kernel,
        out_shape=[jax.ShapeDtypeStruct(shape, dtype) for shape, dtype in outs],
        compiler_params=pltpu.CompilerParams(vmem_limit_bytes=VMEM_LIMIT),
        cost_estimate=pl.CostEstimate(flops=1 << 22, bytes_accessed=1 << 19, transcendentals=0),
        name=name,
        **spec,
    )


def body(
    lifted_field,
    spectral_weight,
    mix_weight,
    mix_bias,
    head_weight,
    head_bias,
    out_weight,
    cotangent,
):
    wide = lax.axis_size("wide")
    narrow = lax.axis_size("narrow")
    devices = wide * narrow
    _, channels, rows_y, z_count = lifted_field.shape
    modes, kz = spectral_weight.shape[:2]
    hidden_units = head_weight.shape[1]
    cells = channels * rows_y
    place = Place(wide, narrow, kz, modes, rows_y, channels, z_count, False)
    place.fold = 2 * place.partners == channels and hidden_units == 128 and cells == 256 and kz % 8 == 0
    height = 2 * MZ
    step = 2 * kz
    partners = place.partners
    mode_lines = modes * 2 * kz

    y_forward, y_inverse = y_tables(rows_y * narrow, rows_y, kz, modes)
    if len(y_forward) > 1:
        block = lax.axis_index("wide") % len(y_forward)
        y_forward = lax.dynamic_index_in_dim(jnp.asarray(y_forward), block, 0, False)
        y_inverse = lax.dynamic_index_in_dim(jnp.asarray(y_inverse), block, 0, False)
    else:
        y_forward, y_inverse = jnp.asarray(y_forward[0]), jnp.asarray(y_inverse[0])

    def to_twin(send):
        pairs = [(p, p ^ narrow) for p in range(devices)]
        return lax.ppermute(send, ("wide", "narrow"), pairs)

    def exchange(send, transform):
        firsts = place.firsts[transform]
        groups = [
            [
                (2 * place.listed(outer, firsts, inner) + inner) * narrow + n
                for outer in range(place.outer)
                for n in range(narrow)
            ]
            for inner in range(2)
        ]
        pieces = send.reshape(partners, -1, send.shape[1])
        got = lax.all_to_all(
            pieces, ("wide", "narrow"), 0, 0, axis_index_groups=groups, tiled=True
        )
        return got.reshape(send.shape)

    plain = ((partners * step, cells), BF16)
    shared = ((partners * (2 * step + 8), cells // 2), BF16) if place.fold else plain
    twin_plain = ((height, cells), BF16)
    twin_shared = ((height + 2 * channels, cells), BF16) if place.fold else twin_plain
    sums_shape = ((2 * channels, hidden_units), F32)
    own_lines = ((height, cells), F32)
    across = (channels, rows_y * z_count)

    def run(kernel, outs, name, **spec):
        return call(functools.partial(kernel, place), outs, name, **spec)

    flat_field = lifted_field.reshape(cells, z_count)
    twin_field = to_twin(flat_field)
    field, spectra = run(own_kernel, [(across, BF16), twin_plain], "own")(flat_field)
    (send,) = run(start_kernel, [plain], "start")(spectra, twin_field)
    packed_shape = ((modes // 4, kz * channels, 8 * channels), BF16)
    inverse_shape = ((2 * height, wide // 2 * height), BF16)
    weight, inverse = run(pack_kernel, [packed_shape, inverse_shape], "pack")(spectral_weight)
    spectrum, send = run(mode_kernel, [((mode_lines, channels), F32), plain], "mode")(
        exchange(send, 0), y_forward, y_inverse, weight
    )
    own, send = run(part_kernel, [own_lines, twin_plain], "part")(exchange(send, 1), inverse)
    pointwise, head_turned, z_doubled = run(
        ready_kernel,
        [(across, F32), ((hidden_units, channels), BF16), ((height, z_count), BF16)],
        "ready",
    )(field, mix_weight, mix_bias[:, None], head_weight)
    prediction, grad_pre, send, hidden, head_slope = run(
        cell_kernel,
        [
            ((rows_y, z_count), F32),
            (across, BF16),
            twin_plain,
            (across, BF16),
            ((hidden_units, rows_y * z_count), BF16),
        ],
        "cell",
    )(
        own,
        to_twin(send),
        z_doubled,
        pointwise,
        head_weight,
        head_turned,
        head_bias[:, None],
        out_weight[None],
        out_weight.astype(F32)[:, None],
        cotangent[0],
    )
    if place.fold:
        outs = [((8 * partners, hidden_units), BF16)]
    else:
        outs = [((channels, channels), F32), ((channels, hidden_units), F32)]
    outs += [((wide // 2 * height, 4 * height), BF16)]
    *sums, forward = run(sums_kernel, outs, "sums")(field, grad_pre, hidden, head_slope)
    if not place.fold:
        totals = lax.psum(tuple(sums), ("wide", "narrow"))
        sums = []
    (send,) = run(fold_kernel, [shared], "fold")(send, to_twin(send), forward, *sums)
    adjoint, send = run(back_kernel, [((mode_lines, channels), F32), shared], "back")(
        exchange(send, 2), y_forward, y_inverse, weight
    )
    some = max(1, modes // 4)
    grad_spectral, done = pl.pallas_call(
        outer_kernel,
        grid=(modes // some,),
        in_specs=[pl.BlockSpec((some, 2 * kz, channels), lambda j: (j, 0, 0))] * 2,
        out_specs=[
            pl.BlockSpec((some, kz, 2, channels, channels), lambda j: (j, 0, 0, 0, 0)),
            pl.BlockSpec((8, 128), lambda j: (0, 0)),
        ],
        out_shape=[
            jax.ShapeDtypeStruct(spectral_weight.shape, F32),
            jax.ShapeDtypeStruct((8, 128), F32),
        ],
        compiler_params=pltpu.CompilerParams(vmem_limit_bytes=VMEM_LIMIT),
        cost_estimate=pl.CostEstimate(flops=1 << 22, bytes_accessed=5 << 20, transcendentals=0),
        name="outer",
    )(spectrum.reshape(modes, 2 * kz, channels), adjoint.reshape(modes, 2 * kz, channels))
    pointwise, z_plain, turn = run(
        pointwise_kernel,
        [
            ((channels, rows_y, z_count), F32),
            ((height, z_count), BF16),
            ((cells, cells), BF16),
        ],
        "pointwise",
    )(mix_weight, grad_pre)
    outs = [own_lines, twin_shared] + ([sums_shape] if place.fold else [])
    after = (done,) if place.fold else ()
    own, send, *sums = run(part_kernel, outs, "part")(exchange(send, 3), inverse, *after)
    outs = [((cells, z_count), BF16), ((rows_y, z_count), F32)]
    if place.fold:
        outs += [((channels, channels), F32), ((channels, hidden_units), F32)]
    grad_field, prediction, *summed = run(finish_kernel, outs, "finish")(
        own, to_twin(send), z_plain, turn, pointwise, prediction, *sums
    )
    grad_mix, grad_head = summed if place.fold else totals
    return (
        prediction[None],
        grad_field.reshape(lifted_field.shape),
        grad_spectral,
        grad_mix,
        grad_head,
    )


def solution(mesh):
    return jax.shard_map(
        body,
        mesh=mesh,
        in_specs=(
            P("wide", None, "narrow", None),
            P("wide", "narrow", None, None, None),
            P(),
            P(),
            P(),
            P(),
            P(),
            P("wide", "narrow", None),
        ),
        out_specs=(
            P("wide", "narrow", None),
            P("wide", None, "narrow", None),
            P("wide", "narrow", None, None, None),
            P(),
            P(),
        ),
        check_vma=False,
    )
```

```python
import functools
import math

import jax
import jax.numpy as jnp
import numpy as np
from jax import lax
from jax.experimental import pallas as pl
from jax.experimental.pallas import tpu as pltpu
from jax.sharding import PartitionSpec as P

MX = 16
MY = 16
MZ = 16
F32 = jnp.float32
BF16 = jnp.bfloat16
VMEM_LIMIT = 32 * 1024 * 1024

TAIL_SLOPE = 0.275
TAIL = (
    0.11780925840139389,
    0.04211147502064705,
    0.3339323103427887,
    -0.3309934139251709,
    0.4519987106323242,
    -0.11485832929611206,
)


def signed(indices, count):
    return np.where(indices < count // 2, indices, indices - count)


def wave(positions, frequency, length):
    turned = np.mod(np.multiply.outer(positions, frequency), length)
    angles = turned.astype(np.float32) * np.float32(2.0 * math.pi / length)
    scale = np.float32(1.0 / math.sqrt(length))
    return np.cos(angles) * scale, np.sin(angles) * scale


def pair(cosine, sine, sign):
    return np.stack(
        [np.stack([cosine, -sign * sine], -1), np.stack([sign * sine, cosine], -1)], -2
    )


def y_tables(total_y, rows_y, kz, modes):
    cosine, sine = wave(np.arange(total_y), signed(np.arange(MY), MY), total_y)
    narrow = total_y // rows_y
    same = np.eye(kz, dtype=np.float32)
    forward = pair(cosine, sine, -1.0).reshape(narrow, rows_y, MY // modes, modes, 2, 2)
    inverse = pair(cosine, sine, 1.0).reshape(narrow, rows_y, MY // modes, modes, 2, 2)
    forward = np.einsum("nybjtr,kl->bjtkynlr", forward, same)
    inverse = np.einsum("nybjst,kl->bnyksjtl", inverse, same)
    blocks = MY // modes
    forward = forward.reshape(blocks, modes * 2 * kz, rows_y * narrow * kz * 2)
    inverse = inverse.reshape(blocks, narrow * rows_y * kz * 2, modes * 2 * kz)
    return forward.astype(BF16), inverse.astype(BF16)


def dot(a, b):
    return jnp.dot(a, b, preferred_element_type=F32)


def dot_nt(a, b):
    return lax.dot_general(a, b, (((1,), (1,)), ((), ())), preferred_element_type=F32)


def dot_tn(a, b):
    return lax.dot_general(a, b, (((0,), (0,)), ((), ())), preferred_element_type=F32)


def grid_of(rows, columns):
    shape = (rows, columns)
    return lax.broadcasted_iota(jnp.int32, shape, 0), lax.broadcasted_iota(jnp.int32, shape, 1)


def selector(rows, columns, condition):
    return jnp.where(condition(*grid_of(rows, columns)), 1.0, 0.0).astype(BF16)


def halves(values):
    high = values.astype(BF16)
    return high, (values - high.astype(F32)).astype(BF16)


def stacked(refs, lanes=slice(None)):
    return jnp.concatenate([ref[:, lanes] for ref in refs], axis=0)


def cosine_of(phase, length):
    angles = (phase & (length - 1)).astype(F32) * (2.0 * math.pi / length)
    return jnp.cos(angles) * (1.0 / math.sqrt(length))


class Place:
    def __init__(self, wide, narrow, kz, modes, rows_y, channels, z_count, fold):
        self.wide, self.narrow, self.kz, self.modes = wide, narrow, kz, modes
        self.rows_y, self.channels, self.z_count, self.fold = rows_y, channels, z_count, fold
        self.outer = wide // 2
        self.partners = self.outer * narrow
        self.lanes = rows_y * channels
        middle, last = self.outer // 4, self.outer // 2 - 1
        self.firsts = ((last, last), (middle, middle - 1), (middle, middle - 1), (middle, middle - 1))

    def here(self):
        wide = lax.axis_index("wide")
        return wide // 2, wide % 2

    def listed(self, position, firsts, inner):
        lines = self.outer // 2
        first = firsts[0] + (firsts[1] - firsts[0]) * inner
        return ((first + position // 2) & (lines - 1)) * 2 + position % 2

    def frequency(self, wide):
        index = (wide * self.modes) // MY
        return jnp.where(index < MX // 2, index, index - MX)

    def z_table(self, doubled):
        row, z = grid_of(2 * MZ, self.z_count)
        frequency = row >> 1
        value = cosine_of(z * frequency + (row & 1) * (self.z_count // 4), self.z_count)
        if doubled:
            value = jnp.where(frequency > 0, 2.0 * value, value)
        return value.astype(BF16)

    def expanded(self, small):
        row, column = grid_of(2 * MZ, small.shape[1])
        same = (row >> 1) == ((column >> 1) & (MZ - 1))
        blocks = []
        for g in range(small.shape[0] // 2):
            value = jnp.where((row & 1) == 0, small[2 * g : 2 * g + 1], small[2 * g + 1 : 2 * g + 2])
            blocks.append(jnp.where(same, value, 0.0))
        return jnp.concatenate(blocks, axis=0)

    def forward_x(self, firsts):
        outer, inner = self.here()
        row, column = grid_of(2 * self.outer, 4 * MZ)
        x = 2 * outer + (inner ^ (column // (2 * MZ)))
        frequency = self.frequency(2 * self.listed(row >> 1, firsts, inner) + inner)
        quarter = self.wide // 4
        small = cosine_of(x * frequency + quarter * ((row & 1) - (column & 1)), self.wide)
        return self.expanded(small)

    def inverse_x(self, firsts):
        outer, inner = self.here()
        row, column = grid_of(4, self.outer * 2 * MZ)
        x = 2 * outer + (inner ^ (row >> 1))
        frequency = self.frequency(2 * self.listed(column // (2 * MZ), firsts, inner) + inner)
        quarter = self.wide // 4
        small = cosine_of(x * frequency + quarter * ((column & 1) - (row & 1)), self.wide)
        return self.expanded(small).astype(BF16)


def repeat_rows(out_ref, block):
    height = block.shape[0]
    for first in range(0, out_ref.shape[0], height):
        out_ref[first : first + height] = block


def write_pieces(place, send_ref, block, shares):
    step, half = 2 * place.kz, place.lanes // 2
    height = send_ref.shape[0] // place.partners
    for p in range(place.partners):
        own = block[p * step % block.shape[0] :][:step]
        first = p * height
        send_ref[first : first + step] = own[:, :half]
        send_ref[first + step : first + 2 * step] = own[:, half:]
        send_ref[first + 2 * step : first + height] = shares[p * 8 % shares.shape[0] :][:8]


def read_pieces(place, pieces_ref):
    step = 2 * place.kz
    if pieces_ref.shape[1] == place.lanes:
        return pieces_ref[...], None
    height = pieces_ref.shape[0] // place.partners
    blocks, shares = [], []
    for p in range(place.partners):
        first = p * height
        left = pieces_ref[first : first + step]
        right = pieces_ref[first + step : first + 2 * step]
        blocks.append(jnp.concatenate([left, right], axis=1))
        shares.append(pieces_ref[first + 2 * step : first + height].astype(F32))
    return jnp.concatenate(blocks, axis=0), shares


def lane_sum(values, width):
    while values.shape[1] > 128:
        half = values.shape[1] // 2
        values = values[:, :half] + values[:, half:]
    if values.shape[1] < 128:
        blocks = range(0, values.shape[1], width)
        return sum(values[:, first : first + width] for first in blocks)
    shift = 64
    while shift >= width:
        values = values + pltpu.roll(values, shift, 1)
        shift //= 2
    return values[:, :width]


def analysed(place, pieces, y_forward, copies):
    height = 2 * MZ
    turned = sum(
        pieces[first : first + height].astype(F32) for first in range(0, pieces.shape[0], height)
    )
    channels = place.channels
    lines = jnp.concatenate(
        [turned[:, y * channels : (y + 1) * channels] for y in range(place.rows_y)], axis=0
    )
    return dot(y_forward, jnp.concatenate([lines.astype(BF16)] * copies, axis=1))


def spread_lines(place, modes, y_inverse):
    lines = dot(y_inverse, modes)
    step = 2 * place.kz
    blocks = []
    for n in range(place.narrow):
        first = n * place.rows_y
        parts = [lines[(first + y) * step : (first + y + 1) * step] for y in range(place.rows_y)]
        blocks.append(jnp.concatenate(parts, axis=1))
    return jnp.concatenate(blocks, axis=0).astype(BF16)


def turn_matrix(place, forward):
    channels, rows_y = place.channels, place.rows_y

    def same(row, column):
        if forward:
            row, column = column, row
        return (row % channels == column // rows_y) & (row // channels == column % rows_y)

    return selector(place.lanes, place.lanes, same)


def side_by_side(values, count):
    height = values.shape[0] // count
    return jnp.concatenate([values[y * height : (y + 1) * height] for y in range(count)], axis=1)


def one_below_other(values, count):
    width = values.shape[1] // count
    return jnp.concatenate([values[:, y * width : (y + 1) * width] for y in range(count)], axis=0)


def own_kernel(place, field_ref, field_out_ref, spectra_ref):
    turned = dot(turn_matrix(place, False), field_ref[...]).astype(BF16)
    field_out_ref[...] = side_by_side(turned, place.rows_y)
    spectra_ref[...] = dot_nt(place.z_table(False), turned).astype(BF16)


def start_kernel(place, spectra_ref, twin_ref, send_ref):
    twin = dot_nt(place.z_table(False), twin_ref[...]).astype(BF16)
    twin = dot(twin, turn_matrix(place, True)).astype(BF16)
    values = jnp.concatenate([spectra_ref[...], twin], axis=0)
    tables = jnp.concatenate(halves(place.forward_x(place.firsts[0])), axis=1)
    send_ref[...] = dot(tables, jnp.concatenate([values, values], axis=0)).astype(BF16)


def pack_kernel(place, weight_ref, packed_ref, inverse_ref):
    inverse_ref[...] = place.inverse_x(place.firsts[1])
    modes, kz, _, channels, _ = weight_ref.shape
    for q in range(modes // 4):
        parts = [weight_ref[4 * q + j // 2, :, j % 2] for j in range(8)]
        packed = jnp.concatenate(parts, axis=-1).reshape(kz * channels, 8 * channels)
        packed_ref[q] = packed.astype(BF16)


def ready_kernel(place, field_ref, mix_ref, mix_bias_ref, head_ref, *refs):
    pointwise_ref, head_out_ref, z_doubled_ref = refs
    pointwise_ref[...] = dot_tn(mix_ref[...], field_ref[...]) + mix_bias_ref[...]
    head_out_ref[...] = jnp.transpose(head_ref[...].astype(F32)).astype(BF16)
    z_doubled_ref[...] = place.z_table(True)


def fold_kernel(place, own_ref, got_ref, tables_ref, *refs):
    values = jnp.concatenate([own_ref[...], got_ref[...]], axis=0)
    values = jnp.concatenate([values, values], axis=0)
    partial = dot(tables_ref[...], values).astype(BF16)
    if place.fold:
        shares_ref, send_ref = refs
        write_pieces(place, send_ref, partial, shares_ref[...])
    else:
        refs[0][...] = partial


def mode_kernel(
    place, pieces_ref, y_forward_ref, y_inverse_ref, weight_ref, spectrum_ref, send_ref
):
    kz, channels = place.kz, place.channels
    spectrum = analysed(place, pieces_ref[...], y_forward_ref[...], kz)
    spectrum_ref[...] = spectrum[:, :channels]
    row, lane = grid_of(*spectrum.shape)
    blocked = jnp.where(row % kz == lane // channels, spectrum, 0.0)
    mixed = []
    for q in range(place.modes // 4):
        left = blocked[q * 8 * kz : (q + 1) * 8 * kz].astype(BF16)
        product = dot(left, weight_ref[q])
        for j in range(4):
            own = product[j * 2 * kz : (j + 1) * 2 * kz, j * 2 * channels : (j + 1) * 2 * channels]
            real, imag = own[:, :channels], own[:, channels:]
            mixed.append(real[:kz] - imag[kz:])
            mixed.append(imag[:kz] + real[kz:])
    mode = jnp.concatenate(mixed, axis=0).astype(BF16)
    repeat_rows(send_ref, spread_lines(place, mode, y_inverse_ref[...]))


def part_kernel(place, pieces_ref, table_ref, *refs):
    pieces, shares = read_pieces(place, pieces_ref)
    lines = dot(table_ref[...], pieces)
    height = 2 * MZ
    if shares is None:
        own_ref, send_ref = refs
        own_ref[...] = lines[:height]
        send_ref[...] = lines[height:].astype(BF16)
        return
    _, own_ref, send_ref, sums_ref = refs
    own_ref[...] = lines[:height]
    send_ref[:height] = lines[height:].astype(BF16)
    got = jnp.concatenate(shares, axis=0).astype(BF16)
    channels = place.channels

    def chosen(part):
        def condition(row, column):
            owner, source = (row % channels) // 2, column // 8
            return (
                (owner == source)
                & (column % 8 == 4 * part + 2 * (row // channels) + row % 2)
            )

        return dot(selector(2 * channels, got.shape[0], condition), got)

    high, low = chosen(0), chosen(1)
    sums_ref[...] = high + low
    send_ref[height:] = jnp.concatenate([high, low], axis=1).astype(BF16)


def normal(values):
    scaled = pl.reciprocal(1.0 + jnp.abs(TAIL_SLOPE * values), approx=True)
    decay = jnp.exp2(values * values * (-0.5 / math.log(2.0)))
    tail = TAIL[-1]
    for factor in TAIL[-2::-1]:
        tail = tail * scaled + factor
    tail = tail * (scaled * decay)
    cumulative = jnp.where(values > 0.0, 1.0 - tail, tail)
    return values * cumulative, cumulative + values * (decay * (1.0 / math.sqrt(2.0 * math.pi)))


def cell_kernel(place, *refs):
    own_ref, got_ref, z_table_ref, pointwise_ref, head_ref, head_turned_ref = refs[:6]
    head_bias_ref, out_row_ref, out_column_ref, cotangent_ref = refs[6:10]
    prediction_ref, grad_pre_ref, send_ref, hidden_ref, head_slope_ref = refs[10:]
    rows_y, z_count = place.rows_y, place.z_count
    z_table = z_table_ref[...]
    lines = (own_ref[...] + got_ref[...].astype(F32)).astype(BF16)
    pre_act = side_by_side(dot_tn(lines, z_table), rows_y) + pointwise_ref[...]
    head, head_turned = head_ref[...], head_turned_ref[...]
    head_bias, out_row, out_column = head_bias_ref[...], out_row_ref[...], out_column_ref[...]
    width = 2 * z_count
    slopes, head_pre = [], []
    for first in range(0, rows_y * z_count, width):
        value, slope = normal(pre_act[:, first : first + width])
        hidden = value.astype(BF16)
        hidden_ref[:, first : first + width] = hidden
        slopes.append(slope)
        head_pre.append(dot(head_turned, hidden))
    gradients = []
    for index, first in enumerate(range(0, rows_y, 2)):
        target = jnp.concatenate(
            [cotangent_ref[y : y + 1] for y in range(first, first + 2)], axis=1
        )
        active, slope = normal(head_pre[index] + head_bias)
        predicted = dot(out_row, active.astype(BF16))
        prediction_ref[first : first + 1] = predicted[:, :z_count]
        prediction_ref[first + 1 : first + 2] = predicted[:, z_count:]
        head_slope = (target * out_column * slope).astype(BF16)
        head_slope_ref[:, first * z_count : first * z_count + width] = head_slope
        gradients.append((dot(head, head_slope) * slopes[index]).astype(BF16))
    gradient = jnp.concatenate(gradients, axis=1)
    grad_pre_ref[...] = gradient
    send_ref[...] = dot_nt(z_table, one_below_other(gradient, rows_y)).astype(BF16)


def sums_kernel(place, field_ref, gradient_ref, hidden_ref, head_slope_ref, *refs):
    refs[-1][...] = jnp.concatenate(halves(place.forward_x(place.firsts[2])), axis=1)
    grad_mix = dot_nt(field_ref[...], gradient_ref[...])
    grad_head = dot_nt(hidden_ref[...], head_slope_ref[...])
    if not place.fold:
        refs[0][...] = grad_mix
        refs[1][...] = grad_head
        return
    channels, hidden_units = grad_head.shape
    rest = jnp.zeros((channels, hidden_units - channels), F32)
    wide_mix = jnp.concatenate([grad_mix, rest], axis=1)
    high, low = halves(jnp.concatenate([grad_head, wide_mix], axis=0))
    split = jnp.concatenate([high, low], axis=0)
    place_of = selector(
        8 * place.partners,
        4 * channels,
        lambda row, column: (column % channels == 2 * (row // 8) + row % 2)
        & (column // channels == (row % 8) // 2),
    )
    refs[0][...] = dot(place_of, split).astype(BF16)


def back_kernel(
    place, pieces_ref, y_forward_ref, y_inverse_ref, weight_ref, adjoint_ref, send_ref
):
    kz, channels = place.kz, place.channels
    pieces, shares = read_pieces(place, pieces_ref)
    adjoint = analysed(place, pieces, y_forward_ref[...], 1)
    adjoint_ref[...] = adjoint
    turned = []
    for first in range(0, adjoint.shape[0], 2 * kz):
        turned += [adjoint[first + kz : first + 2 * kz], -adjoint[first : first + kz]]
    left = jnp.concatenate([adjoint, jnp.concatenate(turned, axis=0)], axis=1)
    left = jnp.concatenate([left] * 4, axis=1)
    row, lane = grid_of(*left.shape)
    same = (row // (2 * kz)) % 4 == lane // (2 * channels)
    left = jnp.where(same, left, 0.0).astype(BF16)
    block = 8 * kz
    pulled = [
        dot_nt(left[q * block : (q + 1) * block], weight_ref[q]) for q in range(place.modes // 4)
    ]
    pulled = jnp.concatenate(pulled, axis=0)
    row, lane = grid_of(*pulled.shape)
    pulled = jnp.where(row % kz == lane // channels, pulled, 0.0)
    modes_back = lane_sum(pulled, channels).astype(BF16)
    block = spread_lines(place, modes_back, y_inverse_ref[...])
    if shares is None:
        repeat_rows(send_ref, block)
        return
    total = sum(shares[1:], shares[0])
    high, low = halves(total[0:4] + total[4:8])
    split = jnp.concatenate([high.astype(F32), low.astype(F32)], axis=0)
    write_pieces(place, send_ref, block, split.astype(BF16))


def outer_kernel(spectrum_ref, adjoint_ref, out_ref, done_ref):
    done_ref[...] = jnp.zeros(done_ref.shape, F32)
    modes, kz = out_ref.shape[:2]
    for j in range(modes):
        columns = jnp.transpose(spectrum_ref[j])
        adjoint = adjoint_ref[j]
        for k in range(kz):
            s_real, s_imag = columns[:, k : k + 1], columns[:, kz + k : kz + k + 1]
            a_real, a_imag = adjoint[k : k + 1], adjoint[kz + k : kz + k + 1]
            out_ref[j, k, 0] = s_real * a_real + s_imag * a_imag
            out_ref[j, k, 1] = s_real * a_imag - s_imag * a_real


def pointwise_kernel(place, mix_ref, gradient_ref, out_ref, z_plain_ref, turn_ref):
    z_plain_ref[...] = place.z_table(False)
    turn_ref[...] = turn_matrix(place, False)
    z_count = place.z_count
    product = dot(mix_ref[...], gradient_ref[...])
    for y in range(place.rows_y):
        out_ref[:, y, :] = product[:, y * z_count : (y + 1) * z_count]


def finish_kernel(place, *refs):
    own_ref, got_ref, z_table_ref, turn_ref, pointwise_ref, prediction_ref = refs[:6]
    refs = refs[6:]
    height = 2 * MZ
    channels = place.channels
    lines = (own_ref[...] + got_ref[:height].astype(F32)).astype(BF16)
    lines = dot(lines, turn_ref[...]).astype(BF16)
    pointwise = pointwise_ref[...].reshape(place.lanes, place.z_count)
    grad_field = (dot_tn(lines, z_table_ref[...]) + pointwise).astype(BF16)
    if not place.fold:
        refs[0][...] = grad_field
        refs[1][...] = prediction_ref[...]
        return
    sums_ref, grad_field_ref, out_ref, grad_mix_ref, grad_head_ref = refs
    grad_field_ref[...] = grad_field
    out_ref[...] = prediction_ref[...]
    got = got_ref[height:].astype(F32)
    width = sums_ref.shape[1]
    total = sums_ref[...] + got[:, :width] + got[:, width:]
    grad_head_ref[...] = total[:channels]
    grad_mix_ref[...] = total[channels:, :channels]


def call(kernel, outs, name, **spec):
    return pl.pallas_call(
        kernel,
        out_shape=[jax.ShapeDtypeStruct(shape, dtype) for shape, dtype in outs],
        compiler_params=pltpu.CompilerParams(vmem_limit_bytes=VMEM_LIMIT),
        cost_estimate=pl.CostEstimate(flops=1 << 22, bytes_accessed=1 << 19, transcendentals=0),
        name=name,
        **spec,
    )


def body(
    lifted_field,
    spectral_weight,
    mix_weight,
    mix_bias,
    head_weight,
    head_bias,
    out_weight,
    cotangent,
):
    wide = lax.axis_size("wide")
    narrow = lax.axis_size("narrow")
    devices = wide * narrow
    _, channels, rows_y, z_count = lifted_field.shape
    modes, kz = spectral_weight.shape[:2]
    hidden_units = head_weight.shape[1]
    cells = channels * rows_y
    place = Place(wide, narrow, kz, modes, rows_y, channels, z_count, False)
    place.fold = 2 * place.partners == channels and hidden_units == 128 and cells == 256 and kz % 8 == 0
    height = 2 * MZ
    step = 2 * kz
    partners = place.partners
    mode_lines = modes * 2 * kz

    y_forward, y_inverse = y_tables(rows_y * narrow, rows_y, kz, modes)
    if len(y_forward) > 1:
        block = lax.axis_index("wide") % len(y_forward)
        y_forward = lax.dynamic_index_in_dim(jnp.asarray(y_forward), block, 0, False)
        y_inverse = lax.dynamic_index_in_dim(jnp.asarray(y_inverse), block, 0, False)
    else:
        y_forward, y_inverse = jnp.asarray(y_forward[0]), jnp.asarray(y_inverse[0])

    def to_twin(send):
        pairs = [(p, p ^ narrow) for p in range(devices)]
        return lax.ppermute(send, ("wide", "narrow"), pairs)

    def exchange(send, transform):
        firsts = place.firsts[transform]
        groups = [
            [
                (2 * place.listed(outer, firsts, inner) + inner) * narrow + n
                for outer in range(place.outer)
                for n in range(narrow)
            ]
            for inner in range(2)
        ]
        pieces = send.reshape(partners, -1, send.shape[1])
        got = lax.all_to_all(
            pieces, ("wide", "narrow"), 0, 0, axis_index_groups=groups, tiled=True
        )
        return got.reshape(send.shape)

    plain = ((partners * step, cells), BF16)
    shared = ((partners * (2 * step + 8), cells // 2), BF16) if place.fold else plain
    twin_plain = ((height, cells), BF16)
    twin_shared = ((height + 2 * channels, cells), BF16) if place.fold else twin_plain
    sums_shape = ((2 * channels, hidden_units), F32)
    own_lines = ((height, cells), F32)
    across = (channels, rows_y * z_count)

    def run(kernel, outs, name, **spec):
        return call(functools.partial(kernel, place), outs, name, **spec)

    flat_field = lifted_field.reshape(cells, z_count)
    twin_field = to_twin(flat_field)
    field, spectra = run(own_kernel, [(across, BF16), twin_plain], "own")(flat_field)
    (send,) = run(start_kernel, [plain], "start")(spectra, twin_field)
    packed_shape = ((modes // 4, kz * channels, 8 * channels), BF16)
    inverse_shape = ((2 * height, wide // 2 * height), BF16)
    weight, inverse = run(pack_kernel, [packed_shape, inverse_shape], "pack")(spectral_weight)
    spectrum, send = run(mode_kernel, [((mode_lines, channels), F32), plain], "mode")(
        exchange(send, 0), y_forward, y_inverse, weight
    )
    own, send = run(part_kernel, [own_lines, twin_plain], "part")(exchange(send, 1), inverse)
    pointwise, head_turned, z_doubled = run(
        ready_kernel,
        [(across, F32), ((hidden_units, channels), BF16), ((height, z_count), BF16)],
        "ready",
    )(field, mix_weight, mix_bias[:, None], head_weight)
    prediction, grad_pre, send, hidden, head_slope = run(
        cell_kernel,
        [
            ((rows_y, z_count), F32),
            (across, BF16),
            twin_plain,
            (across, BF16),
            ((hidden_units, rows_y * z_count), BF16),
        ],
        "cell",
    )(
        own,
        to_twin(send),
        z_doubled,
        pointwise,
        head_weight,
        head_turned,
        head_bias[:, None],
        out_weight[None],
        out_weight.astype(F32)[:, None],
        cotangent[0],
    )
    if place.fold:
        outs = [((8 * partners, hidden_units), BF16)]
    else:
        outs = [((channels, channels), F32), ((channels, hidden_units), F32)]
    outs += [((wide // 2 * height, 4 * height), BF16)]
    *sums, forward = run(sums_kernel, outs, "sums")(field, grad_pre, hidden, head_slope)
    if not place.fold:
        totals = lax.psum(tuple(sums), ("wide", "narrow"))
        sums = []
    (send,) = run(fold_kernel, [shared], "fold")(send, to_twin(send), forward, *sums)
    adjoint, send = run(back_kernel, [((mode_lines, channels), F32), shared], "back")(
        exchange(send, 2), y_forward, y_inverse, weight
    )
    some = max(1, modes // 4)
    grad_spectral, done = pl.pallas_call(
        outer_kernel,
        grid=(modes // some,),
        in_specs=[pl.BlockSpec((some, 2 * kz, channels), lambda j: (j, 0, 0))] * 2,
        out_specs=[
            pl.BlockSpec((some, kz, 2, channels, channels), lambda j: (j, 0, 0, 0, 0)),
            pl.BlockSpec((8, 128), lambda j: (0, 0)),
        ],
        out_shape=[
            jax.ShapeDtypeStruct(spectral_weight.shape, F32),
            jax.ShapeDtypeStruct((8, 128), F32),
        ],
        compiler_params=pltpu.CompilerParams(vmem_limit_bytes=VMEM_LIMIT),
        cost_estimate=pl.CostEstimate(flops=1 << 22, bytes_accessed=5 << 20, transcendentals=0),
        name="outer",
    )(spectrum.reshape(modes, 2 * kz, channels), adjoint.reshape(modes, 2 * kz, channels))
    pointwise, z_plain, turn = run(
        pointwise_kernel,
        [
            ((channels, rows_y, z_count), F32),
            ((height, z_count), BF16),
            ((cells, cells), BF16),
        ],
        "pointwise",
    )(mix_weight, grad_pre)
    outs = [own_lines, twin_shared] + ([sums_shape] if place.fold else [])
    after = (done,) if place.fold else ()
    own, send, *sums = run(part_kernel, outs, "part")(exchange(send, 3), inverse, *after)
    outs = [((cells, z_count), BF16), ((rows_y, z_count), F32)]
    if place.fold:
        outs += [((channels, channels), F32), ((channels, hidden_units), F32)]
    grad_field, prediction, *summed = run(finish_kernel, outs, "finish")(
        own, to_twin(send), z_plain, turn, pointwise, prediction, *sums
    )
    grad_mix, grad_head = summed if place.fold else totals
    return (
        prediction[None],
        grad_field.reshape(lifted_field.shape),
        grad_spectral,
        grad_mix,
        grad_head,
    )


def solution(mesh):
    return jax.shard_map(
        body,
        mesh=mesh,
        in_specs=(
            P("wide", None, "narrow", None),
            P("wide", "narrow", None, None, None),
            P(),
            P(),
            P(),
            P(),
            P(),
            P("wide", "narrow", None),
        ),
        out_specs=(
            P("wide", "narrow", None),
            P("wide", None, "narrow", None),
            P("wide", "narrow", None, None, None),
            P(),
            P(),
        ),
        check_vma=False,
    )
```

```python
import functools
import math

import jax
import jax.numpy as jnp
import numpy as np
from jax import lax
from jax.experimental import pallas as pl
from jax.experimental.pallas import tpu as pltpu
from jax.sharding import PartitionSpec as P

MX = 16
MY = 16
MZ = 16
BLOCK = 32
F32 = jnp.float32
BF16 = jnp.bfloat16
VMEM_LIMIT = 32 * 1024 * 1024

TAIL_SLOPE = 0.275
TAIL = (
    0.11780925840139389,
    0.04211147502064705,
    0.3339323103427887,
    -0.3309934139251709,
    0.4519987106323242,
    -0.11485832929611206,
)


def signed(indices, count):
    return np.where(indices < count // 2, indices, indices - count)


def wave(positions, frequency, length):
    turned = np.mod(np.multiply.outer(positions, frequency), length)
    angles = turned.astype(np.float32) * np.float32(2.0 * math.pi / length)
    scale = np.float32(1.0 / math.sqrt(length))
    return np.cos(angles) * scale, np.sin(angles) * scale


def pair(cosine, sine, sign):
    return np.stack(
        [np.stack([cosine, -sign * sine], -1), np.stack([sign * sine, cosine], -1)], -2
    )


def y_tables(total_y, rows_y, kz, modes):
    cosine, sine = wave(np.arange(total_y), signed(np.arange(MY), MY), total_y)
    narrow = total_y // rows_y
    same = np.eye(kz, dtype=np.float32)
    forward = pair(cosine, sine, -1.0).reshape(narrow, rows_y, MY // modes, modes, 2, 2)
    inverse = pair(cosine, sine, 1.0).reshape(narrow, rows_y, MY // modes, modes, 2, 2)
    forward = np.einsum("nybjtr,kl->bjtkynlr", forward, same)
    inverse = np.einsum("nybjst,kl->bnyksjtl", inverse, same)
    blocks = MY // modes
    forward = forward.reshape(blocks, modes * 2 * kz, rows_y * narrow * kz * 2)
    inverse = inverse.reshape(blocks, narrow * rows_y * kz * 2, modes * 2 * kz)
    return forward.astype(BF16), inverse.astype(BF16)


def dot(a, b):
    return jnp.dot(a, b, preferred_element_type=F32)


def dot_nt(a, b):
    return lax.dot_general(a, b, (((1,), (1,)), ((), ())), preferred_element_type=F32)


def dot_tn(a, b):
    return lax.dot_general(a, b, (((0,), (0,)), ((), ())), preferred_element_type=F32)


def grid_of(rows, columns):
    shape = (rows, columns)
    return lax.broadcasted_iota(jnp.int32, shape, 0), lax.broadcasted_iota(jnp.int32, shape, 1)


def selector(rows, columns, condition):
    return jnp.where(condition(*grid_of(rows, columns)), 1.0, 0.0).astype(BF16)


def halves(values):
    high = values.astype(BF16)
    return high, (values - high.astype(F32)).astype(BF16)


def stacked(refs, lanes=slice(None)):
    return jnp.concatenate([ref[:, lanes] for ref in refs], axis=0)


def cosine_of(phase, length):
    angles = (phase & (length - 1)).astype(F32) * (2.0 * math.pi / length)
    return jnp.cos(angles) * (1.0 / math.sqrt(length))


class Place:
    def __init__(self, wide, narrow, kz, modes, rows_y, channels, z_count, fold):
        self.wide, self.narrow, self.kz, self.modes = wide, narrow, kz, modes
        self.rows_y, self.channels, self.z_count, self.fold = rows_y, channels, z_count, fold
        self.outer = wide // 2
        self.partners = self.outer * narrow
        self.lanes = rows_y * channels
        middle, last = self.outer // 4, self.outer // 2 - 1
        self.firsts = (last, middle, middle, middle)

    def here(self):
        wide = lax.axis_index("wide")
        return wide // 2, wide % 2

    def listed(self, position, first):
        lines = self.outer // 2
        return ((first + position // 2) & (lines - 1)) * 2 + position % 2

    def frequency(self, wide):
        index = (wide * self.modes) // MY
        return jnp.where(index < MX // 2, index, index - MX)

    def z_table(self, doubled):
        row, z = grid_of(2 * MZ, self.z_count)
        frequency = row >> 1
        value = cosine_of(z * frequency + (row & 1) * (self.z_count // 4), self.z_count)
        if doubled:
            value = jnp.where(frequency > 0, 2.0 * value, value)
        return value.astype(BF16)

    def expanded(self, small):
        row, column = grid_of(2 * MZ, small.shape[1])
        same = (row >> 1) == ((column >> 1) & (MZ - 1))
        blocks = []
        for g in range(small.shape[0] // 2):
            value = jnp.where((row & 1) == 0, small[2 * g : 2 * g + 1], small[2 * g + 1 : 2 * g + 2])
            blocks.append(jnp.where(same, value, 0.0))
        return jnp.concatenate(blocks, axis=0)

    def forward_x(self, first):
        outer, inner = self.here()
        row, column = grid_of(2 * self.outer, 4 * MZ)
        x = 2 * outer + (inner ^ (column // (2 * MZ)))
        frequency = self.frequency(2 * self.listed(row >> 1, first) + inner)
        quarter = self.wide // 4
        small = cosine_of(x * frequency + quarter * ((row & 1) - (column & 1)), self.wide)
        return self.expanded(small)

    def inverse_x(self, first):
        outer, inner = self.here()
        row, column = grid_of(4, self.outer * 2 * MZ)
        x = 2 * outer + (inner ^ (row >> 1))
        frequency = self.frequency(2 * self.listed(column // (2 * MZ), first) + inner)
        quarter = self.wide // 4
        small = cosine_of(x * frequency + quarter * ((column & 1) - (row & 1)), self.wide)
        return self.expanded(small).astype(BF16)


def repeat_rows(out_ref, block):
    height = block.shape[0]
    for first in range(0, out_ref.shape[0], height):
        out_ref[first : first + height] = block


def write_pieces(place, send_ref, block, shares):
    step, half = 2 * place.kz, place.lanes // 2
    height = send_ref.shape[0] // place.partners
    for p in range(place.partners):
        own = block[p * step % block.shape[0] :][:step]
        first = p * height
        send_ref[first : first + step] = own[:, :half]
        send_ref[first + step : first + 2 * step] = own[:, half:]
        send_ref[first + 2 * step : first + height] = shares[p * 8 % shares.shape[0] :][:8]


def read_pieces(place, pieces_ref):
    step = 2 * place.kz
    if pieces_ref.shape[1] == place.lanes:
        return pieces_ref[...], None
    height = pieces_ref.shape[0] // place.partners
    blocks, shares = [], []
    for p in range(place.partners):
        first = p * height
        left = pieces_ref[first : first + step]
        right = pieces_ref[first + step : first + 2 * step]
        blocks.append(jnp.concatenate([left, right], axis=1))
        shares.append(pieces_ref[first + 2 * step : first + height].astype(F32))
    return jnp.concatenate(blocks, axis=0), shares


def lane_sum(values, width):
    while values.shape[1] > 128:
        half = values.shape[1] // 2
        values = values[:, :half] + values[:, half:]
    if values.shape[1] < 128:
        blocks = range(0, values.shape[1], width)
        return sum(values[:, first : first + width] for first in blocks)
    shift = 64
    while shift >= width:
        values = values + pltpu.roll(values, shift, 1)
        shift //= 2
    return values[:, :width]


def diagonal_blocks(count, width, rows):
    row, lane = grid_of(count, count * width)
    pattern = jnp.where(row == lane // width, 1.0, 0.0)
    return jnp.concatenate([pattern] * (rows // count), axis=0)


def analysed(place, pieces, y_forward, copies):
    height = 2 * MZ
    turned = sum(
        pieces[first : first + height].astype(F32) for first in range(0, pieces.shape[0], height)
    )
    channels = place.channels
    lines = jnp.concatenate(
        [turned[:, y * channels : (y + 1) * channels] for y in range(place.rows_y)], axis=0
    )
    return dot(y_forward, jnp.concatenate([lines.astype(BF16)] * copies, axis=1))


def spread_lines(place, modes, y_inverse):
    lines = dot(y_inverse, modes)
    step = 2 * place.kz
    blocks = []
    for n in range(place.narrow):
        first = n * place.rows_y
        parts = [lines[(first + y) * step : (first + y + 1) * step] for y in range(place.rows_y)]
        blocks.append(jnp.concatenate(parts, axis=1))
    return jnp.concatenate(blocks, axis=0).astype(BF16)


def turn_matrix(place, forward):
    channels, rows_y = place.channels, place.rows_y

    def same(row, column):
        if forward:
            row, column = column, row
        return (row % channels == column // rows_y) & (row // channels == column % rows_y)

    return selector(place.lanes, place.lanes, same)


def side_by_side(values, count):
    height = values.shape[0] // count
    return jnp.concatenate([values[y * height : (y + 1) * height] for y in range(count)], axis=1)


def one_below_other(values, count):
    width = values.shape[1] // count
    return jnp.concatenate([values[:, y * width : (y + 1) * width] for y in range(count)], axis=0)


def own_kernel(place, field_ref, field_out_ref, spectra_ref):
    turned = dot(turn_matrix(place, False), field_ref[...]).astype(BF16)
    field_out_ref[...] = side_by_side(turned, place.rows_y)
    spectra_ref[...] = dot_nt(place.z_table(False), turned).astype(BF16)


def start_kernel(place, spectra_ref, twin_ref, send_ref):
    twin = dot_nt(place.z_table(False), twin_ref[...]).astype(BF16)
    twin = dot(twin, turn_matrix(place, True)).astype(BF16)
    values = jnp.concatenate([spectra_ref[...], twin], axis=0)
    tables = jnp.concatenate(halves(place.forward_x(place.firsts[0])), axis=1)
    send_ref[...] = dot(tables, jnp.concatenate([values, values], axis=0)).astype(BF16)


def pack_kernel(place, weight_ref, packed_ref, inverse_ref):
    inverse_ref[...] = place.inverse_x(place.firsts[1])
    modes, kz, _, channels, _ = weight_ref.shape
    for q in range(modes // 4):
        parts = [weight_ref[4 * q + j // 2, :, j % 2] for j in range(8)]
        packed = jnp.concatenate(parts, axis=-1).reshape(kz * channels, 8 * channels)
        packed_ref[q] = packed.astype(BF16)


def ready_kernel(place, field_ref, mix_ref, mix_bias_ref, head_ref, *refs):
    pointwise_ref, head_out_ref, z_doubled_ref = refs
    pointwise_ref[...] = dot_tn(mix_ref[...], field_ref[...]) + mix_bias_ref[...]
    head_out_ref[...] = jnp.transpose(head_ref[...].astype(F32)).astype(BF16)
    z_doubled_ref[...] = place.z_table(True)


def fold_kernel(place, own_ref, got_ref, tables_ref, *refs):
    values = jnp.concatenate([own_ref[...], got_ref[...]], axis=0)
    values = jnp.concatenate([values, values], axis=0)
    partial = dot(tables_ref[...], values).astype(BF16)
    if place.fold:
        shares_ref, send_ref = refs
        write_pieces(place, send_ref, partial, shares_ref[...])
    else:
        refs[0][...] = partial


def mode_kernel(
    place, pieces_ref, y_forward_ref, y_inverse_ref, weight_ref, spectrum_ref, send_ref
):
    kz, channels = place.kz, place.channels
    spectrum = analysed(place, pieces_ref[...], y_forward_ref[...], kz)
    spectrum_ref[...] = spectrum[:, :channels]
    diagonal = diagonal_blocks(kz, channels, 8 * kz)
    mixed = []
    for q in range(place.modes // 4):
        left = (spectrum[q * 8 * kz : (q + 1) * 8 * kz] * diagonal).astype(BF16)
        product = dot(left, weight_ref[q])
        for j in range(4):
            own = product[j * 2 * kz : (j + 1) * 2 * kz, j * 2 * channels : (j + 1) * 2 * channels]
            real, imag = own[:, :channels], own[:, channels:]
            mixed.append(real[:kz] - imag[kz:])
            mixed.append(imag[:kz] + real[kz:])
    mode = jnp.concatenate(mixed, axis=0).astype(BF16)
    repeat_rows(send_ref, spread_lines(place, mode, y_inverse_ref[...]))


def part_kernel(place, pieces_ref, table_ref, *refs):
    pieces, shares = read_pieces(place, pieces_ref)
    lines = dot(table_ref[...], pieces)
    height = 2 * MZ
    if shares is None:
        own_ref, send_ref = refs
        own_ref[...] = lines[:height]
        send_ref[...] = lines[height:].astype(BF16)
        return
    _, own_ref, send_ref, sums_ref = refs
    own_ref[...] = lines[:height]
    send_ref[:height] = lines[height:].astype(BF16)
    got = jnp.concatenate(shares, axis=0).astype(BF16)
    channels = place.channels

    def chosen(part):
        def condition(row, column):
            owner, source = (row % channels) // 2, column // 8
            return (
                (owner == source)
                & (column % 8 == 4 * part + 2 * (row // channels) + row % 2)
            )

        return dot(selector(2 * channels, got.shape[0], condition), got)

    high, low = chosen(0), chosen(1)
    sums_ref[...] = high + low
    send_ref[height:] = jnp.concatenate([high, low], axis=1).astype(BF16)


def normal(values):
    scaled = pl.reciprocal(1.0 + jnp.abs(TAIL_SLOPE * values), approx=True)
    decay = jnp.exp2(values * values * (-0.5 / math.log(2.0)))
    tail = TAIL[-1]
    for factor in TAIL[-2::-1]:
        tail = tail * scaled + factor
    tail = tail * (scaled * decay)
    cumulative = jnp.where(values > 0.0, 1.0 - tail, tail)
    return values * cumulative, cumulative + values * (decay * (1.0 / math.sqrt(2.0 * math.pi)))


def cell_kernel(place, *refs):
    own_ref, got_ref, z_table_ref, pointwise_ref, head_ref, head_turned_ref = refs[:6]
    head_bias_ref, out_column_ref, cotangent_ref = refs[6:9]
    prediction_ref, grad_pre_ref, send_ref, hidden_ref, head_slope_ref = refs[9:]
    rows_y, z_count = place.rows_y, place.z_count
    z_table = z_table_ref[...]
    lines = (own_ref[...] + got_ref[...].astype(F32)).astype(BF16)
    pre_act = side_by_side(dot_tn(lines, z_table), rows_y) + pointwise_ref[...]
    head, head_turned = head_ref[...], head_turned_ref[...]
    head_bias, out_column = head_bias_ref[...], out_column_ref[...]
    width = 2 * z_count
    slopes, head_pre = [], []
    for first in range(0, rows_y * z_count, width):
        value, slope = normal(pre_act[:, first : first + width])
        hidden = value.astype(BF16)
        hidden_ref[:, first : first + width] = hidden
        slopes.append(slope)
        head_pre.append(dot(head_turned, hidden))
    gradients = []
    for index, first in enumerate(range(0, rows_y, 2)):
        target = jnp.concatenate(
            [cotangent_ref[y : y + 1] for y in range(first, first + 2)], axis=1
        )
        predicted, parts = 0.0, []
        for top in range(0, head_bias.shape[0], BLOCK):
            rows = slice(top, top + BLOCK)
            active, slope = normal(head_pre[index][rows] + head_bias[rows])
            predicted = predicted + active.astype(BF16).astype(F32) * out_column[rows]
            parts.append((target * out_column[rows] * slope).astype(BF16))
        predicted = jnp.sum(predicted, axis=0, keepdims=True)
        prediction_ref[first : first + 1] = predicted[:, :z_count]
        prediction_ref[first + 1 : first + 2] = predicted[:, z_count:]
        head_slope = jnp.concatenate(parts, axis=0)
        head_slope_ref[:, first * z_count : first * z_count + width] = head_slope
        gradients.append((dot(head, head_slope) * slopes[index]).astype(BF16))
    gradient = jnp.concatenate(gradients, axis=1)
    grad_pre_ref[...] = gradient
    send_ref[...] = dot_nt(z_table, one_below_other(gradient, rows_y)).astype(BF16)


def sums_kernel(place, field_ref, gradient_ref, hidden_ref, head_slope_ref, *refs):
    refs[-1][...] = jnp.concatenate(halves(place.forward_x(place.firsts[2])), axis=1)
    grad_mix = dot_nt(field_ref[...], gradient_ref[...])
    grad_head = dot_nt(hidden_ref[...], head_slope_ref[...])
    if not place.fold:
        refs[0][...] = grad_mix
        refs[1][...] = grad_head
        return
    channels, hidden_units = grad_head.shape
    rest = jnp.zeros((channels, hidden_units - channels), F32)
    wide_mix = jnp.concatenate([grad_mix, rest], axis=1)
    high, low = halves(jnp.concatenate([grad_head, wide_mix], axis=0))
    split = jnp.concatenate([high, low], axis=0)
    place_of = selector(
        8 * place.partners,
        4 * channels,
        lambda row, column: (column % channels == 2 * (row // 8) + row % 2)
        & (column // channels == (row % 8) // 2),
    )
    refs[0][...] = dot(place_of, split).astype(BF16)


def back_kernel(
    place, pieces_ref, y_forward_ref, y_inverse_ref, weight_ref, adjoint_ref, send_ref
):
    kz, channels = place.kz, place.channels
    pieces, shares = read_pieces(place, pieces_ref)
    adjoint = analysed(place, pieces, y_forward_ref[...], 1)
    adjoint_ref[...] = adjoint
    turned = []
    for first in range(0, adjoint.shape[0], 2 * kz):
        turned += [adjoint[first + kz : first + 2 * kz], -adjoint[first : first + kz]]
    left = jnp.concatenate([adjoint, jnp.concatenate(turned, axis=0)], axis=1)
    left = jnp.concatenate([left] * 4, axis=1)
    row, lane = grid_of(8 * kz, 8 * channels)
    same = jnp.where(row // (2 * kz) == lane // (2 * channels), 1.0, 0.0)
    diagonal = diagonal_blocks(kz, channels, 8 * kz)
    block = 8 * kz
    pulled = []
    for q in range(place.modes // 4):
        own = (left[q * block : (q + 1) * block] * same).astype(BF16)
        pulled.append(lane_sum(dot_nt(own, weight_ref[q]) * diagonal, channels))
    modes_back = jnp.concatenate(pulled, axis=0).astype(BF16)
    block = spread_lines(place, modes_back, y_inverse_ref[...])
    if shares is None:
        repeat_rows(send_ref, block)
        return
    total = sum(shares[1:], shares[0])
    high, low = halves(total[0:4] + total[4:8])
    split = jnp.concatenate([high.astype(F32), low.astype(F32)], axis=0)
    write_pieces(place, send_ref, block, split.astype(BF16))


def outer_kernel(spectrum_ref, adjoint_ref, out_ref, done_ref):
    done_ref[...] = jnp.zeros(done_ref.shape, F32)
    modes, kz = out_ref.shape[:2]
    for j in range(modes):
        columns = jnp.transpose(spectrum_ref[j])
        adjoint = adjoint_ref[j]
        for k in range(kz):
            s_real, s_imag = columns[:, k : k + 1], columns[:, kz + k : kz + k + 1]
            a_real, a_imag = adjoint[k : k + 1], adjoint[kz + k : kz + k + 1]
            out_ref[j, k, 0] = s_real * a_real + s_imag * a_imag
            out_ref[j, k, 1] = s_real * a_imag - s_imag * a_real


def pointwise_kernel(place, mix_ref, gradient_ref, out_ref, z_plain_ref, turn_ref):
    z_plain_ref[...] = place.z_table(False)
    turn_ref[...] = turn_matrix(place, False)
    z_count = place.z_count
    product = dot(mix_ref[...], gradient_ref[...])
    for y in range(place.rows_y):
        out_ref[:, y, :] = product[:, y * z_count : (y + 1) * z_count]


def finish_kernel(place, *refs):
    own_ref, got_ref, z_table_ref, turn_ref, pointwise_ref, prediction_ref = refs[:6]
    refs = refs[6:]
    height = 2 * MZ
    channels = place.channels
    lines = (own_ref[...] + got_ref[:height].astype(F32)).astype(BF16)
    lines = dot(lines, turn_ref[...]).astype(BF16)
    pointwise = pointwise_ref[...].reshape(place.lanes, place.z_count)
    grad_field = (dot_tn(lines, z_table_ref[...]) + pointwise).astype(BF16)
    if not place.fold:
        refs[0][...] = grad_field
        refs[1][...] = prediction_ref[...]
        return
    sums_ref, grad_field_ref, out_ref, grad_mix_ref, grad_head_ref = refs
    grad_field_ref[...] = grad_field
    out_ref[...] = prediction_ref[...]
    got = got_ref[height:].astype(F32)
    width = sums_ref.shape[1]
    total = sums_ref[...] + got[:, :width] + got[:, width:]
    grad_head_ref[...] = total[:channels]
    grad_mix_ref[...] = total[channels:, :channels]


def call(kernel, outs, name, **spec):
    return pl.pallas_call(
        kernel,
        out_shape=[jax.ShapeDtypeStruct(shape, dtype) for shape, dtype in outs],
        compiler_params=pltpu.CompilerParams(vmem_limit_bytes=VMEM_LIMIT),
        cost_estimate=pl.CostEstimate(flops=1 << 22, bytes_accessed=1 << 19, transcendentals=0),
        name=name,
        **spec,
    )


def body(
    lifted_field,
    spectral_weight,
    mix_weight,
    mix_bias,
    head_weight,
    head_bias,
    out_weight,
    cotangent,
):
    wide = lax.axis_size("wide")
    narrow = lax.axis_size("narrow")
    devices = wide * narrow
    _, channels, rows_y, z_count = lifted_field.shape
    modes, kz = spectral_weight.shape[:2]
    hidden_units = head_weight.shape[1]
    cells = channels * rows_y
    place = Place(wide, narrow, kz, modes, rows_y, channels, z_count, False)
    place.fold = 2 * place.partners == channels and hidden_units == 128 and cells == 256 and kz % 8 == 0
    height = 2 * MZ
    step = 2 * kz
    partners = place.partners
    mode_lines = modes * 2 * kz

    y_forward, y_inverse = y_tables(rows_y * narrow, rows_y, kz, modes)
    if len(y_forward) > 1:
        block = lax.axis_index("wide") % len(y_forward)
        y_forward = lax.dynamic_index_in_dim(jnp.asarray(y_forward), block, 0, False)
        y_inverse = lax.dynamic_index_in_dim(jnp.asarray(y_inverse), block, 0, False)
    else:
        y_forward, y_inverse = jnp.asarray(y_forward[0]), jnp.asarray(y_inverse[0])

    def to_twin(send):
        pairs = [(p, p ^ narrow) for p in range(devices)]
        return lax.ppermute(send, ("wide", "narrow"), pairs)

    def exchange(send, transform):
        first = place.firsts[transform]
        groups = [
            [
                (2 * place.listed(outer, first) + inner) * narrow + n
                for outer in range(place.outer)
                for n in range(narrow)
            ]
            for inner in range(2)
        ]
        pieces = send.reshape(partners, -1, send.shape[1])
        got = lax.all_to_all(
            pieces, ("wide", "narrow"), 0, 0, axis_index_groups=groups, tiled=True
        )
        return got.reshape(send.shape)

    plain = ((partners * step, cells), BF16)
    shared = ((partners * (2 * step + 8), cells // 2), BF16) if place.fold else plain
    twin_plain = ((height, cells), BF16)
    twin_shared = ((height + 2 * channels, cells), BF16) if place.fold else twin_plain
    sums_shape = ((2 * channels, hidden_units), F32)
    own_lines = ((height, cells), F32)
    across = (channels, rows_y * z_count)

    def run(kernel, outs, name, **spec):
        return call(functools.partial(kernel, place), outs, name, **spec)

    flat_field = lifted_field.reshape(cells, z_count)
    twin_field = to_twin(flat_field)
    field, spectra = run(own_kernel, [(across, BF16), twin_plain], "own")(flat_field)
    (send,) = run(start_kernel, [plain], "start")(spectra, twin_field)
    packed_shape = ((modes // 4, kz * channels, 8 * channels), BF16)
    inverse_shape = ((2 * height, wide // 2 * height), BF16)
    weight, inverse = run(pack_kernel, [packed_shape, inverse_shape], "pack")(spectral_weight)
    spectrum, send = run(mode_kernel, [((mode_lines, channels), F32), plain], "mode")(
        exchange(send, 0), y_forward, y_inverse, weight
    )
    own, send = run(part_kernel, [own_lines, twin_plain], "part")(exchange(send, 1), inverse)
    pointwise, head_turned, z_doubled = run(
        ready_kernel,
        [(across, F32), ((hidden_units, channels), BF16), ((height, z_count), BF16)],
        "ready",
    )(field, mix_weight, mix_bias[:, None], head_weight)
    prediction, grad_pre, send, hidden, head_slope = run(
        cell_kernel,
        [
            ((rows_y, z_count), F32),
            (across, BF16),
            twin_plain,
            (across, BF16),
            ((hidden_units, rows_y * z_count), BF16),
        ],
        "cell",
    )(
        own,
        to_twin(send),
        z_doubled,
        pointwise,
        head_weight,
        head_turned,
        head_bias[:, None],
        out_weight.astype(F32)[:, None],
        cotangent[0],
    )
    if place.fold:
        outs = [((8 * partners, hidden_units), BF16)]
    else:
        outs = [((channels, channels), F32), ((channels, hidden_units), F32)]
    outs += [((wide // 2 * height, 4 * height), BF16)]
    *sums, forward = run(sums_kernel, outs, "sums")(field, grad_pre, hidden, head_slope)
    if not place.fold:
        totals = lax.psum(tuple(sums), ("wide", "narrow"))
        sums = []
    (send,) = run(fold_kernel, [shared], "fold")(send, to_twin(send), forward, *sums)
    adjoint, send = run(back_kernel, [((mode_lines, channels), F32), shared], "back")(
        exchange(send, 2), y_forward, y_inverse, weight
    )
    some = max(1, modes // 4)
    grad_spectral, done = pl.pallas_call(
        outer_kernel,
        grid=(modes // some,),
        in_specs=[pl.BlockSpec((some, 2 * kz, channels), lambda j: (j, 0, 0))] * 2,
        out_specs=[
            pl.BlockSpec((some, kz, 2, channels, channels), lambda j: (j, 0, 0, 0, 0)),
            pl.BlockSpec((8, 128), lambda j: (0, 0)),
        ],
        out_shape=[
            jax.ShapeDtypeStruct(spectral_weight.shape, F32),
            jax.ShapeDtypeStruct((8, 128), F32),
        ],
        compiler_params=pltpu.CompilerParams(vmem_limit_bytes=VMEM_LIMIT),
        cost_estimate=pl.CostEstimate(flops=1 << 22, bytes_accessed=5 << 20, transcendentals=0),
        name="outer",
    )(spectrum.reshape(modes, 2 * kz, channels), adjoint.reshape(modes, 2 * kz, channels))
    pointwise, z_plain, turn = run(
        pointwise_kernel,
        [
            ((channels, rows_y, z_count), F32),
            ((height, z_count), BF16),
            ((cells, cells), BF16),
        ],
        "pointwise",
    )(mix_weight, grad_pre)
    outs = [own_lines, twin_shared] + ([sums_shape] if place.fold else [])
    after = (done,) if place.fold else ()
    own, send, *sums = run(part_kernel, outs, "part")(exchange(send, 3), inverse, *after)
    outs = [((cells, z_count), BF16), ((rows_y, z_count), F32)]
    if place.fold:
        outs += [((channels, channels), F32), ((channels, hidden_units), F32)]
    grad_field, prediction, *summed = run(finish_kernel, outs, "finish")(
        own, to_twin(send), z_plain, turn, pointwise, prediction, *sums
    )
    grad_mix, grad_head = summed if place.fold else totals
    return (
        prediction[None],
        grad_field.reshape(lifted_field.shape),
        grad_spectral,
        grad_mix,
        grad_head,
    )


def solution(mesh):
    return jax.shard_map(
        body,
        mesh=mesh,
        in_specs=(
            P("wide", None, "narrow", None),
            P("wide", "narrow", None, None, None),
            P(),
            P(),
            P(),
            P(),
            P(),
            P("wide", "narrow", None),
        ),
        out_specs=(
            P("wide", "narrow", None),
            P("wide", None, "narrow", None),
            P("wide", "narrow", None, None, None),
            P(),
            P(),
        ),
        check_vma=False,
    )
```

```python
import functools
import math

import jax
import jax.numpy as jnp
import numpy as np
from jax import lax
from jax.experimental import pallas as pl
from jax.experimental.pallas import tpu as pltpu
from jax.sharding import PartitionSpec as P

MX = 16
MY = 16
MZ = 16
BLOCK = 32
F32 = jnp.float32
BF16 = jnp.bfloat16
VMEM_LIMIT = 32 * 1024 * 1024

TAIL_SLOPE = 0.275
TAIL = (
    0.11780925840139389,
    0.04211147502064705,
    0.3339323103427887,
    -0.3309934139251709,
    0.4519987106323242,
    -0.11485832929611206,
)


def signed(indices, count):
    return np.where(indices < count // 2, indices, indices - count)


def wave(positions, frequency, length):
    turned = np.mod(np.multiply.outer(positions, frequency), length)
    angles = turned.astype(np.float32) * np.float32(2.0 * math.pi / length)
    scale = np.float32(1.0 / math.sqrt(length))
    return np.cos(angles) * scale, np.sin(angles) * scale


def pair(cosine, sine, sign):
    return np.stack(
        [np.stack([cosine, -sign * sine], -1), np.stack([sign * sine, cosine], -1)], -2
    )


def y_tables(total_y, rows_y, kz, modes):
    cosine, sine = wave(np.arange(total_y), signed(np.arange(MY), MY), total_y)
    narrow = total_y // rows_y
    same = np.eye(kz, dtype=np.float32)
    forward = pair(cosine, sine, -1.0).reshape(narrow, rows_y, MY // modes, modes, 2, 2)
    inverse = pair(cosine, sine, 1.0).reshape(narrow, rows_y, MY // modes, modes, 2, 2)
    forward = np.einsum("nybjtr,kl->bjtkynlr", forward, same)
    inverse = np.einsum("nybjst,kl->bnyksjtl", inverse, same)
    blocks = MY // modes
    forward = forward.reshape(blocks, modes * 2 * kz, rows_y * narrow * kz * 2)
    inverse = inverse.reshape(blocks, narrow * rows_y * kz * 2, modes * 2 * kz)
    return forward.astype(BF16), inverse.astype(BF16)


def dot(a, b):
    return jnp.dot(a, b, preferred_element_type=F32)


def dot_nt(a, b):
    return lax.dot_general(a, b, (((1,), (1,)), ((), ())), preferred_element_type=F32)


def dot_tn(a, b):
    return lax.dot_general(a, b, (((0,), (0,)), ((), ())), preferred_element_type=F32)


def grid_of(rows, columns):
    shape = (rows, columns)
    return lax.broadcasted_iota(jnp.int32, shape, 0), lax.broadcasted_iota(jnp.int32, shape, 1)


def selector(rows, columns, condition):
    return jnp.where(condition(*grid_of(rows, columns)), 1.0, 0.0).astype(BF16)


def halves(values):
    high = values.astype(BF16)
    return high, (values - high.astype(F32)).astype(BF16)


def stacked(refs, lanes=slice(None)):
    return jnp.concatenate([ref[:, lanes] for ref in refs], axis=0)


def cosine_of(phase, length):
    angles = (phase & (length - 1)).astype(F32) * (2.0 * math.pi / length)
    return jnp.cos(angles) * (1.0 / math.sqrt(length))


class Place:
    def __init__(self, wide, narrow, kz, modes, rows_y, channels, z_count, fold):
        self.wide, self.narrow, self.kz, self.modes = wide, narrow, kz, modes
        self.rows_y, self.channels, self.z_count, self.fold = rows_y, channels, z_count, fold
        self.outer = wide // 2
        self.partners = self.outer * narrow
        self.lanes = rows_y * channels
        self.along = kz % 8 == 0
        middle, last = self.outer // 4, self.outer // 2 - 1
        self.firsts = (last, middle, middle, middle)

    def here(self):
        wide = lax.axis_index("wide")
        return wide // 2, wide % 2

    def listed(self, position, first):
        lines = self.outer // 2
        if self.along:
            line, rest = position % lines, position // lines
            return ((first + line) & (lines - 1)) * 2 + rest // self.narrow, rest % self.narrow
        line, rest = position // (2 * self.narrow), position % (2 * self.narrow)
        return ((first + line) & (lines - 1)) * 2 + rest // self.narrow, rest % self.narrow

    def frequency(self, wide):
        index = (wide * self.modes) // MY
        return jnp.where(index < MX // 2, index, index - MX)

    def z_table(self, doubled):
        row, z = grid_of(2 * MZ, self.z_count)
        frequency = row >> 1
        value = cosine_of(z * frequency + (row & 1) * (self.z_count // 4), self.z_count)
        if doubled:
            value = jnp.where(frequency > 0, 2.0 * value, value)
        return value.astype(BF16)

    def forward_x(self, first):
        outer, inner = self.here()
        step, quarter = 2 * self.kz, self.wide // 4
        row, column = grid_of(2 * self.partners, 4 * MZ)
        x = 2 * outer + (inner ^ (column // (2 * MZ)))
        frequency = self.frequency(2 * self.listed(row >> 1, first)[0] + inner)
        small = cosine_of(x * frequency + quarter * ((row & 1) - (column & 1)), self.wide)
        row, column = grid_of(step, 4 * MZ)
        blocks = []
        for p in range(self.partners):
            _, narrow = self.listed(p, first)
            same = narrow * self.kz + (row >> 1) == ((column >> 1) & (MZ - 1))
            value = jnp.where((row & 1) == 0, small[2 * p : 2 * p + 1], small[2 * p + 1 : 2 * p + 2])
            blocks.append(jnp.where(same, value, 0.0))
        return jnp.concatenate(blocks, axis=0)

    def inverse_x(self, first):
        outer, inner = self.here()
        step, quarter = 2 * self.kz, self.wide // 4
        row, column = grid_of(4, self.partners * step)
        x = 2 * outer + (inner ^ (row >> 1))
        frequency = self.frequency(2 * self.listed(column // step, first)[0] + inner)
        small = cosine_of(x * frequency + quarter * ((column & 1) - (row & 1)), self.wide)
        row, column = grid_of(2 * MZ, self.partners * step)
        narrow = self.listed(column // step, first)[1]
        same = (row >> 1) == narrow * self.kz + (column >> 1) % self.kz
        blocks = []
        for g in range(2):
            value = jnp.where((row & 1) == 0, small[2 * g : 2 * g + 1], small[2 * g + 1 : 2 * g + 2])
            blocks.append(jnp.where(same, value, 0.0))
        return jnp.concatenate(blocks, axis=0).astype(BF16)


def repeat_rows(place, out_ref, block, first):
    step, height = 2 * place.kz, block.shape[0]
    if not place.along:
        for start in range(0, out_ref.shape[0], height):
            out_ref[start : start + height] = block
        return
    for p in range(place.partners):
        _, narrow = place.listed(p, first)
        out_ref[p * step : (p + 1) * step] = block[narrow * step : (narrow + 1) * step]


def write_pieces(place, send_ref, block, shares, first=None):
    step, half = 2 * place.kz, place.lanes // 2
    height = send_ref.shape[0] // place.partners
    for p in range(place.partners):
        index = p if first is None else place.listed(p, first)[1]
        own = block[index * step : (index + 1) * step]
        start = p * height
        send_ref[start : start + step] = own[:, :half]
        send_ref[start + step : start + 2 * step] = own[:, half:]
        send_ref[start + 2 * step : start + height] = shares[p * 8 % shares.shape[0] :][:8]


def read_pieces(place, pieces_ref):
    step = 2 * place.kz
    if pieces_ref.shape[1] == place.lanes:
        return pieces_ref[...], None
    height = pieces_ref.shape[0] // place.partners
    blocks, shares = [], []
    for p in range(place.partners):
        first = p * height
        left = pieces_ref[first : first + step]
        right = pieces_ref[first + step : first + 2 * step]
        blocks.append(jnp.concatenate([left, right], axis=1))
        shares.append(pieces_ref[first + 2 * step : first + height].astype(F32))
    return jnp.concatenate(blocks, axis=0), shares


def lane_sum(values, width):
    while values.shape[1] > 128:
        half = values.shape[1] // 2
        values = values[:, :half] + values[:, half:]
    if values.shape[1] < 128:
        blocks = range(0, values.shape[1], width)
        return sum(values[:, first : first + width] for first in blocks)
    shift = 64
    while shift >= width:
        values = values + pltpu.roll(values, shift, 1)
        shift //= 2
    return values[:, :width]


def diagonal_blocks(count, width, rows):
    row, lane = grid_of(count, count * width)
    pattern = jnp.where(row == lane // width, 1.0, 0.0)
    return jnp.concatenate([pattern] * (rows // count), axis=0)


def analysed(place, pieces, y_forward, copies, first):
    if place.along:
        step = 2 * place.kz
        halves_of = [[] for _ in range(place.narrow)]
        for p in range(place.partners):
            part = pieces[p * step : (p + 1) * step].astype(F32)
            halves_of[place.listed(p, first)[1]].append(part)
        turned = jnp.concatenate([sum(parts[1:], parts[0]) for parts in halves_of], axis=0)
    else:
        height = 2 * MZ
        turned = sum(
            pieces[start : start + height].astype(F32) for start in range(0, pieces.shape[0], height)
        )
    channels = place.channels
    lines = jnp.concatenate(
        [turned[:, y * channels : (y + 1) * channels] for y in range(place.rows_y)], axis=0
    )
    return dot(y_forward, jnp.concatenate([lines.astype(BF16)] * copies, axis=1))


def spread_lines(place, modes, y_inverse):
    lines = dot(y_inverse, modes)
    step = 2 * place.kz
    blocks = []
    for n in range(place.narrow):
        first = n * place.rows_y
        parts = [lines[(first + y) * step : (first + y + 1) * step] for y in range(place.rows_y)]
        blocks.append(jnp.concatenate(parts, axis=1))
    return jnp.concatenate(blocks, axis=0).astype(BF16)


def turn_matrix(place, forward):
    channels, rows_y = place.channels, place.rows_y

    def same(row, column):
        if forward:
            row, column = column, row
        return (row % channels == column // rows_y) & (row // channels == column % rows_y)

    return selector(place.lanes, place.lanes, same)


def side_by_side(values, count):
    height = values.shape[0] // count
    return jnp.concatenate([values[y * height : (y + 1) * height] for y in range(count)], axis=1)


def one_below_other(values, count):
    width = values.shape[1] // count
    return jnp.concatenate([values[:, y * width : (y + 1) * width] for y in range(count)], axis=0)


def own_kernel(place, field_ref, field_out_ref, spectra_ref):
    turned = dot(turn_matrix(place, False), field_ref[...]).astype(BF16)
    field_out_ref[...] = side_by_side(turned, place.rows_y)
    spectra_ref[...] = dot_nt(place.z_table(False), turned).astype(BF16)


def start_kernel(place, spectra_ref, twin_ref, send_ref):
    twin = dot_nt(place.z_table(False), twin_ref[...]).astype(BF16)
    twin = dot(twin, turn_matrix(place, True)).astype(BF16)
    values = jnp.concatenate([spectra_ref[...], twin], axis=0)
    tables = jnp.concatenate(halves(place.forward_x(place.firsts[0])), axis=1)
    send_ref[...] = dot(tables, jnp.concatenate([values, values], axis=0)).astype(BF16)


def pack_kernel(place, weight_ref, packed_ref, inverse_ref):
    inverse_ref[...] = place.inverse_x(place.firsts[1])
    modes, kz, _, channels, _ = weight_ref.shape
    for q in range(modes // 4):
        parts = [weight_ref[4 * q + j // 2, :, j % 2] for j in range(8)]
        packed = jnp.concatenate(parts, axis=-1).reshape(kz * channels, 8 * channels)
        packed_ref[q] = packed.astype(BF16)


def ready_kernel(place, field_ref, mix_ref, mix_bias_ref, head_ref, *refs):
    pointwise_ref, head_out_ref, z_doubled_ref = refs
    pointwise_ref[...] = dot_tn(mix_ref[...], field_ref[...]) + mix_bias_ref[...]
    head_out_ref[...] = jnp.transpose(head_ref[...].astype(F32)).astype(BF16)
    z_doubled_ref[...] = place.z_table(True)


def fold_kernel(place, own_ref, got_ref, tables_ref, *refs):
    values = jnp.concatenate([own_ref[...], got_ref[...]], axis=0)
    values = jnp.concatenate([values, values], axis=0)
    partial = dot(tables_ref[...], values).astype(BF16)
    if place.fold:
        shares_ref, send_ref = refs
        write_pieces(place, send_ref, partial, shares_ref[...])
    else:
        refs[0][...] = partial


def mode_kernel(
    place, pieces_ref, y_forward_ref, y_inverse_ref, weight_ref, spectrum_ref, send_ref
):
    kz, channels = place.kz, place.channels
    spectrum = analysed(place, pieces_ref[...], y_forward_ref[...], kz, place.firsts[0])
    spectrum_ref[...] = spectrum[:, :channels]
    diagonal = diagonal_blocks(kz, channels, 8 * kz)
    mixed = []
    for q in range(place.modes // 4):
        left = (spectrum[q * 8 * kz : (q + 1) * 8 * kz] * diagonal).astype(BF16)
        product = dot(left, weight_ref[q])
        for j in range(4):
            own = product[j * 2 * kz : (j + 1) * 2 * kz, j * 2 * channels : (j + 1) * 2 * channels]
            real, imag = own[:, :channels], own[:, channels:]
            mixed.append(real[:kz] - imag[kz:])
            mixed.append(imag[:kz] + real[kz:])
    mode = jnp.concatenate(mixed, axis=0).astype(BF16)
    repeat_rows(place, send_ref, spread_lines(place, mode, y_inverse_ref[...]), place.firsts[1])


def part_kernel(place, pieces_ref, table_ref, *refs):
    pieces, shares = read_pieces(place, pieces_ref)
    lines = dot(table_ref[...], pieces)
    height = 2 * MZ
    if shares is None:
        own_ref, send_ref = refs
        own_ref[...] = lines[:height]
        send_ref[...] = lines[height:].astype(BF16)
        return
    _, own_ref, send_ref, sums_ref = refs
    own_ref[...] = lines[:height]
    send_ref[:height] = lines[height:].astype(BF16)
    got = jnp.concatenate(shares, axis=0).astype(BF16)
    channels = place.channels

    def chosen(part):
        def condition(row, column):
            owner = place.listed((row % channels) // 2, place.firsts[2])
            source = place.listed(column // 8, place.firsts[3])
            return (
                (owner[0] == source[0])
                & (owner[1] == source[1])
                & (column % 8 == 4 * part + 2 * (row // channels) + row % 2)
            )

        return dot(selector(2 * channels, got.shape[0], condition), got)

    high, low = chosen(0), chosen(1)
    sums_ref[...] = high + low
    send_ref[height:] = jnp.concatenate([high, low], axis=1).astype(BF16)


def normal(values):
    scaled = pl.reciprocal(1.0 + jnp.abs(TAIL_SLOPE * values), approx=True)
    decay = jnp.exp2(values * values * (-0.5 / math.log(2.0)))
    tail = TAIL[-1]
    for factor in TAIL[-2::-1]:
        tail = tail * scaled + factor
    tail = tail * (scaled * decay)
    cumulative = jnp.where(values > 0.0, 1.0 - tail, tail)
    return values * cumulative, cumulative + values * (decay * (1.0 / math.sqrt(2.0 * math.pi)))


def cell_kernel(place, *refs):
    own_ref, got_ref, z_table_ref, pointwise_ref, head_ref, head_turned_ref = refs[:6]
    head_bias_ref, out_column_ref, cotangent_ref = refs[6:9]
    prediction_ref, grad_pre_ref, send_ref, hidden_ref, head_slope_ref = refs[9:]
    rows_y, z_count = place.rows_y, place.z_count
    z_table = z_table_ref[...]
    lines = (own_ref[...] + got_ref[...].astype(F32)).astype(BF16)
    pre_act = side_by_side(dot_tn(lines, z_table), rows_y) + pointwise_ref[...]
    head, head_turned = head_ref[...], head_turned_ref[...]
    head_bias, out_column = head_bias_ref[...], out_column_ref[...]
    width = 2 * z_count
    slopes, head_pre = [], []
    for first in range(0, rows_y * z_count, width):
        value, slope = normal(pre_act[:, first : first + width])
        hidden = value.astype(BF16)
        hidden_ref[:, first : first + width] = hidden
        slopes.append(slope)
        head_pre.append(dot(head_turned, hidden))
    gradients = []
    for index, first in enumerate(range(0, rows_y, 2)):
        target = jnp.concatenate(
            [cotangent_ref[y : y + 1] for y in range(first, first + 2)], axis=1
        )
        predicted, parts = 0.0, []
        for top in range(0, head_bias.shape[0], BLOCK):
            rows = slice(top, top + BLOCK)
            active, slope = normal(head_pre[index][rows] + head_bias[rows])
            predicted = predicted + active.astype(BF16).astype(F32) * out_column[rows]
            parts.append((target * out_column[rows] * slope).astype(BF16))
        predicted = jnp.sum(predicted, axis=0, keepdims=True)
        prediction_ref[first : first + 1] = predicted[:, :z_count]
        prediction_ref[first + 1 : first + 2] = predicted[:, z_count:]
        head_slope = jnp.concatenate(parts, axis=0)
        head_slope_ref[:, first * z_count : first * z_count + width] = head_slope
        gradients.append((dot(head, head_slope) * slopes[index]).astype(BF16))
    gradient = jnp.concatenate(gradients, axis=1)
    grad_pre_ref[...] = gradient
    send_ref[...] = dot_nt(z_table, one_below_other(gradient, rows_y)).astype(BF16)


def sums_kernel(place, field_ref, gradient_ref, hidden_ref, head_slope_ref, *refs):
    refs[-1][...] = jnp.concatenate(halves(place.forward_x(place.firsts[2])), axis=1)
    grad_mix = dot_nt(field_ref[...], gradient_ref[...])
    grad_head = dot_nt(hidden_ref[...], head_slope_ref[...])
    if not place.fold:
        refs[0][...] = grad_mix
        refs[1][...] = grad_head
        return
    channels, hidden_units = grad_head.shape
    rest = jnp.zeros((channels, hidden_units - channels), F32)
    wide_mix = jnp.concatenate([grad_mix, rest], axis=1)
    high, low = halves(jnp.concatenate([grad_head, wide_mix], axis=0))
    split = jnp.concatenate([high, low], axis=0)
    place_of = selector(
        8 * place.partners,
        4 * channels,
        lambda row, column: (column % channels == 2 * (row // 8) + row % 2)
        & (column // channels == (row % 8) // 2),
    )
    refs[0][...] = dot(place_of, split).astype(BF16)


def back_kernel(
    place, pieces_ref, y_forward_ref, y_inverse_ref, weight_ref, adjoint_ref, send_ref
):
    kz, channels = place.kz, place.channels
    pieces, shares = read_pieces(place, pieces_ref)
    adjoint = analysed(place, pieces, y_forward_ref[...], 1, place.firsts[2])
    adjoint_ref[...] = adjoint
    turned = []
    for first in range(0, adjoint.shape[0], 2 * kz):
        turned += [adjoint[first + kz : first + 2 * kz], -adjoint[first : first + kz]]
    left = jnp.concatenate([adjoint, jnp.concatenate(turned, axis=0)], axis=1)
    left = jnp.concatenate([left] * 4, axis=1)
    row, lane = grid_of(8 * kz, 8 * channels)
    same = jnp.where(row // (2 * kz) == lane // (2 * channels), 1.0, 0.0)
    diagonal = diagonal_blocks(kz, channels, 8 * kz)
    block = 8 * kz
    pulled = []
    for q in range(place.modes // 4):
        own = (left[q * block : (q + 1) * block] * same).astype(BF16)
        pulled.append(lane_sum(dot_nt(own, weight_ref[q]) * diagonal, channels))
    modes_back = jnp.concatenate(pulled, axis=0).astype(BF16)
    block = spread_lines(place, modes_back, y_inverse_ref[...])
    if shares is None:
        repeat_rows(place, send_ref, block, place.firsts[3])
        return
    total = sum(shares[1:], shares[0])
    high, low = halves(total[0:4] + total[4:8])
    split = jnp.concatenate([high.astype(F32), low.astype(F32)], axis=0)
    write_pieces(place, send_ref, block, split.astype(BF16), place.firsts[3])


def outer_kernel(spectrum_ref, adjoint_ref, out_ref, done_ref):
    done_ref[...] = jnp.zeros(done_ref.shape, F32)
    modes, kz = out_ref.shape[:2]
    for j in range(modes):
        columns = jnp.transpose(spectrum_ref[j])
        adjoint = adjoint_ref[j]
        for k in range(kz):
            s_real, s_imag = columns[:, k : k + 1], columns[:, kz + k : kz + k + 1]
            a_real, a_imag = adjoint[k : k + 1], adjoint[kz + k : kz + k + 1]
            out_ref[j, k, 0] = s_real * a_real + s_imag * a_imag
            out_ref[j, k, 1] = s_real * a_imag - s_imag * a_real


def pointwise_kernel(place, mix_ref, gradient_ref, out_ref, z_plain_ref, turn_ref):
    z_plain_ref[...] = place.z_table(False)
    turn_ref[...] = turn_matrix(place, False)
    z_count = place.z_count
    product = dot(mix_ref[...], gradient_ref[...])
    for y in range(place.rows_y):
        out_ref[:, y, :] = product[:, y * z_count : (y + 1) * z_count]


def finish_kernel(place, *refs):
    own_ref, got_ref, z_table_ref, turn_ref, pointwise_ref, prediction_ref = refs[:6]
    refs = refs[6:]
    height = 2 * MZ
    channels = place.channels
    lines = (own_ref[...] + got_ref[:height].astype(F32)).astype(BF16)
    lines = dot(lines, turn_ref[...]).astype(BF16)
    pointwise = pointwise_ref[...].reshape(place.lanes, place.z_count)
    grad_field = (dot_tn(lines, z_table_ref[...]) + pointwise).astype(BF16)
    if not place.fold:
        refs[0][...] = grad_field
        refs[1][...] = prediction_ref[...]
        return
    sums_ref, grad_field_ref, out_ref, grad_mix_ref, grad_head_ref = refs
    grad_field_ref[...] = grad_field
    out_ref[...] = prediction_ref[...]
    got = got_ref[height:].astype(F32)
    width = sums_ref.shape[1]
    total = sums_ref[...] + got[:, :width] + got[:, width:]
    grad_head_ref[...] = total[:channels]
    grad_mix_ref[...] = total[channels:, :channels]


def call(kernel, outs, name, **spec):
    return pl.pallas_call(
        kernel,
        out_shape=[jax.ShapeDtypeStruct(shape, dtype) for shape, dtype in outs],
        compiler_params=pltpu.CompilerParams(vmem_limit_bytes=VMEM_LIMIT),
        cost_estimate=pl.CostEstimate(flops=1 << 22, bytes_accessed=1 << 19, transcendentals=0),
        name=name,
        **spec,
    )


def body(
    lifted_field,
    spectral_weight,
    mix_weight,
    mix_bias,
    head_weight,
    head_bias,
    out_weight,
    cotangent,
):
    wide = lax.axis_size("wide")
    narrow = lax.axis_size("narrow")
    devices = wide * narrow
    _, channels, rows_y, z_count = lifted_field.shape
    modes, kz = spectral_weight.shape[:2]
    hidden_units = head_weight.shape[1]
    cells = channels * rows_y
    place = Place(wide, narrow, kz, modes, rows_y, channels, z_count, False)
    place.fold = 2 * place.partners == channels and hidden_units == 128 and cells == 256 and kz % 8 == 0
    height = 2 * MZ
    step = 2 * kz
    partners = place.partners
    mode_lines = modes * 2 * kz

    y_forward, y_inverse = y_tables(rows_y * narrow, rows_y, kz, modes)
    if len(y_forward) > 1:
        block = lax.axis_index("wide") % len(y_forward)
        y_forward = lax.dynamic_index_in_dim(jnp.asarray(y_forward), block, 0, False)
        y_inverse = lax.dynamic_index_in_dim(jnp.asarray(y_inverse), block, 0, False)
    else:
        y_forward, y_inverse = jnp.asarray(y_forward[0]), jnp.asarray(y_inverse[0])

    def to_twin(send):
        pairs = [(p, p ^ narrow) for p in range(devices)]
        return lax.ppermute(send, ("wide", "narrow"), pairs)

    def exchange(send, transform):
        first = place.firsts[transform]
        listed = [place.listed(p, first) for p in range(partners)]
        groups = [[(2 * outer + inner) * narrow + n for outer, n in listed] for inner in range(2)]
        pieces = send.reshape(partners, -1, send.shape[1])
        got = lax.all_to_all(
            pieces, ("wide", "narrow"), 0, 0, axis_index_groups=groups, tiled=True
        )
        return got.reshape(send.shape)

    plain = ((partners * step, cells), BF16)
    shared = ((partners * (2 * step + 8), cells // 2), BF16) if place.fold else plain
    twin_plain = ((height, cells), BF16)
    twin_shared = ((height + 2 * channels, cells), BF16) if place.fold else twin_plain
    sums_shape = ((2 * channels, hidden_units), F32)
    own_lines = ((height, cells), F32)
    across = (channels, rows_y * z_count)

    def run(kernel, outs, name, **spec):
        return call(functools.partial(kernel, place), outs, name, **spec)

    flat_field = lifted_field.reshape(cells, z_count)
    twin_field = to_twin(flat_field)
    field, spectra = run(own_kernel, [(across, BF16), twin_plain], "own")(flat_field)
    (send,) = run(start_kernel, [plain], "start")(spectra, twin_field)
    packed_shape = ((modes // 4, kz * channels, 8 * channels), BF16)
    inverse_shape = ((2 * height, wide // 2 * height), BF16)
    weight, inverse = run(pack_kernel, [packed_shape, inverse_shape], "pack")(spectral_weight)
    spectrum, send = run(mode_kernel, [((mode_lines, channels), F32), plain], "mode")(
        exchange(send, 0), y_forward, y_inverse, weight
    )
    own, send = run(part_kernel, [own_lines, twin_plain], "part")(exchange(send, 1), inverse)
    pointwise, head_turned, z_doubled = run(
        ready_kernel,
        [(across, F32), ((hidden_units, channels), BF16), ((height, z_count), BF16)],
        "ready",
    )(field, mix_weight, mix_bias[:, None], head_weight)
    prediction, grad_pre, send, hidden, head_slope = run(
        cell_kernel,
        [
            ((rows_y, z_count), F32),
            (across, BF16),
            twin_plain,
            (across, BF16),
            ((hidden_units, rows_y * z_count), BF16),
        ],
        "cell",
    )(
        own,
        to_twin(send),
        z_doubled,
        pointwise,
        head_weight,
        head_turned,
        head_bias[:, None],
        out_weight.astype(F32)[:, None],
        cotangent[0],
    )
    if place.fold:
        outs = [((8 * partners, hidden_units), BF16)]
    else:
        outs = [((channels, channels), F32), ((channels, hidden_units), F32)]
    outs += [((wide // 2 * height, 4 * height), BF16)]
    *sums, forward = run(sums_kernel, outs, "sums")(field, grad_pre, hidden, head_slope)
    if not place.fold:
        totals = lax.psum(tuple(sums), ("wide", "narrow"))
        sums = []
    (send,) = run(fold_kernel, [shared], "fold")(send, to_twin(send), forward, *sums)
    adjoint, send = run(back_kernel, [((mode_lines, channels), F32), shared], "back")(
        exchange(send, 2), y_forward, y_inverse, weight
    )
    some = max(1, modes // 4)
    grad_spectral, done = pl.pallas_call(
        outer_kernel,
        grid=(modes // some,),
        in_specs=[pl.BlockSpec((some, 2 * kz, channels), lambda j: (j, 0, 0))] * 2,
        out_specs=[
            pl.BlockSpec((some, kz, 2, channels, channels), lambda j: (j, 0, 0, 0, 0)),
            pl.BlockSpec((8, 128), lambda j: (0, 0)),
        ],
        out_shape=[
            jax.ShapeDtypeStruct(spectral_weight.shape, F32),
            jax.ShapeDtypeStruct((8, 128), F32),
        ],
        compiler_params=pltpu.CompilerParams(vmem_limit_bytes=VMEM_LIMIT),
        cost_estimate=pl.CostEstimate(flops=1 << 22, bytes_accessed=5 << 20, transcendentals=0),
        name="outer",
    )(spectrum.reshape(modes, 2 * kz, channels), adjoint.reshape(modes, 2 * kz, channels))
    pointwise, z_plain, turn = run(
        pointwise_kernel,
        [
            ((channels, rows_y, z_count), F32),
            ((height, z_count), BF16),
            ((cells, cells), BF16),
        ],
        "pointwise",
    )(mix_weight, grad_pre)
    outs = [own_lines, twin_shared] + ([sums_shape] if place.fold else [])
    after = (done,) if place.fold else ()
    own, send, *sums = run(part_kernel, outs, "part")(exchange(send, 3), inverse, *after)
    outs = [((cells, z_count), BF16), ((rows_y, z_count), F32)]
    if place.fold:
        outs += [((channels, channels), F32), ((channels, hidden_units), F32)]
    grad_field, prediction, *summed = run(finish_kernel, outs, "finish")(
        own, to_twin(send), z_plain, turn, pointwise, prediction, *sums
    )
    grad_mix, grad_head = summed if place.fold else totals
    return (
        prediction[None],
        grad_field.reshape(lifted_field.shape),
        grad_spectral,
        grad_mix,
        grad_head,
    )


def solution(mesh):
    return jax.shard_map(
        body,
        mesh=mesh,
        in_specs=(
            P("wide", None, "narrow", None),
            P("wide", "narrow", None, None, None),
            P(),
            P(),
            P(),
            P(),
            P(),
            P("wide", "narrow", None),
        ),
        out_specs=(
            P("wide", "narrow", None),
            P("wide", None, "narrow", None),
            P("wide", "narrow", None, None, None),
            P(),
            P(),
        ),
        check_vma=False,
    )
```

```python
import functools
import math

import jax
import jax.numpy as jnp
import numpy as np
from jax import lax
from jax.experimental import pallas as pl
from jax.experimental.pallas import tpu as pltpu
from jax.sharding import PartitionSpec as P

MX = 16
MY = 16
MZ = 16
BLOCK = 32
F32 = jnp.float32
BF16 = jnp.bfloat16
VMEM_LIMIT = 32 * 1024 * 1024

TAIL_SLOPE = 0.275
TAIL = (
    0.11780925840139389,
    0.04211147502064705,
    0.3339323103427887,
    -0.3309934139251709,
    0.4519987106323242,
    -0.11485832929611206,
)


def signed(indices, count):
    return np.where(indices < count // 2, indices, indices - count)


def wave(positions, frequency, length):
    turned = np.mod(np.multiply.outer(positions, frequency), length)
    angles = turned.astype(np.float32) * np.float32(2.0 * math.pi / length)
    scale = np.float32(1.0 / math.sqrt(length))
    return np.cos(angles) * scale, np.sin(angles) * scale


def pair(cosine, sine, sign):
    return np.stack(
        [np.stack([cosine, -sign * sine], -1), np.stack([sign * sine, cosine], -1)], -2
    )


def y_tables(total_y, rows_y, kz, modes):
    cosine, sine = wave(np.arange(total_y), signed(np.arange(MY), MY), total_y)
    narrow = total_y // rows_y
    same = np.eye(kz, dtype=np.float32)
    forward = pair(cosine, sine, -1.0).reshape(narrow, rows_y, MY // modes, modes, 2, 2)
    inverse = pair(cosine, sine, 1.0).reshape(narrow, rows_y, MY // modes, modes, 2, 2)
    forward = np.einsum("nybjtr,kl->bjtkynlr", forward, same)
    inverse = np.einsum("nybjst,kl->bnyksjtl", inverse, same)
    blocks = MY // modes
    forward = forward.reshape(blocks, modes * 2 * kz, rows_y * narrow * kz * 2)
    inverse = inverse.reshape(blocks, narrow * rows_y * kz * 2, modes * 2 * kz)
    return forward.astype(BF16), inverse.astype(BF16)


def dot(a, b):
    return jnp.dot(a, b, preferred_element_type=F32)


def dot_nt(a, b):
    return lax.dot_general(a, b, (((1,), (1,)), ((), ())), preferred_element_type=F32)


def dot_tn(a, b):
    return lax.dot_general(a, b, (((0,), (0,)), ((), ())), preferred_element_type=F32)


def grid_of(rows, columns):
    shape = (rows, columns)
    return lax.broadcasted_iota(jnp.int32, shape, 0), lax.broadcasted_iota(jnp.int32, shape, 1)


def selector(rows, columns, condition):
    return jnp.where(condition(*grid_of(rows, columns)), 1.0, 0.0).astype(BF16)


def halves(values):
    high = values.astype(BF16)
    return high, (values - high.astype(F32)).astype(BF16)


def stacked(refs, lanes=slice(None)):
    return jnp.concatenate([ref[:, lanes] for ref in refs], axis=0)


def cosine_of(phase, length):
    angles = (phase & (length - 1)).astype(F32) * (2.0 * math.pi / length)
    return jnp.cos(angles) * (1.0 / math.sqrt(length))


class Place:
    def __init__(self, wide, narrow, kz, modes, rows_y, channels, z_count, fold):
        self.wide, self.narrow, self.kz, self.modes = wide, narrow, kz, modes
        self.rows_y, self.channels, self.z_count, self.fold = rows_y, channels, z_count, fold
        self.outer = wide // 2
        self.partners = self.outer * narrow
        self.lanes = rows_y * channels
        middle = self.outer // 4
        self.firsts = (middle, middle, middle, middle)

    def here(self):
        wide = lax.axis_index("wide")
        return wide // 2, wide % 2

    def listed(self, position, first):
        lines = self.outer // 2
        return ((first + position // 2) & (lines - 1)) * 2 + position % 2

    def frequency(self, wide):
        index = (wide * self.modes) // MY
        return jnp.where(index < MX // 2, index, index - MX)

    def z_table(self, doubled):
        row, z = grid_of(2 * MZ, self.z_count)
        frequency = row >> 1
        value = cosine_of(z * frequency + (row & 1) * (self.z_count // 4), self.z_count)
        if doubled:
            value = jnp.where(frequency > 0, 2.0 * value, value)
        return value.astype(BF16)

    def expanded(self, small):
        row, column = grid_of(2 * MZ, small.shape[1])
        same = (row >> 1) == ((column >> 1) & (MZ - 1))
        blocks = []
        for g in range(small.shape[0] // 2):
            value = jnp.where((row & 1) == 0, small[2 * g : 2 * g + 1], small[2 * g + 1 : 2 * g + 2])
            blocks.append(jnp.where(same, value, 0.0))
        return jnp.concatenate(blocks, axis=0)

    def forward_x(self, first):
        outer, inner = self.here()
        row, column = grid_of(2 * self.outer, 4 * MZ)
        x = 2 * outer + (inner ^ (column // (2 * MZ)))
        frequency = self.frequency(2 * self.listed(row >> 1, first) + inner)
        quarter = self.wide // 4
        small = cosine_of(x * frequency + quarter * ((row & 1) - (column & 1)), self.wide)
        return self.expanded(small)

    def inverse_x(self, first):
        outer, inner = self.here()
        row, column = grid_of(4, self.outer * 2 * MZ)
        x = 2 * outer + (inner ^ (row >> 1))
        frequency = self.frequency(2 * self.listed(column // (2 * MZ), first) + inner)
        quarter = self.wide // 4
        small = cosine_of(x * frequency + quarter * ((column & 1) - (row & 1)), self.wide)
        return self.expanded(small).astype(BF16)


def repeat_rows(out_ref, block):
    height = block.shape[0]
    for first in range(0, out_ref.shape[0], height):
        out_ref[first : first + height] = block


def write_pieces(place, send_ref, block, shares):
    step, half = 2 * place.kz, place.lanes // 2
    height = send_ref.shape[0] // place.partners
    for p in range(place.partners):
        own = block[p * step % block.shape[0] :][:step]
        first = p * height
        send_ref[first : first + step] = own[:, :half]
        send_ref[first + step : first + 2 * step] = own[:, half:]
        send_ref[first + 2 * step : first + height] = shares[p * 8 % shares.shape[0] :][:8]


def read_pieces(place, pieces_ref):
    step = 2 * place.kz
    if pieces_ref.shape[1] == place.lanes:
        return pieces_ref[...], None
    height = pieces_ref.shape[0] // place.partners
    blocks, shares = [], []
    for p in range(place.partners):
        first = p * height
        left = pieces_ref[first : first + step]
        right = pieces_ref[first + step : first + 2 * step]
        blocks.append(jnp.concatenate([left, right], axis=1))
        shares.append(pieces_ref[first + 2 * step : first + height].astype(F32))
    return jnp.concatenate(blocks, axis=0), shares


def lane_sum(values, width):
    while values.shape[1] > 128:
        half = values.shape[1] // 2
        values = values[:, :half] + values[:, half:]
    if values.shape[1] < 128:
        blocks = range(0, values.shape[1], width)
        return sum(values[:, first : first + width] for first in blocks)
    shift = 64
    while shift >= width:
        values = values + pltpu.roll(values, shift, 1)
        shift //= 2
    return values[:, :width]


def diagonal_blocks(count, width, rows):
    row, lane = grid_of(count, count * width)
    pattern = jnp.where(row == lane // width, 1.0, 0.0)
    return jnp.concatenate([pattern] * (rows // count), axis=0)


def analysed(place, pieces, y_forward, copies):
    height = 2 * MZ
    turned = sum(
        pieces[first : first + height].astype(F32) for first in range(0, pieces.shape[0], height)
    )
    channels = place.channels
    lines = jnp.concatenate(
        [turned[:, y * channels : (y + 1) * channels] for y in range(place.rows_y)], axis=0
    )
    return dot(y_forward, jnp.concatenate([lines.astype(BF16)] * copies, axis=1))


def spread_lines(place, modes, y_inverse):
    lines = dot(y_inverse, modes)
    step = 2 * place.kz
    blocks = []
    for n in range(place.narrow):
        first = n * place.rows_y
        parts = [lines[(first + y) * step : (first + y + 1) * step] for y in range(place.rows_y)]
        blocks.append(jnp.concatenate(parts, axis=1))
    return jnp.concatenate(blocks, axis=0).astype(BF16)


def turn_matrix(place, forward):
    channels, rows_y = place.channels, place.rows_y

    def same(row, column):
        if forward:
            row, column = column, row
        return (row % channels == column // rows_y) & (row // channels == column % rows_y)

    return selector(place.lanes, place.lanes, same)


def side_by_side(values, count):
    height = values.shape[0] // count
    return jnp.concatenate([values[y * height : (y + 1) * height] for y in range(count)], axis=1)


def one_below_other(values, count):
    width = values.shape[1] // count
    return jnp.concatenate([values[:, y * width : (y + 1) * width] for y in range(count)], axis=0)


def own_kernel(place, field_ref, field_out_ref, spectra_ref, z_table_ref, turn_ref, tables_ref):
    z_table = place.z_table(False)
    turned = dot(turn_matrix(place, False), field_ref[...]).astype(BF16)
    field_out_ref[...] = side_by_side(turned, place.rows_y)
    spectra_ref[...] = dot_nt(z_table, turned).astype(BF16)
    z_table_ref[...] = z_table
    turn_ref[...] = turn_matrix(place, True)
    tables_ref[...] = jnp.concatenate(halves(place.forward_x(place.firsts[0])), axis=1)


def start_kernel(place, spectra_ref, twin_ref, z_table_ref, turn_ref, tables_ref, send_ref):
    twin = dot_nt(z_table_ref[...], twin_ref[...]).astype(BF16)
    twin = dot(twin, turn_ref[...]).astype(BF16)
    values = jnp.concatenate([spectra_ref[...], twin], axis=0)
    send_ref[...] = dot(tables_ref[...], jnp.concatenate([values, values], axis=0)).astype(BF16)


def pack_kernel(place, weight_ref, packed_ref, inverse_ref):
    inverse_ref[...] = place.inverse_x(place.firsts[1])
    modes, kz, _, channels, _ = weight_ref.shape
    for q in range(modes // 4):
        parts = [weight_ref[4 * q + j // 2, :, j % 2] for j in range(8)]
        packed = jnp.concatenate(parts, axis=-1).reshape(kz * channels, 8 * channels)
        packed_ref[q] = packed.astype(BF16)


def ready_kernel(place, field_ref, mix_ref, mix_bias_ref, head_ref, *refs):
    pointwise_ref, head_out_ref, z_doubled_ref = refs
    pointwise_ref[...] = dot_tn(mix_ref[...], field_ref[...]) + mix_bias_ref[...]
    head_out_ref[...] = jnp.transpose(head_ref[...].astype(F32)).astype(BF16)
    z_doubled_ref[...] = place.z_table(True)


def fold_kernel(place, own_ref, got_ref, tables_ref, *refs):
    values = jnp.concatenate([own_ref[...], got_ref[...]], axis=0)
    values = jnp.concatenate([values, values], axis=0)
    partial = dot(tables_ref[...], values).astype(BF16)
    if place.fold:
        shares_ref, send_ref = refs
        write_pieces(place, send_ref, partial, shares_ref[...])
    else:
        refs[0][...] = partial


def mode_kernel(
    place, pieces_ref, y_forward_ref, y_inverse_ref, weight_ref, spectrum_ref, send_ref
):
    kz, channels = place.kz, place.channels
    spectrum = analysed(place, pieces_ref[...], y_forward_ref[...], kz)
    spectrum_ref[...] = spectrum[:, :channels]
    diagonal = diagonal_blocks(kz, channels, 8 * kz)
    mixed = []
    for q in range(place.modes // 4):
        left = (spectrum[q * 8 * kz : (q + 1) * 8 * kz] * diagonal).astype(BF16)
        product = dot(left, weight_ref[q])
        for j in range(4):
            own = product[j * 2 * kz : (j + 1) * 2 * kz, j * 2 * channels : (j + 1) * 2 * channels]
            real, imag = own[:, :channels], own[:, channels:]
            mixed.append(real[:kz] - imag[kz:])
            mixed.append(imag[:kz] + real[kz:])
    mode = jnp.concatenate(mixed, axis=0).astype(BF16)
    repeat_rows(send_ref, spread_lines(place, mode, y_inverse_ref[...]))


def part_kernel(place, pieces_ref, table_ref, *refs):
    pieces, shares = read_pieces(place, pieces_ref)
    lines = dot(table_ref[...], pieces)
    height = 2 * MZ
    if shares is None:
        own_ref, send_ref = refs
        own_ref[...] = lines[:height]
        send_ref[...] = lines[height:].astype(BF16)
        return
    _, own_ref, send_ref, sums_ref = refs
    own_ref[...] = lines[:height]
    send_ref[:height] = lines[height:].astype(BF16)
    got = jnp.concatenate(shares, axis=0).astype(BF16)
    channels = place.channels

    def chosen(part):
        def condition(row, column):
            owner, source = (row % channels) // 2, column // 8
            return (
                (owner == source)
                & (column % 8 == 4 * part + 2 * (row // channels) + row % 2)
            )

        return dot(selector(2 * channels, got.shape[0], condition), got)

    high, low = chosen(0), chosen(1)
    sums_ref[...] = high + low
    send_ref[height:] = jnp.concatenate([high, low], axis=1).astype(BF16)


def normal(values):
    scaled = pl.reciprocal(1.0 + jnp.abs(TAIL_SLOPE * values), approx=True)
    decay = jnp.exp2(values * values * (-0.5 / math.log(2.0)))
    tail = TAIL[-1]
    for factor in TAIL[-2::-1]:
        tail = tail * scaled + factor
    tail = tail * (scaled * decay)
    cumulative = jnp.where(values > 0.0, 1.0 - tail, tail)
    return values * cumulative, cumulative + values * (decay * (1.0 / math.sqrt(2.0 * math.pi)))


def cell_kernel(place, *refs):
    own_ref, got_ref, z_table_ref, pointwise_ref, head_ref, head_turned_ref = refs[:6]
    head_bias_ref, out_column_ref, cotangent_ref = refs[6:9]
    prediction_ref, grad_pre_ref, send_ref, hidden_ref, head_slope_ref = refs[9:]
    rows_y, z_count = place.rows_y, place.z_count
    z_table = z_table_ref[...]
    lines = (own_ref[...] + got_ref[...].astype(F32)).astype(BF16)
    pre_act = side_by_side(dot_tn(lines, z_table), rows_y) + pointwise_ref[...]
    head, head_turned = head_ref[...], head_turned_ref[...]
    head_bias, out_column = head_bias_ref[...], out_column_ref[...]
    width = 2 * z_count
    slopes, head_pre = [], []
    for first in range(0, rows_y * z_count, width):
        value, slope = normal(pre_act[:, first : first + width])
        hidden = value.astype(BF16)
        hidden_ref[:, first : first + width] = hidden
        slopes.append(slope)
        head_pre.append(dot(head_turned, hidden))
    gradients = []
    for index, first in enumerate(range(0, rows_y, 2)):
        target = jnp.concatenate(
            [cotangent_ref[y : y + 1] for y in range(first, first + 2)], axis=1
        )
        predicted, parts = 0.0, []
        for top in range(0, head_bias.shape[0], BLOCK):
            rows = slice(top, top + BLOCK)
            active, slope = normal(head_pre[index][rows] + head_bias[rows])
            predicted = predicted + active.astype(BF16).astype(F32) * out_column[rows]
            parts.append((target * out_column[rows] * slope).astype(BF16))
        predicted = jnp.sum(predicted, axis=0, keepdims=True)
        prediction_ref[first : first + 1] = predicted[:, :z_count]
        prediction_ref[first + 1 : first + 2] = predicted[:, z_count:]
        head_slope = jnp.concatenate(parts, axis=0)
        head_slope_ref[:, first * z_count : first * z_count + width] = head_slope
        gradients.append((dot(head, head_slope) * slopes[index]).astype(BF16))
    gradient = jnp.concatenate(gradients, axis=1)
    grad_pre_ref[...] = gradient
    send_ref[...] = dot_nt(z_table, one_below_other(gradient, rows_y)).astype(BF16)


def sums_kernel(place, field_ref, gradient_ref, hidden_ref, head_slope_ref, *refs):
    refs[-1][...] = jnp.concatenate(halves(place.forward_x(place.firsts[2])), axis=1)
    grad_mix = dot_nt(field_ref[...], gradient_ref[...])
    grad_head = dot_nt(hidden_ref[...], head_slope_ref[...])
    if not place.fold:
        refs[0][...] = grad_mix
        refs[1][...] = grad_head
        return
    channels, hidden_units = grad_head.shape
    rest = jnp.zeros((channels, hidden_units - channels), F32)
    wide_mix = jnp.concatenate([grad_mix, rest], axis=1)
    high, low = halves(jnp.concatenate([grad_head, wide_mix], axis=0))
    split = jnp.concatenate([high, low], axis=0)
    place_of = selector(
        8 * place.partners,
        4 * channels,
        lambda row, column: (column % channels == 2 * (row // 8) + row % 2)
        & (column // channels == (row % 8) // 2),
    )
    refs[0][...] = dot(place_of, split).astype(BF16)


def back_kernel(
    place, pieces_ref, y_forward_ref, y_inverse_ref, weight_ref, adjoint_ref, send_ref
):
    kz, channels = place.kz, place.channels
    pieces, shares = read_pieces(place, pieces_ref)
    adjoint = analysed(place, pieces, y_forward_ref[...], 1)
    adjoint_ref[...] = adjoint
    turned = []
    for first in range(0, adjoint.shape[0], 2 * kz):
        turned += [adjoint[first + kz : first + 2 * kz], -adjoint[first : first + kz]]
    left = jnp.concatenate([adjoint, jnp.concatenate(turned, axis=0)], axis=1)
    left = jnp.concatenate([left] * 4, axis=1)
    row, lane = grid_of(8 * kz, 8 * channels)
    same = jnp.where(row // (2 * kz) == lane // (2 * channels), 1.0, 0.0)
    diagonal = diagonal_blocks(kz, channels, 8 * kz)
    block = 8 * kz
    pulled = []
    for q in range(place.modes // 4):
        own = (left[q * block : (q + 1) * block] * same).astype(BF16)
        pulled.append(lane_sum(dot_nt(own, weight_ref[q]) * diagonal, channels))
    modes_back = jnp.concatenate(pulled, axis=0).astype(BF16)
    block = spread_lines(place, modes_back, y_inverse_ref[...])
    if shares is None:
        repeat_rows(send_ref, block)
        return
    total = sum(shares[1:], shares[0])
    high, low = halves(total[0:4] + total[4:8])
    split = jnp.concatenate([high.astype(F32), low.astype(F32)], axis=0)
    write_pieces(place, send_ref, block, split.astype(BF16))


def outer_kernel(spectrum_ref, adjoint_ref, out_ref, done_ref):
    done_ref[...] = jnp.zeros(done_ref.shape, F32)
    modes, kz = out_ref.shape[:2]
    for j in range(modes):
        columns = jnp.transpose(spectrum_ref[j])
        adjoint = adjoint_ref[j]
        for k in range(kz):
            s_real, s_imag = columns[:, k : k + 1], columns[:, kz + k : kz + k + 1]
            a_real, a_imag = adjoint[k : k + 1], adjoint[kz + k : kz + k + 1]
            out_ref[j, k, 0] = s_real * a_real + s_imag * a_imag
            out_ref[j, k, 1] = s_real * a_imag - s_imag * a_real


def pointwise_kernel(place, mix_ref, gradient_ref, out_ref, z_plain_ref, turn_ref):
    z_plain_ref[...] = place.z_table(False)
    turn_ref[...] = turn_matrix(place, False)
    z_count = place.z_count
    product = dot(mix_ref[...], gradient_ref[...])
    for y in range(place.rows_y):
        out_ref[:, y, :] = product[:, y * z_count : (y + 1) * z_count]


def finish_kernel(place, *refs):
    own_ref, got_ref, z_table_ref, turn_ref, pointwise_ref, prediction_ref = refs[:6]
    refs = refs[6:]
    height = 2 * MZ
    channels = place.channels
    lines = (own_ref[...] + got_ref[:height].astype(F32)).astype(BF16)
    lines = dot(lines, turn_ref[...]).astype(BF16)
    pointwise = pointwise_ref[...].reshape(place.lanes, place.z_count)
    grad_field = (dot_tn(lines, z_table_ref[...]) + pointwise).astype(BF16)
    if not place.fold:
        refs[0][...] = grad_field
        refs[1][...] = prediction_ref[...]
        return
    sums_ref, grad_field_ref, out_ref, grad_mix_ref, grad_head_ref = refs
    grad_field_ref[...] = grad_field
    out_ref[...] = prediction_ref[...]
    got = got_ref[height:].astype(F32)
    width = sums_ref.shape[1]
    total = sums_ref[...] + got[:, :width] + got[:, width:]
    grad_head_ref[...] = total[:channels]
    grad_mix_ref[...] = total[channels:, :channels]


def call(kernel, outs, name, **spec):
    return pl.pallas_call(
        kernel,
        out_shape=[jax.ShapeDtypeStruct(shape, dtype) for shape, dtype in outs],
        compiler_params=pltpu.CompilerParams(vmem_limit_bytes=VMEM_LIMIT),
        cost_estimate=pl.CostEstimate(flops=1 << 22, bytes_accessed=1 << 19, transcendentals=0),
        name=name,
        **spec,
    )


def body(
    lifted_field,
    spectral_weight,
    mix_weight,
    mix_bias,
    head_weight,
    head_bias,
    out_weight,
    cotangent,
):
    wide = lax.axis_size("wide")
    narrow = lax.axis_size("narrow")
    devices = wide * narrow
    _, channels, rows_y, z_count = lifted_field.shape
    modes, kz = spectral_weight.shape[:2]
    hidden_units = head_weight.shape[1]
    cells = channels * rows_y
    place = Place(wide, narrow, kz, modes, rows_y, channels, z_count, False)
    place.fold = 2 * place.partners == channels and hidden_units == 128 and cells == 256 and kz % 8 == 0
    height = 2 * MZ
    step = 2 * kz
    partners = place.partners
    mode_lines = modes * 2 * kz

    y_forward, y_inverse = y_tables(rows_y * narrow, rows_y, kz, modes)
    if len(y_forward) > 1:
        block = lax.axis_index("wide") % len(y_forward)
        y_forward = lax.dynamic_index_in_dim(jnp.asarray(y_forward), block, 0, False)
        y_inverse = lax.dynamic_index_in_dim(jnp.asarray(y_inverse), block, 0, False)
    else:
        y_forward, y_inverse = jnp.asarray(y_forward[0]), jnp.asarray(y_inverse[0])

    def to_twin(send):
        pairs = [(p, p ^ narrow) for p in range(devices)]
        return lax.ppermute(send, ("wide", "narrow"), pairs)

    def exchange(send, transform):
        first = place.firsts[transform]
        groups = [
            [
                (2 * place.listed(outer, first) + inner) * narrow + n
                for outer in range(place.outer)
                for n in range(narrow)
            ]
            for inner in range(2)
        ]
        pieces = send.reshape(partners, -1, send.shape[1])
        got = lax.all_to_all(
            pieces, ("wide", "narrow"), 0, 0, axis_index_groups=groups, tiled=True
        )
        return got.reshape(send.shape)

    plain = ((partners * step, cells), BF16)
    shared = ((partners * (2 * step + 8), cells // 2), BF16) if place.fold else plain
    twin_plain = ((height, cells), BF16)
    twin_shared = ((height + 2 * channels, cells), BF16) if place.fold else twin_plain
    sums_shape = ((2 * channels, hidden_units), F32)
    own_lines = ((height, cells), F32)
    across = (channels, rows_y * z_count)

    def run(kernel, outs, name, **spec):
        return call(functools.partial(kernel, place), outs, name, **spec)

    flat_field = lifted_field.reshape(cells, z_count)
    twin_field = to_twin(flat_field)
    tables_shape = ((wide // 2 * height, 4 * height), BF16)
    field, spectra, *tables = run(
        own_kernel,
        [(across, BF16), twin_plain, ((height, z_count), BF16), ((cells, cells), BF16), tables_shape],
        "own",
    )(flat_field)
    (send,) = run(start_kernel, [plain], "start")(spectra, twin_field, *tables)
    packed_shape = ((modes // 4, kz * channels, 8 * channels), BF16)
    inverse_shape = ((2 * height, wide // 2 * height), BF16)
    weight, inverse = run(pack_kernel, [packed_shape, inverse_shape], "pack")(spectral_weight)
    spectrum, send = run(mode_kernel, [((mode_lines, channels), F32), plain], "mode")(
        exchange(send, 0), y_forward, y_inverse, weight
    )
    own, send = run(part_kernel, [own_lines, twin_plain], "part")(exchange(send, 1), inverse)
    pointwise, head_turned, z_doubled = run(
        ready_kernel,
        [(across, F32), ((hidden_units, channels), BF16), ((height, z_count), BF16)],
        "ready",
    )(field, mix_weight, mix_bias[:, None], head_weight)
    prediction, grad_pre, send, hidden, head_slope = run(
        cell_kernel,
        [
            ((rows_y, z_count), F32),
            (across, BF16),
            twin_plain,
            (across, BF16),
            ((hidden_units, rows_y * z_count), BF16),
        ],
        "cell",
    )(
        own,
        to_twin(send),
        z_doubled,
        pointwise,
        head_weight,
        head_turned,
        head_bias[:, None],
        out_weight.astype(F32)[:, None],
        cotangent[0],
    )
    if place.fold:
        outs = [((8 * partners, hidden_units), BF16)]
    else:
        outs = [((channels, channels), F32), ((channels, hidden_units), F32)]
    outs += [((wide // 2 * height, 4 * height), BF16)]
    *sums, forward = run(sums_kernel, outs, "sums")(field, grad_pre, hidden, head_slope)
    if not place.fold:
        totals = lax.psum(tuple(sums), ("wide", "narrow"))
        sums = []
    (send,) = run(fold_kernel, [shared], "fold")(send, to_twin(send), forward, *sums)
    adjoint, send = run(back_kernel, [((mode_lines, channels), F32), shared], "back")(
        exchange(send, 2), y_forward, y_inverse, weight
    )
    some = max(1, modes // 4)
    grad_spectral, done = pl.pallas_call(
        outer_kernel,
        grid=(modes // some,),
        in_specs=[pl.BlockSpec((some, 2 * kz, channels), lambda j: (j, 0, 0))] * 2,
        out_specs=[
            pl.BlockSpec((some, kz, 2, channels, channels), lambda j: (j, 0, 0, 0, 0)),
            pl.BlockSpec((8, 128), lambda j: (0, 0)),
        ],
        out_shape=[
            jax.ShapeDtypeStruct(spectral_weight.shape, F32),
            jax.ShapeDtypeStruct((8, 128), F32),
        ],
        compiler_params=pltpu.CompilerParams(vmem_limit_bytes=VMEM_LIMIT),
        cost_estimate=pl.CostEstimate(flops=1 << 22, bytes_accessed=5 << 20, transcendentals=0),
        name="outer",
    )(spectrum.reshape(modes, 2 * kz, channels), adjoint.reshape(modes, 2 * kz, channels))
    pointwise, z_plain, turn = run(
        pointwise_kernel,
        [
            ((channels, rows_y, z_count), F32),
            ((height, z_count), BF16),
            ((cells, cells), BF16),
        ],
        "pointwise",
    )(mix_weight, grad_pre)
    outs = [own_lines, twin_shared] + ([sums_shape] if place.fold else [])
    after = (done,) if place.fold else ()
    own, send, *sums = run(part_kernel, outs, "part")(exchange(send, 3), inverse, *after)
    outs = [((cells, z_count), BF16), ((rows_y, z_count), F32)]
    if place.fold:
        outs += [((channels, channels), F32), ((channels, hidden_units), F32)]
    grad_field, prediction, *summed = run(finish_kernel, outs, "finish")(
        own, to_twin(send), z_plain, turn, pointwise, prediction, *sums
    )
    grad_mix, grad_head = summed if place.fold else totals
    return (
        prediction[None],
        grad_field.reshape(lifted_field.shape),
        grad_spectral,
        grad_mix,
        grad_head,
    )


def solution(mesh):
    return jax.shard_map(
        body,
        mesh=mesh,
        in_specs=(
            P("wide", None, "narrow", None),
            P("wide", "narrow", None, None, None),
            P(),
            P(),
            P(),
            P(),
            P(),
            P("wide", "narrow", None),
        ),
        out_specs=(
            P("wide", "narrow", None),
            P("wide", None, "narrow", None),
            P("wide", "narrow", None, None, None),
            P(),
            P(),
        ),
        check_vma=False,
    )
```

```python
import functools
import math

import jax
import jax.numpy as jnp
import numpy as np
from jax import lax
from jax.experimental import pallas as pl
from jax.experimental.pallas import tpu as pltpu
from jax.sharding import PartitionSpec as P

MX = 16
MY = 16
MZ = 16
BLOCK = 32
F32 = jnp.float32
BF16 = jnp.bfloat16
VMEM_LIMIT = 32 * 1024 * 1024

TAIL_SLOPE = 0.275
TAIL = (
    0.11780925840139389,
    0.04211147502064705,
    0.3339323103427887,
    -0.3309934139251709,
    0.4519987106323242,
    -0.11485832929611206,
)


def signed(indices, count):
    return np.where(indices < count // 2, indices, indices - count)


def wave(positions, frequency, length):
    turned = np.mod(np.multiply.outer(positions, frequency), length)
    angles = turned.astype(np.float32) * np.float32(2.0 * math.pi / length)
    scale = np.float32(1.0 / math.sqrt(length))
    return np.cos(angles) * scale, np.sin(angles) * scale


def pair(cosine, sine, sign):
    return np.stack(
        [np.stack([cosine, -sign * sine], -1), np.stack([sign * sine, cosine], -1)], -2
    )


def y_tables(total_y, rows_y, kz, modes):
    cosine, sine = wave(np.arange(total_y), signed(np.arange(MY), MY), total_y)
    narrow = total_y // rows_y
    same = np.eye(kz, dtype=np.float32)
    forward = pair(cosine, sine, -1.0).reshape(narrow, rows_y, MY // modes, modes, 2, 2)
    inverse = pair(cosine, sine, 1.0).reshape(narrow, rows_y, MY // modes, modes, 2, 2)
    forward = np.einsum("nybjtr,kl->bjtkynlr", forward, same)
    inverse = np.einsum("nybjst,kl->bnyksjtl", inverse, same)
    blocks = MY // modes
    forward = forward.reshape(blocks, modes * 2 * kz, rows_y * narrow * kz * 2)
    inverse = inverse.reshape(blocks, narrow * rows_y * kz * 2, modes * 2 * kz)
    return forward.astype(BF16), inverse.astype(BF16)


def dot(a, b):
    return jnp.dot(a, b, preferred_element_type=F32)


def dot_nt(a, b):
    return lax.dot_general(a, b, (((1,), (1,)), ((), ())), preferred_element_type=F32)


def dot_tn(a, b):
    return lax.dot_general(a, b, (((0,), (0,)), ((), ())), preferred_element_type=F32)


def grid_of(rows, columns):
    shape = (rows, columns)
    return lax.broadcasted_iota(jnp.int32, shape, 0), lax.broadcasted_iota(jnp.int32, shape, 1)


def selector(rows, columns, condition):
    return jnp.where(condition(*grid_of(rows, columns)), 1.0, 0.0).astype(BF16)


def halves(values):
    high = values.astype(BF16)
    return high, (values - high.astype(F32)).astype(BF16)


def stacked(refs, lanes=slice(None)):
    return jnp.concatenate([ref[:, lanes] for ref in refs], axis=0)


def cosine_of(phase, length):
    angles = (phase & (length - 1)).astype(F32) * (2.0 * math.pi / length)
    return jnp.cos(angles) * (1.0 / math.sqrt(length))


class Place:
    def __init__(self, wide, narrow, kz, modes, rows_y, channels, z_count, fold):
        self.wide, self.narrow, self.kz, self.modes = wide, narrow, kz, modes
        self.rows_y, self.channels, self.z_count, self.fold = rows_y, channels, z_count, fold
        self.outer = wide // 2
        self.partners = self.outer * narrow
        self.lanes = rows_y * channels
        middle = self.outer // 4
        self.firsts = (middle, middle, middle, middle)

    def here(self):
        wide = lax.axis_index("wide")
        return wide // 2, wide % 2

    def listed(self, position, first, inner):
        lines = self.outer // 2
        return ((first + (1 - 2 * inner) * (position // 2)) & (lines - 1)) * 2 + position % 2

    def frequency(self, wide):
        index = (wide * self.modes) // MY
        return jnp.where(index < MX // 2, index, index - MX)

    def z_table(self, doubled):
        row, z = grid_of(2 * MZ, self.z_count)
        frequency = row >> 1
        value = cosine_of(z * frequency + (row & 1) * (self.z_count // 4), self.z_count)
        if doubled:
            value = jnp.where(frequency > 0, 2.0 * value, value)
        return value.astype(BF16)

    def expanded(self, small):
        row, column = grid_of(2 * MZ, small.shape[1])
        same = (row >> 1) == ((column >> 1) & (MZ - 1))
        blocks = []
        for g in range(small.shape[0] // 2):
            value = jnp.where((row & 1) == 0, small[2 * g : 2 * g + 1], small[2 * g + 1 : 2 * g + 2])
            blocks.append(jnp.where(same, value, 0.0))
        return jnp.concatenate(blocks, axis=0)

    def forward_x(self, first):
        outer, inner = self.here()
        row, column = grid_of(2 * self.outer, 4 * MZ)
        x = 2 * outer + (inner ^ (column // (2 * MZ)))
        frequency = self.frequency(2 * self.listed(row >> 1, first, inner) + inner)
        quarter = self.wide // 4
        small = cosine_of(x * frequency + quarter * ((row & 1) - (column & 1)), self.wide)
        return self.expanded(small)

    def inverse_x(self, first):
        outer, inner = self.here()
        row, column = grid_of(4, self.outer * 2 * MZ)
        x = 2 * outer + (inner ^ (row >> 1))
        frequency = self.frequency(2 * self.listed(column // (2 * MZ), first, inner) + inner)
        quarter = self.wide // 4
        small = cosine_of(x * frequency + quarter * ((column & 1) - (row & 1)), self.wide)
        return self.expanded(small).astype(BF16)


def repeat_rows(out_ref, block):
    height = block.shape[0]
    for first in range(0, out_ref.shape[0], height):
        out_ref[first : first + height] = block


def write_pieces(place, send_ref, block, shares):
    step, half = 2 * place.kz, place.lanes // 2
    height = send_ref.shape[0] // place.partners
    for p in range(place.partners):
        own = block[p * step % block.shape[0] :][:step]
        first = p * height
        send_ref[first : first + step] = own[:, :half]
        send_ref[first + step : first + 2 * step] = own[:, half:]
        send_ref[first + 2 * step : first + height] = shares[p * 8 % shares.shape[0] :][:8]


def read_pieces(place, pieces_ref):
    step = 2 * place.kz
    if pieces_ref.shape[1] == place.lanes:
        return pieces_ref[...], None
    height = pieces_ref.shape[0] // place.partners
    blocks, shares = [], []
    for p in range(place.partners):
        first = p * height
        left = pieces_ref[first : first + step]
        right = pieces_ref[first + step : first + 2 * step]
        blocks.append(jnp.concatenate([left, right], axis=1))
        shares.append(pieces_ref[first + 2 * step : first + height].astype(F32))
    return jnp.concatenate(blocks, axis=0), shares


def lane_sum(values, width):
    while values.shape[1] > 128:
        half = values.shape[1] // 2
        values = values[:, :half] + values[:, half:]
    if values.shape[1] < 128:
        blocks = range(0, values.shape[1], width)
        return sum(values[:, first : first + width] for first in blocks)
    shift = 64
    while shift >= width:
        values = values + pltpu.roll(values, shift, 1)
        shift //= 2
    return values[:, :width]


def diagonal_blocks(count, width, rows):
    row, lane = grid_of(count, count * width)
    pattern = jnp.where(row == lane // width, 1.0, 0.0)
    return jnp.concatenate([pattern] * (rows // count), axis=0)


def analysed(place, pieces, y_forward, copies):
    height = 2 * MZ
    turned = sum(
        pieces[first : first + height].astype(F32) for first in range(0, pieces.shape[0], height)
    )
    channels = place.channels
    lines = jnp.concatenate(
        [turned[:, y * channels : (y + 1) * channels] for y in range(place.rows_y)], axis=0
    )
    return dot(y_forward, jnp.concatenate([lines.astype(BF16)] * copies, axis=1))


def spread_lines(place, modes, y_inverse):
    lines = dot(y_inverse, modes)
    step = 2 * place.kz
    blocks = []
    for n in range(place.narrow):
        first = n * place.rows_y
        parts = [lines[(first + y) * step : (first + y + 1) * step] for y in range(place.rows_y)]
        blocks.append(jnp.concatenate(parts, axis=1))
    return jnp.concatenate(blocks, axis=0).astype(BF16)


def turn_matrix(place, forward):
    channels, rows_y = place.channels, place.rows_y

    def same(row, column):
        if forward:
            row, column = column, row
        return (row % channels == column // rows_y) & (row // channels == column % rows_y)

    return selector(place.lanes, place.lanes, same)


def side_by_side(values, count):
    height = values.shape[0] // count
    return jnp.concatenate([values[y * height : (y + 1) * height] for y in range(count)], axis=1)


def one_below_other(values, count):
    width = values.shape[1] // count
    return jnp.concatenate([values[:, y * width : (y + 1) * width] for y in range(count)], axis=0)


def own_kernel(place, field_ref, field_out_ref, spectra_ref, z_table_ref, turn_ref, tables_ref):
    z_table = place.z_table(False)
    turned = dot(turn_matrix(place, False), field_ref[...]).astype(BF16)
    field_out_ref[...] = side_by_side(turned, place.rows_y)
    spectra_ref[...] = dot_nt(z_table, turned).astype(BF16)
    z_table_ref[...] = z_table
    turn_ref[...] = turn_matrix(place, True)
    tables_ref[...] = jnp.concatenate(halves(place.forward_x(place.firsts[0])), axis=1)


def start_kernel(place, spectra_ref, twin_ref, z_table_ref, turn_ref, tables_ref, send_ref):
    twin = dot_nt(z_table_ref[...], twin_ref[...]).astype(BF16)
    twin = dot(twin, turn_ref[...]).astype(BF16)
    values = jnp.concatenate([spectra_ref[...], twin], axis=0)
    send_ref[...] = dot(tables_ref[...], jnp.concatenate([values, values], axis=0)).astype(BF16)


def pack_kernel(place, weight_ref, packed_ref, inverse_ref):
    inverse_ref[...] = place.inverse_x(place.firsts[1])
    modes, kz, _, channels, _ = weight_ref.shape
    for q in range(modes // 4):
        parts = [weight_ref[4 * q + j // 2, :, j % 2] for j in range(8)]
        packed = jnp.concatenate(parts, axis=-1).reshape(kz * channels, 8 * channels)
        packed_ref[q] = packed.astype(BF16)


def ready_kernel(place, field_ref, mix_ref, mix_bias_ref, head_ref, *refs):
    pointwise_ref, head_out_ref, z_doubled_ref = refs
    pointwise_ref[...] = dot_tn(mix_ref[...], field_ref[...]) + mix_bias_ref[...]
    head_out_ref[...] = jnp.transpose(head_ref[...].astype(F32)).astype(BF16)
    z_doubled_ref[...] = place.z_table(True)


def fold_kernel(place, own_ref, got_ref, tables_ref, *refs):
    values = jnp.concatenate([own_ref[...], got_ref[...]], axis=0)
    values = jnp.concatenate([values, values], axis=0)
    partial = dot(tables_ref[...], values).astype(BF16)
    if place.fold:
        shares_ref, send_ref = refs
        write_pieces(place, send_ref, partial, shares_ref[...])
    else:
        refs[0][...] = partial


def mode_kernel(
    place, pieces_ref, y_forward_ref, y_inverse_ref, weight_ref, spectrum_ref, send_ref
):
    kz, channels = place.kz, place.channels
    spectrum = analysed(place, pieces_ref[...], y_forward_ref[...], kz)
    spectrum_ref[...] = spectrum[:, :channels]
    diagonal = diagonal_blocks(kz, channels, 8 * kz)
    mixed = []
    for q in range(place.modes // 4):
        left = (spectrum[q * 8 * kz : (q + 1) * 8 * kz] * diagonal).astype(BF16)
        product = dot(left, weight_ref[q])
        for j in range(4):
            own = product[j * 2 * kz : (j + 1) * 2 * kz, j * 2 * channels : (j + 1) * 2 * channels]
            real, imag = own[:, :channels], own[:, channels:]
            mixed.append(real[:kz] - imag[kz:])
            mixed.append(imag[:kz] + real[kz:])
    mode = jnp.concatenate(mixed, axis=0).astype(BF16)
    repeat_rows(send_ref, spread_lines(place, mode, y_inverse_ref[...]))


def part_kernel(place, pieces_ref, table_ref, *refs):
    pieces, shares = read_pieces(place, pieces_ref)
    lines = dot(table_ref[...], pieces)
    height = 2 * MZ
    if shares is None:
        own_ref, send_ref = refs
        own_ref[...] = lines[:height]
        send_ref[...] = lines[height:].astype(BF16)
        return
    _, own_ref, send_ref, sums_ref = refs
    own_ref[...] = lines[:height]
    send_ref[:height] = lines[height:].astype(BF16)
    got = jnp.concatenate(shares, axis=0).astype(BF16)
    channels = place.channels

    def chosen(part):
        def condition(row, column):
            owner, source = (row % channels) // 2, column // 8
            return (
                (owner == source)
                & (column % 8 == 4 * part + 2 * (row // channels) + row % 2)
            )

        return dot(selector(2 * channels, got.shape[0], condition), got)

    high, low = chosen(0), chosen(1)
    sums_ref[...] = high + low
    send_ref[height:] = jnp.concatenate([high, low], axis=1).astype(BF16)


def normal(values):
    scaled = pl.reciprocal(1.0 + jnp.abs(TAIL_SLOPE * values), approx=True)
    decay = jnp.exp2(values * values * (-0.5 / math.log(2.0)))
    tail = TAIL[-1]
    for factor in TAIL[-2::-1]:
        tail = tail * scaled + factor
    tail = tail * (scaled * decay)
    cumulative = jnp.where(values > 0.0, 1.0 - tail, tail)
    return values * cumulative, cumulative + values * (decay * (1.0 / math.sqrt(2.0 * math.pi)))


def cell_kernel(place, *refs):
    own_ref, got_ref, z_table_ref, pointwise_ref, head_ref, head_turned_ref = refs[:6]
    head_bias_ref, out_column_ref, cotangent_ref = refs[6:9]
    prediction_ref, grad_pre_ref, send_ref, hidden_ref, head_slope_ref = refs[9:]
    rows_y, z_count = place.rows_y, place.z_count
    z_table = z_table_ref[...]
    lines = (own_ref[...] + got_ref[...].astype(F32)).astype(BF16)
    pre_act = side_by_side(dot_tn(lines, z_table), rows_y) + pointwise_ref[...]
    head, head_turned = head_ref[...], head_turned_ref[...]
    head_bias, out_column = head_bias_ref[...], out_column_ref[...]
    width = 2 * z_count
    slopes, head_pre = [], []
    for first in range(0, rows_y * z_count, width):
        value, slope = normal(pre_act[:, first : first + width])
        hidden = value.astype(BF16)
        hidden_ref[:, first : first + width] = hidden
        slopes.append(slope)
        head_pre.append(dot(head_turned, hidden))
    gradients = []
    for index, first in enumerate(range(0, rows_y, 2)):
        target = jnp.concatenate(
            [cotangent_ref[y : y + 1] for y in range(first, first + 2)], axis=1
        )
        predicted, parts = 0.0, []
        for top in range(0, head_bias.shape[0], BLOCK):
            rows = slice(top, top + BLOCK)
            active, slope = normal(head_pre[index][rows] + head_bias[rows])
            predicted = predicted + active.astype(BF16).astype(F32) * out_column[rows]
            parts.append((target * out_column[rows] * slope).astype(BF16))
        predicted = jnp.sum(predicted, axis=0, keepdims=True)
        prediction_ref[first : first + 1] = predicted[:, :z_count]
        prediction_ref[first + 1 : first + 2] = predicted[:, z_count:]
        head_slope = jnp.concatenate(parts, axis=0)
        head_slope_ref[:, first * z_count : first * z_count + width] = head_slope
        gradients.append((dot(head, head_slope) * slopes[index]).astype(BF16))
    gradient = jnp.concatenate(gradients, axis=1)
    grad_pre_ref[...] = gradient
    send_ref[...] = dot_nt(z_table, one_below_other(gradient, rows_y)).astype(BF16)


def sums_kernel(place, field_ref, gradient_ref, hidden_ref, head_slope_ref, *refs):
    refs[-1][...] = jnp.concatenate(halves(place.forward_x(place.firsts[2])), axis=1)
    grad_mix = dot_nt(field_ref[...], gradient_ref[...])
    grad_head = dot_nt(hidden_ref[...], head_slope_ref[...])
    if not place.fold:
        refs[0][...] = grad_mix
        refs[1][...] = grad_head
        return
    channels, hidden_units = grad_head.shape
    rest = jnp.zeros((channels, hidden_units - channels), F32)
    wide_mix = jnp.concatenate([grad_mix, rest], axis=1)
    high, low = halves(jnp.concatenate([grad_head, wide_mix], axis=0))
    split = jnp.concatenate([high, low], axis=0)
    place_of = selector(
        8 * place.partners,
        4 * channels,
        lambda row, column: (column % channels == 2 * (row // 8) + row % 2)
        & (column // channels == (row % 8) // 2),
    )
    refs[0][...] = dot(place_of, split).astype(BF16)


def back_kernel(
    place, pieces_ref, y_forward_ref, y_inverse_ref, weight_ref, adjoint_ref, send_ref
):
    kz, channels = place.kz, place.channels
    pieces, shares = read_pieces(place, pieces_ref)
    adjoint = analysed(place, pieces, y_forward_ref[...], 1)
    adjoint_ref[...] = adjoint
    turned = []
    for first in range(0, adjoint.shape[0], 2 * kz):
        turned += [adjoint[first + kz : first + 2 * kz], -adjoint[first : first + kz]]
    left = jnp.concatenate([adjoint, jnp.concatenate(turned, axis=0)], axis=1)
    left = jnp.concatenate([left] * 4, axis=1)
    row, lane = grid_of(8 * kz, 8 * channels)
    same = jnp.where(row // (2 * kz) == lane // (2 * channels), 1.0, 0.0)
    diagonal = diagonal_blocks(kz, channels, 8 * kz)
    block = 8 * kz
    pulled = []
    for q in range(place.modes // 4):
        own = (left[q * block : (q + 1) * block] * same).astype(BF16)
        pulled.append(lane_sum(dot_nt(own, weight_ref[q]) * diagonal, channels))
    modes_back = jnp.concatenate(pulled, axis=0).astype(BF16)
    block = spread_lines(place, modes_back, y_inverse_ref[...])
    if shares is None:
        repeat_rows(send_ref, block)
        return
    total = sum(shares[1:], shares[0])
    high, low = halves(total[0:4] + total[4:8])
    split = jnp.concatenate([high.astype(F32), low.astype(F32)], axis=0)
    write_pieces(place, send_ref, block, split.astype(BF16))


def outer_kernel(spectrum_ref, adjoint_ref, out_ref, done_ref):
    done_ref[...] = jnp.zeros(done_ref.shape, F32)
    modes, kz = out_ref.shape[:2]
    for j in range(modes):
        columns = jnp.transpose(spectrum_ref[j])
        adjoint = adjoint_ref[j]
        for k in range(kz):
            s_real, s_imag = columns[:, k : k + 1], columns[:, kz + k : kz + k + 1]
            a_real, a_imag = adjoint[k : k + 1], adjoint[kz + k : kz + k + 1]
            out_ref[j, k, 0] = s_real * a_real + s_imag * a_imag
            out_ref[j, k, 1] = s_real * a_imag - s_imag * a_real


def pointwise_kernel(place, mix_ref, gradient_ref, out_ref, z_plain_ref, turn_ref):
    z_plain_ref[...] = place.z_table(False)
    turn_ref[...] = turn_matrix(place, False)
    z_count = place.z_count
    product = dot(mix_ref[...], gradient_ref[...])
    for y in range(place.rows_y):
        out_ref[:, y, :] = product[:, y * z_count : (y + 1) * z_count]


def finish_kernel(place, *refs):
    own_ref, got_ref, z_table_ref, turn_ref, pointwise_ref, prediction_ref = refs[:6]
    refs = refs[6:]
    height = 2 * MZ
    channels = place.channels
    lines = (own_ref[...] + got_ref[:height].astype(F32)).astype(BF16)
    lines = dot(lines, turn_ref[...]).astype(BF16)
    pointwise = pointwise_ref[...].reshape(place.lanes, place.z_count)
    grad_field = (dot_tn(lines, z_table_ref[...]) + pointwise).astype(BF16)
    if not place.fold:
        refs[0][...] = grad_field
        refs[1][...] = prediction_ref[...]
        return
    sums_ref, grad_field_ref, out_ref, grad_mix_ref, grad_head_ref = refs
    grad_field_ref[...] = grad_field
    out_ref[...] = prediction_ref[...]
    got = got_ref[height:].astype(F32)
    width = sums_ref.shape[1]
    total = sums_ref[...] + got[:, :width] + got[:, width:]
    grad_head_ref[...] = total[:channels]
    grad_mix_ref[...] = total[channels:, :channels]


def call(kernel, outs, name, **spec):
    return pl.pallas_call(
        kernel,
        out_shape=[jax.ShapeDtypeStruct(shape, dtype) for shape, dtype in outs],
        compiler_params=pltpu.CompilerParams(vmem_limit_bytes=VMEM_LIMIT),
        cost_estimate=pl.CostEstimate(flops=1 << 22, bytes_accessed=1 << 19, transcendentals=0),
        name=name,
        **spec,
    )


def body(
    lifted_field,
    spectral_weight,
    mix_weight,
    mix_bias,
    head_weight,
    head_bias,
    out_weight,
    cotangent,
):
    wide = lax.axis_size("wide")
    narrow = lax.axis_size("narrow")
    devices = wide * narrow
    _, channels, rows_y, z_count = lifted_field.shape
    modes, kz = spectral_weight.shape[:2]
    hidden_units = head_weight.shape[1]
    cells = channels * rows_y
    place = Place(wide, narrow, kz, modes, rows_y, channels, z_count, False)
    place.fold = 2 * place.partners == channels and hidden_units == 128 and cells == 256 and kz % 8 == 0
    height = 2 * MZ
    step = 2 * kz
    partners = place.partners
    mode_lines = modes * 2 * kz

    y_forward, y_inverse = y_tables(rows_y * narrow, rows_y, kz, modes)
    if len(y_forward) > 1:
        block = lax.axis_index("wide") % len(y_forward)
        y_forward = lax.dynamic_index_in_dim(jnp.asarray(y_forward), block, 0, False)
        y_inverse = lax.dynamic_index_in_dim(jnp.asarray(y_inverse), block, 0, False)
    else:
        y_forward, y_inverse = jnp.asarray(y_forward[0]), jnp.asarray(y_inverse[0])

    def to_twin(send):
        pairs = [(p, p ^ narrow) for p in range(devices)]
        return lax.ppermute(send, ("wide", "narrow"), pairs)

    def exchange(send, transform):
        first = place.firsts[transform]
        groups = [
            [
                (2 * place.listed(outer, first, inner) + inner) * narrow + n
                for outer in range(place.outer)
                for n in range(narrow)
            ]
            for inner in range(2)
        ]
        pieces = send.reshape(partners, -1, send.shape[1])
        got = lax.all_to_all(
            pieces, ("wide", "narrow"), 0, 0, axis_index_groups=groups, tiled=True
        )
        return got.reshape(send.shape)

    plain = ((partners * step, cells), BF16)
    shared = ((partners * (2 * step + 8), cells // 2), BF16) if place.fold else plain
    twin_plain = ((height, cells), BF16)
    twin_shared = ((height + 2 * channels, cells), BF16) if place.fold else twin_plain
    sums_shape = ((2 * channels, hidden_units), F32)
    own_lines = ((height, cells), F32)
    across = (channels, rows_y * z_count)

    def run(kernel, outs, name, **spec):
        return call(functools.partial(kernel, place), outs, name, **spec)

    flat_field = lifted_field.reshape(cells, z_count)
    twin_field = to_twin(flat_field)
    tables_shape = ((wide // 2 * height, 4 * height), BF16)
    field, spectra, *tables = run(
        own_kernel,
        [(across, BF16), twin_plain, ((height, z_count), BF16), ((cells, cells), BF16), tables_shape],
        "own",
    )(flat_field)
    (send,) = run(start_kernel, [plain], "start")(spectra, twin_field, *tables)
    packed_shape = ((modes // 4, kz * channels, 8 * channels), BF16)
    inverse_shape = ((2 * height, wide // 2 * height), BF16)
    weight, inverse = run(pack_kernel, [packed_shape, inverse_shape], "pack")(spectral_weight)
    spectrum, send = run(mode_kernel, [((mode_lines, channels), F32), plain], "mode")(
        exchange(send, 0), y_forward, y_inverse, weight
    )
    own, send = run(part_kernel, [own_lines, twin_plain], "part")(exchange(send, 1), inverse)
    pointwise, head_turned, z_doubled = run(
        ready_kernel,
        [(across, F32), ((hidden_units, channels), BF16), ((height, z_count), BF16)],
        "ready",
    )(field, mix_weight, mix_bias[:, None], head_weight)
    prediction, grad_pre, send, hidden, head_slope = run(
        cell_kernel,
        [
            ((rows_y, z_count), F32),
            (across, BF16),
            twin_plain,
            (across, BF16),
            ((hidden_units, rows_y * z_count), BF16),
        ],
        "cell",
    )(
        own,
        to_twin(send),
        z_doubled,
        pointwise,
        head_weight,
        head_turned,
        head_bias[:, None],
        out_weight.astype(F32)[:, None],
        cotangent[0],
    )
    if place.fold:
        outs = [((8 * partners, hidden_units), BF16)]
    else:
        outs = [((channels, channels), F32), ((channels, hidden_units), F32)]
    outs += [((wide // 2 * height, 4 * height), BF16)]
    *sums, forward = run(sums_kernel, outs, "sums")(field, grad_pre, hidden, head_slope)
    if not place.fold:
        totals = lax.psum(tuple(sums), ("wide", "narrow"))
        sums = []
    (send,) = run(fold_kernel, [shared], "fold")(send, to_twin(send), forward, *sums)
    adjoint, send = run(back_kernel, [((mode_lines, channels), F32), shared], "back")(
        exchange(send, 2), y_forward, y_inverse, weight
    )
    some = max(1, modes // 4)
    grad_spectral, done = pl.pallas_call(
        outer_kernel,
        grid=(modes // some,),
        in_specs=[pl.BlockSpec((some, 2 * kz, channels), lambda j: (j, 0, 0))] * 2,
        out_specs=[
            pl.BlockSpec((some, kz, 2, channels, channels), lambda j: (j, 0, 0, 0, 0)),
            pl.BlockSpec((8, 128), lambda j: (0, 0)),
        ],
        out_shape=[
            jax.ShapeDtypeStruct(spectral_weight.shape, F32),
            jax.ShapeDtypeStruct((8, 128), F32),
        ],
        compiler_params=pltpu.CompilerParams(vmem_limit_bytes=VMEM_LIMIT),
        cost_estimate=pl.CostEstimate(flops=1 << 22, bytes_accessed=5 << 20, transcendentals=0),
        name="outer",
    )(spectrum.reshape(modes, 2 * kz, channels), adjoint.reshape(modes, 2 * kz, channels))
    pointwise, z_plain, turn = run(
        pointwise_kernel,
        [
            ((channels, rows_y, z_count), F32),
            ((height, z_count), BF16),
            ((cells, cells), BF16),
        ],
        "pointwise",
    )(mix_weight, grad_pre)
    outs = [own_lines, twin_shared] + ([sums_shape] if place.fold else [])
    after = (done,) if place.fold else ()
    own, send, *sums = run(part_kernel, outs, "part")(exchange(send, 3), inverse, *after)
    outs = [((cells, z_count), BF16), ((rows_y, z_count), F32)]
    if place.fold:
        outs += [((channels, channels), F32), ((channels, hidden_units), F32)]
    grad_field, prediction, *summed = run(finish_kernel, outs, "finish")(
        own, to_twin(send), z_plain, turn, pointwise, prediction, *sums
    )
    grad_mix, grad_head = summed if place.fold else totals
    return (
        prediction[None],
        grad_field.reshape(lifted_field.shape),
        grad_spectral,
        grad_mix,
        grad_head,
    )


def solution(mesh):
    return jax.shard_map(
        body,
        mesh=mesh,
        in_specs=(
            P("wide", None, "narrow", None),
            P("wide", "narrow", None, None, None),
            P(),
            P(),
            P(),
            P(),
            P(),
            P("wide", "narrow", None),
        ),
        out_specs=(
            P("wide", "narrow", None),
            P("wide", None, "narrow", None),
            P("wide", "narrow", None, None, None),
            P(),
            P(),
        ),
        check_vma=False,
    )
```

```python
import functools
import math

import jax
import jax.numpy as jnp
import numpy as np
from jax import lax
from jax.experimental import pallas as pl
from jax.experimental.pallas import tpu as pltpu
from jax.sharding import PartitionSpec as P

MX = 16
MY = 16
MZ = 16
BLOCK = 32
F32 = jnp.float32
BF16 = jnp.bfloat16
VMEM_LIMIT = 32 * 1024 * 1024

TAIL_SLOPE = 0.275
TAIL = (
    0.11780925840139389,
    0.04211147502064705,
    0.3339323103427887,
    -0.3309934139251709,
    0.4519987106323242,
    -0.11485832929611206,
)


def signed(indices, count):
    return np.where(indices < count // 2, indices, indices - count)


def wave(positions, frequency, length):
    turned = np.mod(np.multiply.outer(positions, frequency), length)
    angles = turned.astype(np.float32) * np.float32(2.0 * math.pi / length)
    scale = np.float32(1.0 / math.sqrt(length))
    return np.cos(angles) * scale, np.sin(angles) * scale


def pair(cosine, sine, sign):
    return np.stack(
        [np.stack([cosine, -sign * sine], -1), np.stack([sign * sine, cosine], -1)], -2
    )


def y_tables(total_y, rows_y, kz, modes):
    cosine, sine = wave(np.arange(total_y), signed(np.arange(MY), MY), total_y)
    narrow = total_y // rows_y
    same = np.eye(kz, dtype=np.float32)
    forward = pair(cosine, sine, -1.0).reshape(narrow, rows_y, MY // modes, modes, 2, 2)
    inverse = pair(cosine, sine, 1.0).reshape(narrow, rows_y, MY // modes, modes, 2, 2)
    forward = np.einsum("nybjtr,kl->bjtkynlr", forward, same)
    inverse = np.einsum("nybjst,kl->bnyksjtl", inverse, same)
    blocks = MY // modes
    forward = forward.reshape(blocks, modes * 2 * kz, rows_y * narrow * kz * 2)
    inverse = inverse.reshape(blocks, narrow * rows_y * kz * 2, modes * 2 * kz)
    return forward.astype(BF16), inverse.astype(BF16)


def dot(a, b):
    return jnp.dot(a, b, preferred_element_type=F32)


def dot_nt(a, b):
    return lax.dot_general(a, b, (((1,), (1,)), ((), ())), preferred_element_type=F32)


def dot_tn(a, b):
    return lax.dot_general(a, b, (((0,), (0,)), ((), ())), preferred_element_type=F32)


def grid_of(rows, columns):
    shape = (rows, columns)
    return lax.broadcasted_iota(jnp.int32, shape, 0), lax.broadcasted_iota(jnp.int32, shape, 1)


def selector(rows, columns, condition):
    return jnp.where(condition(*grid_of(rows, columns)), 1.0, 0.0).astype(BF16)


def halves(values):
    high = values.astype(BF16)
    return high, (values - high.astype(F32)).astype(BF16)


def stacked(refs, lanes=slice(None)):
    return jnp.concatenate([ref[:, lanes] for ref in refs], axis=0)


def cosine_of(phase, length):
    angles = (phase & (length - 1)).astype(F32) * (2.0 * math.pi / length)
    return jnp.cos(angles) * (1.0 / math.sqrt(length))


class Place:
    def __init__(self, wide, narrow, kz, modes, rows_y, channels, z_count, fold):
        self.wide, self.narrow, self.kz, self.modes = wide, narrow, kz, modes
        self.rows_y, self.channels, self.z_count, self.fold = rows_y, channels, z_count, fold
        self.outer = wide // 2
        self.partners = self.outer * narrow
        self.lanes = rows_y * channels
        middle = self.outer // 4
        self.firsts = (middle, middle, middle, middle)

    def here(self):
        wide = lax.axis_index("wide")
        return wide // 2, wide % 2

    def listed(self, position, first, inner):
        lines = self.outer // 2
        return ((first + (1 - 2 * inner) * (position // 2)) & (lines - 1)) * 2 + (position % 2 ^ inner)

    def frequency(self, wide):
        index = (wide * self.modes) // MY
        return jnp.where(index < MX // 2, index, index - MX)

    def z_table(self, doubled):
        row, z = grid_of(2 * MZ, self.z_count)
        frequency = row >> 1
        value = cosine_of(z * frequency + (row & 1) * (self.z_count // 4), self.z_count)
        if doubled:
            value = jnp.where(frequency > 0, 2.0 * value, value)
        return value.astype(BF16)

    def expanded(self, small):
        row, column = grid_of(2 * MZ, small.shape[1])
        same = (row >> 1) == ((column >> 1) & (MZ - 1))
        blocks = []
        for g in range(small.shape[0] // 2):
            value = jnp.where((row & 1) == 0, small[2 * g : 2 * g + 1], small[2 * g + 1 : 2 * g + 2])
            blocks.append(jnp.where(same, value, 0.0))
        return jnp.concatenate(blocks, axis=0)

    def forward_x(self, first):
        outer, inner = self.here()
        row, column = grid_of(2 * self.outer, 4 * MZ)
        x = 2 * outer + (inner ^ (column // (2 * MZ)))
        frequency = self.frequency(2 * self.listed(row >> 1, first, inner) + inner)
        quarter = self.wide // 4
        small = cosine_of(x * frequency + quarter * ((row & 1) - (column & 1)), self.wide)
        return self.expanded(small)

    def inverse_x(self, first):
        outer, inner = self.here()
        row, column = grid_of(4, self.outer * 2 * MZ)
        x = 2 * outer + (inner ^ (row >> 1))
        frequency = self.frequency(2 * self.listed(column // (2 * MZ), first, inner) + inner)
        quarter = self.wide // 4
        small = cosine_of(x * frequency + quarter * ((column & 1) - (row & 1)), self.wide)
        return self.expanded(small).astype(BF16)


def repeat_rows(out_ref, block):
    height = block.shape[0]
    for first in range(0, out_ref.shape[0], height):
        out_ref[first : first + height] = block


def write_pieces(place, send_ref, block, shares):
    step, half = 2 * place.kz, place.lanes // 2
    height = send_ref.shape[0] // place.partners
    for p in range(place.partners):
        own = block[p * step % block.shape[0] :][:step]
        first = p * height
        send_ref[first : first + step] = own[:, :half]
        send_ref[first + step : first + 2 * step] = own[:, half:]
        send_ref[first + 2 * step : first + height] = shares[p * 8 % shares.shape[0] :][:8]


def read_pieces(place, pieces_ref):
    step = 2 * place.kz
    if pieces_ref.shape[1] == place.lanes:
        return pieces_ref[...], None
    height = pieces_ref.shape[0] // place.partners
    blocks, shares = [], []
    for p in range(place.partners):
        first = p * height
        left = pieces_ref[first : first + step]
        right = pieces_ref[first + step : first + 2 * step]
        blocks.append(jnp.concatenate([left, right], axis=1))
        shares.append(pieces_ref[first + 2 * step : first + height].astype(F32))
    return jnp.concatenate(blocks, axis=0), shares


def lane_sum(values, width):
    while values.shape[1] > 128:
        half = values.shape[1] // 2
        values = values[:, :half] + values[:, half:]
    if values.shape[1] < 128:
        blocks = range(0, values.shape[1], width)
        return sum(values[:, first : first + width] for first in blocks)
    shift = 64
    while shift >= width:
        values = values + pltpu.roll(values, shift, 1)
        shift //= 2
    return values[:, :width]


def diagonal_blocks(count, width, rows):
    row, lane = grid_of(count, count * width)
    pattern = jnp.where(row == lane // width, 1.0, 0.0)
    return jnp.concatenate([pattern] * (rows // count), axis=0)


def analysed(place, pieces, y_forward, copies):
    height = 2 * MZ
    turned = sum(
        pieces[first : first + height].astype(F32) for first in range(0, pieces.shape[0], height)
    )
    channels = place.channels
    lines = jnp.concatenate(
        [turned[:, y * channels : (y + 1) * channels] for y in range(place.rows_y)], axis=0
    )
    return dot(y_forward, jnp.concatenate([lines.astype(BF16)] * copies, axis=1))


def spread_lines(place, modes, y_inverse):
    lines = dot(y_inverse, modes)
    step = 2 * place.kz
    blocks = []
    for n in range(place.narrow):
        first = n * place.rows_y
        parts = [lines[(first + y) * step : (first + y + 1) * step] for y in range(place.rows_y)]
        blocks.append(jnp.concatenate(parts, axis=1))
    return jnp.concatenate(blocks, axis=0).astype(BF16)


def turn_matrix(place, forward):
    channels, rows_y = place.channels, place.rows_y

    def same(row, column):
        if forward:
            row, column = column, row
        return (row % channels == column // rows_y) & (row // channels == column % rows_y)

    return selector(place.lanes, place.lanes, same)


def side_by_side(values, count):
    height = values.shape[0] // count
    return jnp.concatenate([values[y * height : (y + 1) * height] for y in range(count)], axis=1)


def one_below_other(values, count):
    width = values.shape[1] // count
    return jnp.concatenate([values[:, y * width : (y + 1) * width] for y in range(count)], axis=0)


def own_kernel(place, field_ref, field_out_ref, spectra_ref, z_table_ref, turn_ref, tables_ref):
    z_table = place.z_table(False)
    turned = dot(turn_matrix(place, False), field_ref[...]).astype(BF16)
    field_out_ref[...] = side_by_side(turned, place.rows_y)
    spectra_ref[...] = dot_nt(z_table, turned).astype(BF16)
    z_table_ref[...] = z_table
    turn_ref[...] = turn_matrix(place, True)
    tables_ref[...] = jnp.concatenate(halves(place.forward_x(place.firsts[0])), axis=1)


def start_kernel(place, spectra_ref, twin_ref, z_table_ref, turn_ref, tables_ref, send_ref):
    twin = dot_nt(z_table_ref[...], twin_ref[...]).astype(BF16)
    twin = dot(twin, turn_ref[...]).astype(BF16)
    values = jnp.concatenate([spectra_ref[...], twin], axis=0)
    send_ref[...] = dot(tables_ref[...], jnp.concatenate([values, values], axis=0)).astype(BF16)


def pack_kernel(place, weight_ref, packed_ref, inverse_ref):
    inverse_ref[...] = place.inverse_x(place.firsts[1])
    modes, kz, _, channels, _ = weight_ref.shape
    for q in range(modes // 4):
        parts = [weight_ref[4 * q + j // 2, :, j % 2] for j in range(8)]
        packed = jnp.concatenate(parts, axis=-1).reshape(kz * channels, 8 * channels)
        packed_ref[q] = packed.astype(BF16)


def ready_kernel(place, field_ref, mix_ref, mix_bias_ref, head_ref, *refs):
    pointwise_ref, head_out_ref, z_doubled_ref = refs
    pointwise_ref[...] = dot_tn(mix_ref[...], field_ref[...]) + mix_bias_ref[...]
    head_out_ref[...] = jnp.transpose(head_ref[...].astype(F32)).astype(BF16)
    z_doubled_ref[...] = place.z_table(True)


def fold_kernel(place, own_ref, got_ref, tables_ref, *refs):
    values = jnp.concatenate([own_ref[...], got_ref[...]], axis=0)
    values = jnp.concatenate([values, values], axis=0)
    partial = dot(tables_ref[...], values).astype(BF16)
    if place.fold:
        shares_ref, send_ref = refs
        write_pieces(place, send_ref, partial, shares_ref[...])
    else:
        refs[0][...] = partial


def mode_kernel(
    place, pieces_ref, y_forward_ref, y_inverse_ref, weight_ref, spectrum_ref, send_ref
):
    kz, channels = place.kz, place.channels
    spectrum = analysed(place, pieces_ref[...], y_forward_ref[...], kz)
    spectrum_ref[...] = spectrum[:, :channels]
    diagonal = diagonal_blocks(kz, channels, 8 * kz)
    mixed = []
    for q in range(place.modes // 4):
        left = (spectrum[q * 8 * kz : (q + 1) * 8 * kz] * diagonal).astype(BF16)
        product = dot(left, weight_ref[q])
        for j in range(4):
            own = product[j * 2 * kz : (j + 1) * 2 * kz, j * 2 * channels : (j + 1) * 2 * channels]
            real, imag = own[:, :channels], own[:, channels:]
            mixed.append(real[:kz] - imag[kz:])
            mixed.append(imag[:kz] + real[kz:])
    mode = jnp.concatenate(mixed, axis=0).astype(BF16)
    repeat_rows(send_ref, spread_lines(place, mode, y_inverse_ref[...]))


def part_kernel(place, pieces_ref, table_ref, *refs):
    pieces, shares = read_pieces(place, pieces_ref)
    lines = dot(table_ref[...], pieces)
    height = 2 * MZ
    if shares is None:
        own_ref, send_ref = refs
        own_ref[...] = lines[:height]
        send_ref[...] = lines[height:].astype(BF16)
        return
    _, own_ref, send_ref, sums_ref = refs
    own_ref[...] = lines[:height]
    send_ref[:height] = lines[height:].astype(BF16)
    got = jnp.concatenate(shares, axis=0).astype(BF16)
    channels = place.channels

    def chosen(part):
        def condition(row, column):
            owner, source = (row % channels) // 2, column // 8
            return (
                (owner == source)
                & (column % 8 == 4 * part + 2 * (row // channels) + row % 2)
            )

        return dot(selector(2 * channels, got.shape[0], condition), got)

    high, low = chosen(0), chosen(1)
    sums_ref[...] = high + low
    send_ref[height:] = jnp.concatenate([high, low], axis=1).astype(BF16)


def normal(values):
    scaled = pl.reciprocal(1.0 + jnp.abs(TAIL_SLOPE * values), approx=True)
    decay = jnp.exp2(values * values * (-0.5 / math.log(2.0)))
    tail = TAIL[-1]
    for factor in TAIL[-2::-1]:
        tail = tail * scaled + factor
    tail = tail * (scaled * decay)
    cumulative = jnp.where(values > 0.0, 1.0 - tail, tail)
    return values * cumulative, cumulative + values * (decay * (1.0 / math.sqrt(2.0 * math.pi)))


def cell_kernel(place, *refs):
    own_ref, got_ref, z_table_ref, pointwise_ref, head_ref, head_turned_ref = refs[:6]
    head_bias_ref, out_column_ref, cotangent_ref = refs[6:9]
    prediction_ref, grad_pre_ref, send_ref, hidden_ref, head_slope_ref = refs[9:]
    rows_y, z_count = place.rows_y, place.z_count
    z_table = z_table_ref[...]
    lines = (own_ref[...] + got_ref[...].astype(F32)).astype(BF16)
    pre_act = side_by_side(dot_tn(lines, z_table), rows_y) + pointwise_ref[...]
    head, head_turned = head_ref[...], head_turned_ref[...]
    head_bias, out_column = head_bias_ref[...], out_column_ref[...]
    width = 2 * z_count
    slopes, head_pre = [], []
    for first in range(0, rows_y * z_count, width):
        value, slope = normal(pre_act[:, first : first + width])
        hidden = value.astype(BF16)
        hidden_ref[:, first : first + width] = hidden
        slopes.append(slope)
        head_pre.append(dot(head_turned, hidden))
    gradients = []
    for index, first in enumerate(range(0, rows_y, 2)):
        target = jnp.concatenate(
            [cotangent_ref[y : y + 1] for y in range(first, first + 2)], axis=1
        )
        predicted, parts = 0.0, []
        for top in range(0, head_bias.shape[0], BLOCK):
            rows = slice(top, top + BLOCK)
            active, slope = normal(head_pre[index][rows] + head_bias[rows])
            predicted = predicted + active.astype(BF16).astype(F32) * out_column[rows]
            parts.append((target * out_column[rows] * slope).astype(BF16))
        predicted = jnp.sum(predicted, axis=0, keepdims=True)
        prediction_ref[first : first + 1] = predicted[:, :z_count]
        prediction_ref[first + 1 : first + 2] = predicted[:, z_count:]
        head_slope = jnp.concatenate(parts, axis=0)
        head_slope_ref[:, first * z_count : first * z_count + width] = head_slope
        gradients.append((dot(head, head_slope) * slopes[index]).astype(BF16))
    gradient = jnp.concatenate(gradients, axis=1)
    grad_pre_ref[...] = gradient
    send_ref[...] = dot_nt(z_table, one_below_other(gradient, rows_y)).astype(BF16)


def sums_kernel(place, field_ref, gradient_ref, hidden_ref, head_slope_ref, *refs):
    refs[-1][...] = jnp.concatenate(halves(place.forward_x(place.firsts[2])), axis=1)
    grad_mix = dot_nt(field_ref[...], gradient_ref[...])
    grad_head = dot_nt(hidden_ref[...], head_slope_ref[...])
    if not place.fold:
        refs[0][...] = grad_mix
        refs[1][...] = grad_head
        return
    channels, hidden_units = grad_head.shape
    rest = jnp.zeros((channels, hidden_units - channels), F32)
    wide_mix = jnp.concatenate([grad_mix, rest], axis=1)
    high, low = halves(jnp.concatenate([grad_head, wide_mix], axis=0))
    split = jnp.concatenate([high, low], axis=0)
    place_of = selector(
        8 * place.partners,
        4 * channels,
        lambda row, column: (column % channels == 2 * (row // 8) + row % 2)
        & (column // channels == (row % 8) // 2),
    )
    refs[0][...] = dot(place_of, split).astype(BF16)


def back_kernel(
    place, pieces_ref, y_forward_ref, y_inverse_ref, weight_ref, adjoint_ref, send_ref
):
    kz, channels = place.kz, place.channels
    pieces, shares = read_pieces(place, pieces_ref)
    adjoint = analysed(place, pieces, y_forward_ref[...], 1)
    adjoint_ref[...] = adjoint
    turned = []
    for first in range(0, adjoint.shape[0], 2 * kz):
        turned += [adjoint[first + kz : first + 2 * kz], -adjoint[first : first + kz]]
    left = jnp.concatenate([adjoint, jnp.concatenate(turned, axis=0)], axis=1)
    left = jnp.concatenate([left] * 4, axis=1)
    row, lane = grid_of(8 * kz, 8 * channels)
    same = jnp.where(row // (2 * kz) == lane // (2 * channels), 1.0, 0.0)
    diagonal = diagonal_blocks(kz, channels, 8 * kz)
    block = 8 * kz
    pulled = []
    for q in range(place.modes // 4):
        own = (left[q * block : (q + 1) * block] * same).astype(BF16)
        pulled.append(lane_sum(dot_nt(own, weight_ref[q]) * diagonal, channels))
    modes_back = jnp.concatenate(pulled, axis=0).astype(BF16)
    block = spread_lines(place, modes_back, y_inverse_ref[...])
    if shares is None:
        repeat_rows(send_ref, block)
        return
    total = sum(shares[1:], shares[0])
    high, low = halves(total[0:4] + total[4:8])
    split = jnp.concatenate([high.astype(F32), low.astype(F32)], axis=0)
    write_pieces(place, send_ref, block, split.astype(BF16))


def outer_kernel(spectrum_ref, adjoint_ref, out_ref, done_ref):
    done_ref[...] = jnp.zeros(done_ref.shape, F32)
    modes, kz = out_ref.shape[:2]
    for j in range(modes):
        columns = jnp.transpose(spectrum_ref[j])
        adjoint = adjoint_ref[j]
        for k in range(kz):
            s_real, s_imag = columns[:, k : k + 1], columns[:, kz + k : kz + k + 1]
            a_real, a_imag = adjoint[k : k + 1], adjoint[kz + k : kz + k + 1]
            out_ref[j, k, 0] = s_real * a_real + s_imag * a_imag
            out_ref[j, k, 1] = s_real * a_imag - s_imag * a_real


def pointwise_kernel(place, mix_ref, gradient_ref, out_ref, z_plain_ref, turn_ref):
    z_plain_ref[...] = place.z_table(False)
    turn_ref[...] = turn_matrix(place, False)
    z_count = place.z_count
    product = dot(mix_ref[...], gradient_ref[...])
    for y in range(place.rows_y):
        out_ref[:, y, :] = product[:, y * z_count : (y + 1) * z_count]


def finish_kernel(place, *refs):
    own_ref, got_ref, z_table_ref, turn_ref, pointwise_ref, prediction_ref = refs[:6]
    refs = refs[6:]
    height = 2 * MZ
    channels = place.channels
    lines = (own_ref[...] + got_ref[:height].astype(F32)).astype(BF16)
    lines = dot(lines, turn_ref[...]).astype(BF16)
    pointwise = pointwise_ref[...].reshape(place.lanes, place.z_count)
    grad_field = (dot_tn(lines, z_table_ref[...]) + pointwise).astype(BF16)
    if not place.fold:
        refs[0][...] = grad_field
        refs[1][...] = prediction_ref[...]
        return
    sums_ref, grad_field_ref, out_ref, grad_mix_ref, grad_head_ref = refs
    grad_field_ref[...] = grad_field
    out_ref[...] = prediction_ref[...]
    got = got_ref[height:].astype(F32)
    width = sums_ref.shape[1]
    total = sums_ref[...] + got[:, :width] + got[:, width:]
    grad_head_ref[...] = total[:channels]
    grad_mix_ref[...] = total[channels:, :channels]


def call(kernel, outs, name, **spec):
    return pl.pallas_call(
        kernel,
        out_shape=[jax.ShapeDtypeStruct(shape, dtype) for shape, dtype in outs],
        compiler_params=pltpu.CompilerParams(vmem_limit_bytes=VMEM_LIMIT),
        cost_estimate=pl.CostEstimate(flops=1 << 22, bytes_accessed=1 << 19, transcendentals=0),
        name=name,
        **spec,
    )


def body(
    lifted_field,
    spectral_weight,
    mix_weight,
    mix_bias,
    head_weight,
    head_bias,
    out_weight,
    cotangent,
):
    wide = lax.axis_size("wide")
    narrow = lax.axis_size("narrow")
    devices = wide * narrow
    _, channels, rows_y, z_count = lifted_field.shape
    modes, kz = spectral_weight.shape[:2]
    hidden_units = head_weight.shape[1]
    cells = channels * rows_y
    place = Place(wide, narrow, kz, modes, rows_y, channels, z_count, False)
    place.fold = 2 * place.partners == channels and hidden_units == 128 and cells == 256 and kz % 8 == 0
    height = 2 * MZ
    step = 2 * kz
    partners = place.partners
    mode_lines = modes * 2 * kz

    y_forward, y_inverse = y_tables(rows_y * narrow, rows_y, kz, modes)
    if len(y_forward) > 1:
        block = lax.axis_index("wide") % len(y_forward)
        y_forward = lax.dynamic_index_in_dim(jnp.asarray(y_forward), block, 0, False)
        y_inverse = lax.dynamic_index_in_dim(jnp.asarray(y_inverse), block, 0, False)
    else:
        y_forward, y_inverse = jnp.asarray(y_forward[0]), jnp.asarray(y_inverse[0])

    def to_twin(send):
        pairs = [(p, p ^ narrow) for p in range(devices)]
        return lax.ppermute(send, ("wide", "narrow"), pairs)

    def exchange(send, transform):
        first = place.firsts[transform]
        groups = [
            [
                (2 * place.listed(outer, first, inner) + inner) * narrow + n
                for outer in range(place.outer)
                for n in range(narrow)
            ]
            for inner in range(2)
        ]
        pieces = send.reshape(partners, -1, send.shape[1])
        got = lax.all_to_all(
            pieces, ("wide", "narrow"), 0, 0, axis_index_groups=groups, tiled=True
        )
        return got.reshape(send.shape)

    plain = ((partners * step, cells), BF16)
    shared = ((partners * (2 * step + 8), cells // 2), BF16) if place.fold else plain
    twin_plain = ((height, cells), BF16)
    twin_shared = ((height + 2 * channels, cells), BF16) if place.fold else twin_plain
    sums_shape = ((2 * channels, hidden_units), F32)
    own_lines = ((height, cells), F32)
    across = (channels, rows_y * z_count)

    def run(kernel, outs, name, **spec):
        return call(functools.partial(kernel, place), outs, name, **spec)

    flat_field = lifted_field.reshape(cells, z_count)
    twin_field = to_twin(flat_field)
    tables_shape = ((wide // 2 * height, 4 * height), BF16)
    field, spectra, *tables = run(
        own_kernel,
        [(across, BF16), twin_plain, ((height, z_count), BF16), ((cells, cells), BF16), tables_shape],
        "own",
    )(flat_field)
    (send,) = run(start_kernel, [plain], "start")(spectra, twin_field, *tables)
    packed_shape = ((modes // 4, kz * channels, 8 * channels), BF16)
    inverse_shape = ((2 * height, wide // 2 * height), BF16)
    weight, inverse = run(pack_kernel, [packed_shape, inverse_shape], "pack")(spectral_weight)
    spectrum, send = run(mode_kernel, [((mode_lines, channels), F32), plain], "mode")(
        exchange(send, 0), y_forward, y_inverse, weight
    )
    own, send = run(part_kernel, [own_lines, twin_plain], "part")(exchange(send, 1), inverse)
    pointwise, head_turned, z_doubled = run(
        ready_kernel,
        [(across, F32), ((hidden_units, channels), BF16), ((height, z_count), BF16)],
        "ready",
    )(field, mix_weight, mix_bias[:, None], head_weight)
    prediction, grad_pre, send, hidden, head_slope = run(
        cell_kernel,
        [
            ((rows_y, z_count), F32),
            (across, BF16),
            twin_plain,
            (across, BF16),
            ((hidden_units, rows_y * z_count), BF16),
        ],
        "cell",
    )(
        own,
        to_twin(send),
        z_doubled,
        pointwise,
        head_weight,
        head_turned,
        head_bias[:, None],
        out_weight.astype(F32)[:, None],
        cotangent[0],
    )
    if place.fold:
        outs = [((8 * partners, hidden_units), BF16)]
    else:
        outs = [((channels, channels), F32), ((channels, hidden_units), F32)]
    outs += [((wide // 2 * height, 4 * height), BF16)]
    *sums, forward = run(sums_kernel, outs, "sums")(field, grad_pre, hidden, head_slope)
    if not place.fold:
        totals = lax.psum(tuple(sums), ("wide", "narrow"))
        sums = []
    (send,) = run(fold_kernel, [shared], "fold")(send, to_twin(send), forward, *sums)
    adjoint, send = run(back_kernel, [((mode_lines, channels), F32), shared], "back")(
        exchange(send, 2), y_forward, y_inverse, weight
    )
    some = max(1, modes // 4)
    grad_spectral, done = pl.pallas_call(
        outer_kernel,
        grid=(modes // some,),
        in_specs=[pl.BlockSpec((some, 2 * kz, channels), lambda j: (j, 0, 0))] * 2,
        out_specs=[
            pl.BlockSpec((some, kz, 2, channels, channels), lambda j: (j, 0, 0, 0, 0)),
            pl.BlockSpec((8, 128), lambda j: (0, 0)),
        ],
        out_shape=[
            jax.ShapeDtypeStruct(spectral_weight.shape, F32),
            jax.ShapeDtypeStruct((8, 128), F32),
        ],
        compiler_params=pltpu.CompilerParams(vmem_limit_bytes=VMEM_LIMIT),
        cost_estimate=pl.CostEstimate(flops=1 << 22, bytes_accessed=5 << 20, transcendentals=0),
        name="outer",
    )(spectrum.reshape(modes, 2 * kz, channels), adjoint.reshape(modes, 2 * kz, channels))
    pointwise, z_plain, turn = run(
        pointwise_kernel,
        [
            ((channels, rows_y, z_count), F32),
            ((height, z_count), BF16),
            ((cells, cells), BF16),
        ],
        "pointwise",
    )(mix_weight, grad_pre)
    outs = [own_lines, twin_shared] + ([sums_shape] if place.fold else [])
    after = (done,) if place.fold else ()
    own, send, *sums = run(part_kernel, outs, "part")(exchange(send, 3), inverse, *after)
    outs = [((cells, z_count), BF16), ((rows_y, z_count), F32)]
    if place.fold:
        outs += [((channels, channels), F32), ((channels, hidden_units), F32)]
    grad_field, prediction, *summed = run(finish_kernel, outs, "finish")(
        own, to_twin(send), z_plain, turn, pointwise, prediction, *sums
    )
    grad_mix, grad_head = summed if place.fold else totals
    return (
        prediction[None],
        grad_field.reshape(lifted_field.shape),
        grad_spectral,
        grad_mix,
        grad_head,
    )


def solution(mesh):
    return jax.shard_map(
        body,
        mesh=mesh,
        in_specs=(
            P("wide", None, "narrow", None),
            P("wide", "narrow", None, None, None),
            P(),
            P(),
            P(),
            P(),
            P(),
            P("wide", "narrow", None),
        ),
        out_specs=(
            P("wide", "narrow", None),
            P("wide", None, "narrow", None),
            P("wide", "narrow", None, None, None),
            P(),
            P(),
        ),
        check_vma=False,
    )
```

```python
import functools
import math

import jax
import jax.numpy as jnp
import numpy as np
from jax import lax
from jax.experimental import pallas as pl
from jax.experimental.pallas import tpu as pltpu
from jax.sharding import PartitionSpec as P

MX = 16
MY = 16
MZ = 16
BLOCK = 32
F32 = jnp.float32
BF16 = jnp.bfloat16
VMEM_LIMIT = 32 * 1024 * 1024

TAIL_SLOPE = 0.275
TAIL = (
    0.11780925840139389,
    0.04211147502064705,
    0.3339323103427887,
    -0.3309934139251709,
    0.4519987106323242,
    -0.11485832929611206,
)


def signed(indices, count):
    return np.where(indices < count // 2, indices, indices - count)


def wave(positions, frequency, length):
    turned = np.mod(np.multiply.outer(positions, frequency), length)
    angles = turned.astype(np.float32) * np.float32(2.0 * math.pi / length)
    scale = np.float32(1.0 / math.sqrt(length))
    return np.cos(angles) * scale, np.sin(angles) * scale


def pair(cosine, sine, sign):
    return np.stack(
        [np.stack([cosine, -sign * sine], -1), np.stack([sign * sine, cosine], -1)], -2
    )


def y_tables(total_y, rows_y, kz, modes):
    cosine, sine = wave(np.arange(total_y), signed(np.arange(MY), MY), total_y)
    narrow = total_y // rows_y
    same = np.eye(kz, dtype=np.float32)
    forward = pair(cosine, sine, -1.0).reshape(narrow, rows_y, MY // modes, modes, 2, 2)
    inverse = pair(cosine, sine, 1.0).reshape(narrow, rows_y, MY // modes, modes, 2, 2)
    forward = np.einsum("nybjtr,kl->bjtkynlr", forward, same)
    inverse = np.einsum("nybjst,kl->bnyksjtl", inverse, same)
    blocks = MY // modes
    forward = forward.reshape(blocks, modes * 2 * kz, rows_y * narrow * kz * 2)
    inverse = inverse.reshape(blocks, narrow * rows_y * kz * 2, modes * 2 * kz)
    return forward.astype(BF16), inverse.astype(BF16)


def dot(a, b):
    return jnp.dot(a, b, preferred_element_type=F32)


def dot_nt(a, b):
    return lax.dot_general(a, b, (((1,), (1,)), ((), ())), preferred_element_type=F32)


def dot_tn(a, b):
    return lax.dot_general(a, b, (((0,), (0,)), ((), ())), preferred_element_type=F32)


def grid_of(rows, columns):
    shape = (rows, columns)
    return lax.broadcasted_iota(jnp.int32, shape, 0), lax.broadcasted_iota(jnp.int32, shape, 1)


def selector(rows, columns, condition):
    return jnp.where(condition(*grid_of(rows, columns)), 1.0, 0.0).astype(BF16)


def halves(values):
    high = values.astype(BF16)
    return high, (values - high.astype(F32)).astype(BF16)


def stacked(refs, lanes=slice(None)):
    return jnp.concatenate([ref[:, lanes] for ref in refs], axis=0)


def cosine_of(phase, length):
    angles = (phase & (length - 1)).astype(F32) * (2.0 * math.pi / length)
    return jnp.cos(angles) * (1.0 / math.sqrt(length))


class Place:
    def __init__(self, wide, narrow, kz, modes, rows_y, channels, z_count, fold):
        self.wide, self.narrow, self.kz, self.modes = wide, narrow, kz, modes
        self.rows_y, self.channels, self.z_count, self.fold = rows_y, channels, z_count, fold
        self.outer = wide // 2
        self.partners = self.outer * narrow
        self.lanes = rows_y * channels
        middle = self.outer // 4
        self.firsts = (middle, middle, middle, middle)

    def here(self):
        wide = lax.axis_index("wide")
        return wide // 2, wide % 2

    def listed(self, position, first, inner):
        lines = self.outer // 2
        return ((first + (2 * inner - 1) * (position // 2)) & (lines - 1)) * 2 + position % 2

    def frequency(self, wide):
        index = (wide * self.modes) // MY
        return jnp.where(index < MX // 2, index, index - MX)

    def z_table(self, doubled):
        row, z = grid_of(2 * MZ, self.z_count)
        frequency = row >> 1
        value = cosine_of(z * frequency + (row & 1) * (self.z_count // 4), self.z_count)
        if doubled:
            value = jnp.where(frequency > 0, 2.0 * value, value)
        return value.astype(BF16)

    def expanded(self, small):
        row, column = grid_of(2 * MZ, small.shape[1])
        same = (row >> 1) == ((column >> 1) & (MZ - 1))
        blocks = []
        for g in range(small.shape[0] // 2):
            value = jnp.where((row & 1) == 0, small[2 * g : 2 * g + 1], small[2 * g + 1 : 2 * g + 2])
            blocks.append(jnp.where(same, value, 0.0))
        return jnp.concatenate(blocks, axis=0)

    def forward_x(self, first):
        outer, inner = self.here()
        row, column = grid_of(2 * self.outer, 4 * MZ)
        x = 2 * outer + (inner ^ (column // (2 * MZ)))
        frequency = self.frequency(2 * self.listed(row >> 1, first, inner) + inner)
        quarter = self.wide // 4
        small = cosine_of(x * frequency + quarter * ((row & 1) - (column & 1)), self.wide)
        return self.expanded(small)

    def inverse_x(self, first):
        outer, inner = self.here()
        row, column = grid_of(4, self.outer * 2 * MZ)
        x = 2 * outer + (inner ^ (row >> 1))
        frequency = self.frequency(2 * self.listed(column // (2 * MZ), first, inner) + inner)
        quarter = self.wide // 4
        small = cosine_of(x * frequency + quarter * ((column & 1) - (row & 1)), self.wide)
        return self.expanded(small).astype(BF16)


def repeat_rows(out_ref, block):
    height = block.shape[0]
    for first in range(0, out_ref.shape[0], height):
        out_ref[first : first + height] = block


def write_pieces(place, send_ref, block, shares):
    step, half = 2 * place.kz, place.lanes // 2
    height = send_ref.shape[0] // place.partners
    for p in range(place.partners):
        own = block[p * step % block.shape[0] :][:step]
        first = p * height
        send_ref[first : first + step] = own[:, :half]
        send_ref[first + step : first + 2 * step] = own[:, half:]
        send_ref[first + 2 * step : first + height] = shares[p * 8 % shares.shape[0] :][:8]


def read_pieces(place, pieces_ref):
    step = 2 * place.kz
    if pieces_ref.shape[1] == place.lanes:
        return pieces_ref[...], None
    height = pieces_ref.shape[0] // place.partners
    blocks, shares = [], []
    for p in range(place.partners):
        first = p * height
        left = pieces_ref[first : first + step]
        right = pieces_ref[first + step : first + 2 * step]
        blocks.append(jnp.concatenate([left, right], axis=1))
        shares.append(pieces_ref[first + 2 * step : first + height].astype(F32))
    return jnp.concatenate(blocks, axis=0), shares


def lane_sum(values, width):
    while values.shape[1] > 128:
        half = values.shape[1] // 2
        values = values[:, :half] + values[:, half:]
    if values.shape[1] < 128:
        blocks = range(0, values.shape[1], width)
        return sum(values[:, first : first + width] for first in blocks)
    shift = 64
    while shift >= width:
        values = values + pltpu.roll(values, shift, 1)
        shift //= 2
    return values[:, :width]


def diagonal_blocks(count, width, rows):
    row, lane = grid_of(count, count * width)
    pattern = jnp.where(row == lane // width, 1.0, 0.0)
    return jnp.concatenate([pattern] * (rows // count), axis=0)


def analysed(place, pieces, y_forward, copies):
    height = 2 * MZ
    turned = sum(
        pieces[first : first + height].astype(F32) for first in range(0, pieces.shape[0], height)
    )
    channels = place.channels
    lines = jnp.concatenate(
        [turned[:, y * channels : (y + 1) * channels] for y in range(place.rows_y)], axis=0
    )
    return dot(y_forward, jnp.concatenate([lines.astype(BF16)] * copies, axis=1))


def spread_lines(place, modes, y_inverse):
    lines = dot(y_inverse, modes)
    step = 2 * place.kz
    blocks = []
    for n in range(place.narrow):
        first = n * place.rows_y
        parts = [lines[(first + y) * step : (first + y + 1) * step] for y in range(place.rows_y)]
        blocks.append(jnp.concatenate(parts, axis=1))
    return jnp.concatenate(blocks, axis=0).astype(BF16)


def turn_matrix(place, forward):
    channels, rows_y = place.channels, place.rows_y

    def same(row, column):
        if forward:
            row, column = column, row
        return (row % channels == column // rows_y) & (row // channels == column % rows_y)

    return selector(place.lanes, place.lanes, same)


def side_by_side(values, count):
    height = values.shape[0] // count
    return jnp.concatenate([values[y * height : (y + 1) * height] for y in range(count)], axis=1)


def one_below_other(values, count):
    width = values.shape[1] // count
    return jnp.concatenate([values[:, y * width : (y + 1) * width] for y in range(count)], axis=0)


def own_kernel(place, field_ref, field_out_ref, spectra_ref, z_table_ref, turn_ref, tables_ref):
    z_table = place.z_table(False)
    turned = dot(turn_matrix(place, False), field_ref[...]).astype(BF16)
    field_out_ref[...] = side_by_side(turned, place.rows_y)
    spectra_ref[...] = dot_nt(z_table, turned).astype(BF16)
    z_table_ref[...] = z_table
    turn_ref[...] = turn_matrix(place, True)
    tables_ref[...] = jnp.concatenate(halves(place.forward_x(place.firsts[0])), axis=1)


def start_kernel(place, spectra_ref, twin_ref, z_table_ref, turn_ref, tables_ref, send_ref):
    twin = dot_nt(z_table_ref[...], twin_ref[...]).astype(BF16)
    twin = dot(twin, turn_ref[...]).astype(BF16)
    values = jnp.concatenate([spectra_ref[...], twin], axis=0)
    send_ref[...] = dot(tables_ref[...], jnp.concatenate([values, values], axis=0)).astype(BF16)


def pack_kernel(place, weight_ref, packed_ref, inverse_ref):
    inverse_ref[...] = place.inverse_x(place.firsts[1])
    modes, kz, _, channels, _ = weight_ref.shape
    for q in range(modes // 4):
        parts = [weight_ref[4 * q + j // 2, :, j % 2] for j in range(8)]
        packed = jnp.concatenate(parts, axis=-1).reshape(kz * channels, 8 * channels)
        packed_ref[q] = packed.astype(BF16)


def ready_kernel(place, field_ref, mix_ref, mix_bias_ref, head_ref, *refs):
    pointwise_ref, head_out_ref, z_doubled_ref = refs
    pointwise_ref[...] = dot_tn(mix_ref[...], field_ref[...]) + mix_bias_ref[...]
    head_out_ref[...] = jnp.transpose(head_ref[...].astype(F32)).astype(BF16)
    z_doubled_ref[...] = place.z_table(True)


def fold_kernel(place, own_ref, got_ref, tables_ref, *refs):
    values = jnp.concatenate([own_ref[...], got_ref[...]], axis=0)
    values = jnp.concatenate([values, values], axis=0)
    partial = dot(tables_ref[...], values).astype(BF16)
    if place.fold:
        shares_ref, send_ref = refs
        write_pieces(place, send_ref, partial, shares_ref[...])
    else:
        refs[0][...] = partial


def mode_kernel(
    place, pieces_ref, y_forward_ref, y_inverse_ref, weight_ref, spectrum_ref, send_ref
):
    kz, channels = place.kz, place.channels
    spectrum = analysed(place, pieces_ref[...], y_forward_ref[...], kz)
    spectrum_ref[...] = spectrum[:, :channels]
    diagonal = diagonal_blocks(kz, channels, 8 * kz)
    mixed = []
    for q in range(place.modes // 4):
        left = (spectrum[q * 8 * kz : (q + 1) * 8 * kz] * diagonal).astype(BF16)
        product = dot(left, weight_ref[q])
        for j in range(4):
            own = product[j * 2 * kz : (j + 1) * 2 * kz, j * 2 * channels : (j + 1) * 2 * channels]
            real, imag = own[:, :channels], own[:, channels:]
            mixed.append(real[:kz] - imag[kz:])
            mixed.append(imag[:kz] + real[kz:])
    mode = jnp.concatenate(mixed, axis=0).astype(BF16)
    repeat_rows(send_ref, spread_lines(place, mode, y_inverse_ref[...]))


def part_kernel(place, pieces_ref, table_ref, *refs):
    pieces, shares = read_pieces(place, pieces_ref)
    lines = dot(table_ref[...], pieces)
    height = 2 * MZ
    if shares is None:
        own_ref, send_ref = refs
        own_ref[...] = lines[:height]
        send_ref[...] = lines[height:].astype(BF16)
        return
    _, own_ref, send_ref, sums_ref = refs
    own_ref[...] = lines[:height]
    send_ref[:height] = lines[height:].astype(BF16)
    got = jnp.concatenate(shares, axis=0).astype(BF16)
    channels = place.channels

    def chosen(part):
        def condition(row, column):
            owner, source = (row % channels) // 2, column // 8
            return (
                (owner == source)
                & (column % 8 == 4 * part + 2 * (row // channels) + row % 2)
            )

        return dot(selector(2 * channels, got.shape[0], condition), got)

    high, low = chosen(0), chosen(1)
    sums_ref[...] = high + low
    send_ref[height:] = jnp.concatenate([high, low], axis=1).astype(BF16)


def normal(values):
    scaled = pl.reciprocal(1.0 + jnp.abs(TAIL_SLOPE * values), approx=True)
    decay = jnp.exp2(values * values * (-0.5 / math.log(2.0)))
    tail = TAIL[-1]
    for factor in TAIL[-2::-1]:
        tail = tail * scaled + factor
    tail = tail * (scaled * decay)
    cumulative = jnp.where(values > 0.0, 1.0 - tail, tail)
    return values * cumulative, cumulative + values * (decay * (1.0 / math.sqrt(2.0 * math.pi)))


def cell_kernel(place, *refs):
    own_ref, got_ref, z_table_ref, pointwise_ref, head_ref, head_turned_ref = refs[:6]
    head_bias_ref, out_column_ref, cotangent_ref = refs[6:9]
    prediction_ref, grad_pre_ref, send_ref, hidden_ref, head_slope_ref = refs[9:]
    rows_y, z_count = place.rows_y, place.z_count
    z_table = z_table_ref[...]
    lines = (own_ref[...] + got_ref[...].astype(F32)).astype(BF16)
    pre_act = side_by_side(dot_tn(lines, z_table), rows_y) + pointwise_ref[...]
    head, head_turned = head_ref[...], head_turned_ref[...]
    head_bias, out_column = head_bias_ref[...], out_column_ref[...]
    width = 2 * z_count
    slopes, head_pre = [], []
    for first in range(0, rows_y * z_count, width):
        value, slope = normal(pre_act[:, first : first + width])
        hidden = value.astype(BF16)
        hidden_ref[:, first : first + width] = hidden
        slopes.append(slope)
        head_pre.append(dot(head_turned, hidden))
    gradients = []
    for index, first in enumerate(range(0, rows_y, 2)):
        target = jnp.concatenate(
            [cotangent_ref[y : y + 1] for y in range(first, first + 2)], axis=1
        )
        predicted, parts = 0.0, []
        for top in range(0, head_bias.shape[0], BLOCK):
            rows = slice(top, top + BLOCK)
            active, slope = normal(head_pre[index][rows] + head_bias[rows])
            predicted = predicted + active.astype(BF16).astype(F32) * out_column[rows]
            parts.append((target * out_column[rows] * slope).astype(BF16))
        predicted = jnp.sum(predicted, axis=0, keepdims=True)
        prediction_ref[first : first + 1] = predicted[:, :z_count]
        prediction_ref[first + 1 : first + 2] = predicted[:, z_count:]
        head_slope = jnp.concatenate(parts, axis=0)
        head_slope_ref[:, first * z_count : first * z_count + width] = head_slope
        gradients.append((dot(head, head_slope) * slopes[index]).astype(BF16))
    gradient = jnp.concatenate(gradients, axis=1)
    grad_pre_ref[...] = gradient
    send_ref[...] = dot_nt(z_table, one_below_other(gradient, rows_y)).astype(BF16)


def sums_kernel(place, field_ref, gradient_ref, hidden_ref, head_slope_ref, *refs):
    refs[-1][...] = jnp.concatenate(halves(place.forward_x(place.firsts[2])), axis=1)
    grad_mix = dot_nt(field_ref[...], gradient_ref[...])
    grad_head = dot_nt(hidden_ref[...], head_slope_ref[...])
    if not place.fold:
        refs[0][...] = grad_mix
        refs[1][...] = grad_head
        return
    channels, hidden_units = grad_head.shape
    rest = jnp.zeros((channels, hidden_units - channels), F32)
    wide_mix = jnp.concatenate([grad_mix, rest], axis=1)
    high, low = halves(jnp.concatenate([grad_head, wide_mix], axis=0))
    split = jnp.concatenate([high, low], axis=0)
    place_of = selector(
        8 * place.partners,
        4 * channels,
        lambda row, column: (column % channels == 2 * (row // 8) + row % 2)
        & (column // channels == (row % 8) // 2),
    )
    refs[0][...] = dot(place_of, split).astype(BF16)


def back_kernel(
    place, pieces_ref, y_forward_ref, y_inverse_ref, weight_ref, adjoint_ref, send_ref
):
    kz, channels = place.kz, place.channels
    pieces, shares = read_pieces(place, pieces_ref)
    adjoint = analysed(place, pieces, y_forward_ref[...], 1)
    adjoint_ref[...] = adjoint
    turned = []
    for first in range(0, adjoint.shape[0], 2 * kz):
        turned += [adjoint[first + kz : first + 2 * kz], -adjoint[first : first + kz]]
    left = jnp.concatenate([adjoint, jnp.concatenate(turned, axis=0)], axis=1)
    left = jnp.concatenate([left] * 4, axis=1)
    row, lane = grid_of(8 * kz, 8 * channels)
    same = jnp.where(row // (2 * kz) == lane // (2 * channels), 1.0, 0.0)
    diagonal = diagonal_blocks(kz, channels, 8 * kz)
    block = 8 * kz
    pulled = []
    for q in range(place.modes // 4):
        own = (left[q * block : (q + 1) * block] * same).astype(BF16)
        pulled.append(lane_sum(dot_nt(own, weight_ref[q]) * diagonal, channels))
    modes_back = jnp.concatenate(pulled, axis=0).astype(BF16)
    block = spread_lines(place, modes_back, y_inverse_ref[...])
    if shares is None:
        repeat_rows(send_ref, block)
        return
    total = sum(shares[1:], shares[0])
    high, low = halves(total[0:4] + total[4:8])
    split = jnp.concatenate([high.astype(F32), low.astype(F32)], axis=0)
    write_pieces(place, send_ref, block, split.astype(BF16))


def outer_kernel(spectrum_ref, adjoint_ref, out_ref, done_ref):
    done_ref[...] = jnp.zeros(done_ref.shape, F32)
    modes, kz = out_ref.shape[:2]
    for j in range(modes):
        columns = jnp.transpose(spectrum_ref[j])
        adjoint = adjoint_ref[j]
        for k in range(kz):
            s_real, s_imag = columns[:, k : k + 1], columns[:, kz + k : kz + k + 1]
            a_real, a_imag = adjoint[k : k + 1], adjoint[kz + k : kz + k + 1]
            out_ref[j, k, 0] = s_real * a_real + s_imag * a_imag
            out_ref[j, k, 1] = s_real * a_imag - s_imag * a_real


def pointwise_kernel(place, mix_ref, gradient_ref, out_ref, z_plain_ref, turn_ref):
    z_plain_ref[...] = place.z_table(False)
    turn_ref[...] = turn_matrix(place, False)
    z_count = place.z_count
    product = dot(mix_ref[...], gradient_ref[...])
    for y in range(place.rows_y):
        out_ref[:, y, :] = product[:, y * z_count : (y + 1) * z_count]


def finish_kernel(place, *refs):
    own_ref, got_ref, z_table_ref, turn_ref, pointwise_ref, prediction_ref = refs[:6]
    refs = refs[6:]
    height = 2 * MZ
    channels = place.channels
    lines = (own_ref[...] + got_ref[:height].astype(F32)).astype(BF16)
    lines = dot(lines, turn_ref[...]).astype(BF16)
    pointwise = pointwise_ref[...].reshape(place.lanes, place.z_count)
    grad_field = (dot_tn(lines, z_table_ref[...]) + pointwise).astype(BF16)
    if not place.fold:
        refs[0][...] = grad_field
        refs[1][...] = prediction_ref[...]
        return
    sums_ref, grad_field_ref, out_ref, grad_mix_ref, grad_head_ref = refs
    grad_field_ref[...] = grad_field
    out_ref[...] = prediction_ref[...]
    got = got_ref[height:].astype(F32)
    width = sums_ref.shape[1]
    total = sums_ref[...] + got[:, :width] + got[:, width:]
    grad_head_ref[...] = total[:channels]
    grad_mix_ref[...] = total[channels:, :channels]


def call(kernel, outs, name, **spec):
    return pl.pallas_call(
        kernel,
        out_shape=[jax.ShapeDtypeStruct(shape, dtype) for shape, dtype in outs],
        compiler_params=pltpu.CompilerParams(vmem_limit_bytes=VMEM_LIMIT),
        cost_estimate=pl.CostEstimate(flops=1 << 22, bytes_accessed=1 << 19, transcendentals=0),
        name=name,
        **spec,
    )


def body(
    lifted_field,
    spectral_weight,
    mix_weight,
    mix_bias,
    head_weight,
    head_bias,
    out_weight,
    cotangent,
):
    wide = lax.axis_size("wide")
    narrow = lax.axis_size("narrow")
    devices = wide * narrow
    _, channels, rows_y, z_count = lifted_field.shape
    modes, kz = spectral_weight.shape[:2]
    hidden_units = head_weight.shape[1]
    cells = channels * rows_y
    place = Place(wide, narrow, kz, modes, rows_y, channels, z_count, False)
    place.fold = 2 * place.partners == channels and hidden_units == 128 and cells == 256 and kz % 8 == 0
    height = 2 * MZ
    step = 2 * kz
    partners = place.partners
    mode_lines = modes * 2 * kz

    y_forward, y_inverse = y_tables(rows_y * narrow, rows_y, kz, modes)
    if len(y_forward) > 1:
        block = lax.axis_index("wide") % len(y_forward)
        y_forward = lax.dynamic_index_in_dim(jnp.asarray(y_forward), block, 0, False)
        y_inverse = lax.dynamic_index_in_dim(jnp.asarray(y_inverse), block, 0, False)
    else:
        y_forward, y_inverse = jnp.asarray(y_forward[0]), jnp.asarray(y_inverse[0])

    def to_twin(send):
        pairs = [(p, p ^ narrow) for p in range(devices)]
        return lax.ppermute(send, ("wide", "narrow"), pairs)

    def exchange(send, transform):
        first = place.firsts[transform]
        groups = [
            [
                (2 * place.listed(outer, first, inner) + inner) * narrow + n
                for outer in range(place.outer)
                for n in range(narrow)
            ]
            for inner in range(2)
        ]
        pieces = send.reshape(partners, -1, send.shape[1])
        got = lax.all_to_all(
            pieces, ("wide", "narrow"), 0, 0, axis_index_groups=groups, tiled=True
        )
        return got.reshape(send.shape)

    plain = ((partners * step, cells), BF16)
    shared = ((partners * (2 * step + 8), cells // 2), BF16) if place.fold else plain
    twin_plain = ((height, cells), BF16)
    twin_shared = ((height + 2 * channels, cells), BF16) if place.fold else twin_plain
    sums_shape = ((2 * channels, hidden_units), F32)
    own_lines = ((height, cells), F32)
    across = (channels, rows_y * z_count)

    def run(kernel, outs, name, **spec):
        return call(functools.partial(kernel, place), outs, name, **spec)

    flat_field = lifted_field.reshape(cells, z_count)
    twin_field = to_twin(flat_field)
    tables_shape = ((wide // 2 * height, 4 * height), BF16)
    field, spectra, *tables = run(
        own_kernel,
        [(across, BF16), twin_plain, ((height, z_count), BF16), ((cells, cells), BF16), tables_shape],
        "own",
    )(flat_field)
    (send,) = run(start_kernel, [plain], "start")(spectra, twin_field, *tables)
    packed_shape = ((modes // 4, kz * channels, 8 * channels), BF16)
    inverse_shape = ((2 * height, wide // 2 * height), BF16)
    weight, inverse = run(pack_kernel, [packed_shape, inverse_shape], "pack")(spectral_weight)
    spectrum, send = run(mode_kernel, [((mode_lines, channels), F32), plain], "mode")(
        exchange(send, 0), y_forward, y_inverse, weight
    )
    own, send = run(part_kernel, [own_lines, twin_plain], "part")(exchange(send, 1), inverse)
    pointwise, head_turned, z_doubled = run(
        ready_kernel,
        [(across, F32), ((hidden_units, channels), BF16), ((height, z_count), BF16)],
        "ready",
    )(field, mix_weight, mix_bias[:, None], head_weight)
    prediction, grad_pre, send, hidden, head_slope = run(
        cell_kernel,
        [
            ((rows_y, z_count), F32),
            (across, BF16),
            twin_plain,
            (across, BF16),
            ((hidden_units, rows_y * z_count), BF16),
        ],
        "cell",
    )(
        own,
        to_twin(send),
        z_doubled,
        pointwise,
        head_weight,
        head_turned,
        head_bias[:, None],
        out_weight.astype(F32)[:, None],
        cotangent[0],
    )
    if place.fold:
        outs = [((8 * partners, hidden_units), BF16)]
    else:
        outs = [((channels, channels), F32), ((channels, hidden_units), F32)]
    outs += [((wide // 2 * height, 4 * height), BF16)]
    *sums, forward = run(sums_kernel, outs, "sums")(field, grad_pre, hidden, head_slope)
    if not place.fold:
        totals = lax.psum(tuple(sums), ("wide", "narrow"))
        sums = []
    (send,) = run(fold_kernel, [shared], "fold")(send, to_twin(send), forward, *sums)
    adjoint, send = run(back_kernel, [((mode_lines, channels), F32), shared], "back")(
        exchange(send, 2), y_forward, y_inverse, weight
    )
    some = max(1, modes // 4)
    grad_spectral, done = pl.pallas_call(
        outer_kernel,
        grid=(modes // some,),
        in_specs=[pl.BlockSpec((some, 2 * kz, channels), lambda j: (j, 0, 0))] * 2,
        out_specs=[
            pl.BlockSpec((some, kz, 2, channels, channels), lambda j: (j, 0, 0, 0, 0)),
            pl.BlockSpec((8, 128), lambda j: (0, 0)),
        ],
        out_shape=[
            jax.ShapeDtypeStruct(spectral_weight.shape, F32),
            jax.ShapeDtypeStruct((8, 128), F32),
        ],
        compiler_params=pltpu.CompilerParams(vmem_limit_bytes=VMEM_LIMIT),
        cost_estimate=pl.CostEstimate(flops=1 << 22, bytes_accessed=5 << 20, transcendentals=0),
        name="outer",
    )(spectrum.reshape(modes, 2 * kz, channels), adjoint.reshape(modes, 2 * kz, channels))
    pointwise, z_plain, turn = run(
        pointwise_kernel,
        [
            ((channels, rows_y, z_count), F32),
            ((height, z_count), BF16),
            ((cells, cells), BF16),
        ],
        "pointwise",
    )(mix_weight, grad_pre)
    outs = [own_lines, twin_shared] + ([sums_shape] if place.fold else [])
    after = (done,) if place.fold else ()
    own, send, *sums = run(part_kernel, outs, "part")(exchange(send, 3), inverse, *after)
    outs = [((cells, z_count), BF16), ((rows_y, z_count), F32)]
    if place.fold:
        outs += [((channels, channels), F32), ((channels, hidden_units), F32)]
    grad_field, prediction, *summed = run(finish_kernel, outs, "finish")(
        own, to_twin(send), z_plain, turn, pointwise, prediction, *sums
    )
    grad_mix, grad_head = summed if place.fold else totals
    return (
        prediction[None],
        grad_field.reshape(lifted_field.shape),
        grad_spectral,
        grad_mix,
        grad_head,
    )


def solution(mesh):
    return jax.shard_map(
        body,
        mesh=mesh,
        in_specs=(
            P("wide", None, "narrow", None),
            P("wide", "narrow", None, None, None),
            P(),
            P(),
            P(),
            P(),
            P(),
            P("wide", "narrow", None),
        ),
        out_specs=(
            P("wide", "narrow", None),
            P("wide", None, "narrow", None),
            P("wide", "narrow", None, None, None),
            P(),
            P(),
        ),
        check_vma=False,
    )
```

```python
import functools
import math

import jax
import jax.numpy as jnp
import numpy as np
from jax import lax
from jax.experimental import pallas as pl
from jax.experimental.pallas import tpu as pltpu
from jax.sharding import PartitionSpec as P

MX = 16
MY = 16
MZ = 16
BLOCK = 32
F32 = jnp.float32
BF16 = jnp.bfloat16
VMEM_LIMIT = 32 * 1024 * 1024

TAIL_SLOPE = 0.275
TAIL = (
    0.11780925840139389,
    0.04211147502064705,
    0.3339323103427887,
    -0.3309934139251709,
    0.4519987106323242,
    -0.11485832929611206,
)


def signed(indices, count):
    return np.where(indices < count // 2, indices, indices - count)


def wave(positions, frequency, length):
    turned = np.mod(np.multiply.outer(positions, frequency), length)
    angles = turned.astype(np.float32) * np.float32(2.0 * math.pi / length)
    scale = np.float32(1.0 / math.sqrt(length))
    return np.cos(angles) * scale, np.sin(angles) * scale


def pair(cosine, sine, sign):
    return np.stack(
        [np.stack([cosine, -sign * sine], -1), np.stack([sign * sine, cosine], -1)], -2
    )


def y_tables(total_y, rows_y, kz, modes):
    cosine, sine = wave(np.arange(total_y), signed(np.arange(MY), MY), total_y)
    narrow = total_y // rows_y
    same = np.eye(kz, dtype=np.float32)
    forward = pair(cosine, sine, -1.0).reshape(narrow, rows_y, MY // modes, modes, 2, 2)
    inverse = pair(cosine, sine, 1.0).reshape(narrow, rows_y, MY // modes, modes, 2, 2)
    forward = np.einsum("nybjtr,kl->bjtkynlr", forward, same)
    inverse = np.einsum("nybjst,kl->bnyksjtl", inverse, same)
    blocks = MY // modes
    forward = forward.reshape(blocks, modes * 2 * kz, rows_y * narrow * kz * 2)
    inverse = inverse.reshape(blocks, narrow * rows_y * kz * 2, modes * 2 * kz)
    return forward.astype(BF16), inverse.astype(BF16)


def dot(a, b):
    return jnp.dot(a, b, preferred_element_type=F32)


def dot_nt(a, b):
    return lax.dot_general(a, b, (((1,), (1,)), ((), ())), preferred_element_type=F32)


def dot_tn(a, b):
    return lax.dot_general(a, b, (((0,), (0,)), ((), ())), preferred_element_type=F32)


def grid_of(rows, columns):
    shape = (rows, columns)
    return lax.broadcasted_iota(jnp.int32, shape, 0), lax.broadcasted_iota(jnp.int32, shape, 1)


def selector(rows, columns, condition):
    return jnp.where(condition(*grid_of(rows, columns)), 1.0, 0.0).astype(BF16)


def halves(values):
    high = values.astype(BF16)
    return high, (values - high.astype(F32)).astype(BF16)


def stacked(refs, lanes=slice(None)):
    return jnp.concatenate([ref[:, lanes] for ref in refs], axis=0)


def cosine_of(phase, length):
    angles = (phase & (length - 1)).astype(F32) * (2.0 * math.pi / length)
    return jnp.cos(angles) * (1.0 / math.sqrt(length))


class Place:
    def __init__(self, wide, narrow, kz, modes, rows_y, channels, z_count, fold):
        self.wide, self.narrow, self.kz, self.modes = wide, narrow, kz, modes
        self.rows_y, self.channels, self.z_count, self.fold = rows_y, channels, z_count, fold
        self.outer = wide // 2
        self.partners = self.outer * narrow
        self.lanes = rows_y * channels
        middle = self.outer // 4
        self.firsts = (self.outer // 2 - 1, middle, middle, middle)

    def here(self):
        wide = lax.axis_index("wide")
        return wide // 2, wide % 2

    def listed(self, position, first, inner):
        lines = self.outer // 2
        return ((first + (1 - 2 * inner) * (position // 2)) & (lines - 1)) * 2 + position % 2

    def frequency(self, wide):
        index = (wide * self.modes) // MY
        return jnp.where(index < MX // 2, index, index - MX)

    def z_table(self, doubled):
        row, z = grid_of(2 * MZ, self.z_count)
        frequency = row >> 1
        value = cosine_of(z * frequency + (row & 1) * (self.z_count // 4), self.z_count)
        if doubled:
            value = jnp.where(frequency > 0, 2.0 * value, value)
        return value.astype(BF16)

    def expanded(self, small):
        row, column = grid_of(2 * MZ, small.shape[1])
        same = (row >> 1) == ((column >> 1) & (MZ - 1))
        blocks = []
        for g in range(small.shape[0] // 2):
            value = jnp.where((row & 1) == 0, small[2 * g : 2 * g + 1], small[2 * g + 1 : 2 * g + 2])
            blocks.append(jnp.where(same, value, 0.0))
        return jnp.concatenate(blocks, axis=0)

    def forward_x(self, first):
        outer, inner = self.here()
        row, column = grid_of(2 * self.outer, 4 * MZ)
        x = 2 * outer + (inner ^ (column // (2 * MZ)))
        frequency = self.frequency(2 * self.listed(row >> 1, first, inner) + inner)
        quarter = self.wide // 4
        small = cosine_of(x * frequency + quarter * ((row & 1) - (column & 1)), self.wide)
        return self.expanded(small)

    def inverse_x(self, first):
        outer, inner = self.here()
        row, column = grid_of(4, self.outer * 2 * MZ)
        x = 2 * outer + (inner ^ (row >> 1))
        frequency = self.frequency(2 * self.listed(column // (2 * MZ), first, inner) + inner)
        quarter = self.wide // 4
        small = cosine_of(x * frequency + quarter * ((column & 1) - (row & 1)), self.wide)
        return self.expanded(small).astype(BF16)


def repeat_rows(out_ref, block):
    height = block.shape[0]
    for first in range(0, out_ref.shape[0], height):
        out_ref[first : first + height] = block


def write_pieces(place, send_ref, block, shares):
    step, half = 2 * place.kz, place.lanes // 2
    height = send_ref.shape[0] // place.partners
    for p in range(place.partners):
        own = block[p * step % block.shape[0] :][:step]
        first = p * height
        send_ref[first : first + step] = own[:, :half]
        send_ref[first + step : first + 2 * step] = own[:, half:]
        send_ref[first + 2 * step : first + height] = shares[p * 8 % shares.shape[0] :][:8]


def read_pieces(place, pieces_ref):
    step = 2 * place.kz
    if pieces_ref.shape[1] == place.lanes:
        return pieces_ref[...], None
    height = pieces_ref.shape[0] // place.partners
    blocks, shares = [], []
    for p in range(place.partners):
        first = p * height
        left = pieces_ref[first : first + step]
        right = pieces_ref[first + step : first + 2 * step]
        blocks.append(jnp.concatenate([left, right], axis=1))
        shares.append(pieces_ref[first + 2 * step : first + height].astype(F32))
    return jnp.concatenate(blocks, axis=0), shares


def lane_sum(values, width):
    while values.shape[1] > 128:
        half = values.shape[1] // 2
        values = values[:, :half] + values[:, half:]
    if values.shape[1] < 128:
        blocks = range(0, values.shape[1], width)
        return sum(values[:, first : first + width] for first in blocks)
    shift = 64
    while shift >= width:
        values = values + pltpu.roll(values, shift, 1)
        shift //= 2
    return values[:, :width]


def diagonal_blocks(count, width, rows):
    row, lane = grid_of(count, count * width)
    pattern = jnp.where(row == lane // width, 1.0, 0.0)
    return jnp.concatenate([pattern] * (rows // count), axis=0)


def analysed(place, pieces, y_forward, copies):
    height = 2 * MZ
    turned = sum(
        pieces[first : first + height].astype(F32) for first in range(0, pieces.shape[0], height)
    )
    channels = place.channels
    lines = jnp.concatenate(
        [turned[:, y * channels : (y + 1) * channels] for y in range(place.rows_y)], axis=0
    )
    return dot(y_forward, jnp.concatenate([lines.astype(BF16)] * copies, axis=1))


def spread_lines(place, modes, y_inverse):
    lines = dot(y_inverse, modes)
    step = 2 * place.kz
    blocks = []
    for n in range(place.narrow):
        first = n * place.rows_y
        parts = [lines[(first + y) * step : (first + y + 1) * step] for y in range(place.rows_y)]
        blocks.append(jnp.concatenate(parts, axis=1))
    return jnp.concatenate(blocks, axis=0).astype(BF16)


def turn_matrix(place, forward):
    channels, rows_y = place.channels, place.rows_y

    def same(row, column):
        if forward:
            row, column = column, row
        return (row % channels == column // rows_y) & (row // channels == column % rows_y)

    return selector(place.lanes, place.lanes, same)


def side_by_side(values, count):
    height = values.shape[0] // count
    return jnp.concatenate([values[y * height : (y + 1) * height] for y in range(count)], axis=1)


def one_below_other(values, count):
    width = values.shape[1] // count
    return jnp.concatenate([values[:, y * width : (y + 1) * width] for y in range(count)], axis=0)


def own_kernel(place, field_ref, field_out_ref, spectra_ref, z_table_ref, turn_ref, tables_ref):
    z_table = place.z_table(False)
    turned = dot(turn_matrix(place, False), field_ref[...]).astype(BF16)
    field_out_ref[...] = side_by_side(turned, place.rows_y)
    spectra_ref[...] = dot_nt(z_table, turned).astype(BF16)
    z_table_ref[...] = z_table
    turn_ref[...] = turn_matrix(place, True)
    tables_ref[...] = jnp.concatenate(halves(place.forward_x(place.firsts[0])), axis=1)


def start_kernel(place, spectra_ref, twin_ref, z_table_ref, turn_ref, tables_ref, send_ref):
    twin = dot_nt(z_table_ref[...], twin_ref[...]).astype(BF16)
    twin = dot(twin, turn_ref[...]).astype(BF16)
    values = jnp.concatenate([spectra_ref[...], twin], axis=0)
    send_ref[...] = dot(tables_ref[...], jnp.concatenate([values, values], axis=0)).astype(BF16)


def pack_kernel(place, weight_ref, packed_ref, inverse_ref):
    inverse_ref[...] = place.inverse_x(place.firsts[1])
    modes, kz, _, channels, _ = weight_ref.shape
    for q in range(modes // 4):
        parts = [weight_ref[4 * q + j // 2, :, j % 2] for j in range(8)]
        packed = jnp.concatenate(parts, axis=-1).reshape(kz * channels, 8 * channels)
        packed_ref[q] = packed.astype(BF16)


def ready_kernel(place, field_ref, mix_ref, mix_bias_ref, head_ref, *refs):
    pointwise_ref, head_out_ref, z_doubled_ref = refs
    pointwise_ref[...] = dot_tn(mix_ref[...], field_ref[...]) + mix_bias_ref[...]
    head_out_ref[...] = jnp.transpose(head_ref[...].astype(F32)).astype(BF16)
    z_doubled_ref[...] = place.z_table(True)


def fold_kernel(place, own_ref, got_ref, tables_ref, *refs):
    values = jnp.concatenate([own_ref[...], got_ref[...]], axis=0)
    values = jnp.concatenate([values, values], axis=0)
    partial = dot(tables_ref[...], values).astype(BF16)
    if place.fold:
        shares_ref, send_ref = refs
        write_pieces(place, send_ref, partial, shares_ref[...])
    else:
        refs[0][...] = partial


def mode_kernel(
    place, pieces_ref, y_forward_ref, y_inverse_ref, weight_ref, spectrum_ref, send_ref
):
    kz, channels = place.kz, place.channels
    spectrum = analysed(place, pieces_ref[...], y_forward_ref[...], kz)
    spectrum_ref[...] = spectrum[:, :channels]
    diagonal = diagonal_blocks(kz, channels, 8 * kz)
    mixed = []
    for q in range(place.modes // 4):
        left = (spectrum[q * 8 * kz : (q + 1) * 8 * kz] * diagonal).astype(BF16)
        product = dot(left, weight_ref[q])
        for j in range(4):
            own = product[j * 2 * kz : (j + 1) * 2 * kz, j * 2 * channels : (j + 1) * 2 * channels]
            real, imag = own[:, :channels], own[:, channels:]
            mixed.append(real[:kz] - imag[kz:])
            mixed.append(imag[:kz] + real[kz:])
    mode = jnp.concatenate(mixed, axis=0).astype(BF16)
    repeat_rows(send_ref, spread_lines(place, mode, y_inverse_ref[...]))


def part_kernel(place, pieces_ref, table_ref, *refs):
    pieces, shares = read_pieces(place, pieces_ref)
    lines = dot(table_ref[...], pieces)
    height = 2 * MZ
    if shares is None:
        own_ref, send_ref = refs
        own_ref[...] = lines[:height]
        send_ref[...] = lines[height:].astype(BF16)
        return
    _, own_ref, send_ref, sums_ref = refs
    own_ref[...] = lines[:height]
    send_ref[:height] = lines[height:].astype(BF16)
    got = jnp.concatenate(shares, axis=0).astype(BF16)
    channels = place.channels

    def chosen(part):
        def condition(row, column):
            owner, source = (row % channels) // 2, column // 8
            return (
                (owner == source)
                & (column % 8 == 4 * part + 2 * (row // channels) + row % 2)
            )

        return dot(selector(2 * channels, got.shape[0], condition), got)

    high, low = chosen(0), chosen(1)
    sums_ref[...] = high + low
    send_ref[height:] = jnp.concatenate([high, low], axis=1).astype(BF16)


def normal(values):
    scaled = pl.reciprocal(1.0 + jnp.abs(TAIL_SLOPE * values), approx=True)
    decay = jnp.exp2(values * values * (-0.5 / math.log(2.0)))
    tail = TAIL[-1]
    for factor in TAIL[-2::-1]:
        tail = tail * scaled + factor
    tail = tail * (scaled * decay)
    cumulative = jnp.where(values > 0.0, 1.0 - tail, tail)
    return values * cumulative, cumulative + values * (decay * (1.0 / math.sqrt(2.0 * math.pi)))


def cell_kernel(place, *refs):
    own_ref, got_ref, z_table_ref, pointwise_ref, head_ref, head_turned_ref = refs[:6]
    head_bias_ref, out_column_ref, cotangent_ref = refs[6:9]
    prediction_ref, grad_pre_ref, send_ref, hidden_ref, head_slope_ref = refs[9:]
    rows_y, z_count = place.rows_y, place.z_count
    z_table = z_table_ref[...]
    lines = (own_ref[...] + got_ref[...].astype(F32)).astype(BF16)
    pre_act = side_by_side(dot_tn(lines, z_table), rows_y) + pointwise_ref[...]
    head, head_turned = head_ref[...], head_turned_ref[...]
    head_bias, out_column = head_bias_ref[...], out_column_ref[...]
    width = 2 * z_count
    slopes, head_pre = [], []
    for first in range(0, rows_y * z_count, width):
        value, slope = normal(pre_act[:, first : first + width])
        hidden = value.astype(BF16)
        hidden_ref[:, first : first + width] = hidden
        slopes.append(slope)
        head_pre.append(dot(head_turned, hidden))
    gradients = []
    for index, first in enumerate(range(0, rows_y, 2)):
        target = jnp.concatenate(
            [cotangent_ref[y : y + 1] for y in range(first, first + 2)], axis=1
        )
        predicted, parts = 0.0, []
        for top in range(0, head_bias.shape[0], BLOCK):
            rows = slice(top, top + BLOCK)
            active, slope = normal(head_pre[index][rows] + head_bias[rows])
            predicted = predicted + active.astype(BF16).astype(F32) * out_column[rows]
            parts.append((target * out_column[rows] * slope).astype(BF16))
        predicted = jnp.sum(predicted, axis=0, keepdims=True)
        prediction_ref[first : first + 1] = predicted[:, :z_count]
        prediction_ref[first + 1 : first + 2] = predicted[:, z_count:]
        head_slope = jnp.concatenate(parts, axis=0)
        head_slope_ref[:, first * z_count : first * z_count + width] = head_slope
        gradients.append((dot(head, head_slope) * slopes[index]).astype(BF16))
    gradient = jnp.concatenate(gradients, axis=1)
    grad_pre_ref[...] = gradient
    send_ref[...] = dot_nt(z_table, one_below_other(gradient, rows_y)).astype(BF16)


def sums_kernel(place, field_ref, gradient_ref, hidden_ref, head_slope_ref, *refs):
    refs[-1][...] = jnp.concatenate(halves(place.forward_x(place.firsts[2])), axis=1)
    grad_mix = dot_nt(field_ref[...], gradient_ref[...])
    grad_head = dot_nt(hidden_ref[...], head_slope_ref[...])
    if not place.fold:
        refs[0][...] = grad_mix
        refs[1][...] = grad_head
        return
    channels, hidden_units = grad_head.shape
    rest = jnp.zeros((channels, hidden_units - channels), F32)
    wide_mix = jnp.concatenate([grad_mix, rest], axis=1)
    high, low = halves(jnp.concatenate([grad_head, wide_mix], axis=0))
    split = jnp.concatenate([high, low], axis=0)
    place_of = selector(
        8 * place.partners,
        4 * channels,
        lambda row, column: (column % channels == 2 * (row // 8) + row % 2)
        & (column // channels == (row % 8) // 2),
    )
    refs[0][...] = dot(place_of, split).astype(BF16)


def back_kernel(
    place, pieces_ref, y_forward_ref, y_inverse_ref, weight_ref, adjoint_ref, send_ref
):
    kz, channels = place.kz, place.channels
    pieces, shares = read_pieces(place, pieces_ref)
    adjoint = analysed(place, pieces, y_forward_ref[...], 1)
    adjoint_ref[...] = adjoint
    turned = []
    for first in range(0, adjoint.shape[0], 2 * kz):
        turned += [adjoint[first + kz : first + 2 * kz], -adjoint[first : first + kz]]
    left = jnp.concatenate([adjoint, jnp.concatenate(turned, axis=0)], axis=1)
    left = jnp.concatenate([left] * 4, axis=1)
    row, lane = grid_of(8 * kz, 8 * channels)
    same = jnp.where(row // (2 * kz) == lane // (2 * channels), 1.0, 0.0)
    diagonal = diagonal_blocks(kz, channels, 8 * kz)
    block = 8 * kz
    pulled = []
    for q in range(place.modes // 4):
        own = (left[q * block : (q + 1) * block] * same).astype(BF16)
        pulled.append(lane_sum(dot_nt(own, weight_ref[q]) * diagonal, channels))
    modes_back = jnp.concatenate(pulled, axis=0).astype(BF16)
    block = spread_lines(place, modes_back, y_inverse_ref[...])
    if shares is None:
        repeat_rows(send_ref, block)
        return
    total = sum(shares[1:], shares[0])
    high, low = halves(total[0:4] + total[4:8])
    split = jnp.concatenate([high.astype(F32), low.astype(F32)], axis=0)
    write_pieces(place, send_ref, block, split.astype(BF16))


def outer_kernel(spectrum_ref, adjoint_ref, out_ref, done_ref):
    done_ref[...] = jnp.zeros(done_ref.shape, F32)
    modes, kz = out_ref.shape[:2]
    for j in range(modes):
        columns = jnp.transpose(spectrum_ref[j])
        adjoint = adjoint_ref[j]
        for k in range(kz):
            s_real, s_imag = columns[:, k : k + 1], columns[:, kz + k : kz + k + 1]
            a_real, a_imag = adjoint[k : k + 1], adjoint[kz + k : kz + k + 1]
            out_ref[j, k, 0] = s_real * a_real + s_imag * a_imag
            out_ref[j, k, 1] = s_real * a_imag - s_imag * a_real


def pointwise_kernel(place, mix_ref, gradient_ref, out_ref, z_plain_ref, turn_ref):
    z_plain_ref[...] = place.z_table(False)
    turn_ref[...] = turn_matrix(place, False)
    z_count = place.z_count
    product = dot(mix_ref[...], gradient_ref[...])
    for y in range(place.rows_y):
        out_ref[:, y, :] = product[:, y * z_count : (y + 1) * z_count]


def finish_kernel(place, *refs):
    own_ref, got_ref, z_table_ref, turn_ref, pointwise_ref, prediction_ref = refs[:6]
    refs = refs[6:]
    height = 2 * MZ
    channels = place.channels
    lines = (own_ref[...] + got_ref[:height].astype(F32)).astype(BF16)
    lines = dot(lines, turn_ref[...]).astype(BF16)
    pointwise = pointwise_ref[...].reshape(place.lanes, place.z_count)
    grad_field = (dot_tn(lines, z_table_ref[...]) + pointwise).astype(BF16)
    if not place.fold:
        refs[0][...] = grad_field
        refs[1][...] = prediction_ref[...]
        return
    sums_ref, grad_field_ref, out_ref, grad_mix_ref, grad_head_ref = refs
    grad_field_ref[...] = grad_field
    out_ref[...] = prediction_ref[...]
    got = got_ref[height:].astype(F32)
    width = sums_ref.shape[1]
    total = sums_ref[...] + got[:, :width] + got[:, width:]
    grad_head_ref[...] = total[:channels]
    grad_mix_ref[...] = total[channels:, :channels]


def call(kernel, outs, name, **spec):
    return pl.pallas_call(
        kernel,
        out_shape=[jax.ShapeDtypeStruct(shape, dtype) for shape, dtype in outs],
        compiler_params=pltpu.CompilerParams(vmem_limit_bytes=VMEM_LIMIT),
        cost_estimate=pl.CostEstimate(flops=1 << 22, bytes_accessed=1 << 19, transcendentals=0),
        name=name,
        **spec,
    )


def body(
    lifted_field,
    spectral_weight,
    mix_weight,
    mix_bias,
    head_weight,
    head_bias,
    out_weight,
    cotangent,
):
    wide = lax.axis_size("wide")
    narrow = lax.axis_size("narrow")
    devices = wide * narrow
    _, channels, rows_y, z_count = lifted_field.shape
    modes, kz = spectral_weight.shape[:2]
    hidden_units = head_weight.shape[1]
    cells = channels * rows_y
    place = Place(wide, narrow, kz, modes, rows_y, channels, z_count, False)
    place.fold = 2 * place.partners == channels and hidden_units == 128 and cells == 256 and kz % 8 == 0
    height = 2 * MZ
    step = 2 * kz
    partners = place.partners
    mode_lines = modes * 2 * kz

    y_forward, y_inverse = y_tables(rows_y * narrow, rows_y, kz, modes)
    if len(y_forward) > 1:
        block = lax.axis_index("wide") % len(y_forward)
        y_forward = lax.dynamic_index_in_dim(jnp.asarray(y_forward), block, 0, False)
        y_inverse = lax.dynamic_index_in_dim(jnp.asarray(y_inverse), block, 0, False)
    else:
        y_forward, y_inverse = jnp.asarray(y_forward[0]), jnp.asarray(y_inverse[0])

    def to_twin(send):
        pairs = [(p, p ^ narrow) for p in range(devices)]
        return lax.ppermute(send, ("wide", "narrow"), pairs)

    def exchange(send, transform):
        first = place.firsts[transform]
        groups = [
            [
                (2 * place.listed(outer, first, inner) + inner) * narrow + n
                for outer in range(place.outer)
                for n in range(narrow)
            ]
            for inner in range(2)
        ]
        pieces = send.reshape(partners, -1, send.shape[1])
        got = lax.all_to_all(
            pieces, ("wide", "narrow"), 0, 0, axis_index_groups=groups, tiled=True
        )
        return got.reshape(send.shape)

    plain = ((partners * step, cells), BF16)
    shared = ((partners * (2 * step + 8), cells // 2), BF16) if place.fold else plain
    twin_plain = ((height, cells), BF16)
    twin_shared = ((height + 2 * channels, cells), BF16) if place.fold else twin_plain
    sums_shape = ((2 * channels, hidden_units), F32)
    own_lines = ((height, cells), F32)
    across = (channels, rows_y * z_count)

    def run(kernel, outs, name, **spec):
        return call(functools.partial(kernel, place), outs, name, **spec)

    flat_field = lifted_field.reshape(cells, z_count)
    twin_field = to_twin(flat_field)
    tables_shape = ((wide // 2 * height, 4 * height), BF16)
    field, spectra, *tables = run(
        own_kernel,
        [(across, BF16), twin_plain, ((height, z_count), BF16), ((cells, cells), BF16), tables_shape],
        "own",
    )(flat_field)
    (send,) = run(start_kernel, [plain], "start")(spectra, twin_field, *tables)
    packed_shape = ((modes // 4, kz * channels, 8 * channels), BF16)
    inverse_shape = ((2 * height, wide // 2 * height), BF16)
    weight, inverse = run(pack_kernel, [packed_shape, inverse_shape], "pack")(spectral_weight)
    spectrum, send = run(mode_kernel, [((mode_lines, channels), F32), plain], "mode")(
        exchange(send, 0), y_forward, y_inverse, weight
    )
    own, send = run(part_kernel, [own_lines, twin_plain], "part")(exchange(send, 1), inverse)
    pointwise, head_turned, z_doubled = run(
        ready_kernel,
        [(across, F32), ((hidden_units, channels), BF16), ((height, z_count), BF16)],
        "ready",
    )(field, mix_weight, mix_bias[:, None], head_weight)
    prediction, grad_pre, send, hidden, head_slope = run(
        cell_kernel,
        [
            ((rows_y, z_count), F32),
            (across, BF16),
            twin_plain,
            (across, BF16),
            ((hidden_units, rows_y * z_count), BF16),
        ],
        "cell",
    )(
        own,
        to_twin(send),
        z_doubled,
        pointwise,
        head_weight,
        head_turned,
        head_bias[:, None],
        out_weight.astype(F32)[:, None],
        cotangent[0],
    )
    if place.fold:
        outs = [((8 * partners, hidden_units), BF16)]
    else:
        outs = [((channels, channels), F32), ((channels, hidden_units), F32)]
    outs += [((wide // 2 * height, 4 * height), BF16)]
    *sums, forward = run(sums_kernel, outs, "sums")(field, grad_pre, hidden, head_slope)
    if not place.fold:
        totals = lax.psum(tuple(sums), ("wide", "narrow"))
        sums = []
    (send,) = run(fold_kernel, [shared], "fold")(send, to_twin(send), forward, *sums)
    adjoint, send = run(back_kernel, [((mode_lines, channels), F32), shared], "back")(
        exchange(send, 2), y_forward, y_inverse, weight
    )
    some = max(1, modes // 4)
    grad_spectral, done = pl.pallas_call(
        outer_kernel,
        grid=(modes // some,),
        in_specs=[pl.BlockSpec((some, 2 * kz, channels), lambda j: (j, 0, 0))] * 2,
        out_specs=[
            pl.BlockSpec((some, kz, 2, channels, channels), lambda j: (j, 0, 0, 0, 0)),
            pl.BlockSpec((8, 128), lambda j: (0, 0)),
        ],
        out_shape=[
            jax.ShapeDtypeStruct(spectral_weight.shape, F32),
            jax.ShapeDtypeStruct((8, 128), F32),
        ],
        compiler_params=pltpu.CompilerParams(vmem_limit_bytes=VMEM_LIMIT),
        cost_estimate=pl.CostEstimate(flops=1 << 22, bytes_accessed=5 << 20, transcendentals=0),
        name="outer",
    )(spectrum.reshape(modes, 2 * kz, channels), adjoint.reshape(modes, 2 * kz, channels))
    pointwise, z_plain, turn = run(
        pointwise_kernel,
        [
            ((channels, rows_y, z_count), F32),
            ((height, z_count), BF16),
            ((cells, cells), BF16),
        ],
        "pointwise",
    )(mix_weight, grad_pre)
    outs = [own_lines, twin_shared] + ([sums_shape] if place.fold else [])
    after = (done,) if place.fold else ()
    own, send, *sums = run(part_kernel, outs, "part")(exchange(send, 3), inverse, *after)
    outs = [((cells, z_count), BF16), ((rows_y, z_count), F32)]
    if place.fold:
        outs += [((channels, channels), F32), ((channels, hidden_units), F32)]
    grad_field, prediction, *summed = run(finish_kernel, outs, "finish")(
        own, to_twin(send), z_plain, turn, pointwise, prediction, *sums
    )
    grad_mix, grad_head = summed if place.fold else totals
    return (
        prediction[None],
        grad_field.reshape(lifted_field.shape),
        grad_spectral,
        grad_mix,
        grad_head,
    )


def solution(mesh):
    return jax.shard_map(
        body,
        mesh=mesh,
        in_specs=(
            P("wide", None, "narrow", None),
            P("wide", "narrow", None, None, None),
            P(),
            P(),
            P(),
            P(),
            P(),
            P("wide", "narrow", None),
        ),
        out_specs=(
            P("wide", "narrow", None),
            P("wide", None, "narrow", None),
            P("wide", "narrow", None, None, None),
            P(),
            P(),
        ),
        check_vma=False,
    )
```
